32 devices in a mesh: dp: 8 (over z, x), space: 4 (over y, core).
Axes of the slice: x: 2, y: 2, z: 4, core: 2. Of those that a mesh axis runs over, the one named last changes fastest.
Arguments:
- branch_zero: float32 [16, 128, 4096], P('dp', 'space'), may hold values from -6 to 6
- branch_one: float32 [16, 64, 4096], P('dp', 'space'), may hold values from -6 to 6
- branch_two: float32 [16, 32, 4096], P('dp', 'space'), may hold values from -6 to 6
- branch_three: float32 [16, 16, 4096], P('dp', 'space'), may hold values from -6 to 6
- convs_zero: float32 [18432], P(('dp', 'space')), may hold values from -0.375 to 0.375
- convs_one: float32 [73728], P(('dp', 'space')), may hold values from -0.25 to 0.25
- convs_two: float32 [294912], P(('dp', 'space')), may hold values from -0.1875 to 0.1875
- convs_three: float32 [1179648], P(('dp', 'space')), may hold values from -0.125 to 0.125
- unite_one: float32 [2048], P(('dp', 'space')), may hold values from -0.75 to 0.75
- unite_two: float32 [4096], P(('dp', 'space')), may hold values from -0.5 to 0.5
- unite_three: float32 [8192], P(('dp', 'space')), may hold values from -0.375 to 0.375
- norm_gain: float32 [1056], replicated, may hold values from 0.1 to 1.9
- norm_shift: float32 [1056], replicated, may hold values from -3 to 3
- head_weight: float32 [32, 17], replicated, may hold values from -1 to 1
- head_bias: float32 [17], replicated, may hold values from -3 to 3
- targets: float32 [16, 17, 128, 128], P('dp', None, 'space'), may hold values from -6 to 6
- crowd_mask: int32 [16, 128, 128], P('dp', 'space'), may hold values 0 or 1
- person_count: int32 [16], P('dp'), may hold values from 1 to 8
- flip_order: int32 [17], replicated, may hold values from 0 to 16, each once
Outputs:
- loss_value: float32 [], replicated
- heat_mean: float32 [16, 17, 128, 128], P('dp', None, 'space')
- grad_branch_zero: float32 [16, 128, 4096], P('dp', 'space')
- grad_branch_one: float32 [16, 64, 4096], P('dp', 'space')
- grad_branch_two: float32 [16, 32, 4096], P('dp', 'space')
- grad_branch_three: float32 [16, 16, 4096], P('dp', 'space')
- grad_convs_zero: float32 [18432], P(('dp', 'space'))
- grad_convs_one: float32 [73728], P(('dp', 'space'))
- grad_convs_two: float32 [294912], P(('dp', 'space'))
- grad_convs_three: float32 [1179648], P(('dp', 'space'))
- grad_unite_one: float32 [2048], P(('dp', 'space'))
- grad_unite_two: float32 [4096], P(('dp', 'space'))
- grad_unite_three: float32 [8192], P(('dp', 'space'))
- grad_norm_gain: float32 [1056], replicated
- grad_norm_shift: float32 [1056], replicated
- grad_head_weight: float32 [32, 17], replicated
- grad_head_bias: float32 [17], replicated
The draws below stay inside these ranges and needn't reach their ends.
Inputs may be any that keep to these rules, and one draw needn't show every extreme that they name: flip_order is a permutation of the 17 joints.
All inputs are finite; a program needn't handle non-finite values. No bound on the sum of `crowd_mask` on one device may be relied on, other than what follows from the above.
Results may differ from the reference program's by a relative error of at most 0.0003.
Values sent between devices are 32-bit elements; how exact they have to be, the bound alone decides.
No kernel may reach another device: no remote copies, remote signals or barrier semaphores. Data moves between devices by JAX's collectives and lax.ppermute only.
A program may use at most 256 MiB of HBM per device.

```python
from functools import partial
import jax
import jax.numpy as jnp
from jax import lax

C0 = 32
C1 = 64
C2 = 128
C3 = 256
J = 17
H0 = 128
IMAGES = 16


def touch_ends(result, own_key, low, largest):
    place = [jax.random.randint(jax.random.fold_in(own_key, axis), (), 0, length) for axis, length in enumerate(result.shape)]
    widest = result.shape.index(max(result.shape))
    beside = place[:widest] + [(place[widest] + 1) % result.shape[widest]] + place[widest + 1:]
    return result.at[tuple(place)].set(low).at[tuple(beside)].set(largest)


def steps_of(key, shape, split, least, top_value):
    level = 1.0
    for position, blocks in split:
        steps = jax.random.uniform(jax.random.fold_in(jax.random.fold_in(key, 6), position), (blocks,), jnp.float32, least / len(split), top_value / len(split))
        level = level * jnp.repeat(jnp.exp(steps), shape[position] // blocks).reshape((-1,) + (1,) * (len(shape) - 1 - position))
    return level


def bell_draw(rng, dims, deviation, limit, shards=(), dtype=jnp.bfloat16):
    level = steps_of(rng, dims, shards, -0.22, 0.18) if shards else 1.0
    values = jax.random.normal(rng, dims, jnp.float32) * deviation * level
    return jnp.minimum(jnp.maximum(values, -limit), limit).astype(dtype)


def setup_inputs(seed: int = 0) -> dict:
    splits = jax.random.split(jax.random.key(seed), 20)
    branch_zero = bell_draw(splits[0], (IMAGES, H0, H0 * C0), 1.0, 6.0, ((0, 8), (1, 4)), jnp.float32)
    branch_one = bell_draw(splits[1], (IMAGES, H0 // 2, (H0 // 2) * C1), 1.0, 6.0, ((0, 8), (1, 4)), jnp.float32)
    branch_two = bell_draw(splits[2], (IMAGES, H0 // 4, (H0 // 4) * C2), 1.0, 6.0, ((0, 8), (1, 4)), jnp.float32)
    branch_three = bell_draw(splits[3], (IMAGES, H0 // 8, (H0 // 8) * C3), 1.0, 6.0, ((0, 8), (1, 4)), jnp.float32)
    convs_zero = bell_draw(splits[4], (18 * C0 * C0,), (9 * C0) ** -0.5, 0.375, ((0, 32),), jnp.float32)
    convs_one = bell_draw(splits[5], (18 * C1 * C1,), (9 * C1) ** -0.5, 0.25, ((0, 32),), jnp.float32)
    convs_two = bell_draw(splits[6], (18 * C2 * C2,), (9 * C2) ** -0.5, 0.1875, ((0, 32),), jnp.float32)
    convs_three = bell_draw(splits[7], (18 * C3 * C3,), (9 * C3) ** -0.5, 0.125, ((0, 32),), jnp.float32)
    unite_one = bell_draw(splits[8], (C1 * C0,), C1 ** -0.5, 0.75, ((0, 32),), jnp.float32)
    unite_two = bell_draw(splits[9], (C2 * C0,), C2 ** -0.5, 0.5, ((0, 32),), jnp.float32)
    unite_three = bell_draw(splits[10], (C3 * C0,), C3 ** -0.5, 0.375, ((0, 32),), jnp.float32)
    norm_gain = jnp.clip(1.0 + 0.18 * jax.random.normal(splits[11], (2 * (C0 + C1 + C2 + C3) + 3 * C0,), jnp.float32), 0.1, 1.9)
    norm_shift = bell_draw(splits[12], (2 * (C0 + C1 + C2 + C3) + 3 * C0,), 0.5, 3.0, (), jnp.float32)
    head_weight = bell_draw(splits[13], (C0, J), C0 ** -0.5, 1.0, (), jnp.float32)
    head_bias = bell_draw(splits[14], (J,), 0.5, 3.0, (), jnp.float32)
    targets = bell_draw(splits[15], (IMAGES, J, H0, H0), 1.0, 6.0, ((0, 8), (2, 4)), jnp.float32)
    crowd_mask = touch_ends((jax.random.randint(splits[16], (IMAGES, H0, H0), 0, 8) < 7).astype(jnp.int32), jax.random.fold_in(splits[16], 1), 0, 1)
    person_count = touch_ends(jax.random.randint(splits[17], (IMAGES,), 1, 9), jax.random.fold_in(splits[17], 1), 1, 8).astype(jnp.int32)
    flip_order = jax.random.permutation(splits[18], J).astype(jnp.int32)
    return {"branch_zero": branch_zero, "branch_one": branch_one, "branch_two": branch_two, "branch_three": branch_three, "convs_zero": convs_zero, "convs_one": convs_one, "convs_two": convs_two, "convs_three": convs_three, "unite_one": unite_one, "unite_two": unite_two, "unite_three": unite_three, "norm_gain": norm_gain, "norm_shift": norm_shift, "head_weight": head_weight, "head_bias": head_bias, "targets": targets, "crowd_mask": crowd_mask, "person_count": person_count, "flip_order": flip_order}


highest = lax.Precision.HIGHEST
epsilon = 1e-05

@jax.custom_vjp
def low(v):
    return lax.optimization_barrier(v.astype(jnp.bfloat16)).astype(jnp.float32)

@jax.custom_vjp
def low_back(v):
    return v

def low_keep(v):
    return (low(v), None)

def low_pass(kept, grad):
    return (grad,)

def back_keep(v):
    return (v, None)

def back_low(kept, grad):
    return (low(grad),)
low.defvjp(low_keep, low_pass)
low_back.defvjp(back_keep, back_low)

def norm_layout():
    places = []
    offset = 0
    for channels in (C0, C1, C2, C3):
        places.append((offset, channels))
        places.append((offset + channels, channels))
        offset = offset + 2 * channels
    for branch in range(3):
        places.append((offset + branch * C0, C0))
    return places

def conv_valid(padded, kernel, columns):
    images, extent, flat_size = padded.shape
    channels = flat_size // columns
    row_count = extent - 2
    out_channels = kernel.shape[3]
    cells = jnp.pad(padded.reshape(images, extent, columns, channels), ((0, 0), (0, 0), (1, 1), (0, 0)))
    summed = jnp.zeros((images, row_count, columns, out_channels), jnp.float32)
    for tap_row in range(3):
        for tap_col in range(3):
            window = cells[:, tap_row:tap_row + row_count, tap_col:tap_col + columns]
            summed = summed + jnp.einsum('nhwc,cd->nhwd', window, kernel[tap_row, tap_col], precision=highest)
    return summed.reshape(images, row_count, columns * out_channels)

@partial(jax.checkpoint, static_argnums=(2,))
def conv_kept(padded, kernel, columns):
    return conv_valid(padded, kernel, columns)

def conv_same(field_in, kernel, columns):
    return conv_kept(jnp.pad(field_in, ((0, 0), (1, 1), (0, 0))), kernel, columns)

def norm_apply(field_in, channels, gain_part, shift_part, given_stats):
    cells = field_in.reshape(-1, channels)
    if given_stats is None:
        mean_value = lax.optimization_barrier(jnp.mean(cells, 0))
        mean_square = lax.optimization_barrier(jnp.mean(cells * cells, 0))
        inv_std = lax.rsqrt(mean_square - mean_value * mean_value + epsilon)
    else:
        mean_value, inv_std = given_stats
    normed = (cells - mean_value) * inv_std * gain_part + shift_part
    return (normed.reshape(field_in.shape), (mean_value, inv_std))

def network(params, given_stats):
    channel_list = (C0, C1, C2, C3)
    places = norm_layout()
    gain = params[11]
    shift = params[12]
    head_weight = params[13]
    head_bias = params[14]
    norm_stats = []
    results = []
    for branch in range(4):
        channels = channel_list[branch]
        source = params[branch]
        columns = source.shape[2] // channels
        kernels = params[4 + branch].reshape(2, 3, 3, channels, channels)
        start_a = places[2 * branch][0]
        start_b = places[2 * branch + 1][0]
        stat_in = None if given_stats is None else given_stats[2 * branch]
        normed_a, stat_a = norm_apply(conv_same(source, kernels[0], columns), channels, gain[start_a:start_a + channels], shift[start_a:start_a + channels], stat_in)
        middle = jax.nn.silu(normed_a)
        stat_in = None if given_stats is None else given_stats[2 * branch + 1]
        normed_b, stat_b = norm_apply(conv_same(middle, kernels[1], columns), channels, gain[start_b:start_b + channels], shift[start_b:start_b + channels], stat_in)
        results.append(jax.nn.silu(normed_b + source))
        norm_stats.append(stat_a)
        norm_stats.append(stat_b)
    images, top_rows, top_flat = params[0].shape
    top_cols = top_flat // C0
    pre_sum = results[0]
    for level in range(1, 4):
        channels = channel_list[level]
        coarse = results[level]
        low_rows = coarse.shape[1]
        low_cols = coarse.shape[2] // channels
        mixer = params[7 + level].reshape(channels, C0)
        mixed = jnp.einsum('nrwc,cd->nrwd', coarse.reshape(images, low_rows, low_cols, channels), mixer, precision=highest)
        start = places[7 + level][0]
        stat_in = None if given_stats is None else given_stats[7 + level]
        normed, stat_f = norm_apply(mixed.reshape(images, low_rows, low_cols * C0), C0, gain[start:start + C0], shift[start:start + C0], stat_in)
        norm_stats.append(stat_f)
        factor = 2 ** level
        blocks = normed.reshape(images, low_rows, low_cols, C0)
        blocks = jnp.repeat(jnp.repeat(blocks, factor, 1), factor, 2)
        pre_sum = pre_sum + blocks.reshape(images, top_rows, top_flat)
    united_map = jax.nn.silu(pre_sum)
    heat_map = jnp.einsum('nrwc,cj->njrw', united_map.reshape(images, top_rows, top_cols, C0), head_weight, precision=highest)
    heat_map = heat_map + head_bias[None, :, None, None]
    return (heat_map, norm_stats)

def flip_field(field_in, channels):
    images, row_count, flat_size = field_in.shape
    return field_in.reshape(images, row_count, flat_size // channels, channels)[:, :, ::-1].reshape(field_in.shape)

def reference(branch_zero, branch_one, branch_two, branch_three, convs_zero, convs_one, convs_two, convs_three, unite_one, unite_two, unite_three, norm_gain, norm_shift, head_weight, head_bias, targets, crowd_mask, person_count, flip_order):
    params = (branch_zero, branch_one, branch_two, branch_three, convs_zero, convs_one, convs_two, convs_three, unite_one, unite_two, unite_three, norm_gain, norm_shift, head_weight, head_bias)
    weight_map = crowd_mask.astype(jnp.float32) / person_count.astype(jnp.float32)[:, None, None]

    def forward(*values):
        heat_map, norm_stats = network(values, None)
        error_map = heat_map - targets
        loss_value = jnp.sum(weight_map[:, None] * error_map * error_map) / heat_map.size
        return (loss_value, (heat_map, norm_stats))
    loss_value, pullback, extras = jax.vjp(forward, *params, has_aux=True)
    grads = pullback(jnp.ones((), jnp.float32))
    flipped = (flip_field(branch_zero, C0), flip_field(branch_one, C1), flip_field(branch_two, C2), flip_field(branch_three, C3))
    heat_flip, unused_stats = network(flipped + params[4:], extras[1])
    heat_back = jnp.take(heat_flip[:, :, :, ::-1], flip_order, axis=1)
    heat_mean = 0.5 * (extras[0] + heat_back)
    return (loss_value, heat_mean, grads[0], grads[1], grads[2], grads[3], grads[4], grads[5], grads[6], grads[7], grads[8], grads[9], grads[10], grads[11], grads[12], grads[13], grads[14])
```

```python
import functools

import jax
import jax.numpy as jnp
import numpy as np
from jax import lax
from jax.experimental import pallas as pl
from jax.experimental.pallas import tpu as pltpu
from jax.sharding import PartitionSpec as P

C0 = 32
CHANNELS = (32, 64, 128, 256)
SIDES = (128, 128, 256, 512)
AXES = ("dp", "space")
epsilon = 1e-05
f32 = jnp.float32
high = lax.Precision.HIGH


def dot_nn(left, right):
    return lax.dot_general(left, right, (((1,), (0,)), ((), ())), precision=high, preferred_element_type=f32)


def dot_nt(left, right):
    return lax.dot_general(left, right, (((1,), (1,)), ((), ())), precision=high, preferred_element_type=f32)


def dot_tn(left, right):
    return lax.dot_general(left, right, (((0,), (0,)), ((), ())), precision=high, preferred_element_type=f32)


def sigmoid(value):
    return 1.0 / (1.0 + jnp.exp(-value))


def silu(value):
    return value * sigmoid(value)


def silu_slope(value):
    sigma = sigmoid(value)
    return sigma * (1.0 + value * (1.0 - sigma))


def fold(row, channels):
    step = channels
    while step < 256:
        row = row + pltpu.roll(row, step, 1)
        step = 2 * step
    return row


def column_sum(value):
    return jnp.sum(value, axis=0, keepdims=True)


def moments(sums, channels, count):
    mean = fold(sums[0:1], channels) / count
    square = fold(sums[1:2], channels) / count
    return mean, lax.rsqrt(square - mean * mean + epsilon)


def affine(stats, gain, shift):
    scale = stats[1] * gain
    return scale, shift - stats[0] * scale


def load_rows(ref, first, count):
    lanes = ref.shape[2]
    return ref[:, first * 16 : (first + count) * 16, :].reshape(2 * count * 16, lanes)


def group_index(rows):
    return lax.broadcasted_iota(jnp.int32, (rows, 128), 0) % 16


def side_columns(value, channels):
    rows = value.shape[0]
    group = group_index(rows)
    lane = lax.broadcasted_iota(jnp.int32, (rows, 128), 1)

    def before(part):
        return jnp.where(group == 0, 0.0, pltpu.roll(part, 1, 0))

    def after(part):
        return jnp.where(group == 15, 0.0, pltpu.roll(part, rows - 1, 0))

    low, upper = value[:, :128], value[:, 128:]
    if channels == 256:
        return jnp.concatenate([before(low), before(upper), after(low), after(upper)], axis=1)
    if channels == 128:
        return jnp.concatenate([before(upper), after(low)], axis=1)
    return jnp.where(
        lane < channels, after(low), jnp.where(lane >= 128 - channels, before(upper), 0.0)
    )


def build_sides(source, side, channels):
    rows = source.shape[1]
    for image in range(2):
        side[image] = side_columns(source[image], channels)


def patches(source, side, count):
    parts = []
    for tap_row in range(3):
        parts.append(load_rows(source, tap_row, count))
        parts.append(load_rows(side, tap_row, count))
    return jnp.concatenate(parts, axis=1)


def build_band(band, tap, branch, offset):
    channels = CHANNELS[branch]
    groups = 256 // channels
    side = SIDES[branch]
    height = 256 + side
    if channels < 256:
        band[:, offset : offset + 256] = jnp.zeros((3 * height, 256), f32)
    for tap_row in range(3):
        base = tap_row * height
        for tap_col in range(3):
            matrix = tap(tap_row, tap_col)
            for out in range(groups):
                place = out + tap_col - 1
                if place < 0:
                    row = base + 256 + (0 if channels >= 128 else 128 - channels)
                elif place >= groups:
                    row = base + 256 + (side // 2 if channels >= 128 else 0)
                else:
                    row = base + place * channels
                start = offset + out * channels
                band[row : row + channels, start : start + channels] = matrix


def collect_band(product, branch, emit):
    channels = CHANNELS[branch]
    groups = 256 // channels
    side = SIDES[branch]
    height = 256 + side
    for tap_row in range(3):
        base = tap_row * height
        for tap_col in range(3):
            total = None
            for out in range(groups):
                place = out + tap_col - 1
                if place < 0:
                    row = base + 256 + (0 if channels >= 128 else 128 - channels)
                elif place >= groups:
                    row = base + 256 + (side // 2 if channels >= 128 else 0)
                else:
                    row = base + place * channels
                start = out * channels
                if channels >= 128:
                    block = product[row : row + channels, start : start + channels]
                else:
                    tile = start // 128 * 128
                    block = product[row : row + channels, tile : tile + 128]
                    inner = start - tile
                    if inner:
                        block = pltpu.roll(block, 128 - inner, 1)
                total = block if total is None else total + block
            emit(tap_row, tap_col, total[:, :channels])


def tap_reader(ref, branch):
    channels = CHANNELS[branch]
    if channels == 256:

        def tap(tap_row, tap_col):
            first = (3 * tap_row + tap_col) * 512
            return jnp.concatenate(
                [ref[pl.ds(first, 256, stride=2), :], ref[pl.ds(first + 1, 256, stride=2), :]],
                axis=1,
            )

        return tap
    whole = ref[...].reshape(9 * channels, channels)

    def tap(tap_row, tap_col):
        first = (3 * tap_row + tap_col) * channels
        return whole[first : first + channels]

    return tap


def tap_writer(ref, scratch, branch):
    channels = CHANNELS[branch]

    def emit(tap_row, tap_col, value):
        place = 3 * tap_row + tap_col
        if channels == 256:
            ref[pl.ds(place * 512, 256, stride=2), :] = value[:, :128]
            ref[pl.ds(place * 512 + 1, 256, stride=2), :] = value[:, 128:]
        elif channels == 128:
            ref[place * 128 : place * 128 + 128, :] = value
        else:
            scratch[place * channels : (place + 1) * channels, :] = value

    def finish():
        if channels < 128:
            ref[...] = scratch[...].reshape(ref.shape)

    return emit, finish


def mirrored(tap):
    return lambda tap_row, tap_col: tap(tap_row, 2 - tap_col)


def turned(tap):
    return lambda tap_row, tap_col: jnp.transpose(tap(2 - tap_row, 2 - tap_col))


def mask_ends(value, rows, flags):
    place = lax.broadcasted_iota(jnp.int32, value.shape, 0) // 16 % (rows + 2)
    outside = ((place == 0) & (flags[0] == 0)) | ((place == rows + 1) & (flags[1] == 0))
    return jnp.where(outside, 0.0, value)


def mix_matrix(unite, branch):
    channels = CHANNELS[branch]
    groups = 256 // channels
    wide = jnp.concatenate([unite] * 8, axis=1)
    lane = lax.broadcasted_iota(jnp.int32, wide.shape, 1)
    span = 256 // groups
    return jnp.concatenate(
        [jnp.where(lane // span == place, wide, 0.0) for place in range(groups)], axis=0
    )


def split_refs(refs, *counts):
    out, first = [], 0
    for count in counts:
        out.append(refs[first : first + count])
        first += count
    assert first == len(refs)
    return out


def call(kernel, ins, outs, scratch=(), smem=0):
    specs = [pl.BlockSpec(memory_space=pltpu.SMEM)] * smem + [
        pl.BlockSpec(memory_space=pltpu.VMEM)
    ] * (len(ins) - smem)
    return pl.pallas_call(
        kernel,
        in_specs=specs,
        out_specs=[pl.BlockSpec(memory_space=pltpu.VMEM)] * len(outs),
        out_shape=[jax.ShapeDtypeStruct(shape, f32) for shape in outs],
        scratch_shapes=[pltpu.VMEM(shape, f32) for shape in scratch],
        compiler_params=pltpu.CompilerParams(vmem_limit_bytes=60 * 2**20),
    )(*ins)


def band_shape(branch, width):
    return (3 * (256 + SIDES[branch]), width)


def first_kernel(rows, *refs):
    xs, tops, bottoms, taps, tiles, mains, flips, sums, bands, sides = split_refs(
        refs, 4, 1, 1, 4, 4, 4, 4, 1, 4, 4
    )
    sums = sums[0]
    for branch in range(4):
        count = rows[branch]
        tile, side, band = tiles[branch], sides[branch], bands[branch]
        for image in range(2):
            for ref, start, first, extent in (
                (tops[0], 2 * branch, 0, 2),
                (xs[branch], 0, 2, count),
                (bottoms[0], 2 * branch, count + 2, 2),
            ):
                tile[image, first * 16 : (first + extent) * 16, :] = ref[
                    image, start : start + extent, :
                ].reshape(extent * 16, 256)
        build_sides(tile, side, CHANNELS[branch])
        tap = tap_reader(taps[branch], branch)
        build_band(band, tap, branch, 0)
        build_band(band, mirrored(tap), branch, 256)
        out = dot_nn(patches(tile, side, count + 2), band[...])
        out = out.reshape(2, (count + 2) * 16, 512)
        mains[branch][...] = out[:, :, :256]
        flips[branch][...] = out[:, :, 256:]
        inner = load_rows(mains[branch], 1, count)
        sums[2 * branch : 2 * branch + 1, :] = column_sum(inner)
        sums[2 * branch + 1 : 2 * branch + 2, :] = column_sum(inner * inner)


def second_kernel(rows, counts, flags, *refs):
    firsts, stat, norms, taps, outs, sums, hidden, bands, sides = split_refs(
        refs, 4, 1, 1, 4, 4, 1, 4, 4, 4
    )
    stat, norms, sums = stat[0], norms[0], sums[0]
    for branch in range(4):
        count, channels = rows[branch], CHANNELS[branch]
        stats = moments(stat[2 * branch : 2 * branch + 2, :], channels, counts[branch])
        gain = norms[2 * branch : 2 * branch + 1, :]
        shift = norms[11 + 2 * branch : 12 + 2 * branch, :]
        scale, offset = affine(stats, gain, shift)
        value = load_rows(firsts[branch], 0, count + 2) * scale + offset
        value = mask_ends(silu(value), count, flags)
        hidden[branch][...] = value.reshape(2, (count + 2) * 16, 256)
        build_sides(hidden[branch], sides[branch], channels)
        build_band(bands[branch], tap_reader(taps[branch], branch), branch, 0)
        out = dot_nn(patches(hidden[branch], sides[branch], count), bands[branch][...])
        outs[branch][...] = out
        sums[2 * branch : 2 * branch + 1, :] = column_sum(out)
        sums[2 * branch + 1 : 2 * branch + 2, :] = column_sum(out * out)


def second_flip_kernel(rows, counts, flags, *refs):
    firsts, stat, norms, taps, outs, hidden, bands, sides = split_refs(refs, 4, 1, 1, 4, 4, 4, 4, 4)
    stat, norms = stat[0], norms[0]
    for branch in range(4):
        count, channels = rows[branch], CHANNELS[branch]
        stats = moments(stat[2 * branch : 2 * branch + 2, :], channels, counts[branch])
        scale, offset = affine(
            stats,
            norms[2 * branch : 2 * branch + 1, :],
            norms[11 + 2 * branch : 12 + 2 * branch, :],
        )
        value = load_rows(firsts[branch], 0, count + 2) * scale + offset
        value = mask_ends(silu(value), count, flags)
        hidden[branch][...] = value.reshape(2, (count + 2) * 16, 256)
        build_sides(hidden[branch], sides[branch], channels)
        build_band(bands[branch], mirrored(tap_reader(taps[branch], branch)), branch, 0)
        outs[branch][...] = dot_nn(
            patches(hidden[branch], sides[branch], count), bands[branch][...]
        )


def joined(second, tile, stat, norms, branch, count, total):
    stats = moments(stat[2 * branch : 2 * branch + 2, :], CHANNELS[branch], total)
    gain = norms[2 * branch + 1 : 2 * branch + 2, :]
    shift = norms[12 + 2 * branch : 13 + 2 * branch, :]
    scaled = (second - stats[0]) * stats[1]
    return scaled * gain + shift + load_rows(tile, 2, count), scaled, stats


def third_kernel(rows, counts, *refs):
    seconds, tiles, stat, norms, unites, mixes, sums = split_refs(refs, 3, 3, 1, 1, 3, 3, 1)
    stat, norms, sums = stat[0], norms[0], sums[0]
    for level in range(3):
        branch = level + 1
        value, _, _ = joined(
            seconds[level][...], tiles[level], stat, norms, branch, rows[branch], counts[branch]
        )
        unite = unites[level][...].reshape(CHANNELS[branch], C0)
        mixed = dot_nn(silu(value), mix_matrix(unite, branch))
        mixes[level][...] = mixed
        sums[2 * level : 2 * level + 1, :] = column_sum(mixed)
        sums[2 * level + 1 : 2 * level + 2, :] = column_sum(mixed * mixed)
    sums[6:8, :] = jnp.zeros((2, 256), f32)


def spread_rows(value, rows, factor):
    value = value.reshape(2 * rows, 1, 16, 256)
    return jnp.broadcast_to(value, (2 * rows, factor, 16, 256)).reshape(2 * rows * factor * 16, 256)


def gather_rows(value, rows, factor):
    value = value.reshape(2 * rows // factor, factor, 16, 256)
    return jnp.sum(value, axis=1).reshape(2 * rows // factor * 16, 256)


def uniting_stats(stat, level, total):
    return moments(stat[2 * level : 2 * level + 2, :], C0, total * 2.0 ** (level + 1))


def united_sum(base, mixes, stat, norms, rows, counts):
    for level in range(3):
        stats = uniting_stats(stat, level, counts[level + 1])
        scale, offset = affine(
            stats, norms[8 + level : 9 + level, :], norms[19 + level : 20 + level, :]
        )
        base = base + spread_rows(mixes[level] * scale + offset, rows[level + 1], 2 ** (level + 1))
    return base


def head_matrix(weight):
    wide = jnp.concatenate([weight] * 8, axis=1)
    lane = lax.broadcasted_iota(jnp.int32, wide.shape, 1)
    return jnp.concatenate([jnp.where(lane // C0 == place, wide, 0.0) for place in range(8)], axis=0)


def loss_kernel(rows, counts, denominator, *refs):
    ins, outs = split_refs(refs, 12, 7)
    second, tile, stat, mix_one, mix_two, mix_three, mix_stat, norms, weight, bias, targets, mask = ins
    heat_out, pre_grad, sum_one, sum_two, sum_three, sums, join_grad = outs
    count = rows[0]
    join, scaled, _ = joined(second[...], tile, stat, norms, 0, count, counts[0])
    mixes = (mix_one[...], mix_two[...], mix_three[...])
    pre = united_sum(silu(join), mixes, mix_stat, norms, rows, counts)
    united = silu(pre)
    head = head_matrix(weight[...])
    heat = dot_nn(united, head) + bias[...]
    heat_out[...] = heat
    error = heat - targets[...]
    weighted = mask[...] * error
    sums[...] = jnp.zeros(sums.shape, f32)
    sums[6:7, :] = column_sum(weighted * error) / denominator
    heat_grad = weighted * (2.0 / denominator)
    sums[7:8, :] = column_sum(heat_grad)
    product = dot_tn(united, heat_grad)
    total = None
    for place in range(8):
        first = place * C0
        tile_first = first // 128 * 128
        block = product[first : first + C0, tile_first : tile_first + 128]
        if first - tile_first:
            block = pltpu.roll(block, 128 - (first - tile_first), 1)
        total = block if total is None else total + block
    sums[16:48, 0:128] = total
    grad = dot_nt(heat_grad, head) * silu_slope(pre)
    pre_grad[...] = grad
    join_part = grad * silu_slope(join)
    join_grad[...] = join_part
    sums[8:9, :] = column_sum(join_part)
    sums[9:10, :] = column_sum(join_part * scaled)
    for level, out in enumerate((sum_one, sum_two, sum_three)):
        part = gather_rows(grad, count, 2 ** (level + 1))
        out[...] = part
        stats = uniting_stats(mix_stat, level, counts[level + 1])
        normed = (mixes[level] - stats[0]) * stats[1]
        sums[2 * level : 2 * level + 1, :] = column_sum(part)
        sums[2 * level + 1 : 2 * level + 2, :] = column_sum(part * normed)


def flip_kernel(rows, counts, *refs):
    seconds, tiles, stat, unites, mix_stat, norms, weight, bias, heat, out = split_refs(
        refs, 4, 4, 1, 3, 1, 1, 1, 1, 1, 1
    )
    stat, norms = stat[0], norms[0]
    mixes = []
    for branch in range(4):
        value, _, _ = joined(
            seconds[branch][...], tiles[branch], stat, norms, branch, rows[branch], counts[branch]
        )
        if branch == 0:
            base = silu(value)
        else:
            unite = unites[branch - 1][...].reshape(CHANNELS[branch], C0)
            mixes.append(dot_nn(silu(value), mix_matrix(unite, branch)))
    pre = united_sum(base, mixes, mix_stat[0], norms, rows, counts)
    back = dot_nn(silu(pre), head_matrix(weight[0][...])) + bias[0][...]
    out[0][...] = 0.5 * (heat[0][...] + back)


def edge_place(branch, image):
    return (2 * branch + image) * 16


def write_edges(first, last, value, branch, count, base):
    for image in range(2):
        place = base + edge_place(branch, image)
        start = image * count * 16
        first[place : place + 16, :] = value[start : start + 16]
        last[place : place + 16, :] = value[start + (count - 1) * 16 : start + count * 16]


def join_kernel(rows, counts, *refs):
    sums_in, mixes, seconds, tiles, join_zero, stat, mix_stat, head_sums, norms, unites, outs = (
        split_refs(refs, 3, 3, 4, 3, 1, 1, 1, 1, 1, 3, 9)
    )
    stat, mix_stat, head_sums, norms = stat[0], mix_stat[0], head_sums[0], norms[0]
    grads, mixer_grads, sums, first, last = outs[0:3], outs[3:6], outs[6], outs[7], outs[8]
    sums[0:2, :] = jnp.zeros((2, 256), f32)
    write_edges(first, last, join_zero[0][...], 0, rows[0], 0)
    write_edges(first, last, seconds[0][...], 0, rows[0], 128)
    for level in range(3):
        branch = level + 1
        channels, count = CHANNELS[branch], rows[branch]
        groups = 256 // channels
        total = counts[branch]
        stats = uniting_stats(mix_stat, level, total)
        gain = norms[8 + level : 9 + level, :]
        shift_sum = fold(head_sums[2 * level : 2 * level + 1, :], C0)
        gain_sum = fold(head_sums[2 * level + 1 : 2 * level + 2, :], C0)
        normed = (mixes[level][...] - stats[0]) * stats[1]
        share = 1.0 / (total * 2.0 ** (level + 1))
        mixed_grad = (gain * stats[1]) * (
            sums_in[level][...] - shift_sum * share - normed * (gain_sum * share)
        )
        value, scaled, _ = joined(
            seconds[branch][...], tiles[level], stat, norms, branch, count, total
        )
        unite = unites[level][...].reshape(channels, C0)
        product = dot_tn(silu(value), mixed_grad)
        mixer = None
        for place in range(8):
            row = place // (8 // groups) * channels
            tile_first = place * C0 // 128 * 128
            block = product[row : row + channels, tile_first : tile_first + 128]
            inner = place * C0 - tile_first
            if inner:
                block = pltpu.roll(block, 128 - inner, 1)
            mixer = block if mixer is None else mixer + block
        mixer_grads[level][...] = mixer[:, :C0].reshape(mixer_grads[level].shape)
        grad = dot_nt(mixed_grad, mix_matrix(unite, branch)) * silu_slope(value)
        grads[level][...] = grad
        sums[2 * branch : 2 * branch + 1, :] = column_sum(grad)
        sums[2 * branch + 1 : 2 * branch + 2, :] = column_sum(grad * scaled)
        write_edges(first, last, grad, branch, count, 0)
        write_edges(first, last, seconds[branch][...], branch, count, 128)


def norm_input_grad(grad, scaled, stats, gain, sums, channels, total):
    shift_sum = fold(sums[0:1, :], channels) / total
    gain_sum = fold(sums[1:2, :], channels) / total
    return (gain * stats[1]) * (grad - shift_sum - scaled * gain_sum)


def back_second_kernel(rows, counts, flags, *refs):
    ins, outs, scratch = split_refs(refs, 22, 8, 12)
    grads, seconds, firsts, taps = ins[0:4], ins[4:8], ins[8:12], ins[12:16]
    above, below, stat, stat_sums, first_stat, norms = ins[16:22]
    normed_grads, second_grads, = outs[0:4], ()
    sums, first, last = outs[4:7]
    wide = scratch[0:4]
    sides = scratch[4:8]
    bands = scratch[8:12]
    for branch in range(4):
        count, channels, total = rows[branch], CHANNELS[branch], counts[branch]
        stats = moments(stat[2 * branch : 2 * branch + 2, :], channels, total)
        gain = norms[2 * branch + 1 : 2 * branch + 2, :]
        shift_sum = fold(stat_sums[2 * branch : 2 * branch + 1, :], channels) / total
        gain_sum = fold(stat_sums[2 * branch + 1 : 2 * branch + 2, :], channels) / total

        def input_grad(grad, value):
            scaled = (value - stats[0]) * stats[1]
            return (gain * stats[1]) * (grad - shift_sum - scaled * gain_sum)

        inner = input_grad(grads[branch][...], seconds[branch][...])
        wide[branch][:, 16 : (count + 1) * 16, :] = inner.reshape(2, count * 16, 256)
        for image in range(2):
            place = edge_place(branch, image)
            for ref, start, flag in ((above, 0, flags[0]), (below, (count + 1) * 16, flags[1])):
                value = input_grad(
                    ref[place : place + 16, :], ref[128 + place : 144 + place, :]
                )
                wide[branch][image, start : start + 16, :] = jnp.where(flag == 0, 0.0, value)
        build_sides(wide[branch], sides[branch], channels)
        build_band(bands[branch], turned(tap_reader(taps[branch], branch)), branch, 0)
        hidden_grad = dot_nn(patches(wide[branch], sides[branch], count), bands[branch][...])
        first_stats = moments(first_stat[2 * branch : 2 * branch + 2, :], channels, total)
        scaled = (load_rows(firsts[branch], 1, count) - first_stats[0]) * first_stats[1]
        value = (
            scaled * norms[2 * branch : 2 * branch + 1, :]
            + norms[11 + 2 * branch : 12 + 2 * branch, :]
        )
        grad = hidden_grad * silu_slope(value)
        normed_grads[branch][...] = grad
        sums[2 * branch : 2 * branch + 1, :] = column_sum(grad)
        sums[2 * branch + 1 : 2 * branch + 2, :] = column_sum(grad * scaled)
        write_edges(first, last, grad, branch, count, 0)
    outs[7][...] = jnp.zeros(outs[7].shape, f32)


def kernel_grad_second(rows, counts, flags, *refs):
    grads, seconds, firsts, stat, stat_sums, first_stat, norms, outs, hidden, sides, products, small = (
        split_refs(refs, 4, 4, 4, 1, 1, 1, 1, 4, 4, 4, 4, 2)
    )
    stat, stat_sums, first_stat, norms = stat[0], stat_sums[0], first_stat[0], norms[0]
    for branch in range(4):
        count, channels, total = rows[branch], CHANNELS[branch], counts[branch]
        stats = moments(stat[2 * branch : 2 * branch + 2, :], channels, total)
        scaled = (seconds[branch][...] - stats[0]) * stats[1]
        grad = norm_input_grad(
            grads[branch][...],
            scaled,
            stats,
            norms[2 * branch + 1 : 2 * branch + 2, :],
            stat_sums[2 * branch : 2 * branch + 2, :],
            channels,
            total,
        )
        first_stats = moments(first_stat[2 * branch : 2 * branch + 2, :], channels, total)
        scale, offset = affine(
            first_stats,
            norms[2 * branch : 2 * branch + 1, :],
            norms[11 + 2 * branch : 12 + 2 * branch, :],
        )
        value = load_rows(firsts[branch], 0, count + 2) * scale + offset
        value = mask_ends(silu(value), count, flags)
        hidden[branch][...] = value.reshape(2, (count + 2) * 16, 256)
        build_sides(hidden[branch], sides[branch], channels)
        products[branch][...] = dot_tn(patches(hidden[branch], sides[branch], count), grad)
        emit, finish = tap_writer(outs[branch], small[branch] if branch < 2 else None, branch)
        collect_band(products[branch], branch, emit)
        finish()


def back_first_kernel(rows, counts, flags, *refs):
    ins, outs, scratch = split_refs(refs, 25, 8, 18)
    normed_grads, firsts, join_grads, tiles, taps = ins[0:4], ins[4:8], ins[8:12], ins[12:16], ins[16:20]
    above, below, first_stat, first_sums, norms = ins[20:25]
    source_grads, kernel_grads = outs[0:4], outs[4:8]
    wide, sides, bands, products, small = (
        scratch[0:4],
        scratch[4:8],
        scratch[8:12],
        scratch[12:16],
        scratch[16:18],
    )
    for branch in range(4):
        count, channels, total = rows[branch], CHANNELS[branch], counts[branch]
        stats = moments(first_stat[2 * branch : 2 * branch + 2, :], channels, total)
        gain = norms[2 * branch : 2 * branch + 1, :]
        shift_sum = fold(first_sums[2 * branch : 2 * branch + 1, :], channels) / total
        gain_sum = fold(first_sums[2 * branch + 1 : 2 * branch + 2, :], channels) / total

        def input_grad(grad, value):
            scaled = (value - stats[0]) * stats[1]
            return (gain * stats[1]) * (grad - shift_sum - scaled * gain_sum)

        inner = input_grad(normed_grads[branch][...], load_rows(firsts[branch], 1, count))
        wide[branch][:, 16 : (count + 1) * 16, :] = inner.reshape(2, count * 16, 256)
        for image in range(2):
            place = edge_place(branch, image)
            for ref, start, flag in ((above, 0, flags[0]), (below, (count + 1) * 16, flags[1])):
                value = input_grad(
                    ref[place : place + 16, :], firsts[branch][image, start : start + 16, :]
                )
                wide[branch][image, start : start + 16, :] = jnp.where(flag == 0, 0.0, value)
        build_sides(wide[branch], sides[branch], channels)
        build_band(bands[branch], turned(tap_reader(taps[branch], branch)), branch, 0)
        grad = dot_nn(patches(wide[branch], sides[branch], count), bands[branch][...])
        grad = (grad + join_grads[branch][...]).reshape(2, count * 16, 256)
        for image in range(2):
            source_grads[branch][image] = grad[image].reshape(count, 4096)
        part = wide[branch]
        part[...] = tiles[branch][:, 16 : (count + 3) * 16, :]
        build_sides(part, sides[branch], channels)
        products[branch][...] = dot_tn(patches(part, sides[branch], count), inner)
        emit, finish = tap_writer(kernel_grads[branch], small[branch] if branch < 2 else None, branch)
        collect_band(products[branch], branch, emit)
        finish()


def device_count():
    return lax.axis_size("dp") * lax.axis_size("space")


def exchange(value, bit):
    return lax.ppermute(value, AXES, [(i, i ^ bit) for i in range(device_count())])


def total_sum(value):
    bit = 1
    while bit < device_count():
        value = value + exchange(value, bit)
        bit = 2 * bit
    return value


def move_rows(first, last):
    devices = lax.axis_size("space")
    down = [(i, i + 1) for i in range(devices - 1)]
    up = [(i + 1, i) for i in range(devices - 1)]
    return lax.ppermute(last, "space", down), lax.ppermute(first, "space", up)


def gather_shards(shard):
    devices = device_count()
    index = lax.axis_index("dp") * lax.axis_size("space") + lax.axis_index("space")
    whole = shard[None]
    bits = [1 << i for i in range(devices.bit_length() - 1)]
    shape = (1,)
    held = {}
    order = bits[::-1]
    for bit in order:
        other = exchange(whole, bit)
        mine = (index & bit) == 0
        whole = jnp.where(mine, jnp.stack([whole, other]), jnp.stack([other, whole]))
    count = len(bits)
    whole = whole.reshape((2,) * count + shard.shape)
    whole = jnp.transpose(whole, tuple(range(count))[::-1] + tuple(range(count, whole.ndim)))
    return whole.reshape((devices,) + shard.shape)


def scatter_sum(whole, order):
    devices = device_count()
    index = lax.axis_index("dp") * lax.axis_size("space") + lax.axis_index("space")
    bits = devices.bit_length() - 1
    left = list(range(bits))[::-1]
    value = whole.reshape((2,) * bits + whole.shape[1:])
    for bit in order:
        dim = left.index(bit)
        mine = (index >> bit) & 1
        keep = lax.dynamic_index_in_dim(value, mine, dim, keepdims=False)
        send = lax.dynamic_index_in_dim(value, 1 - mine, dim, keepdims=False)
        value = keep + exchange(send, 1 << bit)
        left.remove(bit)
    return value


def norm_lanes(values):
    parts, offset = [], 0
    for channels in CHANNELS:
        for _ in range(2):
            parts.append(jnp.tile(values[offset : offset + channels], 256 // channels))
            offset += channels
    for _ in range(3):
        parts.append(jnp.tile(values[offset : offset + C0], 256 // C0))
        offset += C0
    return jnp.stack(parts)


def body(
    branch_zero,
    branch_one,
    branch_two,
    branch_three,
    convs_zero,
    convs_one,
    convs_two,
    convs_three,
    unite_one,
    unite_two,
    unite_three,
    norm_gain,
    norm_shift,
    head_weight,
    head_bias,
    targets,
    crowd_mask,
    person_count,
    flip_order,
):
    inputs = (branch_zero, branch_one, branch_two, branch_three)
    devices = device_count()
    spaces = lax.axis_size("space")
    place = lax.axis_index("space")
    rows = tuple(value.shape[1] for value in inputs)
    groups_of = tuple(256 // channels for channels in CHANNELS)
    counts = tuple(
        float(2 * rows[b] * 16 * groups_of[b] * devices) for b in range(4)
    )
    joints = head_bias.shape[0]
    cells = [2 * rows[b] * 16 for b in range(4)]

    whole_three = lax.all_gather(convs_three, AXES, axis=0, tiled=True).reshape(-1, 128)
    small_parts = (convs_two, convs_one, convs_zero, unite_one, unite_two, unite_three)
    sizes = [part.shape[0] for part in small_parts]
    packed = jnp.concatenate(small_parts)
    padded = -(-packed.shape[0] // 1024) * 1024
    packed = jnp.pad(packed, (0, padded - packed.shape[0])).reshape(-1, 128)
    gathered = gather_shards(packed).reshape(devices, padded)
    whole, offset = [], 0
    for size in sizes:
        whole.append(gathered[:, offset : offset + size].reshape(-1, 128))
        offset += size
    all_taps = (whole[2], whole[1], whole[0], whole_three)
    first_taps = [taps[: taps.shape[0] // 2] for taps in all_taps]
    second_taps = [taps[taps.shape[0] // 2 :] for taps in all_taps]
    unites = whole[3:6]

    last_rows = jnp.concatenate([value[:, -2:] for value in inputs], axis=1)
    first_rows = jnp.concatenate([value[:, :2] for value in inputs], axis=1)
    tops, bottoms = move_rows(first_rows, last_rows)
    flags = jnp.stack([place > 0, place < spaces - 1]).astype(jnp.int32)

    norms = jnp.concatenate([norm_lanes(norm_gain), norm_lanes(norm_shift)])

    def head_parts(weight, bias):
        weight = jnp.pad(weight, ((0, 0), (0, C0 - joints)))
        bias = jnp.tile(jnp.pad(bias, (0, C0 - joints)), 8)[None]
        return weight, bias

    weight, bias = head_parts(head_weight, head_bias)
    flip_weight, flip_bias = head_parts(head_weight[:, flip_order], head_bias[flip_order])
    target_cells = jnp.pad(
        jnp.transpose(targets.reshape(2, joints, rows[0], 16, 8), (0, 2, 3, 4, 1)),
        ((0, 0),) * 4 + ((0, C0 - joints),),
    ).reshape(cells[0], 256)
    loss_weight = crowd_mask.astype(f32) / person_count.astype(f32)[:, None, None]
    loss_weight = jnp.broadcast_to(
        loss_weight.reshape(2, rows[0], 16, 8, 1), (2, rows[0], 16, 8, C0)
    ).reshape(cells[0], 256)

    bands = [band_shape(b, 256) for b in range(4)]
    inner = [(cells[b], 256) for b in range(4)]
    wide = [(2, (rows[b] + 2) * 16, 256) for b in range(4)]
    wider = [(2, (rows[b] + 4) * 16, 256) for b in range(4)]

    def sides_of(shapes):
        return [shape[:2] + (SIDES[b],) for b, shape in enumerate(shapes)]

    small = [(9 * CHANNELS[b], CHANNELS[b]) for b in range(2)]
    eight = (8, 256)

    out = call(
        functools.partial(first_kernel, rows),
        [*inputs, tops, bottoms, *first_taps],
        [*wider, *wide, *wide, eight],
        [band_shape(b, 512) for b in range(4)] + sides_of(wider),
    )
    tiles, firsts, flip_firsts = out[0:4], out[4:8], out[8:12]
    first_stat = total_sum(out[12])

    out = call(
        functools.partial(second_kernel, rows, counts),
        [flags, *firsts, first_stat, norms, *second_taps],
        [*inner, eight],
        wide + bands + sides_of(wide),
        smem=1,
    )
    seconds = out[0:4]
    second_stat = total_sum(out[4])
    flip_seconds = call(
        functools.partial(second_flip_kernel, rows, counts),
        [flags, *flip_firsts, first_stat, norms, *second_taps],
        inner,
        wide + bands + sides_of(wide),
        smem=1,
    )

    out = call(
        functools.partial(third_kernel, rows, counts),
        [*seconds[1:], *tiles[1:], second_stat, norms, *unites],
        [*inner[1:], eight],
    )
    mixes = out[0:3]
    mix_stat = total_sum(out[3])

    denominator = float(counts[0] * joints)
    out = call(
        functools.partial(loss_kernel, rows, counts, denominator),
        [
            seconds[0],
            tiles[0],
            second_stat,
            *mixes,
            mix_stat,
            norms,
            weight,
            bias,
            target_cells,
            loss_weight,
        ],
        [inner[0], inner[0], *inner[1:], (48, 256), inner[0]],
    )
    heat, _, pre_sums, join_zero = out[0], out[1], out[2:5], out[6]
    head_sums = total_sum(out[5])

    (heat_mean,) = call(
        functools.partial(flip_kernel, rows, counts),
        [
            *flip_seconds,
            *tiles,
            second_stat,
            *unites,
            mix_stat,
            norms,
            flip_weight,
            flip_bias,
            heat,
        ],
        [inner[0]],
    )

    out = call(
        functools.partial(join_kernel, rows, counts),
        [
            *pre_sums,
            *mixes,
            *seconds,
            *tiles[1:],
            join_zero,
            second_stat,
            mix_stat,
            head_sums,
            norms,
            *unites,
        ],
        [*inner[1:], *[part.shape for part in unites], eight, (256, 256), (256, 256)],
    )
    join_grads = [join_zero, *out[0:3]]
    mixer_grads = out[3:6]
    above, below = move_rows(out[7], out[8])
    second_sums = total_sum(out[6])
    second_sums = jnp.concatenate([head_sums[8:10], second_sums[2:8]])

    out = call(
        functools.partial(back_second_kernel, rows, counts),
        [
            flags,
            *join_grads,
            *seconds,
            *firsts,
            *second_taps,
            above,
            below,
            second_stat,
            second_sums,
            first_stat,
            norms,
        ],
        [*inner, eight, (128, 256), (128, 256), eight],
        wide + sides_of(wide) + bands,
        smem=1,
    )
    normed_grads = out[0:4]
    above, below = move_rows(out[5], out[6])
    first_sums = total_sum(out[4])
    second_kernels = call(
        functools.partial(kernel_grad_second, rows, counts),
        [
            flags,
            *join_grads,
            *seconds,
            *firsts,
            second_stat,
            second_sums,
            first_stat,
            norms,
        ],
        [taps.shape for taps in second_taps],
        wide + sides_of(wide) + bands + small,
        smem=1,
    )
    out = call(
        functools.partial(back_first_kernel, rows, counts),
        [
            flags,
            *normed_grads,
            *firsts,
            *join_grads,
            *tiles,
            *first_taps,
            above,
            below,
            first_stat,
            first_sums,
            norms,
        ],
        [*[value.shape for value in inputs], *[taps.shape for taps in first_taps]],
        wide + sides_of(wide) + bands + bands + small,
        smem=1,
    )
    source_grads, first_kernels = out[0:4], out[4:8]

    kernel_grads = [
        jnp.concatenate([first_kernels[b], second_kernels[b]]).reshape(devices, -1)
        for b in range(4)
    ]
    flat_grads = [
        kernel_grads[3],
        kernel_grads[2],
        kernel_grads[1],
        kernel_grads[0],
        *[part.reshape(devices, -1) for part in mixer_grads],
    ]
    shard_sizes = [part.shape[1] for part in flat_grads]
    whole_grad = jnp.concatenate(flat_grads, axis=1)
    length = whole_grad.shape[1]
    padded = -(-length // 2048) * 2048
    whole_grad = jnp.pad(whole_grad, ((0, 0), (0, padded - length)))
    bits = devices.bit_length() - 1
    order = list(range(bits))
    swapped = [0, 2, 1] + order[3:]
    halves = [
        scatter_sum(whole_grad[:, : padded // 2].reshape(devices, -1, 128), order),
        scatter_sum(whole_grad[:, padded // 2 :].reshape(devices, -1, 128), swapped),
    ]
    shard = jnp.concatenate([half.reshape(-1) for half in halves])
    shards, offset = [], 0
    for size in shard_sizes:
        shards.append(shard[offset : offset + size])
        offset += size

    def per_channel(row, channels):
        return row.reshape(256 // channels, channels).sum(0)

    gain_grads, shift_grads = [], []
    for branch in range(4):
        channels = CHANNELS[branch]
        for sums in (first_sums, second_sums):
            shift_grads.append(per_channel(sums[2 * branch], channels))
            gain_grads.append(per_channel(sums[2 * branch + 1], channels))
    for level in range(3):
        shift_grads.append(per_channel(head_sums[2 * level], C0))
        gain_grads.append(per_channel(head_sums[2 * level + 1], C0))
    heat_mean = jnp.transpose(
        heat_mean.reshape(2, rows[0], 16, 8, C0)[..., :joints], (0, 4, 1, 2, 3)
    ).reshape(targets.shape)
    return (
        jnp.sum(head_sums[6]),
        heat_mean,
        *source_grads,
        shards[3],
        shards[2],
        shards[1],
        shards[0],
        shards[4],
        shards[5],
        shards[6],
        jnp.concatenate(gain_grads),
        jnp.concatenate(shift_grads),
        head_sums[16:48, :joints],
        per_channel(head_sums[7], C0)[:joints],
    )


def solution(mesh):
    rows = P("dp", "space", None)
    shard = P(("dp", "space"))
    heat = P("dp", None, "space", None)
    return jax.shard_map(
        body,
        mesh=mesh,
        in_specs=(*[rows] * 4, *[shard] * 7, *[P()] * 4, heat, rows, P("dp"), P()),
        out_specs=(P(), heat, *[rows] * 4, *[shard] * 7, *[P()] * 4),
        check_vma=False,
    )
```

```python
import functools

import jax
import jax.numpy as jnp
import numpy as np
from jax import lax
from jax.experimental import pallas as pl
from jax.experimental.pallas import tpu as pltpu
from jax.sharding import PartitionSpec as P

C0 = 32
CHANNELS = (32, 64, 128, 256)
SIDES = (128, 128, 256, 512)
AXES = ("dp", "space")
epsilon = 1e-05
f32 = jnp.float32
high = lax.Precision.HIGH


def dot_nn(left, right):
    return lax.dot_general(left, right, (((1,), (0,)), ((), ())), precision=high, preferred_element_type=f32)


def dot_nt(left, right):
    return lax.dot_general(left, right, (((1,), (1,)), ((), ())), precision=high, preferred_element_type=f32)


def dot_tn(left, right):
    return lax.dot_general(left, right, (((0,), (0,)), ((), ())), precision=high, preferred_element_type=f32)


def sigmoid(value):
    return 1.0 / (1.0 + jnp.exp(-value))


def silu(value):
    return value * sigmoid(value)


def silu_slope(value):
    sigma = sigmoid(value)
    return sigma * (1.0 + value * (1.0 - sigma))


def fold(row, channels):
    step = channels
    while step < 256:
        row = row + pltpu.roll(row, step, 1)
        step = 2 * step
    return row


def column_sum(value):
    return jnp.sum(value, axis=0, keepdims=True)


def moments(sums, channels, count):
    mean = fold(sums[0:1], channels) / count
    square = fold(sums[1:2], channels) / count
    return mean, lax.rsqrt(square - mean * mean + epsilon)


def affine(stats, gain, shift):
    scale = stats[1] * gain
    return scale, shift - stats[0] * scale


def load_rows(ref, first, count):
    lanes = ref.shape[2]
    return ref[:, first * 16 : (first + count) * 16, :].reshape(2 * count * 16, lanes)


def group_index(rows):
    return lax.broadcasted_iota(jnp.int32, (rows, 128), 0) % 16


def side_columns(value, channels):
    rows = value.shape[0]
    group = group_index(rows)
    lane = lax.broadcasted_iota(jnp.int32, (rows, 128), 1)

    def before(part):
        return jnp.where(group == 0, 0.0, pltpu.roll(part, 1, 0))

    def after(part):
        return jnp.where(group == 15, 0.0, pltpu.roll(part, rows - 1, 0))

    low, upper = value[:, :128], value[:, 128:]
    if channels == 256:
        return jnp.concatenate([before(low), before(upper), after(low), after(upper)], axis=1)
    if channels == 128:
        return jnp.concatenate([before(upper), after(low)], axis=1)
    return jnp.where(
        lane < channels, after(low), jnp.where(lane >= 128 - channels, before(upper), 0.0)
    )


def build_sides(source, side, channels):
    rows = source.shape[1]
    for image in range(2):
        side[image] = side_columns(source[image], channels)


def patches(source, side, count):
    parts = []
    for tap_row in range(3):
        parts.append(load_rows(source, tap_row, count))
        parts.append(load_rows(side, tap_row, count))
    return jnp.concatenate(parts, axis=1)


def build_band(band, tap, branch, offset):
    channels = CHANNELS[branch]
    groups = 256 // channels
    side = SIDES[branch]
    height = 256 + side
    if channels < 256:
        band[:, offset : offset + 256] = jnp.zeros((3 * height, 256), f32)
    for tap_row in range(3):
        base = tap_row * height
        for tap_col in range(3):
            matrix = tap(tap_row, tap_col)
            for out in range(groups):
                place = out + tap_col - 1
                if place < 0:
                    row = base + 256 + (0 if channels >= 128 else 128 - channels)
                elif place >= groups:
                    row = base + 256 + (side // 2 if channels >= 128 else 0)
                else:
                    row = base + place * channels
                start = offset + out * channels
                band[row : row + channels, start : start + channels] = matrix


def collect_band(product, branch, emit):
    channels = CHANNELS[branch]
    groups = 256 // channels
    side = SIDES[branch]
    height = 256 + side
    for tap_row in range(3):
        base = tap_row * height
        for tap_col in range(3):
            total = None
            for out in range(groups):
                place = out + tap_col - 1
                if place < 0:
                    row = base + 256 + (0 if channels >= 128 else 128 - channels)
                elif place >= groups:
                    row = base + 256 + (side // 2 if channels >= 128 else 0)
                else:
                    row = base + place * channels
                start = out * channels
                if channels >= 128:
                    block = product[row : row + channels, start : start + channels]
                else:
                    tile = start // 128 * 128
                    block = product[row : row + channels, tile : tile + 128]
                    inner = start - tile
                    if inner:
                        block = pltpu.roll(block, 128 - inner, 1)
                total = block if total is None else total + block
            emit(tap_row, tap_col, total[:, :channels])


def tap_reader(ref, branch):
    channels = CHANNELS[branch]
    if channels == 256:

        def tap(tap_row, tap_col):
            first = (3 * tap_row + tap_col) * 512
            return jnp.concatenate(
                [ref[pl.ds(first, 256, stride=2), :], ref[pl.ds(first + 1, 256, stride=2), :]],
                axis=1,
            )

        return tap

    def tap(tap_row, tap_col):
        first = (3 * tap_row + tap_col) * channels
        return ref[first : first + channels, :]

    return tap


def tap_writer(ref, branch):
    channels = CHANNELS[branch]

    def emit(tap_row, tap_col, value):
        place = 3 * tap_row + tap_col
        if channels == 256:
            ref[pl.ds(place * 512, 256, stride=2), :] = value[:, :128]
            ref[pl.ds(place * 512 + 1, 256, stride=2), :] = value[:, 128:]
        else:
            ref[place * channels : (place + 1) * channels, :] = value

    return emit


SPLIT = 200
SHARD = 392
ROWS_THREE, ROWS_TWO, ROWS_ONE = 288, 72, 18
PER_ZERO, PER_UNITE = 18, (2, 4, 8)
GATHER_ORDER = ((2, 4, 8), (4, 2, 8))
SCATTER_ORDER = ((4, 2, 8), (2, 4, 8))
TAPS_OUT = ((4608, 128), (1152, 128), (576, 64), (288, 32), (32, 32), (64, 32), (128, 32))
PACK_SCRATCH = ((16, 24, 128), (16, 8, 128), (288, 128))
STAGE = ((4608, 128), (1152, 128), (576, 64), (288, 32), (512, 32))


def partner(me, core, place, order):
    bits = sum(bit for i, bit in enumerate(order) if place >> (2 - i) & 1)
    return me ^ (bits + core)


def unpack_taps(me, packs, taps, scratch):
    three, two, one, zero = taps[:4]
    part_one, part_zero, flat_one = scratch
    for core in range(2):
        upper, lower = packs[core], packs[2 + core]
        for place in range(8):
            device = partner(me, core, place, GATHER_ORDER[0])
            start = pl.multiple_of(device * ROWS_THREE, 8)
            three[pl.ds(start, SPLIT), :] = upper[place]
            device = partner(me, core, place, GATHER_ORDER[1])
            rest = ROWS_THREE - SPLIT
            start = pl.multiple_of(device * ROWS_THREE + SPLIT, 8)
            three[pl.ds(start, rest), :] = lower[place, 0:rest]
            start = pl.multiple_of(device * ROWS_TWO, 8)
            two[pl.ds(start, ROWS_TWO), :] = lower[place, rest : rest + ROWS_TWO]
            part_one[device] = lower[place, rest + ROWS_TWO : rest + ROWS_TWO + 24]
            part_zero[device] = lower[place, rest + ROWS_TWO + 24 :]
    for device in range(16):
        flat_one[device * ROWS_ONE : (device + 1) * ROWS_ONE, :] = part_one[device, 0:ROWS_ONE]
    one[...] = flat_one[...].reshape(one.shape)
    narrow = part_zero[...].reshape(128, 128).reshape(512, 32)
    for device in range(16):
        first = device * 32
        for ref, height in zip(taps[3:7], (PER_ZERO, *PER_UNITE)):
            ref[device * height : (device + 1) * height, :] = narrow[first : first + height]
            first += height


def pack_grads(me, stage, unite_grads, packs, scratch):
    three, two, one, zero, narrow = stage
    part_one, part_zero, flat_one = scratch
    flat_one[...] = one[...].reshape(flat_one.shape)
    for device in range(16):
        part_one[device, 0:ROWS_ONE] = flat_one[device * ROWS_ONE : (device + 1) * ROWS_ONE, :]
        part_one[device, ROWS_ONE:24] = jnp.zeros((24 - ROWS_ONE, 128), f32)
        first = device * 32
        for ref, height in zip((zero, *unite_grads), (PER_ZERO, *PER_UNITE)):
            narrow[first : first + height, :] = ref[device * height : (device + 1) * height, :]
            first += height
    part_zero[...] = narrow[...].reshape(128, 128).reshape(16, 8, 128)
    for core in range(2):
        upper, lower = packs[core], packs[2 + core]
        for place in range(8):
            device = partner(me, core, place, SCATTER_ORDER[0])
            start = pl.multiple_of(device * ROWS_THREE, 8)
            upper[place] = three[pl.ds(start, SPLIT), :]
            device = partner(me, core, place, SCATTER_ORDER[1])
            rest = ROWS_THREE - SPLIT
            start = pl.multiple_of(device * ROWS_THREE + SPLIT, 8)
            lower[place, 0:rest] = three[pl.ds(start, rest), :]
            start = pl.multiple_of(device * ROWS_TWO, 8)
            lower[place, rest : rest + ROWS_TWO] = two[pl.ds(start, ROWS_TWO), :]
            lower[place, rest + ROWS_TWO : rest + ROWS_TWO + 24] = part_one[device]
            lower[place, rest + ROWS_TWO + 24 :] = part_zero[device]


PACKS = ((8, SPLIT, 128), (8, SPLIT, 128), (8, SHARD - SPLIT, 128), (8, SHARD - SPLIT, 128))


def mirrored(tap):
    return lambda tap_row, tap_col: tap(tap_row, 2 - tap_col)


def turned(tap):
    return lambda tap_row, tap_col: jnp.transpose(tap(2 - tap_row, 2 - tap_col))


def mask_ends(value, rows, flags):
    place = lax.broadcasted_iota(jnp.int32, value.shape, 0) // 16 % (rows + 2)
    outside = ((place == 0) & (flags[0] == 0)) | ((place == rows + 1) & (flags[1] == 0))
    return jnp.where(outside, 0.0, value)


def mix_matrix(unite, branch):
    channels = CHANNELS[branch]
    groups = 256 // channels
    wide = jnp.concatenate([unite] * 8, axis=1)
    lane = lax.broadcasted_iota(jnp.int32, wide.shape, 1)
    span = 256 // groups
    return jnp.concatenate(
        [jnp.where(lane // span == place, wide, 0.0) for place in range(groups)], axis=0
    )


def split_refs(refs, *counts):
    out, first = [], 0
    for count in counts:
        out.append(refs[first : first + count])
        first += count
    assert first == len(refs)
    return out


class Kept:
    def __init__(self, value):
        self.value = value


def kept(values):
    return [Kept(value) for value in values]


def call(kernel, ins, outs, scratch=(), smem=0, limit=16, cost=1):
    specs = [pl.BlockSpec(memory_space=pltpu.SMEM)] * smem + [
        pl.BlockSpec(memory_space=pltpu.VMEM)
    ] * (len(ins) - smem)
    ins = ins[:smem] + [
        pltpu.with_memory_space_constraint(x.value, pltpu.VMEM)
        if isinstance(x, Kept)
        else pltpu.with_memory_space_constraint(x, pltpu.HBM)
        for x in ins[smem:]
    ]
    shapes = [pltpu.VMEM(x.value, f32) if isinstance(x, Kept) else pltpu.HBM(x, f32) for x in outs]
    results = pl.pallas_call(
        kernel,
        in_specs=specs,
        out_specs=[pl.BlockSpec(memory_space=pltpu.VMEM)] * len(outs),
        out_shape=shapes,
        scratch_shapes=[pltpu.VMEM(shape, f32) for shape in scratch],
        compiler_params=pltpu.CompilerParams(vmem_limit_bytes=limit * 2**20),
        cost_estimate=pl.CostEstimate(
            flops=int(cost * 1.1e9), bytes_accessed=int(cost * 3.0e6), transcendentals=0
        ),
    )(*ins)
    return [Kept(y) if isinstance(x, Kept) else y for x, y in zip(outs, results)]


def band_shape(branch, width):
    return (3 * (256 + SIDES[branch]), width)


def norm_kernel(gain, shift, out):
    for base, ref in ((0, gain), (11, shift)):
        offset = 0
        line = base
        sizes = [channels for channels in CHANNELS for _ in range(2)] + [C0] * 3
        for channels in sizes:
            part = ref[0:1, offset : offset + channels]
            out[line : line + 1, :] = jnp.concatenate([part] * (256 // channels), axis=1)
            offset += channels
            line += 1


def first_kernel(rows, packed, meta, *refs):
    xs, tops, bottoms, packs, tiles, mains, sums, taps, bands, sides, scratch = split_refs(
        refs, 4, 1, 1, 4, 4, 4, 1, 7 * packed, 4, 4, 3 * packed
    )
    sums = sums[0]
    if packed:
        unpack_taps(meta[2], packs, taps, scratch)
    else:
        taps = packs
    for branch in range(4):
        count = rows[branch]
        tile, side, band = tiles[branch], sides[branch], bands[branch]
        for image in range(2):
            for ref, start, first, extent in (
                (tops[0], 2 * branch, 0, 2),
                (xs[branch], 0, 2, count),
                (bottoms[0], 2 * branch, count + 2, 2),
            ):
                tile[image, first * 16 : (first + extent) * 16, :] = ref[
                    image, start : start + extent, :
                ].reshape(extent * 16, 256)
        build_sides(tile, side, CHANNELS[branch])
        build_band(band, tap_reader(taps[3 - branch], branch), branch, 0)
        out = dot_nn(patches(tile, side, count + 2), band[...])
        mains[branch][...] = out.reshape(2, (count + 2) * 16, 256)
        inner = load_rows(mains[branch], 1, count)
        sums[2 * branch : 2 * branch + 1, :] = column_sum(inner)
        sums[2 * branch + 1 : 2 * branch + 2, :] = column_sum(inner * inner)


def first_flip_kernel(rows, meta, *refs):
    tiles, taps, outs, bands, sides = split_refs(refs, 4, 4, 4, 4, 4)
    for branch in range(4):
        count = rows[branch]
        build_sides(tiles[branch], sides[branch], CHANNELS[branch])
        build_band(bands[branch], mirrored(tap_reader(taps[3 - branch], branch)), branch, 0)
        out = dot_nn(patches(tiles[branch], sides[branch], count + 2), bands[branch][...])
        outs[branch][...] = out.reshape(2, (count + 2) * 16, 256)


def fill_hidden(meta, firsts, stat, norms, hidden, branch, count, total):
    stats = moments(stat[2 * branch : 2 * branch + 2, :], CHANNELS[branch], total)
    scale, offset = affine(
        stats,
        norms[2 * branch : 2 * branch + 1, :],
        norms[11 + 2 * branch : 12 + 2 * branch, :],
    )
    value = load_rows(firsts[branch], 0, count + 2) * scale + offset
    value = mask_ends(silu(value), count, meta)
    hidden[branch][...] = value.reshape(2, (count + 2) * 16, 256)


def second_kernel(rows, counts, packed, meta, *refs):
    firsts, stat, norms, packs, outs, sums, taps, hidden, bands, sides, scratch = split_refs(
        refs, 4, 1, 1, 4, 4, 1, 7 * packed, 4, 4, 4, 3 * packed
    )
    sums = sums[0]
    if packed:
        unpack_taps(meta[2], packs, taps, scratch)
    else:
        taps = packs
    for branch in range(4):
        count, channels = rows[branch], CHANNELS[branch]
        fill_hidden(meta, firsts, stat[0], norms[0], hidden, branch, count, counts[branch])
        build_sides(hidden[branch], sides[branch], channels)
        build_band(bands[branch], tap_reader(taps[3 - branch], branch), branch, 0)
        out = dot_nn(patches(hidden[branch], sides[branch], count), bands[branch][...])
        outs[branch][...] = out
        sums[2 * branch : 2 * branch + 1, :] = column_sum(out)
        sums[2 * branch + 1 : 2 * branch + 2, :] = column_sum(out * out)


def second_flip_kernel(rows, counts, meta, *refs):
    firsts, stat, norms, taps, outs, hidden, bands, sides = split_refs(refs, 4, 1, 1, 4, 4, 4, 4, 4)
    for branch in range(4):
        count, channels = rows[branch], CHANNELS[branch]
        fill_hidden(meta, firsts, stat[0], norms[0], hidden, branch, count, counts[branch])
        build_sides(hidden[branch], sides[branch], channels)
        build_band(bands[branch], mirrored(tap_reader(taps[3 - branch], branch)), branch, 0)
        outs[branch][...] = dot_nn(
            patches(hidden[branch], sides[branch], count), bands[branch][...]
        )


def joined(second, tile, stat, norms, branch, count, total):
    stats = moments(stat[2 * branch : 2 * branch + 2, :], CHANNELS[branch], total)
    gain = norms[2 * branch + 1 : 2 * branch + 2, :]
    shift = norms[12 + 2 * branch : 13 + 2 * branch, :]
    scaled = (second - stats[0]) * stats[1]
    return scaled * gain + shift + load_rows(tile, 2, count), scaled, stats


def third_kernel(rows, counts, *refs):
    seconds, tiles, stat, norms, unites, mixes, sums = split_refs(refs, 3, 3, 1, 1, 6, 3, 1)
    stat, norms, sums = stat[0], norms[0], sums[0]
    for level in range(3):
        branch = level + 1
        value, _, _ = joined(
            seconds[level][...], tiles[level], stat, norms, branch, rows[branch], counts[branch]
        )
        unite = jnp.concatenate([unites[level][...], unites[3 + level][...]], axis=0)
        mixed = dot_nn(silu(value), mix_matrix(unite, branch))
        mixes[level][...] = mixed
        sums[2 * level : 2 * level + 1, :] = column_sum(mixed)
        sums[2 * level + 1 : 2 * level + 2, :] = column_sum(mixed * mixed)
    sums[6:8, :] = jnp.zeros((2, 256), f32)


def spread_rows(value, rows, factor):
    value = value.reshape(2 * rows, 1, 16, 256)
    return jnp.broadcast_to(value, (2 * rows, factor, 16, 256)).reshape(2 * rows * factor * 16, 256)


def gather_rows(value, rows, factor):
    value = value.reshape(2 * rows // factor, factor, 16, 256)
    return jnp.sum(value, axis=1).reshape(2 * rows // factor * 16, 256)


def uniting_stats(stat, level, total):
    return moments(stat[2 * level : 2 * level + 2, :], C0, total * 2.0 ** (level + 1))


def united_sum(base, mixes, stat, norms, rows, counts):
    for level in range(3):
        stats = uniting_stats(stat, level, counts[level + 1])
        scale, offset = affine(
            stats, norms[8 + level : 9 + level, :], norms[19 + level : 20 + level, :]
        )
        base = base + spread_rows(mixes[level] * scale + offset, rows[level + 1], 2 ** (level + 1))
    return base


def head_matrix(weight):
    wide = jnp.concatenate([weight] * 8, axis=1)
    lane = lax.broadcasted_iota(jnp.int32, wide.shape, 1)
    return jnp.concatenate([jnp.where(lane // C0 == place, wide, 0.0) for place in range(8)], axis=0)


def loss_kernel(rows, counts, denominator, *refs):
    ins, outs = split_refs(refs, 12, 6)
    second, tile, stat, mix_one, mix_two, mix_three, mix_stat, norms, weight, bias, targets, mask = ins
    heat_out, sum_one, sum_two, sum_three, sums, join_grad = outs
    count = rows[0]
    join, scaled, _ = joined(second[...], tile, stat, norms, 0, count, counts[0])
    mixes = (mix_one[...], mix_two[...], mix_three[...])
    pre = united_sum(silu(join), mixes, mix_stat, norms, rows, counts)
    united = silu(pre)
    head = head_matrix(weight[...])
    heat = dot_nn(united, head) + bias[...]
    heat_out[...] = heat
    error = heat - targets[...]
    weighted = mask[...] * error
    sums[...] = jnp.zeros(sums.shape, f32)
    sums[6:7, :] = column_sum(weighted * error) / denominator
    heat_grad = weighted * (2.0 / denominator)
    sums[7:8, :] = column_sum(heat_grad)
    product = dot_tn(united, heat_grad)
    total = None
    for place in range(8):
        first = place * C0
        tile_first = first // 128 * 128
        block = product[first : first + C0, tile_first : tile_first + 128]
        if first - tile_first:
            block = pltpu.roll(block, 128 - (first - tile_first), 1)
        total = block if total is None else total + block
    sums[16:24, 0:128] = jnp.concatenate(
        [total[8 * part : 8 * part + 8, :C0] for part in range(4)], axis=1
    )
    grad = dot_nt(heat_grad, head) * silu_slope(pre)
    join_part = grad * silu_slope(join)
    join_grad[...] = join_part
    sums[8:9, :] = column_sum(join_part)
    sums[9:10, :] = column_sum(join_part * scaled)
    for level, out in enumerate((sum_one, sum_two, sum_three)):
        part = gather_rows(grad, count, 2 ** (level + 1))
        out[...] = part
        stats = uniting_stats(mix_stat, level, counts[level + 1])
        normed = (mixes[level] - stats[0]) * stats[1]
        sums[2 * level : 2 * level + 1, :] = column_sum(part)
        sums[2 * level + 1 : 2 * level + 2, :] = column_sum(part * normed)


def flip_kernel(rows, counts, *refs):
    seconds, tiles, stat, unites, mix_stat, norms, weight, bias, heat, out = split_refs(
        refs, 4, 4, 1, 6, 1, 1, 1, 1, 1, 1
    )
    stat, norms = stat[0], norms[0]
    mixes = []
    for branch in range(4):
        value, _, _ = joined(
            seconds[branch][...], tiles[branch], stat, norms, branch, rows[branch], counts[branch]
        )
        if branch == 0:
            base = silu(value)
        else:
            unite = jnp.concatenate([unites[branch - 1][...], unites[branch + 2][...]], axis=0)
            mixes.append(dot_nn(silu(value), mix_matrix(unite, branch)))
    pre = united_sum(base, mixes, mix_stat[0], norms, rows, counts)
    back = dot_nn(silu(pre), head_matrix(weight[0][...])) + bias[0][...]
    out[0][...] = 0.5 * (heat[0][...] + back)


def edge_place(branch, image):
    return (2 * branch + image) * 16


def write_edges(first, last, value, branch, count, base):
    for image in range(2):
        place = base + edge_place(branch, image)
        start = image * count * 16
        first[place : place + 16, :] = value[start : start + 16]
        last[place : place + 16, :] = value[start + (count - 1) * 16 : start + count * 16]


def join_kernel(rows, counts, *refs):
    sums_in, mixes, seconds, tiles, join_zero, stat, mix_stat, head_sums, norms, unites, outs = (
        split_refs(refs, 3, 3, 4, 3, 1, 1, 1, 1, 1, 6, 9)
    )
    stat, mix_stat, head_sums, norms = stat[0], mix_stat[0], head_sums[0], norms[0]
    grads, mixer_grads, sums, first, last = outs[0:3], outs[3:6], outs[6], outs[7], outs[8]
    sums[0:2, :] = jnp.zeros((2, 256), f32)
    write_edges(first, last, join_zero[0][...], 0, rows[0], 0)
    write_edges(first, last, seconds[0][...], 0, rows[0], 128)
    for level in range(3):
        branch = level + 1
        channels, count = CHANNELS[branch], rows[branch]
        groups = 256 // channels
        total = counts[branch]
        stats = uniting_stats(mix_stat, level, total)
        gain = norms[8 + level : 9 + level, :]
        shift_sum = fold(head_sums[2 * level : 2 * level + 1, :], C0)
        gain_sum = fold(head_sums[2 * level + 1 : 2 * level + 2, :], C0)
        normed = (mixes[level][...] - stats[0]) * stats[1]
        share = 1.0 / (total * 2.0 ** (level + 1))
        mixed_grad = (gain * stats[1]) * (
            sums_in[level][...] - shift_sum * share - normed * (gain_sum * share)
        )
        value, scaled, _ = joined(
            seconds[branch][...], tiles[level], stat, norms, branch, count, total
        )
        unite = jnp.concatenate([unites[level][...], unites[3 + level][...]], axis=0)
        product = dot_tn(silu(value), mixed_grad)
        mixer = None
        for place in range(8):
            row = place // (8 // groups) * channels
            tile_first = place * C0 // 128 * 128
            block = product[row : row + channels, tile_first : tile_first + 128]
            inner = place * C0 - tile_first
            if inner:
                block = pltpu.roll(block, 128 - inner, 1)
            mixer = block if mixer is None else mixer + block
        mixer_grads[level][...] = mixer[:, :C0]
        grad = dot_nt(mixed_grad, mix_matrix(unite, branch)) * silu_slope(value)
        grads[level][...] = grad
        sums[2 * branch : 2 * branch + 1, :] = column_sum(grad)
        sums[2 * branch + 1 : 2 * branch + 2, :] = column_sum(grad * scaled)
        write_edges(first, last, grad, branch, count, 0)
        write_edges(first, last, seconds[branch][...], branch, count, 128)


def norm_input_grad(grad, scaled, stats, gain, sums, channels, total):
    shift_sum = fold(sums[0:1, :], channels) / total
    gain_sum = fold(sums[1:2, :], channels) / total
    return (gain * stats[1]) * (grad - shift_sum - scaled * gain_sum)


def back_second_kernel(rows, counts, flags, *refs):
    ins, outs, scratch = split_refs(refs, 22, 7, 12)
    grads, seconds, firsts, taps = ins[0:4], ins[4:8], ins[8:12], ins[12:16]
    above, below, stat, stat_sums, first_stat, norms = ins[16:22]
    normed_grads = outs[0:4]
    sums, first, last = outs[4:7]
    wide = scratch[0:4]
    sides = scratch[4:8]
    bands = scratch[8:12]
    for branch in range(4):
        count, channels, total = rows[branch], CHANNELS[branch], counts[branch]
        stats = moments(stat[2 * branch : 2 * branch + 2, :], channels, total)
        gain = norms[2 * branch + 1 : 2 * branch + 2, :]
        shift_sum = fold(stat_sums[2 * branch : 2 * branch + 1, :], channels) / total
        gain_sum = fold(stat_sums[2 * branch + 1 : 2 * branch + 2, :], channels) / total

        def input_grad(grad, value):
            scaled = (value - stats[0]) * stats[1]
            return (gain * stats[1]) * (grad - shift_sum - scaled * gain_sum)

        inner = input_grad(grads[branch][...], seconds[branch][...])
        wide[branch][:, 16 : (count + 1) * 16, :] = inner.reshape(2, count * 16, 256)
        for image in range(2):
            place = edge_place(branch, image)
            for ref, start, flag in ((above, 0, flags[0]), (below, (count + 1) * 16, flags[1])):
                value = input_grad(
                    ref[place : place + 16, :], ref[128 + place : 144 + place, :]
                )
                wide[branch][image, start : start + 16, :] = jnp.where(flag == 0, 0.0, value)
        build_sides(wide[branch], sides[branch], channels)
        build_band(bands[branch], turned(tap_reader(taps[3 - branch], branch)), branch, 0)
        hidden_grad = dot_nn(patches(wide[branch], sides[branch], count), bands[branch][...])
        first_stats = moments(first_stat[2 * branch : 2 * branch + 2, :], channels, total)
        scaled = (load_rows(firsts[branch], 1, count) - first_stats[0]) * first_stats[1]
        value = (
            scaled * norms[2 * branch : 2 * branch + 1, :]
            + norms[11 + 2 * branch : 12 + 2 * branch, :]
        )
        grad = hidden_grad * silu_slope(value)
        normed_grads[branch][...] = grad
        sums[2 * branch : 2 * branch + 1, :] = column_sum(grad)
        sums[2 * branch + 1 : 2 * branch + 2, :] = column_sum(grad * scaled)
        write_edges(first, last, grad, branch, count, 0)


def finish_grads(packed, meta, stage, unite_grads, outs, scratch):
    if packed:
        pack_grads(meta[2], stage, unite_grads, outs, scratch)
    else:
        for ref, value in zip(outs, stage):
            ref[...] = value[...]


def kernel_grad_second(rows, counts, packed, meta, *refs):
    ins, unite_grads, outs, stage, scratch, hidden, sides, products = split_refs(
        refs, 16, 3, 4, 5, 3, 4, 4, 4
    )
    grads, seconds, firsts = ins[0:4], ins[4:8], ins[8:12]
    stat, stat_sums, first_stat, norms = ins[12:16]
    for branch in range(4):
        count, channels, total = rows[branch], CHANNELS[branch], counts[branch]
        stats = moments(stat[2 * branch : 2 * branch + 2, :], channels, total)
        grad = norm_input_grad(
            grads[branch][...],
            (seconds[branch][...] - stats[0]) * stats[1],
            stats,
            norms[2 * branch + 1 : 2 * branch + 2, :],
            stat_sums[2 * branch : 2 * branch + 2, :],
            channels,
            total,
        )
        fill_hidden(meta, firsts, first_stat, norms, hidden, branch, count, total)
        build_sides(hidden[branch], sides[branch], channels)
        products[branch][...] = dot_tn(patches(hidden[branch], sides[branch], count), grad)
        collect_band(products[branch], branch, tap_writer(stage[3 - branch], branch))
    finish_grads(packed, meta, stage, unite_grads, outs, scratch)


def kernel_grad_first(rows, counts, packed, meta, *refs):
    ins, unite_grads, outs, stage, scratch, sources, sides, products = split_refs(
        refs, 15, 3, 4, 5, 3, 4, 4, 4
    )
    grads, firsts, tiles = ins[0:4], ins[4:8], ins[8:12]
    first_stat, first_sums, norms = ins[12:15]
    for branch in range(4):
        count, channels, total = rows[branch], CHANNELS[branch], counts[branch]
        stats = moments(first_stat[2 * branch : 2 * branch + 2, :], channels, total)
        grad = norm_input_grad(
            grads[branch][...],
            (load_rows(firsts[branch], 1, count) - stats[0]) * stats[1],
            stats,
            norms[2 * branch : 2 * branch + 1, :],
            first_sums[2 * branch : 2 * branch + 2, :],
            channels,
            total,
        )
        sources[branch][...] = tiles[branch][:, 16 : (count + 3) * 16, :]
        build_sides(sources[branch], sides[branch], channels)
        products[branch][...] = dot_tn(patches(sources[branch], sides[branch], count), grad)
        collect_band(products[branch], branch, tap_writer(stage[3 - branch], branch))
    finish_grads(packed, meta, stage, unite_grads, outs, scratch)


def back_first_kernel(rows, counts, flags, *refs):
    ins, source_grads, wide, sides, bands = split_refs(refs, 21, 4, 4, 4, 4)
    normed_grads, firsts, join_grads, taps = ins[0:4], ins[4:8], ins[8:12], ins[12:16]
    above, below, first_stat, first_sums, norms = ins[16:21]
    for branch in range(4):
        count, channels, total = rows[branch], CHANNELS[branch], counts[branch]
        stats = moments(first_stat[2 * branch : 2 * branch + 2, :], channels, total)
        gain = norms[2 * branch : 2 * branch + 1, :]
        shift_sum = fold(first_sums[2 * branch : 2 * branch + 1, :], channels) / total
        gain_sum = fold(first_sums[2 * branch + 1 : 2 * branch + 2, :], channels) / total

        def input_grad(grad, value):
            scaled = (value - stats[0]) * stats[1]
            return (gain * stats[1]) * (grad - shift_sum - scaled * gain_sum)

        inner = input_grad(normed_grads[branch][...], load_rows(firsts[branch], 1, count))
        wide[branch][:, 16 : (count + 1) * 16, :] = inner.reshape(2, count * 16, 256)
        for image in range(2):
            place = edge_place(branch, image)
            for ref, start, flag in ((above, 0, flags[0]), (below, (count + 1) * 16, flags[1])):
                value = input_grad(
                    ref[place : place + 16, :], firsts[branch][image, start : start + 16, :]
                )
                wide[branch][image, start : start + 16, :] = jnp.where(flag == 0, 0.0, value)
        build_sides(wide[branch], sides[branch], channels)
        build_band(bands[branch], turned(tap_reader(taps[3 - branch], branch)), branch, 0)
        grad = dot_nn(patches(wide[branch], sides[branch], count), bands[branch][...])
        grad = (grad + join_grads[branch][...]).reshape(2, count * 16, 256)
        for image in range(2):
            source_grads[branch][image] = grad[image].reshape(count, 4096)


def finish_kernel(first_sums, second_sums, head_sums, gain, shift, loss, head_weight, head_bias):
    offset = 0

    def put(sums, line, channels):
        nonlocal offset
        for ref, row in ((shift, line), (gain, line + 1)):
            ref[0:1, offset : offset + channels] = fold(sums[row : row + 1, :], channels)[:, :channels]
        offset += channels

    for branch in range(4):
        for sums in (first_sums, second_sums):
            put(sums, 2 * branch, CHANNELS[branch])
    for level in range(3):
        put(head_sums, 2 * level, C0)
    loss[...] = jnp.sum(head_sums[6:7, :], axis=1, keepdims=True)
    joints = head_bias.shape[1]
    head_bias[...] = fold(head_sums[7:8, :], C0)[:, :joints]
    for part in range(4):
        head_weight[8 * part : 8 * part + 8, :] = head_sums[16:24, C0 * part : C0 * part + joints]


def device_count():
    return lax.axis_size("dp") * lax.axis_size("space")


def exchange(value, bit):
    return lax.ppermute(value, AXES, [(i, i ^ bit) for i in range(device_count())])


def total_sum(value, order=None):
    value = value.value
    for bit in order or [1 << i for i in range(device_count().bit_length() - 1)]:
        value = value + exchange(value, bit)
    return Kept(value)


def move_rows(first, last):
    devices = lax.axis_size("space")
    down = [(i, i + 1) for i in range(devices - 1)]
    up = [(i + 1, i) for i in range(devices - 1)]
    return lax.ppermute(last, "space", down), lax.ppermute(first, "space", up)


def device_index():
    return lax.axis_index("dp") * lax.axis_size("space") + lax.axis_index("space")


def gather_halves(shard):
    first_half = (device_index() & 16) == 0
    other = exchange(shard, 16)
    halves = []
    for own in (jnp.where(first_half, shard, other), jnp.where(first_half, other, shard)):
        far = exchange(own, 8)
        packs = []
        for cut, order in zip((slice(0, SPLIT), slice(SPLIT, SHARD)), GATHER_ORDER):
            part = jnp.stack([own[cut], far[cut]])
            for bit in order[1::-1]:
                part = jnp.concatenate([part, exchange(part, bit)])
            packs += [part, exchange(part, 1)]
        halves.append(packs)
    return halves


def scatter_half(packs):
    parts = []
    for keep, send, order in zip(packs[0::2], packs[1::2], SCATTER_ORDER):
        value = keep + exchange(send, 1)
        for bit in order:
            half = value.shape[0] // 2
            value = value[:half] + exchange(value[half:], bit)
        parts.append(value[0])
    return jnp.concatenate(parts)


def body(
    branch_zero,
    branch_one,
    branch_two,
    branch_three,
    convs_zero,
    convs_one,
    convs_two,
    convs_three,
    unite_one,
    unite_two,
    unite_three,
    norm_gain,
    norm_shift,
    head_weight,
    head_bias,
    targets,
    crowd_mask,
    person_count,
    flip_order,
):
    inputs = (branch_zero, branch_one, branch_two, branch_three)
    devices = device_count()
    spaces = lax.axis_size("space")
    place = lax.axis_index("space")
    rows = tuple(value.shape[1] for value in inputs)
    counts = tuple(
        float(2 * rows[b] * 16 * (256 // CHANNELS[b]) * devices) for b in range(4)
    )
    joints = head_bias.shape[0]
    cells = [2 * rows[b] * 16 for b in range(4)]
    packed = devices == 32
    shards_in = (convs_three, convs_two, convs_one, convs_zero, unite_one, unite_two, unite_three)
    sizes = [part.shape[0] for part in shards_in]

    if packed:
        gap = jnp.zeros(((24 - ROWS_ONE) * 128,), f32)
        flat = jnp.concatenate([*shards_in[:3], gap, *shards_in[3:]])
        first_packs, second_packs = gather_halves(flat.reshape(SHARD, 128))
    else:
        whole = [lax.all_gather(part, AXES, axis=0, tiled=True) for part in shards_in]
        whole = [
            part.reshape(-1, width)
            for part, width in zip(whole, (128, 128, 64, 32, 32, 32, 32))
        ]
        first_packs = [part[: part.shape[0] // 2] for part in whole]
        second_packs = [part[part.shape[0] // 2 :] for part in whole]

    last_rows = jnp.concatenate([value[:, -2:] for value in inputs], axis=1)
    first_rows = jnp.concatenate([value[:, :2] for value in inputs], axis=1)
    tops, bottoms = move_rows(first_rows, last_rows)
    meta = jnp.stack([place > 0, place < spaces - 1, device_index() & 15]).astype(jnp.int32)

    (norms,) = call(norm_kernel, [norm_gain[None], norm_shift[None]], kept([(22, 256)]), limit=4)

    def head_parts(weight, bias):
        weight = jnp.pad(weight, ((0, 0), (0, C0 - joints)))
        bias = jnp.tile(jnp.pad(bias, (0, C0 - joints)), 8)[None]
        return weight, bias

    weight, bias = head_parts(head_weight, head_bias)
    flip_weight, flip_bias = head_parts(head_weight[:, flip_order], head_bias[flip_order])
    target_cells = jnp.pad(
        jnp.transpose(targets.reshape(2, joints, rows[0], 16, 8), (0, 2, 3, 4, 1)),
        ((0, 0),) * 4 + ((0, C0 - joints),),
    ).reshape(cells[0], 256)
    loss_weight = crowd_mask.astype(f32) / person_count.astype(f32)[:, None, None]
    loss_weight = jnp.broadcast_to(
        loss_weight.reshape(2, rows[0], 16, 8, 1), (2, rows[0], 16, 8, C0)
    ).reshape(cells[0], 256)
    first_meta, weight, bias, flip_weight, flip_bias, target_cells, loss_weight = (
        lax.optimization_barrier(
            (meta, weight, bias, flip_weight, flip_bias, target_cells, loss_weight)
        )
    )

    bands = [band_shape(b, 256) for b in range(4)]
    inner = [(cells[b], 256) for b in range(4)]
    wide = [(2, (rows[b] + 2) * 16, 256) for b in range(4)]
    wider = [(2, (rows[b] + 4) * 16, 256) for b in range(4)]

    def sides_of(shapes):
        return [shape[:2] + (SIDES[b],) for b, shape in enumerate(shapes)]

    eight = (8, 256)
    taps_out = kept(TAPS_OUT) if packed else []
    unpack_scratch = list(PACK_SCRATCH) if packed else []

    out = call(
        functools.partial(first_kernel, rows, packed),
        [first_meta, *inputs, tops, bottoms, *first_packs[:4]],
        kept([*wider, *wide, eight]) + taps_out,
        bands + sides_of(wider) + unpack_scratch,
        smem=1,
        cost=7,
    )
    tiles, firsts = out[0:4], out[4:8]
    first_taps = out[9:] if packed else first_packs
    first_stat = total_sum(out[8])

    out = call(
        functools.partial(second_kernel, rows, counts, packed),
        [meta, *firsts, first_stat, norms, *second_packs[:4]],
        kept([*inner, eight]) + taps_out,
        wide + bands + sides_of(wide) + unpack_scratch,
        smem=1,
        cost=7,
    )
    seconds = out[0:4]
    second_taps = out[5:] if packed else second_packs
    unites = [*first_taps[4:7], *second_taps[4:7]]
    first_taps, second_taps = first_taps[:4], second_taps[:4]
    second_stat = total_sum(out[4])

    out = call(
        functools.partial(third_kernel, rows, counts),
        [*seconds[1:], *tiles[1:], second_stat, norms, *unites],
        kept([*inner[1:], eight]),
    )
    mixes = out[0:3]
    mix_stat = total_sum(out[3])

    denominator = float(counts[0] * joints)
    out = call(
        functools.partial(loss_kernel, rows, counts, denominator),
        [
            seconds[0],
            tiles[0],
            second_stat,
            *mixes,
            mix_stat,
            norms,
            weight,
            bias,
            target_cells,
            loss_weight,
        ],
        kept([inner[0], *inner[1:], (24, 256), inner[0]]),
        cost=3,
    )
    heat, pre_sums, join_zero = out[0], out[1:4], out[5]
    head_sums = total_sum(out[4])

    unite_shapes = [(CHANNELS[b], C0) for b in range(1, 4)]
    out = call(
        functools.partial(join_kernel, rows, counts),
        [
            *pre_sums,
            *mixes,
            *seconds,
            *tiles[1:],
            join_zero,
            second_stat,
            mix_stat,
            head_sums,
            norms,
            *unites,
        ],
        kept([*inner[1:], *unite_shapes, eight]) + [(256, 256), (256, 256)],
        cost=2,
    )
    join_grads = [join_zero, *out[0:3]]
    mixer_grads = [part.value for part in out[3:6]]
    first_mixers = [part[: part.shape[0] // 2] for part in mixer_grads]
    second_mixers = [part[part.shape[0] // 2 :] for part in mixer_grads]
    above, below = move_rows(out[7], out[8])
    second_sums = total_sum(out[6]).value
    second_sums = Kept(jnp.concatenate([head_sums.value[8:10], second_sums[2:8]]))

    out = call(
        functools.partial(back_second_kernel, rows, counts),
        [
            meta,
            *join_grads,
            *seconds,
            *firsts,
            *second_taps,
            above,
            below,
            second_stat,
            second_sums,
            first_stat,
            norms,
        ],
        kept([*inner, eight]) + [(128, 256), (128, 256)],
        wide + sides_of(wide) + bands,
        smem=1,
        cost=7,
    )
    normed_grads = out[0:4]
    above, below = move_rows(out[5], out[6])
    first_sums = total_sum(out[4])

    grads_out = list(PACKS) if packed else list(TAPS_OUT[:4])
    second_kernels = call(
        functools.partial(kernel_grad_second, rows, counts, packed),
        [
            meta,
            *join_grads,
            *seconds,
            *firsts,
            second_stat,
            second_sums,
            first_stat,
            norms,
            *second_mixers,
        ],
        grads_out,
        [*STAGE, *PACK_SCRATCH] + wide + sides_of(wide) + bands,
        smem=1,
        cost=8,
    )
    first_kernels = call(
        functools.partial(kernel_grad_first, rows, counts, packed),
        [
            meta,
            *normed_grads,
            *firsts,
            *tiles,
            first_stat,
            first_sums,
            norms,
            *first_mixers,
        ],
        grads_out,
        [*STAGE, *PACK_SCRATCH] + wide + sides_of(wide) + bands,
        smem=1,
        cost=7,
    )
    if packed:
        second_part = scatter_half(second_kernels)
        first_part = scatter_half(first_kernels)

    source_grads = call(
        functools.partial(back_first_kernel, rows, counts),
        [
            meta,
            *normed_grads,
            *firsts,
            *join_grads,
            *first_taps,
            above,
            below,
            first_stat,
            first_sums,
            norms,
        ],
        [value.shape for value in inputs],
        wide + sides_of(wide) + bands,
        smem=1,
        cost=7,
    )

    late_meta, _ = lax.optimization_barrier((meta, first_sums.value))
    flip_firsts = call(
        functools.partial(first_flip_kernel, rows),
        [late_meta, *tiles, *first_taps],
        kept(wide),
        bands + sides_of(wider),
        smem=1,
        cost=6,
    )
    flip_seconds = call(
        functools.partial(second_flip_kernel, rows, counts),
        [late_meta, *flip_firsts, first_stat, norms, *second_taps],
        kept(inner),
        wide + bands + sides_of(wide),
        smem=1,
        cost=6,
    )
    (heat_mean,) = call(
        functools.partial(flip_kernel, rows, counts),
        [
            *flip_seconds,
            *tiles,
            second_stat,
            *unites,
            mix_stat,
            norms,
            flip_weight,
            flip_bias,
            heat,
        ],
        [inner[0]],
        cost=2,
    )

    if packed:
        first_half = (device_index() & 16) == 0
        shard = jnp.where(first_half, first_part, second_part)
        shard = shard + exchange(jnp.where(first_half, second_part, first_part), 16)
        top = ROWS_THREE + ROWS_TWO + ROWS_ONE
        shard = jnp.concatenate([shard[:top].reshape(-1), shard[-8:].reshape(-1)])
        shards, offset = [], 0
        for size in sizes:
            shards.append(shard[offset : offset + size])
            offset += size
    else:
        flat = [
            jnp.concatenate([one.reshape(-1), two.reshape(-1)])
            for one, two in zip([*first_kernels, *first_mixers], [*second_kernels, *second_mixers])
        ]
        shards = [lax.psum_scatter(part, AXES, scatter_dimension=0, tiled=True) for part in flat]

    gain_grad, shift_grad, loss, head_grad, bias_grad = call(
        finish_kernel,
        [first_sums, second_sums, head_sums],
        [norm_gain[None].shape, norm_shift[None].shape, (1, 1), head_weight.shape, (1, joints)],
        limit=4,
    )
    heat_mean = jnp.transpose(
        heat_mean.reshape(2, rows[0], 16, 8, C0)[..., :joints], (0, 4, 1, 2, 3)
    ).reshape(targets.shape)
    return (
        loss[0, 0],
        heat_mean,
        *source_grads,
        shards[3],
        shards[2],
        shards[1],
        shards[0],
        *shards[4:7],
        gain_grad[0],
        shift_grad[0],
        head_grad,
        bias_grad[0],
    )


def solution(mesh):
    rows = P("dp", "space", None)
    shard = P(("dp", "space"))
    heat = P("dp", None, "space", None)
    return jax.shard_map(
        body,
        mesh=mesh,
        in_specs=(*[rows] * 4, *[shard] * 7, *[P()] * 4, heat, rows, P("dp"), P()),
        out_specs=(P(), heat, *[rows] * 4, *[shard] * 7, *[P()] * 4),
        check_vma=False,
    )
```

```python
import functools

import jax
import jax.numpy as jnp
import numpy as np
from jax import lax
from jax.experimental import pallas as pl
from jax.experimental.pallas import tpu as pltpu
from jax.sharding import PartitionSpec as P

C0 = 32
CHANNELS = (32, 64, 128, 256)
SIDES = (128, 128, 256, 512)
AXES = ("dp", "space")
epsilon = 1e-05
f32 = jnp.float32
high = lax.Precision.HIGH


def dot_nn(left, right):
    return lax.dot_general(left, right, (((1,), (0,)), ((), ())), precision=high, preferred_element_type=f32)


def dot_nt(left, right):
    return lax.dot_general(left, right, (((1,), (1,)), ((), ())), precision=high, preferred_element_type=f32)


def dot_tn(left, right):
    return lax.dot_general(left, right, (((0,), (0,)), ((), ())), precision=high, preferred_element_type=f32)


def sigmoid(value):
    return 1.0 / (1.0 + jnp.exp(-value))


def silu(value):
    return value * sigmoid(value)


def silu_slope(value):
    sigma = sigmoid(value)
    return sigma * (1.0 + value * (1.0 - sigma))


def fold(row, channels):
    step = channels
    while step < 256:
        row = row + pltpu.roll(row, step, 1)
        step = 2 * step
    return row


def column_sum(value):
    return jnp.sum(value, axis=0, keepdims=True)


def moments(sums, channels, count):
    mean = fold(sums[0:1], channels) / count
    square = fold(sums[1:2], channels) / count
    return mean, lax.rsqrt(square - mean * mean + epsilon)


def affine(stats, gain, shift):
    scale = stats[1] * gain
    return scale, shift - stats[0] * scale


def load_rows(ref, first, count):
    lanes = ref.shape[2]
    return ref[:, first * 16 : (first + count) * 16, :].reshape(2 * count * 16, lanes)


def group_index(rows):
    return lax.broadcasted_iota(jnp.int32, (rows, 128), 0) % 16


def side_columns(value, channels):
    rows = value.shape[0]
    group = group_index(rows)
    lane = lax.broadcasted_iota(jnp.int32, (rows, 128), 1)

    def before(part):
        return jnp.where(group == 0, 0.0, pltpu.roll(part, 1, 0))

    def after(part):
        return jnp.where(group == 15, 0.0, pltpu.roll(part, rows - 1, 0))

    low, upper = value[:, :128], value[:, 128:]
    if channels == 256:
        return jnp.concatenate([before(low), before(upper), after(low), after(upper)], axis=1)
    if channels == 128:
        return jnp.concatenate([before(upper), after(low)], axis=1)
    return jnp.where(
        lane < channels, after(low), jnp.where(lane >= 128 - channels, before(upper), 0.0)
    )


def build_sides(source, side, channels):
    rows = source.shape[1]
    for image in range(2):
        side[image] = side_columns(source[image], channels)


def patches(source, side, count):
    parts = []
    for tap_row in range(3):
        parts.append(load_rows(source, tap_row, count))
        parts.append(load_rows(side, tap_row, count))
    return jnp.concatenate(parts, axis=1)


def build_band(band, tap, branch, offset):
    channels = CHANNELS[branch]
    groups = 256 // channels
    side = SIDES[branch]
    height = 256 + side
    if channels < 256:
        band[:, offset : offset + 256] = jnp.zeros((3 * height, 256), f32)
    for tap_row in range(3):
        base = tap_row * height
        for tap_col in range(3):
            matrix = tap(tap_row, tap_col)
            for out in range(groups):
                place = out + tap_col - 1
                if place < 0:
                    row = base + 256 + (0 if channels >= 128 else 128 - channels)
                elif place >= groups:
                    row = base + 256 + (side // 2 if channels >= 128 else 0)
                else:
                    row = base + place * channels
                start = offset + out * channels
                band[row : row + channels, start : start + channels] = matrix


def collect_band(product, branch, emit):
    channels = CHANNELS[branch]
    groups = 256 // channels
    side = SIDES[branch]
    height = 256 + side
    for tap_row in range(3):
        base = tap_row * height
        for tap_col in range(3):
            total = None
            for out in range(groups):
                place = out + tap_col - 1
                if place < 0:
                    row = base + 256 + (0 if channels >= 128 else 128 - channels)
                elif place >= groups:
                    row = base + 256 + (side // 2 if channels >= 128 else 0)
                else:
                    row = base + place * channels
                start = out * channels
                if channels >= 128:
                    block = product[row : row + channels, start : start + channels]
                else:
                    tile = start // 128 * 128
                    block = product[row : row + channels, tile : tile + 128]
                    inner = start - tile
                    if inner:
                        block = pltpu.roll(block, 128 - inner, 1)
                total = block if total is None else total + block
            emit(tap_row, tap_col, total[:, :channels])


def tap_reader(ref, branch):
    channels = CHANNELS[branch]
    if channels == 256:

        def tap(tap_row, tap_col):
            first = (3 * tap_row + tap_col) * 512
            return jnp.concatenate(
                [ref[pl.ds(first, 256, stride=2), :], ref[pl.ds(first + 1, 256, stride=2), :]],
                axis=1,
            )

        return tap

    def tap(tap_row, tap_col):
        first = (3 * tap_row + tap_col) * channels
        return ref[first : first + channels, :]

    return tap


def tap_writer(ref, branch):
    channels = CHANNELS[branch]

    def emit(tap_row, tap_col, value):
        place = 3 * tap_row + tap_col
        if channels == 256:
            ref[pl.ds(place * 512, 256, stride=2), :] = value[:, :128]
            ref[pl.ds(place * 512 + 1, 256, stride=2), :] = value[:, 128:]
        else:
            ref[place * channels : (place + 1) * channels, :] = value

    return emit


SHARD = 392
ROWS_THREE, ROWS_TWO, ROWS_ONE = 288, 72, 18
PER_ZERO, PER_UNITE = 18, (2, 4, 8)
CHUNKS = ((0, 128), (128, 256), (256, 392))
STEPS = ((8, 4, 2), (4, 2, 8), (2, 8, 4))
TAPS_OUT = ((4608, 128), (1152, 128), (576, 64), (288, 32), (32, 32), (64, 32), (128, 32))
PACK_SCRATCH = ((16, 24, 128), (16, 8, 128), (288, 128))
STAGE = ((4608, 128), (1152, 128), (576, 64), (288, 32), (512, 32))


def partner(me, core, place, bits):
    return me ^ (core + sum(bit for i, bit in enumerate(bits) if place >> i & 1))


def shard_parts(device, three, two, one, zero):
    start = device * ROWS_THREE
    return (
        ((0, 128, three.at[pl.ds(pl.multiple_of(start, 8), 128), :]),),
        ((128, 256, three.at[pl.ds(pl.multiple_of(start + 128, 8), 128), :]),),
        (
            (256, 288, three.at[pl.ds(pl.multiple_of(start + 256, 8), 32), :]),
            (288, 360, two.at[pl.ds(pl.multiple_of(device * ROWS_TWO, 8), ROWS_TWO), :]),
            (360, 384, one.at[device]),
            (384, 392, zero.at[device]),
        ),
    )


def unpack_taps(me, packs, taps, scratch):
    three, two, one, zero = taps[:4]
    part_one, part_zero, flat_one = scratch
    for core in range(2):
        for place in range(8):
            for chunk in range(3):
                device = partner(me, core, place, STEPS[chunk])
                parts = shard_parts(device, three, two, part_one, part_zero)[chunk]
                for first, last, ref in parts:
                    ref[...] = packs[core][place, first:last]
    for device in range(16):
        flat_one[device * ROWS_ONE : (device + 1) * ROWS_ONE, :] = part_one[device, 0:ROWS_ONE]
    one[...] = flat_one[...].reshape(one.shape)
    narrow = part_zero[...].reshape(128, 128).reshape(512, 32)
    for device in range(16):
        first = device * 32
        for ref, height in zip(taps[3:7], (PER_ZERO, *PER_UNITE)):
            ref[device * height : (device + 1) * height, :] = narrow[first : first + height]
            first += height


def pack_grads(me, stage, unite_grads, packs, scratch):
    three, two, one, zero, narrow = stage
    part_one, part_zero, flat_one = scratch
    flat_one[...] = one[...].reshape(flat_one.shape)
    for device in range(16):
        part_one[device, 0:ROWS_ONE] = flat_one[device * ROWS_ONE : (device + 1) * ROWS_ONE, :]
        part_one[device, ROWS_ONE:24] = jnp.zeros((24 - ROWS_ONE, 128), f32)
        first = device * 32
        for ref, height in zip((zero, *unite_grads), (PER_ZERO, *PER_UNITE)):
            narrow[first : first + height, :] = ref[device * height : (device + 1) * height, :]
            first += height
    part_zero[...] = narrow[...].reshape(128, 128).reshape(16, 8, 128)
    for core in range(2):
        for place in range(8):
            for chunk in range(3):
                device = partner(me, core, place, STEPS[chunk][::-1])
                parts = shard_parts(device, three, two, part_one, part_zero)[chunk]
                for first, last, ref in parts:
                    packs[core][place, first:last] = ref[...]


def split_shard(meta, shard, other, *outs):
    second = meta[3] == 1
    for out, (first, last) in zip(outs, CHUNKS):
        own, far = shard[first:last], other[first:last]
        out[0, 0] = jnp.where(second, far, own)
        out[0, 1] = jnp.where(second, own, far)


def join_chunks(*refs):
    held, received, outs = split_refs(refs, 3, 3, 3)
    for chunk in range(3):
        count = held[chunk].shape[0]
        outs[chunk][0:count] = held[chunk][...]
        outs[chunk][count : 2 * count] = received[chunk][...]


def join_apart(*refs):
    held, received, first, second = split_refs(refs, 3, 3, 3, 3)
    for chunk in range(3):
        count = held[chunk].shape[0]
        for half, outs in ((0, first), (1, second)):
            outs[chunk][0:count] = held[chunk][:, half]
            outs[chunk][count : 2 * count] = received[chunk][:, half]


def join_whole(*refs):
    held, received, out = split_refs(refs, 3, 3, 1)
    for chunk, (first, last) in enumerate(CHUNKS):
        count = held[chunk].shape[0]
        out[0][0:count, first:last] = held[chunk][...]
        out[0][count : 2 * count, first:last] = received[chunk][...]


def add_cores(*refs):
    kept_ones, received, low, high = split_refs(refs, 2, 2, 3, 3)
    for chunk, (first, last) in enumerate(CHUNKS):
        for half in range(2):
            total = kept_ones[half][:, first:last] + received[half][:, first:last]
            low[chunk][:, half] = total[:4]
            high[chunk][:, half] = total[4:]


def add_received(*refs):
    held, received, low, high = split_refs(refs, 3, 3, 3, 3)
    for chunk in range(3):
        half = held[chunk].shape[0] // 2
        low[chunk][...] = held[chunk][0:half] + received[chunk][0:half]
        high[chunk][...] = held[chunk][half:] + received[chunk][half:]


def add_last(meta, *refs):
    held, received, keep, send = split_refs(refs, 3, 3, 1, 1)
    second = meta[3] == 1
    for chunk, (first, last) in enumerate(CHUNKS):
        total = held[chunk][0] + received[chunk][0]
        keep[0][first:last, :] = jnp.where(second, total[1], total[0])
        send[0][first:last, :] = jnp.where(second, total[0], total[1])


def add_shard(keep, received, three, two, one, rest):
    first = 0
    for ref in (three, two, one):
        last = first + ref.shape[0]
        ref[...] = keep[first:last] + received[first:last]
        first = last
    rest[...] = keep[SHARD - 8 :] + received[SHARD - 8 :]


def mirrored(tap):
    return lambda tap_row, tap_col: tap(tap_row, 2 - tap_col)


def turned(tap):
    return lambda tap_row, tap_col: jnp.transpose(tap(2 - tap_row, 2 - tap_col))


def mask_ends(value, rows, flags):
    place = lax.broadcasted_iota(jnp.int32, value.shape, 0) // 16 % (rows + 2)
    outside = ((place == 0) & (flags[0] == 0)) | ((place == rows + 1) & (flags[1] == 0))
    return jnp.where(outside, 0.0, value)


def mix_matrix(unite, branch):
    channels = CHANNELS[branch]
    groups = 256 // channels
    wide = jnp.concatenate([unite] * 8, axis=1)
    lane = lax.broadcasted_iota(jnp.int32, wide.shape, 1)
    span = 256 // groups
    return jnp.concatenate(
        [jnp.where(lane // span == place, wide, 0.0) for place in range(groups)], axis=0
    )


def split_refs(refs, *counts):
    out, first = [], 0
    for count in counts:
        out.append(refs[first : first + count])
        first += count
    assert first == len(refs)
    return out


class Kept:
    def __init__(self, value):
        self.value = value


def kept(values):
    return [Kept(value) for value in values]


def call(kernel, ins, outs, scratch=(), smem=0, limit=16, cost=1):
    specs = [pl.BlockSpec(memory_space=pltpu.SMEM)] * smem + [
        pl.BlockSpec(memory_space=pltpu.VMEM)
    ] * (len(ins) - smem)
    ins = ins[:smem] + [
        pltpu.with_memory_space_constraint(x.value, pltpu.VMEM)
        if isinstance(x, Kept)
        else pltpu.with_memory_space_constraint(x, pltpu.HBM)
        for x in ins[smem:]
    ]
    shapes = [pltpu.VMEM(x.value, f32) if isinstance(x, Kept) else pltpu.HBM(x, f32) for x in outs]
    results = pl.pallas_call(
        kernel,
        in_specs=specs,
        out_specs=[pl.BlockSpec(memory_space=pltpu.VMEM)] * len(outs),
        out_shape=shapes,
        scratch_shapes=[pltpu.VMEM(shape, f32) for shape in scratch],
        compiler_params=pltpu.CompilerParams(vmem_limit_bytes=limit * 2**20),
        cost_estimate=pl.CostEstimate(
            flops=int(cost * 1.1e9), bytes_accessed=int(cost * 3.0e6), transcendentals=0
        ),
    )(*ins)
    return [Kept(y) if isinstance(x, Kept) else y for x, y in zip(outs, results)]


def band_shape(branch, width):
    return (3 * (256 + SIDES[branch]), width)


def swap_blocks(parts):
    rows = parts[0].shape[0]
    group = lax.broadcasted_iota(jnp.int32, (rows, 128), 1) // 8
    step = 1
    while step < 16:
        high = (group & step) != 0
        parts = [
            jnp.where(high, parts[i], pltpu.roll(parts[i - step], 128 - 8 * step, 1))
            if i & step
            else jnp.where(high, pltpu.roll(parts[i + step], 8 * step, 1), parts[i])
            for i in range(16)
        ]
        step = 2 * step
    return parts


def joint_matrix():
    source = lax.broadcasted_iota(jnp.int32, (256, 256), 0)
    lane = lax.broadcasted_iota(jnp.int32, (256, 256), 1)
    matches = (source // 8 == lane % C0) & (source % 8 == lane // C0) & (source < 136)
    return jnp.where(matches, 1.0, 0.0)


def shift_group(value, group):
    return pltpu.roll(value, 128 - 8 * group, 1) if group else value


def prepare_kernel(people, gain, shift, weight, bias, flip, targets, mask, *outs):
    norms, weight_out, bias_out, flip_weight, flip_bias, target_out, mask_out, scratch = outs
    for base, ref in ((0, gain), (11, shift)):
        offset = 0
        line = base
        sizes = [channels for channels in CHANNELS for _ in range(2)] + [C0] * 3
        for channels in sizes:
            part = ref[0:1, offset : offset + channels]
            norms[line : line + 1, :] = jnp.concatenate([part] * (256 // channels), axis=1)
            offset += channels
            line += 1
    joints = weight.shape[1]
    source = lax.broadcasted_iota(jnp.int32, (joints, joints), 0)
    moved = jnp.where(source == flip[...], 1.0, 0.0)
    for matrix, row, matrix_out, row_out in (
        (weight[...], bias[...], weight_out, bias_out),
        (
            jnp.dot(weight[...], moved, precision=lax.Precision.HIGHEST),
            jnp.dot(bias[...], moved, precision=lax.Precision.HIGHEST),
            flip_weight,
            flip_bias,
        ),
    ):
        matrix_out[...] = jnp.zeros((C0, C0), f32)
        matrix_out[:, 0:joints] = matrix
        row_out[...] = jnp.zeros((1, 256), f32)
        for place in range(8):
            row_out[0:1, C0 * place : C0 * place + joints] = row
    lines = 2 * targets.shape[2]
    parts = swap_blocks([targets[:, j].reshape(lines, 128) for j in range(16)])
    last = targets[:, 16].reshape(lines, 128)
    cells = mask[...].reshape(lines, 128).astype(f32)
    lane = lax.broadcasted_iota(jnp.int32, (lines, 128), 1)
    tails = [
        jnp.where(lane < 8, shift_group(last, group), pltpu.roll(shift_group(cells, group), 8, 1))
        for group in range(16)
    ]
    whole = jnp.concatenate(
        [jnp.concatenate([part, tail], axis=1) for part, tail in zip(parts, tails)], axis=0
    )
    source = lax.broadcasted_iota(jnp.int32, (256, 256), 0)
    target_lane = lax.broadcasted_iota(jnp.int32, (256, 256), 1)
    spread = jnp.where((source >= 136) & (source < 144) & (source - 136 == target_lane // C0), 1.0, 0.0)
    target_rows = dot_nn(whole, joint_matrix())
    mask_rows = dot_nn(whole, spread)
    first_image = lax.broadcasted_iota(jnp.int32, (lines, 256), 0) < lines // 2
    share = jnp.where(first_image, people[0].astype(f32), people[1].astype(f32))
    for value, ref in ((target_rows, target_out), (mask_rows, mask_out)):
        for part in range(2):
            for group in range(16):
                span = slice(group * lines, (group + 1) * lines)
                block = value[span, 128 * part : 128 * part + 128]
                if ref is mask_out:
                    block = block / share[:, :128]
                scratch[pl.ds(group, lines, stride=16), :] = block
            ref[:, 128 * part : 128 * part + 128] = scratch[...]


def first_kernel(rows, packed, meta, *refs):
    xs, tops, bottoms, packs, tiles, mains, sums, taps, bands, sides, scratch = split_refs(
        refs, 4, 1, 1, 2 if packed else 4, 4, 4, 1, 7 * packed, 4, 4, 3 * packed
    )
    sums = sums[0]
    if packed:
        unpack_taps(meta[2], packs, taps, scratch)
    else:
        taps = packs
    for branch in range(4):
        count = rows[branch]
        tile, side, band = tiles[branch], sides[branch], bands[branch]
        for image in range(2):
            for ref, start, first, extent in (
                (tops[0], 2 * branch, 0, 2),
                (xs[branch], 0, 2, count),
                (bottoms[0], 2 * branch, count + 2, 2),
            ):
                tile[image, first * 16 : (first + extent) * 16, :] = ref[
                    image, start : start + extent, :
                ].reshape(extent * 16, 256)
        build_sides(tile, side, CHANNELS[branch])
        build_band(band, tap_reader(taps[3 - branch], branch), branch, 0)
        out = dot_nn(patches(tile, side, count + 2), band[...])
        mains[branch][...] = out.reshape(2, (count + 2) * 16, 256)
        inner = load_rows(mains[branch], 1, count)
        sums[2 * branch : 2 * branch + 1, :] = column_sum(inner)
        sums[2 * branch + 1 : 2 * branch + 2, :] = column_sum(inner * inner)


def first_flip_kernel(rows, meta, *refs):
    tiles, taps, outs, bands, sides = split_refs(refs, 4, 4, 4, 4, 4)
    for branch in range(4):
        count = rows[branch]
        build_sides(tiles[branch], sides[branch], CHANNELS[branch])
        build_band(bands[branch], mirrored(tap_reader(taps[3 - branch], branch)), branch, 0)
        out = dot_nn(patches(tiles[branch], sides[branch], count + 2), bands[branch][...])
        outs[branch][...] = out.reshape(2, (count + 2) * 16, 256)


def fill_hidden(meta, firsts, stat, norms, hidden, branch, count, total):
    stats = moments(stat[2 * branch : 2 * branch + 2, :], CHANNELS[branch], total)
    scale, offset = affine(
        stats,
        norms[2 * branch : 2 * branch + 1, :],
        norms[11 + 2 * branch : 12 + 2 * branch, :],
    )
    value = load_rows(firsts[branch], 0, count + 2) * scale + offset
    value = mask_ends(silu(value), count, meta)
    hidden[branch][...] = value.reshape(2, (count + 2) * 16, 256)


def second_kernel(rows, counts, packed, meta, *refs):
    firsts, stat, norms, packs, outs, sums, taps, hidden, bands, sides, scratch = split_refs(
        refs, 4, 1, 1, 2 if packed else 4, 4, 1, 7 * packed, 4, 4, 4, 3 * packed
    )
    sums = sums[0]
    if packed:
        unpack_taps(meta[2], packs, taps, scratch)
    else:
        taps = packs
    for branch in range(4):
        count, channels = rows[branch], CHANNELS[branch]
        fill_hidden(meta, firsts, stat[0], norms[0], hidden, branch, count, counts[branch])
        build_sides(hidden[branch], sides[branch], channels)
        build_band(bands[branch], tap_reader(taps[3 - branch], branch), branch, 0)
        out = dot_nn(patches(hidden[branch], sides[branch], count), bands[branch][...])
        outs[branch][...] = out
        sums[2 * branch : 2 * branch + 1, :] = column_sum(out)
        sums[2 * branch + 1 : 2 * branch + 2, :] = column_sum(out * out)


def second_flip_kernel(rows, counts, meta, *refs):
    firsts, stat, norms, taps, outs, hidden, bands, sides = split_refs(refs, 4, 1, 1, 4, 4, 4, 4, 4)
    for branch in range(4):
        count, channels = rows[branch], CHANNELS[branch]
        fill_hidden(meta, firsts, stat[0], norms[0], hidden, branch, count, counts[branch])
        build_sides(hidden[branch], sides[branch], channels)
        build_band(bands[branch], mirrored(tap_reader(taps[3 - branch], branch)), branch, 0)
        outs[branch][...] = dot_nn(
            patches(hidden[branch], sides[branch], count), bands[branch][...]
        )


def joined(second, tile, stat, norms, branch, count, total):
    stats = moments(stat[2 * branch : 2 * branch + 2, :], CHANNELS[branch], total)
    gain = norms[2 * branch + 1 : 2 * branch + 2, :]
    shift = norms[12 + 2 * branch : 13 + 2 * branch, :]
    scaled = (second - stats[0]) * stats[1]
    return scaled * gain + shift + load_rows(tile, 2, count), scaled, stats


def third_kernel(rows, counts, *refs):
    seconds, tiles, stat, norms, unites, mixes, sums = split_refs(refs, 3, 3, 1, 1, 6, 3, 1)
    stat, norms, sums = stat[0], norms[0], sums[0]
    for level in range(3):
        branch = level + 1
        value, _, _ = joined(
            seconds[level][...], tiles[level], stat, norms, branch, rows[branch], counts[branch]
        )
        unite = jnp.concatenate([unites[level][...], unites[3 + level][...]], axis=0)
        mixed = dot_nn(silu(value), mix_matrix(unite, branch))
        mixes[level][...] = mixed
        sums[2 * level : 2 * level + 1, :] = column_sum(mixed)
        sums[2 * level + 1 : 2 * level + 2, :] = column_sum(mixed * mixed)
    sums[6:8, :] = jnp.zeros((2, 256), f32)


def spread_rows(value, rows, factor):
    value = value.reshape(2 * rows, 1, 16, 256)
    return jnp.broadcast_to(value, (2 * rows, factor, 16, 256)).reshape(2 * rows * factor * 16, 256)


def gather_rows(value, rows, factor):
    value = value.reshape(2 * rows // factor, factor, 16, 256)
    return jnp.sum(value, axis=1).reshape(2 * rows // factor * 16, 256)


def uniting_stats(stat, level, total):
    return moments(stat[2 * level : 2 * level + 2, :], C0, total * 2.0 ** (level + 1))


def united_sum(base, mixes, stat, norms, rows, counts):
    for level in range(3):
        stats = uniting_stats(stat, level, counts[level + 1])
        scale, offset = affine(
            stats, norms[8 + level : 9 + level, :], norms[19 + level : 20 + level, :]
        )
        base = base + spread_rows(mixes[level] * scale + offset, rows[level + 1], 2 ** (level + 1))
    return base


def head_matrix(weight):
    wide = jnp.concatenate([weight] * 8, axis=1)
    lane = lax.broadcasted_iota(jnp.int32, wide.shape, 1)
    return jnp.concatenate([jnp.where(lane // C0 == place, wide, 0.0) for place in range(8)], axis=0)


def loss_kernel(rows, counts, denominator, *refs):
    ins, outs = split_refs(refs, 12, 6)
    second, tile, stat, mix_one, mix_two, mix_three, mix_stat, norms, weight, bias, targets, mask = ins
    heat_out, sum_one, sum_two, sum_three, sums, join_grad = outs
    count = rows[0]
    join, scaled, _ = joined(second[...], tile, stat, norms, 0, count, counts[0])
    mixes = (mix_one[...], mix_two[...], mix_three[...])
    pre = united_sum(silu(join), mixes, mix_stat, norms, rows, counts)
    united = silu(pre)
    head = head_matrix(weight[...])
    heat = dot_nn(united, head) + bias[...]
    heat_out[...] = heat
    error = heat - targets[...]
    weighted = mask[...] * error
    sums[...] = jnp.zeros(sums.shape, f32)
    sums[6:7, :] = column_sum(weighted * error) / denominator
    heat_grad = weighted * (2.0 / denominator)
    sums[7:8, :] = column_sum(heat_grad)
    product = dot_tn(united, heat_grad)
    total = None
    for place in range(8):
        first = place * C0
        tile_first = first // 128 * 128
        block = product[first : first + C0, tile_first : tile_first + 128]
        if first - tile_first:
            block = pltpu.roll(block, 128 - (first - tile_first), 1)
        total = block if total is None else total + block
    sums[16:24, 0:128] = jnp.concatenate(
        [total[8 * part : 8 * part + 8, :C0] for part in range(4)], axis=1
    )
    grad = dot_nt(heat_grad, head) * silu_slope(pre)
    join_part = grad * silu_slope(join)
    join_grad[...] = join_part
    sums[8:9, :] = column_sum(join_part)
    sums[9:10, :] = column_sum(join_part * scaled)
    for level, out in enumerate((sum_one, sum_two, sum_three)):
        part = gather_rows(grad, count, 2 ** (level + 1))
        out[...] = part
        stats = uniting_stats(mix_stat, level, counts[level + 1])
        normed = (mixes[level] - stats[0]) * stats[1]
        sums[2 * level : 2 * level + 1, :] = column_sum(part)
        sums[2 * level + 1 : 2 * level + 2, :] = column_sum(part * normed)


def flip_kernel(rows, counts, *refs):
    seconds, tiles, stat, unites, mix_stat, norms, weight, bias, heat, out, scratch = split_refs(
        refs, 4, 4, 1, 6, 1, 1, 1, 1, 1, 1, 2
    )
    stat, norms = stat[0], norms[0]
    mixes = []
    for branch in range(4):
        value, _, _ = joined(
            seconds[branch][...], tiles[branch], stat, norms, branch, rows[branch], counts[branch]
        )
        if branch == 0:
            base = silu(value)
        else:
            unite = jnp.concatenate([unites[branch - 1][...], unites[branch + 2][...]], axis=0)
            mixes.append(dot_nn(silu(value), mix_matrix(unite, branch)))
    pre = united_sum(base, mixes, mix_stat[0], norms, rows, counts)
    back = dot_nn(silu(pre), head_matrix(weight[0][...])) + bias[0][...]
    moved = dot_nt(0.5 * (heat[0][...] + back), joint_matrix())
    scratch[0][...] = moved[:, :128]
    scratch[1][...] = moved[:, 128:]
    lines = 2 * rows[0]
    parts = [scratch[0][pl.ds(group, lines, stride=16), :] for group in range(16)]
    lane = lax.broadcasted_iota(jnp.int32, (lines, 128), 1)
    last = None
    for group in range(16):
        tail = scratch[1][pl.ds(group, lines, stride=16), :]
        tail = pltpu.roll(tail, 8 * group, 1) if group else tail
        last = tail if last is None else jnp.where(lane // 8 == group, tail, last)
    for joint, value in enumerate([*swap_blocks(parts), last]):
        out[0][:, joint] = value.reshape(2, rows[0], 128)


def edge_place(branch, image):
    return (2 * branch + image) * 16


def write_edges(first, last, value, branch, count, base):
    for image in range(2):
        place = base + edge_place(branch, image)
        start = image * count * 16
        first[place : place + 16, :] = value[start : start + 16]
        last[place : place + 16, :] = value[start + (count - 1) * 16 : start + count * 16]


def join_kernel(rows, counts, *refs):
    sums_in, mixes, seconds, tiles, join_zero, stat, mix_stat, head_sums, norms, unites, outs = (
        split_refs(refs, 3, 3, 4, 3, 1, 1, 1, 1, 1, 6, 9)
    )
    stat, mix_stat, head_sums, norms = stat[0], mix_stat[0], head_sums[0], norms[0]
    grads, mixer_grads, sums, first, last = outs[0:3], outs[3:6], outs[6], outs[7], outs[8]
    sums[0:2, :] = jnp.zeros((2, 256), f32)
    write_edges(first, last, join_zero[0][...], 0, rows[0], 0)
    write_edges(first, last, seconds[0][...], 0, rows[0], 128)
    for level in range(3):
        branch = level + 1
        channels, count = CHANNELS[branch], rows[branch]
        groups = 256 // channels
        total = counts[branch]
        stats = uniting_stats(mix_stat, level, total)
        gain = norms[8 + level : 9 + level, :]
        shift_sum = fold(head_sums[2 * level : 2 * level + 1, :], C0)
        gain_sum = fold(head_sums[2 * level + 1 : 2 * level + 2, :], C0)
        normed = (mixes[level][...] - stats[0]) * stats[1]
        share = 1.0 / (total * 2.0 ** (level + 1))
        mixed_grad = (gain * stats[1]) * (
            sums_in[level][...] - shift_sum * share - normed * (gain_sum * share)
        )
        value, scaled, _ = joined(
            seconds[branch][...], tiles[level], stat, norms, branch, count, total
        )
        unite = jnp.concatenate([unites[level][...], unites[3 + level][...]], axis=0)
        product = dot_tn(silu(value), mixed_grad)
        mixer = None
        for place in range(8):
            row = place // (8 // groups) * channels
            tile_first = place * C0 // 128 * 128
            block = product[row : row + channels, tile_first : tile_first + 128]
            inner = place * C0 - tile_first
            if inner:
                block = pltpu.roll(block, 128 - inner, 1)
            mixer = block if mixer is None else mixer + block
        mixer_grads[level][...] = mixer[:, :C0]
        grad = dot_nt(mixed_grad, mix_matrix(unite, branch)) * silu_slope(value)
        grads[level][...] = grad
        sums[2 * branch : 2 * branch + 1, :] = column_sum(grad)
        sums[2 * branch + 1 : 2 * branch + 2, :] = column_sum(grad * scaled)
        write_edges(first, last, grad, branch, count, 0)
        write_edges(first, last, seconds[branch][...], branch, count, 128)


def norm_input_grad(grad, scaled, stats, gain, sums, channels, total):
    shift_sum = fold(sums[0:1, :], channels) / total
    gain_sum = fold(sums[1:2, :], channels) / total
    return (gain * stats[1]) * (grad - shift_sum - scaled * gain_sum)


def back_second_kernel(rows, counts, flags, *refs):
    ins, outs, scratch = split_refs(refs, 22, 7, 12)
    grads, seconds, firsts, taps = ins[0:4], ins[4:8], ins[8:12], ins[12:16]
    above, below, stat, stat_sums, first_stat, norms = ins[16:22]
    normed_grads = outs[0:4]
    sums, first, last = outs[4:7]
    wide = scratch[0:4]
    sides = scratch[4:8]
    bands = scratch[8:12]
    for branch in range(4):
        count, channels, total = rows[branch], CHANNELS[branch], counts[branch]
        stats = moments(stat[2 * branch : 2 * branch + 2, :], channels, total)
        gain = norms[2 * branch + 1 : 2 * branch + 2, :]
        shift_sum = fold(stat_sums[2 * branch : 2 * branch + 1, :], channels) / total
        gain_sum = fold(stat_sums[2 * branch + 1 : 2 * branch + 2, :], channels) / total

        def input_grad(grad, value):
            scaled = (value - stats[0]) * stats[1]
            return (gain * stats[1]) * (grad - shift_sum - scaled * gain_sum)

        inner = input_grad(grads[branch][...], seconds[branch][...])
        wide[branch][:, 16 : (count + 1) * 16, :] = inner.reshape(2, count * 16, 256)
        for image in range(2):
            place = edge_place(branch, image)
            for ref, start, flag in ((above, 0, flags[0]), (below, (count + 1) * 16, flags[1])):
                value = input_grad(
                    ref[place : place + 16, :], ref[128 + place : 144 + place, :]
                )
                wide[branch][image, start : start + 16, :] = jnp.where(flag == 0, 0.0, value)
        build_sides(wide[branch], sides[branch], channels)
        build_band(bands[branch], turned(tap_reader(taps[3 - branch], branch)), branch, 0)
        hidden_grad = dot_nn(patches(wide[branch], sides[branch], count), bands[branch][...])
        first_stats = moments(first_stat[2 * branch : 2 * branch + 2, :], channels, total)
        scaled = (load_rows(firsts[branch], 1, count) - first_stats[0]) * first_stats[1]
        value = (
            scaled * norms[2 * branch : 2 * branch + 1, :]
            + norms[11 + 2 * branch : 12 + 2 * branch, :]
        )
        grad = hidden_grad * silu_slope(value)
        normed_grads[branch][...] = grad
        sums[2 * branch : 2 * branch + 1, :] = column_sum(grad)
        sums[2 * branch + 1 : 2 * branch + 2, :] = column_sum(grad * scaled)
        write_edges(first, last, grad, branch, count, 0)


def kernel_grad_second(rows, counts, branch, meta, *refs):
    grad, second, first, stat, stat_sums, first_stat, norms, out, hidden, side, product = refs
    count, channels, total = rows[branch], CHANNELS[branch], counts[branch]
    stats = moments(stat[2 * branch : 2 * branch + 2, :], channels, total)
    value = norm_input_grad(
        grad[...],
        (second[...] - stats[0]) * stats[1],
        stats,
        norms[2 * branch + 1 : 2 * branch + 2, :],
        stat_sums[2 * branch : 2 * branch + 2, :],
        channels,
        total,
    )
    fill_hidden(meta, {branch: first}, first_stat, norms, {branch: hidden}, branch, count, total)
    build_sides(hidden, side, channels)
    product[...] = dot_tn(patches(hidden, side, count), value)
    collect_band(product, branch, tap_writer(out, branch))


def pack_kernel(meta, *refs):
    stage, unite_grads, outs, narrow, scratch = split_refs(refs, 4, 3, 2, 1, 3)
    pack_grads(meta[2], [*stage, *narrow], unite_grads, outs, scratch)


def kernel_grad_first(rows, counts, packed, meta, *refs):
    ins, unite_grads, outs, stage, scratch, sources, sides, products = split_refs(
        refs, 15, 3, 2 if packed else 4, 5, 3, 4, 4, 4
    )
    grads, firsts, tiles = ins[0:4], ins[4:8], ins[8:12]
    first_stat, first_sums, norms = ins[12:15]
    for branch in range(4):
        count, channels, total = rows[branch], CHANNELS[branch], counts[branch]
        stats = moments(first_stat[2 * branch : 2 * branch + 2, :], channels, total)
        grad = norm_input_grad(
            grads[branch][...],
            (load_rows(firsts[branch], 1, count) - stats[0]) * stats[1],
            stats,
            norms[2 * branch : 2 * branch + 1, :],
            first_sums[2 * branch : 2 * branch + 2, :],
            channels,
            total,
        )
        sources[branch][...] = tiles[branch][:, 16 : (count + 3) * 16, :]
        build_sides(sources[branch], sides[branch], channels)
        products[branch][...] = dot_tn(patches(sources[branch], sides[branch], count), grad)
        collect_band(products[branch], branch, tap_writer(stage[3 - branch], branch))
    if packed:
        pack_grads(meta[2], stage, unite_grads, outs, scratch)
    else:
        for ref, value in zip(outs, stage):
            ref[...] = value[...]


def back_first_kernel(rows, counts, flags, *refs):
    ins, source_grads, wide, sides, bands = split_refs(refs, 21, 4, 4, 4, 4)
    normed_grads, firsts, join_grads, taps = ins[0:4], ins[4:8], ins[8:12], ins[12:16]
    above, below, first_stat, first_sums, norms = ins[16:21]
    for branch in range(4):
        count, channels, total = rows[branch], CHANNELS[branch], counts[branch]
        stats = moments(first_stat[2 * branch : 2 * branch + 2, :], channels, total)
        gain = norms[2 * branch : 2 * branch + 1, :]
        shift_sum = fold(first_sums[2 * branch : 2 * branch + 1, :], channels) / total
        gain_sum = fold(first_sums[2 * branch + 1 : 2 * branch + 2, :], channels) / total

        def input_grad(grad, value):
            scaled = (value - stats[0]) * stats[1]
            return (gain * stats[1]) * (grad - shift_sum - scaled * gain_sum)

        inner = input_grad(normed_grads[branch][...], load_rows(firsts[branch], 1, count))
        wide[branch][:, 16 : (count + 1) * 16, :] = inner.reshape(2, count * 16, 256)
        for image in range(2):
            place = edge_place(branch, image)
            for ref, start, flag in ((above, 0, flags[0]), (below, (count + 1) * 16, flags[1])):
                value = input_grad(
                    ref[place : place + 16, :], firsts[branch][image, start : start + 16, :]
                )
                wide[branch][image, start : start + 16, :] = jnp.where(flag == 0, 0.0, value)
        build_sides(wide[branch], sides[branch], channels)
        build_band(bands[branch], turned(tap_reader(taps[3 - branch], branch)), branch, 0)
        grad = dot_nn(patches(wide[branch], sides[branch], count), bands[branch][...])
        grad = (grad + join_grads[branch][...]).reshape(2, count * 16, 256)
        for image in range(2):
            source_grads[branch][image] = grad[image].reshape(count, 4096)


def finish_kernel(first_sums, second_sums, head_sums, gain, shift, loss, head_weight, head_bias):
    offset = 0

    def put(sums, line, channels):
        nonlocal offset
        for ref, row in ((shift, line), (gain, line + 1)):
            value = fold(sums[row : row + 1, :], channels)
            done = 0
            while done < channels:
                place = offset + done
                width = min(channels - done, 128 - place % 128)
                ref[place // 128 : place // 128 + 1, place % 128 : place % 128 + width] = value[
                    :, done : done + width
                ]
                done += width
        offset += channels

    for branch in range(4):
        for sums in (first_sums, second_sums):
            put(sums, 2 * branch, CHANNELS[branch])
    for level in range(3):
        put(head_sums, 2 * level, C0)
    loss[...] = jnp.sum(head_sums[6:7, :], axis=1, keepdims=True)
    joints = head_bias.shape[1]
    head_bias[...] = fold(head_sums[7:8, :], C0)[:, :joints]
    total = jnp.concatenate(
        [head_sums[16:24, C0 * part : C0 * part + C0] for part in range(4)], axis=0
    )
    head_weight[...] = jnp.transpose(total)[:joints]


def device_count():
    return lax.axis_size("dp") * lax.axis_size("space")


def exchange(value, bit):
    return lax.ppermute(value, AXES, [(i, i ^ bit) for i in range(device_count())])


def total_sum(value, beside=()):
    value = value.value
    for step in range(device_count().bit_length() - 1):
        other = exchange(value, 1 << step)
        if step < len(beside) and beside[step]:
            other = after(other, beside[step](value))
        value = value + other
    return Kept(value)


def move_rows(first, last):
    devices = lax.axis_size("space")
    down = [(i, i + 1) for i in range(devices - 1)]
    up = [(i + 1, i) for i in range(devices - 1)]
    return lax.ppermute(last, "space", down), lax.ppermute(first, "space", up)


def device_index():
    return lax.axis_index("dp") * lax.axis_size("space") + lax.axis_index("space")


def after(value, *others):
    return lax.optimization_barrier((value, *others))[0]


def swap(parts, step):
    return [Kept(exchange(part.value, STEPS[chunk][step])) for chunk, part in enumerate(parts)]


def gather_shards(meta, flat, beside):
    other = exchange(flat, 16)
    other = after(other, beside(flat))
    shapes = [(1, 2, last - first, 128) for first, last in CHUNKS]
    parts = call(split_shard, [meta, flat, Kept(other)], kept(shapes), smem=1)
    shapes = [(2, *shape[1:]) for shape in shapes]
    parts = call(join_chunks, [*parts, *swap(parts, 0)], kept(shapes))
    shapes = [(4, *shape[2:]) for shape in shapes]
    parts = call(join_apart, [*parts, *swap(parts, 1)], kept(shapes * 2))
    halves = []
    for half in (parts[:3], parts[3:]):
        (whole,) = call(join_whole, [*half, *swap(half, 2)], kept([(8, SHARD, 128)]))
        halves.append([whole, Kept(exchange(whole.value, 1))])
    return halves


def scatter_shards(meta, packs, beside):
    def both(count):
        return kept([(count, 2, last - first, 128) for first, last in CHUNKS] * 2)

    received = [Kept(exchange(send.value, 1)) for _, send in packs]
    received[0] = Kept(after(received[0].value, beside[0](packs[0][1].value)))
    parts = call(add_cores, [*[keep for keep, _ in packs], *received], both(4), cost=2)
    for step in range(3):
        received = swap(parts[3:], step)
        if beside[1 + step]:
            received[0] = Kept(after(received[0].value, beside[1 + step](parts[3].value)))
        if step < 2:
            parts = call(add_received, [*parts[:3], *received], both(2 - step))
        else:
            keep, send = call(
                add_last, [meta, *parts[:3], *received], kept([(SHARD, 128)] * 2), smem=1
            )
    received = exchange(send.value, 16)
    received = after(received, beside[4](send.value))
    shapes = [(ROWS_THREE, 128), (ROWS_TWO, 128), (ROWS_ONE, 128), (8, 128)]
    return call(add_shard, [keep, Kept(received)], shapes)


def body(
    branch_zero,
    branch_one,
    branch_two,
    branch_three,
    convs_zero,
    convs_one,
    convs_two,
    convs_three,
    unite_one,
    unite_two,
    unite_three,
    norm_gain,
    norm_shift,
    head_weight,
    head_bias,
    targets,
    crowd_mask,
    person_count,
    flip_order,
):
    inputs = (branch_zero, branch_one, branch_two, branch_three)
    devices = device_count()
    spaces = lax.axis_size("space")
    place = lax.axis_index("space")
    rows = tuple(value.shape[1] for value in inputs)
    counts = tuple(
        float(2 * rows[b] * 16 * (256 // CHANNELS[b]) * devices) for b in range(4)
    )
    joints = head_bias.shape[0]
    cells = [2 * rows[b] * 16 for b in range(4)]
    packed = devices == 32
    shards_in = (convs_three, convs_two, convs_one, convs_zero, unite_one, unite_two, unite_three)
    sizes = [part.shape[0] for part in shards_in]

    meta = jnp.stack(
        [place > 0, place < spaces - 1, device_index() & 15, (device_index() & 16) // 16]
    ).astype(jnp.int32)

    state = {}

    def prepare(start):
        parts = lax.optimization_barrier((*inputs, start))[:4]
        last_rows = jnp.concatenate([value[:, -2:] for value in parts], axis=1)
        first_rows = jnp.concatenate([value[:, :2] for value in parts], axis=1)
        state["halo"] = move_rows(first_rows, last_rows)
        state["small"] = call(
            prepare_kernel,
            [
                after(person_count, start),
                norm_gain[None],
                norm_shift[None],
                head_weight,
                head_bias[None],
                flip_order[None],
                targets,
                crowd_mask,
            ],
            kept([(22, 256), (C0, C0), (1, 256), (C0, C0), (1, 256)] + [(cells[0], 256)] * 2),
            [(cells[0], 128)],
            smem=1,
            cost=5,
        )
        return state["small"][0].value

    if packed:
        gap = jnp.zeros(((24 - ROWS_ONE) * 128,), f32)
        flat = jnp.concatenate([*shards_in[:3], gap, *shards_in[3:]]).reshape(SHARD, 128)
        first_packs, second_packs = gather_shards(meta, flat, prepare)
        first_meta = after(meta, second_packs[0].value)
    else:
        prepare(meta)
        whole = [lax.all_gather(part, AXES, axis=0, tiled=True) for part in shards_in]
        whole = [
            part.reshape(-1, width)
            for part, width in zip(whole, (128, 128, 64, 32, 32, 32, 32))
        ]
        first_packs = [part[: part.shape[0] // 2] for part in whole]
        second_packs = [part[part.shape[0] // 2 :] for part in whole]
        first_meta = meta
    tops, bottoms = state["halo"]
    norms, weight, bias, flip_weight, flip_bias, target_cells, loss_weight = state["small"]

    bands = [band_shape(b, 256) for b in range(4)]
    inner = [(cells[b], 256) for b in range(4)]
    wide = [(2, (rows[b] + 2) * 16, 256) for b in range(4)]
    wider = [(2, (rows[b] + 4) * 16, 256) for b in range(4)]

    def sides_of(shapes):
        return [shape[:2] + (SIDES[b],) for b, shape in enumerate(shapes)]

    eight = (8, 256)
    taps_out = kept(TAPS_OUT) if packed else []
    unpack_scratch = list(PACK_SCRATCH) if packed else []

    out = call(
        functools.partial(first_kernel, rows, packed),
        [first_meta, *inputs, tops, bottoms, *first_packs[:4]],
        kept([*wider, *wide, eight]) + taps_out,
        bands + sides_of(wider) + unpack_scratch,
        smem=1,
        cost=7,
    )
    tiles, firsts = out[0:4], out[4:8]
    first_taps = out[9:] if packed else first_packs
    first_stat = total_sum(out[8])

    out = call(
        functools.partial(second_kernel, rows, counts, packed),
        [meta, *firsts, first_stat, norms, *second_packs[:4]],
        kept([*inner, eight]) + taps_out,
        wide + bands + sides_of(wide) + unpack_scratch,
        smem=1,
        cost=7,
    )
    seconds = out[0:4]
    second_taps = out[5:] if packed else second_packs
    unites = [*first_taps[4:7], *second_taps[4:7]]
    first_taps, second_taps = first_taps[:4], second_taps[:4]
    second_stat = total_sum(out[4])

    out = call(
        functools.partial(third_kernel, rows, counts),
        [*seconds[1:], *tiles[1:], second_stat, norms, *unites],
        kept([*inner[1:], eight]),
    )
    mixes = out[0:3]
    mix_stat = total_sum(out[3])

    denominator = float(counts[0] * joints)
    out = call(
        functools.partial(loss_kernel, rows, counts, denominator),
        [
            seconds[0],
            tiles[0],
            second_stat,
            *mixes,
            mix_stat,
            norms,
            weight,
            bias,
            target_cells,
            loss_weight,
        ],
        kept([inner[0], *inner[1:], (24, 256), inner[0]]),
        cost=3,
    )
    heat, pre_sums, join_zero = out[0], out[1:4], out[5]
    head_sums = total_sum(out[4])

    unite_shapes = [(CHANNELS[b], C0) for b in range(1, 4)]
    out = call(
        functools.partial(join_kernel, rows, counts),
        [
            *pre_sums,
            *mixes,
            *seconds,
            *tiles[1:],
            join_zero,
            second_stat,
            mix_stat,
            head_sums,
            norms,
            *unites,
        ],
        kept([*inner[1:], *unite_shapes, eight]) + [(256, 256), (256, 256)],
        cost=2,
    )
    join_grads = [join_zero, *out[0:3]]
    mixer_grads = [part.value for part in out[3:6]]
    first_mixers = [part[: part.shape[0] // 2] for part in mixer_grads]
    second_mixers = [part[part.shape[0] // 2 :] for part in mixer_grads]
    above, below = move_rows(out[7], out[8])
    second_sums = total_sum(out[6]).value
    second_sums = Kept(jnp.concatenate([head_sums.value[8:10], second_sums[2:8]]))

    out = call(
        functools.partial(back_second_kernel, rows, counts),
        [
            meta,
            *join_grads,
            *seconds,
            *firsts,
            *second_taps,
            above,
            below,
            second_stat,
            second_sums,
            first_stat,
            norms,
        ],
        kept([*inner, eight]) + [(128, 256), (128, 256)],
        wide + sides_of(wide) + bands,
        smem=1,
        cost=7,
    )
    normed_grads = out[0:4]
    above, below = move_rows(out[5], out[6])
    stage = [None] * 4

    def second_grad(branch):
        def work(start):
            stage[3 - branch] = call(
                functools.partial(kernel_grad_second, rows, counts, branch),
                [
                    after(meta, start),
                    join_grads[branch],
                    seconds[branch],
                    firsts[branch],
                    second_stat,
                    second_sums,
                    first_stat,
                    norms,
                ],
                kept([TAPS_OUT[3 - branch]]),
                [wide[branch], sides_of(wide)[branch], bands[branch]],
                smem=1,
                cost=2,
            )[0]
            return stage[3 - branch].value

        return work

    first_sums = total_sum(out[4], [None] + [second_grad(branch) for branch in range(4)])

    grads_out = kept([(8, SHARD, 128)] * 2) if packed else list(TAPS_OUT[:4])
    first_kernels = call(
        functools.partial(kernel_grad_first, rows, counts, packed),
        [
            meta,
            *normed_grads,
            *firsts,
            *tiles,
            first_stat,
            first_sums,
            norms,
            *first_mixers,
        ],
        grads_out,
        [*STAGE, *PACK_SCRATCH] + wide + sides_of(wide) + bands,
        smem=1,
        cost=7,
    )
    def back_first(start):
        state["source"] = call(
            functools.partial(back_first_kernel, rows, counts),
            [
                after(meta, start),
                *normed_grads,
                *firsts,
                *join_grads,
                *first_taps,
                above,
                below,
                first_stat,
                first_sums,
                norms,
            ],
            [value.shape for value in inputs],
            wide + sides_of(wide) + bands,
            smem=1,
            cost=7,
        )
        return state["source"][0]

    def flip_first(start):
        state["firsts"] = call(
            functools.partial(first_flip_kernel, rows),
            [after(meta, start), *tiles, *first_taps],
            kept(wide),
            bands + sides_of(wider),
            smem=1,
            cost=6,
        )
        return state["firsts"][0].value

    def flip_second(start):
        state["seconds"] = call(
            functools.partial(second_flip_kernel, rows, counts),
            [after(meta, start), *state["firsts"], first_stat, norms, *second_taps],
            kept(inner),
            wide + bands + sides_of(wide),
            smem=1,
            cost=6,
        )
        return state["seconds"][0].value

    def flip_last(start):
        (state["heat"],) = call(
            functools.partial(flip_kernel, rows, counts),
            [
                *state["seconds"],
                *tiles,
                second_stat,
                *unites,
                mix_stat,
                norms,
                flip_weight,
                Kept(after(flip_bias.value, start)),
                heat,
            ],
            [targets.shape],
            [(cells[0], 128)] * 2,
            cost=5,
        )
        return state["heat"]

    if packed:
        second_kernels = call(
            pack_kernel,
            [after(meta, first_sums.value), *stage, *second_mixers],
            grads_out,
            [STAGE[4], *PACK_SCRATCH],
            smem=1,
        )
        shard_parts = scatter_shards(
            meta, (first_kernels, second_kernels), (flip_first, back_first, flip_second, None, flip_last)
        )
        rest, offset, shards = shard_parts[3].reshape(-1), 0, []
        for size in sizes[3:]:
            shards.append(rest[offset : offset + size])
            offset += size
        shards = [*[part.reshape(-1) for part in shard_parts[:3]], *shards]
    else:
        for work in (flip_first, back_first, flip_second, flip_last):
            work(first_sums.value)
        stage = [part.value for part in stage]
        flat = [
            jnp.concatenate([one.reshape(-1), two.reshape(-1)])
            for one, two in zip([*first_kernels, *first_mixers], [*stage, *second_mixers])
        ]
        shards = [lax.psum_scatter(part, AXES, scatter_dimension=0, tiled=True) for part in flat]

    gain_grad, shift_grad, loss, head_grad, bias_grad = call(
        finish_kernel,
        [first_sums, second_sums, head_sums],
        [(9, 128), (9, 128), (1, 1), (joints, C0), (1, joints)],
        limit=4,
    )
    return (
        loss[0, 0],
        state["heat"],
        *state["source"],
        shards[3],
        shards[2],
        shards[1],
        shards[0],
        *shards[4:7],
        gain_grad.reshape(-1)[: norm_gain.shape[0]],
        shift_grad.reshape(-1)[: norm_shift.shape[0]],
        jnp.transpose(head_grad),
        bias_grad[0],
    )


def solution(mesh):
    rows = P("dp", "space", None)
    shard = P(("dp", "space"))
    heat = P("dp", None, "space", None)
    return jax.shard_map(
        body,
        mesh=mesh,
        in_specs=(*[rows] * 4, *[shard] * 7, *[P()] * 4, heat, rows, P("dp"), P()),
        out_specs=(P(), heat, *[rows] * 4, *[shard] * 7, *[P()] * 4),
        check_vma=False,
    )
```

```python
import functools

import jax
import jax.numpy as jnp
import numpy as np
from jax import lax
from jax.experimental import pallas as pl
from jax.experimental.pallas import tpu as pltpu
from jax.sharding import PartitionSpec as P

C0 = 32
CHANNELS = (32, 64, 128, 256)
SIDES = (128, 128, 256, 512)
AXES = ("dp", "space")
epsilon = 1e-05
f32 = jnp.float32
high = lax.Precision.HIGH


def dot_nn(left, right):
    return lax.dot_general(left, right, (((1,), (0,)), ((), ())), precision=high, preferred_element_type=f32)


def dot_nt(left, right):
    return lax.dot_general(left, right, (((1,), (1,)), ((), ())), precision=high, preferred_element_type=f32)


def dot_tn(left, right):
    return lax.dot_general(left, right, (((0,), (0,)), ((), ())), precision=high, preferred_element_type=f32)


def sigmoid(value):
    return 1.0 / (1.0 + jnp.exp(-value))


def silu(value):
    return value * sigmoid(value)


def silu_slope(value):
    sigma = sigmoid(value)
    return sigma * (1.0 + value * (1.0 - sigma))


def fold(row, channels):
    step = channels
    while step < 256:
        row = row + pltpu.roll(row, step, 1)
        step = 2 * step
    return row


def column_sum(value):
    return jnp.sum(value, axis=0, keepdims=True)


def moments(sums, channels, count):
    mean = fold(sums[0:1], channels) / count
    square = fold(sums[1:2], channels) / count
    return mean, lax.rsqrt(square - mean * mean + epsilon)


def affine(stats, gain, shift):
    scale = stats[1] * gain
    return scale, shift - stats[0] * scale


def load_rows(ref, first, count):
    lanes = ref.shape[2]
    return ref[:, first * 16 : (first + count) * 16, :].reshape(2 * count * 16, lanes)


def group_index(rows):
    return lax.broadcasted_iota(jnp.int32, (rows, 128), 0) % 16


def side_columns(value, channels):
    rows = value.shape[0]
    group = group_index(rows)
    lane = lax.broadcasted_iota(jnp.int32, (rows, 128), 1)

    def before(part):
        return jnp.where(group == 0, 0.0, pltpu.roll(part, 1, 0))

    def after(part):
        return jnp.where(group == 15, 0.0, pltpu.roll(part, rows - 1, 0))

    low, upper = value[:, :128], value[:, 128:]
    if channels == 256:
        return jnp.concatenate([before(low), before(upper), after(low), after(upper)], axis=1)
    if channels == 128:
        return jnp.concatenate([before(upper), after(low)], axis=1)
    return jnp.where(
        lane < channels, after(low), jnp.where(lane >= 128 - channels, before(upper), 0.0)
    )


def build_sides(source, side, channels):
    rows = source.shape[1]
    for image in range(2):
        side[image] = side_columns(source[image], channels)


def patches(source, side, count):
    parts = []
    for tap_row in range(3):
        parts.append(load_rows(source, tap_row, count))
        parts.append(load_rows(side, tap_row, count))
    return jnp.concatenate(parts, axis=1)


def build_band(band, tap, branch, offset):
    channels = CHANNELS[branch]
    groups = 256 // channels
    side = SIDES[branch]
    height = 256 + side
    if channels < 256:
        band[:, offset : offset + 256] = jnp.zeros((3 * height, 256), f32)
    for tap_row in range(3):
        base = tap_row * height
        for tap_col in range(3):
            matrix = tap(tap_row, tap_col)
            for out in range(groups):
                place = out + tap_col - 1
                if place < 0:
                    row = base + 256 + (0 if channels >= 128 else 128 - channels)
                elif place >= groups:
                    row = base + 256 + (side // 2 if channels >= 128 else 0)
                else:
                    row = base + place * channels
                start = offset + out * channels
                band[row : row + channels, start : start + channels] = matrix


def collect_band(product, branch, emit):
    channels = CHANNELS[branch]
    groups = 256 // channels
    side = SIDES[branch]
    height = 256 + side
    for tap_row in range(3):
        base = tap_row * height
        for tap_col in range(3):
            total = None
            for out in range(groups):
                place = out + tap_col - 1
                if place < 0:
                    row = base + 256 + (0 if channels >= 128 else 128 - channels)
                elif place >= groups:
                    row = base + 256 + (side // 2 if channels >= 128 else 0)
                else:
                    row = base + place * channels
                start = out * channels
                if channels >= 128:
                    block = product[row : row + channels, start : start + channels]
                else:
                    tile = start // 128 * 128
                    block = product[row : row + channels, tile : tile + 128]
                    inner = start - tile
                    if inner:
                        block = pltpu.roll(block, 128 - inner, 1)
                total = block if total is None else total + block
            emit(tap_row, tap_col, total[:, :channels])


def tap_reader(ref, branch):
    channels = CHANNELS[branch]
    if channels == 256:

        def tap(tap_row, tap_col):
            first = (3 * tap_row + tap_col) * 512
            return jnp.concatenate(
                [ref[pl.ds(first, 256, stride=2), :], ref[pl.ds(first + 1, 256, stride=2), :]],
                axis=1,
            )

        return tap

    def tap(tap_row, tap_col):
        first = (3 * tap_row + tap_col) * channels
        return ref[first : first + channels, :]

    return tap


def tap_writer(ref, branch):
    channels = CHANNELS[branch]

    def emit(tap_row, tap_col, value):
        place = 3 * tap_row + tap_col
        if channels == 256:
            ref[pl.ds(place * 512, 256, stride=2), :] = value[:, :128]
            ref[pl.ds(place * 512 + 1, 256, stride=2), :] = value[:, 128:]
        else:
            ref[place * channels : (place + 1) * channels, :] = value

    return emit


SHARD = 392
ROWS_THREE, ROWS_TWO, ROWS_ONE = 288, 72, 18
PER_ZERO, PER_UNITE = 18, (2, 4, 8)
CHUNKS = ((0, 128), (128, 256), (256, 392))
STEPS = ((8, 4, 2), (4, 2, 8), (2, 8, 4))
TAPS_OUT = ((4608, 128), (1152, 128), (576, 64), (288, 32), (32, 32), (64, 32), (128, 32))
PACK_SCRATCH = ((16, 24, 128), (16, 8, 128), (288, 128))
STAGE = ((4608, 128), (1152, 128), (576, 64), (288, 32), (512, 32))


def partner(me, core, place, bits):
    return me ^ (core + sum(bit for i, bit in enumerate(bits) if place >> i & 1))


def shard_parts(device, three, two, one, zero):
    start = device * ROWS_THREE
    return (
        ((0, 128, three.at[pl.ds(pl.multiple_of(start, 8), 128), :]),),
        ((128, 256, three.at[pl.ds(pl.multiple_of(start + 128, 8), 128), :]),),
        (
            (256, 288, three.at[pl.ds(pl.multiple_of(start + 256, 8), 32), :]),
            (288, 360, two.at[pl.ds(pl.multiple_of(device * ROWS_TWO, 8), ROWS_TWO), :]),
            (360, 384, one.at[device]),
            (384, 392, zero.at[device]),
        ),
    )


def unpack_taps(me, packs, taps, scratch):
    three, two, one, zero = taps[:4]
    part_one, part_zero, flat_one = scratch
    for core in range(2):
        for place in range(8):
            for chunk in range(3):
                device = partner(me, core, place, STEPS[chunk])
                parts = shard_parts(device, three, two, part_one, part_zero)[chunk]
                for first, last, ref in parts:
                    ref[...] = packs[core][place, first:last]
    for device in range(16):
        flat_one[device * ROWS_ONE : (device + 1) * ROWS_ONE, :] = part_one[device, 0:ROWS_ONE]
    one[...] = flat_one[...].reshape(one.shape)
    narrow = part_zero[...].reshape(128, 128).reshape(512, 32)
    for device in range(16):
        first = device * 32
        for ref, height in zip(taps[3:7], (PER_ZERO, *PER_UNITE)):
            ref[device * height : (device + 1) * height, :] = narrow[first : first + height]
            first += height


def pack_grads(me, stage, unite_grads, packs, scratch):
    three, two, one, zero, narrow = stage
    part_one, part_zero, flat_one = scratch
    flat_one[...] = one[...].reshape(flat_one.shape)
    for device in range(16):
        part_one[device, 0:ROWS_ONE] = flat_one[device * ROWS_ONE : (device + 1) * ROWS_ONE, :]
        part_one[device, ROWS_ONE:24] = jnp.zeros((24 - ROWS_ONE, 128), f32)
        first = device * 32
        for ref, height in zip((zero, *unite_grads), (PER_ZERO, *PER_UNITE)):
            narrow[first : first + height, :] = ref[device * height : (device + 1) * height, :]
            first += height
    part_zero[...] = narrow[...].reshape(128, 128).reshape(16, 8, 128)
    for core in range(2):
        for place in range(8):
            for chunk in range(3):
                device = partner(me, core, place, STEPS[chunk][::-1])
                parts = shard_parts(device, three, two, part_one, part_zero)[chunk]
                for first, last, ref in parts:
                    packs[core][place, first:last] = ref[...]


def split_shard(meta, shard, other, *outs):
    second = meta[3] == 1
    for out, (first, last) in zip(outs, CHUNKS):
        own, far = shard[first:last], other[first:last]
        out[0, 0] = jnp.where(second, far, own)
        out[0, 1] = jnp.where(second, own, far)


def join_chunks(*refs):
    held, received, outs = split_refs(refs, 3, 3, 3)
    for chunk in range(3):
        count = held[chunk].shape[0]
        outs[chunk][0:count] = held[chunk][...]
        outs[chunk][count : 2 * count] = received[chunk][...]


def join_apart(*refs):
    held, received, first, second = split_refs(refs, 3, 3, 3, 3)
    for chunk in range(3):
        count = held[chunk].shape[0]
        for half, outs in ((0, first), (1, second)):
            outs[chunk][0:count] = held[chunk][:, half]
            outs[chunk][count : 2 * count] = received[chunk][:, half]


def join_whole(*refs):
    held, received, out = split_refs(refs, 3, 3, 1)
    for chunk, (first, last) in enumerate(CHUNKS):
        count = held[chunk].shape[0]
        out[0][0:count, first:last] = held[chunk][...]
        out[0][count : 2 * count, first:last] = received[chunk][...]


def add_received(*refs):
    held, received, low, high = split_refs(refs, 3, 3, 3, 3)
    for chunk in range(3):
        half = held[chunk].shape[0] // 2
        low[chunk][...] = held[chunk][0:half] + received[chunk][0:half]
        high[chunk][...] = held[chunk][half:] + received[chunk][half:]


def add_cores(keep, received, *refs):
    low, high = split_refs(refs, 3, 3)
    for chunk, (first, last) in enumerate(CHUNKS):
        low[chunk][...] = keep[0:4, first:last] + received[0:4, first:last]
        high[chunk][...] = keep[4:8, first:last] + received[4:8, first:last]


def add_last(*refs):
    held, received, out = split_refs(refs, 3, 3, 1)
    for chunk, (first, last) in enumerate(CHUNKS):
        out[0][first:last, :] = held[chunk][0] + received[chunk][0]


def add_apart(meta, *refs):
    held, received, second, keep, send = split_refs(refs, 3, 3, 1, 1, 1)
    is_second = meta[3] == 1
    for chunk, (first, last) in enumerate(CHUNKS):
        one = held[chunk][0] + received[chunk][0]
        two = second[0][first:last, :]
        keep[0][first:last, :] = jnp.where(is_second, two, one)
        send[0][first:last, :] = jnp.where(is_second, one, two)


def add_shard(keep, received, *outs):
    value = keep[...] + received[...]
    first = 0
    for ref in outs[:3]:
        last = first + ref.shape[0]
        ref[...] = value[first:last]
        first = last
    tail = SHARD - 8
    outs[3][...] = value[tail : tail + 5]
    outs[4][...] = value[tail + 4 : tail + 5, 64:]
    outs[5][...] = value[tail + 5 : tail + 6]
    outs[6][...] = value[tail + 6 : tail + 8]


def mirrored(tap):
    return lambda tap_row, tap_col: tap(tap_row, 2 - tap_col)


def turned(tap):
    return lambda tap_row, tap_col: jnp.transpose(tap(2 - tap_row, 2 - tap_col))


def mask_ends(value, rows, flags):
    place = lax.broadcasted_iota(jnp.int32, value.shape, 0) // 16 % (rows + 2)
    outside = ((place == 0) & (flags[0] == 0)) | ((place == rows + 1) & (flags[1] == 0))
    return jnp.where(outside, 0.0, value)


def mix_matrix(unite, branch):
    channels = CHANNELS[branch]
    groups = 256 // channels
    wide = jnp.concatenate([unite] * 8, axis=1)
    lane = lax.broadcasted_iota(jnp.int32, wide.shape, 1)
    span = 256 // groups
    return jnp.concatenate(
        [jnp.where(lane // span == place, wide, 0.0) for place in range(groups)], axis=0
    )


def split_refs(refs, *counts):
    out, first = [], 0
    for count in counts:
        out.append(refs[first : first + count])
        first += count
    assert first == len(refs)
    return out


class Kept:
    def __init__(self, value):
        self.value = value


def kept(values):
    return [Kept(value) for value in values]


def call(kernel, ins, outs, scratch=(), smem=0, limit=16, cost=1):
    specs = [pl.BlockSpec(memory_space=pltpu.SMEM)] * smem + [
        pl.BlockSpec(memory_space=pltpu.VMEM)
    ] * (len(ins) - smem)
    ins = ins[:smem] + [
        pltpu.with_memory_space_constraint(x.value, pltpu.VMEM)
        if isinstance(x, Kept)
        else pltpu.with_memory_space_constraint(x, pltpu.HBM)
        for x in ins[smem:]
    ]
    shapes = [pltpu.VMEM(x.value, f32) if isinstance(x, Kept) else pltpu.HBM(x, f32) for x in outs]
    results = pl.pallas_call(
        kernel,
        in_specs=specs,
        out_specs=[pl.BlockSpec(memory_space=pltpu.VMEM)] * len(outs),
        out_shape=shapes,
        scratch_shapes=[pltpu.VMEM(shape, f32) for shape in scratch],
        compiler_params=pltpu.CompilerParams(vmem_limit_bytes=limit * 2**20),
        cost_estimate=pl.CostEstimate(
            flops=int(cost * 1.1e9), bytes_accessed=int(cost * 3.0e6), transcendentals=0
        ),
    )(*ins)
    return [Kept(y) if isinstance(x, Kept) else y for x, y in zip(outs, results)]


def band_shape(branch, width):
    return (3 * (256 + SIDES[branch]), width)


def swap_blocks(parts):
    rows = parts[0].shape[0]
    group = lax.broadcasted_iota(jnp.int32, (rows, 128), 1) // 8
    step = 1
    while step < 16:
        high = (group & step) != 0
        parts = [
            jnp.where(high, parts[i], pltpu.roll(parts[i - step], 128 - 8 * step, 1))
            if i & step
            else jnp.where(high, pltpu.roll(parts[i + step], 8 * step, 1), parts[i])
            for i in range(16)
        ]
        step = 2 * step
    return parts


def joint_matrix():
    source = lax.broadcasted_iota(jnp.int32, (256, 256), 0)
    lane = lax.broadcasted_iota(jnp.int32, (256, 256), 1)
    matches = (source // 8 == lane % C0) & (source % 8 == lane // C0) & (source < 136)
    return jnp.where(matches, 1.0, 0.0)


def shift_group(value, group):
    return pltpu.roll(value, 128 - 8 * group, 1) if group else value


def parameter_kernel(gain, shift, weight, bias, flip, *outs):
    norms, weight_out, bias_out, flip_weight, flip_bias = outs
    weight = jnp.transpose(weight[...])
    for base, ref in ((0, gain), (11, shift)):
        offset = 0
        line = base
        sizes = [channels for channels in CHANNELS for _ in range(2)] + [C0] * 3
        for channels in sizes:
            part = ref[0:1, offset : offset + channels]
            norms[line : line + 1, :] = jnp.concatenate([part] * (256 // channels), axis=1)
            offset += channels
            line += 1
    joints = weight.shape[1]
    source = lax.broadcasted_iota(jnp.int32, (joints, joints), 0)
    moved = jnp.where(source == flip[...], 1.0, 0.0)
    for matrix, row, matrix_out, row_out in (
        (weight, bias[...], weight_out, bias_out),
        (
            jnp.dot(weight, moved, precision=lax.Precision.HIGHEST),
            jnp.dot(bias[...], moved, precision=lax.Precision.HIGHEST),
            flip_weight,
            flip_bias,
        ),
    ):
        matrix_out[...] = jnp.zeros((C0, C0), f32)
        matrix_out[:, 0:joints] = matrix
        row_out[...] = jnp.zeros((1, 256), f32)
        for place in range(8):
            row_out[0:1, C0 * place : C0 * place + joints] = row


def target_kernel(people, targets, mask, target_out, mask_out, scratch):
    lines = 2 * targets.shape[2]
    parts = swap_blocks([targets[:, j].reshape(lines, 128) for j in range(16)])
    last = targets[:, 16].reshape(lines, 128)
    cells = mask[...].reshape(lines, 128).astype(f32)
    lane = lax.broadcasted_iota(jnp.int32, (lines, 128), 1)
    tails = [
        jnp.where(lane < 8, shift_group(last, group), pltpu.roll(shift_group(cells, group), 8, 1))
        for group in range(16)
    ]
    whole = jnp.concatenate(
        [jnp.concatenate([part, tail], axis=1) for part, tail in zip(parts, tails)], axis=0
    )
    source = lax.broadcasted_iota(jnp.int32, (256, 256), 0)
    target_lane = lax.broadcasted_iota(jnp.int32, (256, 256), 1)
    spread = jnp.where((source >= 136) & (source < 144) & (source - 136 == target_lane // C0), 1.0, 0.0)
    target_rows = dot_nn(whole, joint_matrix())
    mask_rows = dot_nn(whole, spread)
    first_image = lax.broadcasted_iota(jnp.int32, (lines, 256), 0) < lines // 2
    share = jnp.where(first_image, people[0].astype(f32), people[1].astype(f32))
    for value, ref in ((target_rows, target_out), (mask_rows, mask_out)):
        for part in range(2):
            for group in range(16):
                span = slice(group * lines, (group + 1) * lines)
                block = value[span, 128 * part : 128 * part + 128]
                if ref is mask_out:
                    block = block / share[:, :128]
                scratch[pl.ds(group, lines, stride=16), :] = block
            ref[:, 128 * part : 128 * part + 128] = scratch[...]


def first_kernel(rows, packed, meta, *refs):
    xs, near, far, packs, tiles, mains, sums, taps, bands, sides, scratch = split_refs(
        refs, 4, 1, 1, 2 if packed else 4, 4, 4, 1, 7 * packed, 4, 4, 3 * packed
    )
    sums = sums[0]
    if packed:
        unpack_taps(meta[2], packs, taps, scratch)
    else:
        taps = packs
    odd = meta[4] == 1
    for branch in range(4):
        count = rows[branch]
        tile, side, band = tiles[branch], sides[branch], bands[branch]
        for image in range(2):
            one, two = (ref[0][image, 2 * branch : 2 * branch + 2, :] for ref in (near, far))
            for value, first, extent in (
                (jnp.where(odd, one, two), 0, 2),
                (xs[branch][image], 2, count),
                (jnp.where(odd, two, one), count + 2, 2),
            ):
                tile[image, first * 16 : (first + extent) * 16, :] = value.reshape(extent * 16, 256)
        build_sides(tile, side, CHANNELS[branch])
        build_band(band, tap_reader(taps[3 - branch], branch), branch, 0)
        out = dot_nn(patches(tile, side, count + 2), band[...])
        mains[branch][...] = out.reshape(2, (count + 2) * 16, 256)
        inner = load_rows(mains[branch], 1, count)
        sums[2 * branch : 2 * branch + 1, :] = column_sum(inner)
        sums[2 * branch + 1 : 2 * branch + 2, :] = column_sum(inner * inner)


def first_flip_kernel(rows, branch, meta, tile, taps, out, band, side):
    count = rows[branch]
    build_sides(tile, side, CHANNELS[branch])
    build_band(band, mirrored(tap_reader(taps, branch)), branch, 0)
    value = dot_nn(patches(tile, side, count + 2), band[...])
    out[...] = value.reshape(2, (count + 2) * 16, 256)


def fill_hidden(meta, firsts, stat, norms, hidden, branch, count, total):
    stats = moments(stat[2 * branch : 2 * branch + 2, :], CHANNELS[branch], total)
    scale, offset = affine(
        stats,
        norms[2 * branch : 2 * branch + 1, :],
        norms[11 + 2 * branch : 12 + 2 * branch, :],
    )
    value = load_rows(firsts[branch], 0, count + 2) * scale + offset
    value = mask_ends(silu(value), count, meta)
    hidden[branch][...] = value.reshape(2, (count + 2) * 16, 256)


def band_kernel(packed, meta, *refs):
    packs, taps, bands, scratch = split_refs(refs, 2 if packed else 4, 7 * packed, 4, 3 * packed)
    if packed:
        unpack_taps(meta[2], packs, taps, scratch)
    else:
        taps = packs
    for branch in range(4):
        build_band(bands[branch], tap_reader(taps[3 - branch], branch), branch, 0)


def turned_kernel(meta, *refs):
    taps, bands = split_refs(refs, 4, 4)
    for branch in range(4):
        build_band(bands[branch], turned(tap_reader(taps[3 - branch], branch)), branch, 0)


def second_kernel(rows, counts, meta, *refs):
    firsts, stat, norms, bands, outs, sums, hidden, sides = split_refs(refs, 4, 1, 1, 4, 4, 1, 4, 4)
    sums = sums[0]
    for branch in range(4):
        count, channels = rows[branch], CHANNELS[branch]
        fill_hidden(meta, firsts, stat[0], norms[0], hidden, branch, count, counts[branch])
        build_sides(hidden[branch], sides[branch], channels)
        out = dot_nn(patches(hidden[branch], sides[branch], count), bands[branch][...])
        outs[branch][...] = out
        sums[2 * branch : 2 * branch + 1, :] = column_sum(out)
        sums[2 * branch + 1 : 2 * branch + 2, :] = column_sum(out * out)


def second_flip_kernel(rows, counts, branch, meta, first, stat, norms, taps, out, hidden, band, side):
    count, channels = rows[branch], CHANNELS[branch]
    fill_hidden(meta, {branch: first}, stat, norms, {branch: hidden}, branch, count, counts[branch])
    build_sides(hidden, side, channels)
    build_band(band, mirrored(tap_reader(taps, branch)), branch, 0)
    out[...] = dot_nn(patches(hidden, side, count), band[...])


def joined(second, tile, stat, norms, branch, count, total):
    stats = moments(stat[2 * branch : 2 * branch + 2, :], CHANNELS[branch], total)
    gain = norms[2 * branch + 1 : 2 * branch + 2, :]
    shift = norms[12 + 2 * branch : 13 + 2 * branch, :]
    scaled = (second - stats[0]) * stats[1]
    return scaled * gain + shift + load_rows(tile, 2, count), scaled, stats


def third_kernel(rows, counts, *refs):
    seconds, tiles, stat, norms, unites, mixes, sums = split_refs(refs, 3, 3, 1, 1, 6, 3, 1)
    stat, norms, sums = stat[0], norms[0], sums[0]
    for level in range(3):
        branch = level + 1
        value, _, _ = joined(
            seconds[level][...], tiles[level], stat, norms, branch, rows[branch], counts[branch]
        )
        unite = jnp.concatenate([unites[level][...], unites[3 + level][...]], axis=0)
        mixed = dot_nn(silu(value), mix_matrix(unite, branch))
        mixes[level][...] = mixed
        sums[2 * level : 2 * level + 1, :] = column_sum(mixed)
        sums[2 * level + 1 : 2 * level + 2, :] = column_sum(mixed * mixed)
    sums[6:8, :] = jnp.zeros((2, 256), f32)


def spread_rows(value, rows, factor):
    value = value.reshape(2 * rows, 1, 16, 256)
    return jnp.broadcast_to(value, (2 * rows, factor, 16, 256)).reshape(2 * rows * factor * 16, 256)


def gather_rows(value, rows, factor):
    value = value.reshape(2 * rows // factor, factor, 16, 256)
    return jnp.sum(value, axis=1).reshape(2 * rows // factor * 16, 256)


def uniting_stats(stat, level, total):
    return moments(stat[2 * level : 2 * level + 2, :], C0, total * 2.0 ** (level + 1))


def united_sum(base, mixes, stat, norms, rows, counts):
    for level in range(3):
        stats = uniting_stats(stat, level, counts[level + 1])
        scale, offset = affine(
            stats, norms[8 + level : 9 + level, :], norms[19 + level : 20 + level, :]
        )
        base = base + spread_rows(mixes[level] * scale + offset, rows[level + 1], 2 ** (level + 1))
    return base


def head_matrix(weight):
    wide = jnp.concatenate([weight] * 8, axis=1)
    lane = lax.broadcasted_iota(jnp.int32, wide.shape, 1)
    return jnp.concatenate([jnp.where(lane // C0 == place, wide, 0.0) for place in range(8)], axis=0)


def loss_kernel(rows, counts, denominator, *refs):
    ins, outs = split_refs(refs, 12, 9)
    second, tile, stat, mix_one, mix_two, mix_three, mix_stat, norms, weight, bias, targets, mask = ins
    heat_out, sum_one, sum_two, sum_three, sums, join_grad, zero_sums, united_out, grad_out = outs
    count = rows[0]
    join, scaled, _ = joined(second[...], tile, stat, norms, 0, count, counts[0])
    mixes = (mix_one[...], mix_two[...], mix_three[...])
    pre = united_sum(silu(join), mixes, mix_stat, norms, rows, counts)
    united = silu(pre)
    head = head_matrix(weight[...])
    heat = dot_nn(united, head) + bias[...]
    heat_out[...] = heat
    error = heat - targets[...]
    weighted = mask[...] * error
    sums[6:7, :] = column_sum(weighted * error) / denominator
    heat_grad = weighted * (2.0 / denominator)
    sums[7:8, :] = column_sum(heat_grad)
    united_out[...] = united
    grad_out[...] = heat_grad
    grad = dot_nt(heat_grad, head) * silu_slope(pre)
    join_part = grad * silu_slope(join)
    join_grad[...] = join_part
    zero_sums[0:1, :] = column_sum(join_part)
    zero_sums[1:2, :] = column_sum(join_part * scaled)
    for level, out in enumerate((sum_one, sum_two, sum_three)):
        part = gather_rows(grad, count, 2 ** (level + 1))
        out[...] = part
        stats = uniting_stats(mix_stat, level, counts[level + 1])
        normed = (mixes[level] - stats[0]) * stats[1]
        sums[2 * level : 2 * level + 1, :] = column_sum(part)
        sums[2 * level + 1 : 2 * level + 2, :] = column_sum(part * normed)


def head_kernel(meta, united, heat_grad, out):
    product = dot_tn(united[...], heat_grad[...])
    total = None
    for place in range(8):
        first = place * C0
        tile_first = first // 128 * 128
        block = product[first : first + C0, tile_first : tile_first + 128]
        if first - tile_first:
            block = pltpu.roll(block, 128 - (first - tile_first), 1)
        total = block if total is None else total + block
    out[...] = jnp.zeros(out.shape, f32)
    out[:, 0:128] = jnp.concatenate(
        [total[8 * part : 8 * part + 8, :C0] for part in range(4)], axis=1
    )


def flip_kernel(rows, counts, *refs):
    seconds, tiles, stat, unites, mix_stat, norms, weight, bias, heat, out, scratch = split_refs(
        refs, 4, 4, 1, 6, 1, 1, 1, 1, 1, 1, 2
    )
    stat, norms = stat[0], norms[0]
    mixes = []
    for branch in range(4):
        value, _, _ = joined(
            seconds[branch][...], tiles[branch], stat, norms, branch, rows[branch], counts[branch]
        )
        if branch == 0:
            base = silu(value)
        else:
            unite = jnp.concatenate([unites[branch - 1][...], unites[branch + 2][...]], axis=0)
            mixes.append(dot_nn(silu(value), mix_matrix(unite, branch)))
    pre = united_sum(base, mixes, mix_stat[0], norms, rows, counts)
    back = dot_nn(silu(pre), head_matrix(weight[0][...])) + bias[0][...]
    moved = dot_nt(0.5 * (heat[0][...] + back), joint_matrix())
    scratch[0][...] = moved[:, :128]
    scratch[1][...] = moved[:, 128:]
    lines = 2 * rows[0]
    parts = [scratch[0][pl.ds(group, lines, stride=16), :] for group in range(16)]
    lane = lax.broadcasted_iota(jnp.int32, (lines, 128), 1)
    last = None
    for group in range(16):
        tail = scratch[1][pl.ds(group, lines, stride=16), :]
        tail = pltpu.roll(tail, 8 * group, 1) if group else tail
        last = tail if last is None else jnp.where(lane // 8 == group, tail, last)
    for joint, value in enumerate([*swap_blocks(parts), last]):
        out[0][:, joint] = value.reshape(2, rows[0], 128)


def edge_place(branch, image):
    return (2 * branch + image) * 16


def write_edges(odd, near, far, value, branch, count, base):
    for image in range(2):
        place = base + edge_place(branch, image)
        start = image * count * 16
        first = value[start : start + 16]
        last = value[start + (count - 1) * 16 : start + count * 16]
        near[place : place + 16, :] = jnp.where(odd, first, last)
        far[place : place + 16, :] = jnp.where(odd, last, first)


def join_kernel(rows, counts, meta, *refs):
    sums_in, mixes, seconds, tiles, join_zero, small, unites, outs = split_refs(
        refs, 3, 3, 4, 3, 1, 6, 6, 9
    )
    zero_sums, head_grad, stat, mix_stat, head_sums, norms = small
    grads, mixed_grads, sums, near, far = outs[0:3], outs[3:6], outs[6], outs[7], outs[8]
    odd = meta[4] == 1
    sums[0:2, :] = zero_sums[0:2, :]
    sums[8:16, :] = head_grad[...]
    write_edges(odd, near, far, join_zero[0][...], 0, rows[0], 0)
    write_edges(odd, near, far, seconds[0][...], 0, rows[0], 128)
    for level in range(3):
        branch = level + 1
        channels, count = CHANNELS[branch], rows[branch]
        total = counts[branch]
        stats = uniting_stats(mix_stat, level, total)
        gain = norms[8 + level : 9 + level, :]
        shift_sum = fold(head_sums[2 * level : 2 * level + 1, :], C0)
        gain_sum = fold(head_sums[2 * level + 1 : 2 * level + 2, :], C0)
        normed = (mixes[level][...] - stats[0]) * stats[1]
        share = 1.0 / (total * 2.0 ** (level + 1))
        mixed_grad = (gain * stats[1]) * (
            sums_in[level][...] - shift_sum * share - normed * (gain_sum * share)
        )
        mixed_grads[level][...] = mixed_grad
        value, scaled, _ = joined(
            seconds[branch][...], tiles[level], stat, norms, branch, count, total
        )
        unite = jnp.concatenate([unites[level][...], unites[3 + level][...]], axis=0)
        grad = dot_nt(mixed_grad, mix_matrix(unite, branch)) * silu_slope(value)
        grads[level][...] = grad
        sums[2 * branch : 2 * branch + 1, :] = column_sum(grad)
        sums[2 * branch + 1 : 2 * branch + 2, :] = column_sum(grad * scaled)
        write_edges(odd, near, far, grad, branch, count, 0)
        write_edges(odd, near, far, seconds[branch][...], branch, count, 128)


def mixer_kernel(rows, counts, meta, *refs):
    mixed_grads, seconds, tiles, stat, norms, outs = split_refs(refs, 3, 3, 3, 1, 1, 6)
    for level in range(3):
        branch = level + 1
        channels = CHANNELS[branch]
        value, _, _ = joined(
            seconds[level][...], tiles[level], stat[0], norms[0], branch, rows[branch], counts[branch]
        )
        product = dot_tn(silu(value), mixed_grads[level][...])
        mixer = None
        for place in range(8):
            row = place // (8 * channels // 256) * channels
            tile_first = place * C0 // 128 * 128
            block = product[row : row + channels, tile_first : tile_first + 128]
            inner = place * C0 - tile_first
            if inner:
                block = pltpu.roll(block, 128 - inner, 1)
            mixer = block if mixer is None else mixer + block
        outs[level][...] = mixer[: channels // 2, :C0]
        outs[3 + level][...] = mixer[channels // 2 :, :C0]


def norm_input_grad(grad, scaled, stats, gain, sums, channels, total):
    shift_sum = fold(sums[0:1, :], channels) / total
    gain_sum = fold(sums[1:2, :], channels) / total
    return (gain * stats[1]) * (grad - shift_sum - scaled * gain_sum)


def back_second_kernel(rows, counts, flags, *refs):
    ins, outs, wide, sides = split_refs(refs, 22, 7, 4, 4)
    grads, seconds, firsts, bands = ins[0:4], ins[4:8], ins[8:12], ins[12:16]
    near_in, far_in, stat, stat_sums, first_stat, norms = ins[16:22]
    normed_grads = outs[0:4]
    sums, near, far = outs[4:7]
    odd = flags[4] == 1
    for branch in range(4):
        count, channels, total = rows[branch], CHANNELS[branch], counts[branch]
        stats = moments(stat[2 * branch : 2 * branch + 2, :], channels, total)
        gain = norms[2 * branch + 1 : 2 * branch + 2, :]
        shift_sum = fold(stat_sums[2 * branch : 2 * branch + 1, :], channels) / total
        gain_sum = fold(stat_sums[2 * branch + 1 : 2 * branch + 2, :], channels) / total

        def input_grad(grad, value):
            scaled = (value - stats[0]) * stats[1]
            return (gain * stats[1]) * (grad - shift_sum - scaled * gain_sum)

        inner = input_grad(grads[branch][...], seconds[branch][...])
        wide[branch][:, 16 : (count + 1) * 16, :] = inner.reshape(2, count * 16, 256)
        for image in range(2):
            place = edge_place(branch, image)
            parts = [
                input_grad(ref[place : place + 16, :], ref[128 + place : 144 + place, :])
                for ref in (near_in, far_in)
            ]
            for value, start, flag in (
                (jnp.where(odd, parts[0], parts[1]), 0, flags[0]),
                (jnp.where(odd, parts[1], parts[0]), (count + 1) * 16, flags[1]),
            ):
                wide[branch][image, start : start + 16, :] = jnp.where(flag == 0, 0.0, value)
        build_sides(wide[branch], sides[branch], channels)
        hidden_grad = dot_nn(patches(wide[branch], sides[branch], count), bands[branch][...])
        first_stats = moments(first_stat[2 * branch : 2 * branch + 2, :], channels, total)
        scaled = (load_rows(firsts[branch], 1, count) - first_stats[0]) * first_stats[1]
        value = (
            scaled * norms[2 * branch : 2 * branch + 1, :]
            + norms[11 + 2 * branch : 12 + 2 * branch, :]
        )
        grad = hidden_grad * silu_slope(value)
        normed_grads[branch][...] = grad
        sums[2 * branch : 2 * branch + 1, :] = column_sum(grad)
        sums[2 * branch + 1 : 2 * branch + 2, :] = column_sum(grad * scaled)
        write_edges(odd, near, far, grad, branch, count, 0)


def kernel_grad_second(rows, counts, branch, meta, *refs):
    grad, second, first, stat, stat_sums, first_stat, norms, out, hidden, side, product = refs
    count, channels, total = rows[branch], CHANNELS[branch], counts[branch]
    stats = moments(stat[2 * branch : 2 * branch + 2, :], channels, total)
    value = norm_input_grad(
        grad[...],
        (second[...] - stats[0]) * stats[1],
        stats,
        norms[2 * branch + 1 : 2 * branch + 2, :],
        stat_sums[2 * branch : 2 * branch + 2, :],
        channels,
        total,
    )
    fill_hidden(meta, {branch: first}, first_stat, norms, {branch: hidden}, branch, count, total)
    build_sides(hidden, side, channels)
    product[...] = dot_tn(patches(hidden, side, count), value)
    collect_band(product, branch, tap_writer(out, branch))


def pack_kernel(meta, *refs):
    stage, unite_grads, outs, narrow, scratch = split_refs(refs, 4, 3, 2, 1, 3)
    pack_grads(meta[2], [*stage, *narrow], unite_grads, outs, scratch)


def kernel_grad_first(rows, counts, packed, meta, *refs):
    ins, unite_grads, outs, stage, scratch, sources, sides, products = split_refs(
        refs, 15, 3, 2 if packed else 4, 5, 3, 4, 4, 4
    )
    grads, firsts, tiles = ins[0:4], ins[4:8], ins[8:12]
    first_stat, first_sums, norms = ins[12:15]
    for branch in range(4):
        count, channels, total = rows[branch], CHANNELS[branch], counts[branch]
        stats = moments(first_stat[2 * branch : 2 * branch + 2, :], channels, total)
        grad = norm_input_grad(
            grads[branch][...],
            (load_rows(firsts[branch], 1, count) - stats[0]) * stats[1],
            stats,
            norms[2 * branch : 2 * branch + 1, :],
            first_sums[2 * branch : 2 * branch + 2, :],
            channels,
            total,
        )
        sources[branch][...] = tiles[branch][:, 16 : (count + 3) * 16, :]
        build_sides(sources[branch], sides[branch], channels)
        products[branch][...] = dot_tn(patches(sources[branch], sides[branch], count), grad)
        collect_band(products[branch], branch, tap_writer(stage[3 - branch], branch))
    if packed:
        pack_grads(meta[2], stage, unite_grads, outs, scratch)
    else:
        for ref, value in zip(outs, stage):
            ref[...] = value[...]


def back_first_kernel(rows, counts, flags, *refs):
    ins, source_grads, wide, sides, bands = split_refs(refs, 21, 4, 4, 4, 4)
    normed_grads, firsts, join_grads, taps = ins[0:4], ins[4:8], ins[8:12], ins[12:16]
    near, far, first_stat, first_sums, norms = ins[16:21]
    odd = flags[4] == 1
    for branch in range(4):
        count, channels, total = rows[branch], CHANNELS[branch], counts[branch]
        stats = moments(first_stat[2 * branch : 2 * branch + 2, :], channels, total)
        gain = norms[2 * branch : 2 * branch + 1, :]
        shift_sum = fold(first_sums[2 * branch : 2 * branch + 1, :], channels) / total
        gain_sum = fold(first_sums[2 * branch + 1 : 2 * branch + 2, :], channels) / total

        def input_grad(grad, value):
            scaled = (value - stats[0]) * stats[1]
            return (gain * stats[1]) * (grad - shift_sum - scaled * gain_sum)

        inner = input_grad(normed_grads[branch][...], load_rows(firsts[branch], 1, count))
        wide[branch][:, 16 : (count + 1) * 16, :] = inner.reshape(2, count * 16, 256)
        for image in range(2):
            place = edge_place(branch, image)
            one, two = (ref[place : place + 16, :] for ref in (near, far))
            for grad, start, flag in (
                (jnp.where(odd, one, two), 0, flags[0]),
                (jnp.where(odd, two, one), (count + 1) * 16, flags[1]),
            ):
                value = input_grad(grad, firsts[branch][image, start : start + 16, :])
                wide[branch][image, start : start + 16, :] = jnp.where(flag == 0, 0.0, value)
        build_sides(wide[branch], sides[branch], channels)
        build_band(bands[branch], turned(tap_reader(taps[3 - branch], branch)), branch, 0)
        grad = dot_nn(patches(wide[branch], sides[branch], count), bands[branch][...])
        grad = (grad + join_grads[branch][...]).reshape(2, count * 16, 256)
        for image in range(2):
            source_grads[branch][image] = grad[image].reshape(count, 4096)


def finish_kernel(first_sums, second_sums, head_sums, gain, shift, loss, head_weight, head_bias):
    offset = 0

    def put(sums, line, channels):
        nonlocal offset
        for ref, row in ((shift, line), (gain, line + 1)):
            value = fold(sums[row : row + 1, :], channels)
            done = 0
            while done < channels:
                place = offset + done
                width = min(channels - done, 128 - place % 128)
                ref[place // 128 : place // 128 + 1, place % 128 : place % 128 + width] = value[
                    :, done : done + width
                ]
                done += width
        offset += channels

    for branch in range(4):
        for sums in (first_sums, second_sums):
            put(sums, 2 * branch, CHANNELS[branch])
    for level in range(3):
        put(head_sums, 2 * level, C0)
    loss[...] = jnp.sum(head_sums[6:7, :], axis=1, keepdims=True)
    joints = head_bias.shape[1]
    head_bias[...] = fold(head_sums[7:8, :], C0)[:, :joints]
    total = jnp.concatenate(
        [second_sums[8:16, C0 * part : C0 * part + C0] for part in range(4)], axis=0
    )
    head_weight[...] = jnp.transpose(total)[:joints]


def device_count():
    return lax.axis_size("dp") * lax.axis_size("space")


def exchange(value, bit):
    return lax.ppermute(value, AXES, [(i, i ^ bit) for i in range(device_count())])


def total_sum(value, beside=(), order=None):
    value = value.value
    for step, bit in enumerate(order or [1 << i for i in range(device_count().bit_length() - 1)]):
        other = exchange(value, bit)
        if step < len(beside) and beside[step]:
            other = after(other, *beside[step](value))
        value = value + other
    return Kept(value)


def swap_rows(near, far):
    devices = lax.axis_size("space")
    pairs = [(i, i ^ 1) for i in range(devices)]
    others = [(i, i + 1) for i in range(1, devices - 1, 2)]
    others += [(j, i) for i, j in others]
    return lax.ppermute(near, "space", pairs), lax.ppermute(far, "space", others)


def device_index():
    return lax.axis_index("dp") * lax.axis_size("space") + lax.axis_index("space")


def after(value, *others):
    return lax.optimization_barrier((value, *others))[0]


def swap(parts, step):
    return [Kept(exchange(part.value, STEPS[chunk][step])) for chunk, part in enumerate(parts)]


def gather_shards(meta, flat, beside):
    other = exchange(flat, 16)
    other = after(other, *beside(flat))
    shapes = [(1, 2, last - first, 128) for first, last in CHUNKS]
    parts = call(split_shard, [meta, flat, Kept(other)], kept(shapes), smem=1)
    shapes = [(2, *shape[1:]) for shape in shapes]
    parts = call(join_chunks, [*parts, *swap(parts, 0)], kept(shapes))
    shapes = [(4, *shape[2:]) for shape in shapes]
    parts = call(join_apart, [*parts, *swap(parts, 1)], kept(shapes * 2))
    first, second = parts[:3], parts[3:]
    (whole,) = call(join_whole, [*first, *swap(first, 2)], kept([(8, SHARD, 128)]))
    second[0] = Kept(after(second[0].value, whole.value))
    received = swap(second, 2)

    def rest(start):
        received[0] = Kept(after(received[0].value, start))
        (whole,) = call(join_whole, [*second, *received], kept([(8, SHARD, 128)]))
        return [whole, Kept(exchange(whole.value, 1))]

    return [whole, Kept(exchange(whole.value, 1))], rest


def scatter_start(packs):
    keep, send = packs
    shapes = [(4, last - first, 128) for first, last in CHUNKS]
    return lambda received: call(
        add_cores, [keep, Kept(received)], kept(shapes * 2), cost=2
    ), exchange(send.value, 1)


def scatter_step(parts, step, beside=(), received=None):
    received = received or swap(parts[3:], step)
    if beside:
        received[0] = Kept(after(received[0].value, *beside))
    if step == 2:
        return call(add_last, [*parts[:3], *received], kept([(SHARD, 128)]))
    shapes = [(2 - step, last - first, 128) for first, last in CHUNKS]
    return call(add_received, [*parts[:3], *received], kept(shapes * 2))


def body(
    branch_zero,
    branch_one,
    branch_two,
    branch_three,
    convs_zero,
    convs_one,
    convs_two,
    convs_three,
    unite_one,
    unite_two,
    unite_three,
    norm_gain,
    norm_shift,
    head_weight,
    head_bias,
    targets,
    crowd_mask,
    person_count,
    flip_order,
):
    inputs = (branch_zero, branch_one, branch_two, branch_three)
    devices = device_count()
    spaces = lax.axis_size("space")
    place = lax.axis_index("space")
    rows = tuple(value.shape[1] for value in inputs)
    counts = tuple(
        float(2 * rows[b] * 16 * (256 // CHANNELS[b]) * devices) for b in range(4)
    )
    joints = head_bias.shape[0]
    cells = [2 * rows[b] * 16 for b in range(4)]
    packed = devices == 32
    shards_in = (convs_three, convs_two, convs_one, convs_zero, unite_one, unite_two, unite_three)
    sizes = [part.shape[0] for part in shards_in]

    meta = jnp.stack(
        [
            place > 0,
            place < spaces - 1,
            device_index() & 15,
            (device_index() & 16) // 16,
            place % 2,
        ]
    ).astype(jnp.int32)

    state = {}

    def prepare(start):
        parts = lax.optimization_barrier((*inputs, start))[:4]
        last_rows = jnp.concatenate([value[:, -2:] for value in parts], axis=1)
        first_rows = jnp.concatenate([value[:, :2] for value in parts], axis=1)
        odd = place % 2 == 1
        state["halo"] = swap_rows(
            jnp.where(odd, first_rows, last_rows), jnp.where(odd, last_rows, first_rows)
        )
        state["targets"] = call(
            target_kernel,
            [after(person_count, start), targets, crowd_mask],
            kept([(cells[0], 256)] * 2),
            [(cells[0], 128)],
            smem=1,
            cost=4,
        )
        return [state["targets"][0].value, *state["halo"]]

    def parameters(start):
        state["small"] = call(
            parameter_kernel,
            [
                after(norm_gain, start)[None],
                norm_shift[None],
                jnp.transpose(head_weight),
                head_bias[None],
                flip_order[None],
            ],
            kept([(22, 256), (C0, C0), (1, 256), (C0, C0), (1, 256)]),
        )
        return [state["small"][0].value]

    if packed:
        gap = jnp.zeros(((24 - ROWS_ONE) * 128,), f32)
        flat = jnp.concatenate([*shards_in[:3], gap, *shards_in[3:]]).reshape(SHARD, 128)
        first_packs, rest = gather_shards(meta, flat, prepare)
    else:
        prepare(meta)
        whole = [lax.all_gather(part, AXES, axis=0, tiled=True) for part in shards_in]
        whole = [
            part.reshape(-1, width)
            for part, width in zip(whole, (128, 128, 64, 32, 32, 32, 32))
        ]
        first_packs = [part[: part.shape[0] // 2] for part in whole]
        second_packs = [part[part.shape[0] // 2 :] for part in whole]
    near, far = state["halo"]
    target_cells, loss_weight = state["targets"]

    bands = [band_shape(b, 256) for b in range(4)]
    inner = [(cells[b], 256) for b in range(4)]
    wide = [(2, (rows[b] + 2) * 16, 256) for b in range(4)]
    wider = [(2, (rows[b] + 4) * 16, 256) for b in range(4)]

    def sides_of(shapes):
        return [shape[:2] + (SIDES[b],) for b, shape in enumerate(shapes)]

    eight = (8, 256)
    taps_out = kept(TAPS_OUT) if packed else []
    unpack_scratch = list(PACK_SCRATCH) if packed else []

    out = call(
        functools.partial(first_kernel, rows, packed),
        [meta, *inputs, near, far, *first_packs[:4]],
        kept([*wider, *wide, eight]) + taps_out,
        bands + sides_of(wider) + unpack_scratch,
        smem=1,
        cost=7,
    )
    tiles, firsts = out[0:4], out[4:8]
    first_taps = out[9:] if packed else first_packs
    if packed:
        second_packs = rest(tiles[0].value)

    def second_bands(start):
        state["second"] = call(
            functools.partial(band_kernel, packed),
            [after(meta, start), *second_packs[:4]],
            taps_out + kept(bands),
            unpack_scratch,
            smem=1,
            cost=2,
        )
        return [state["second"][-1].value]

    order = [1 << i for i in range(devices.bit_length() - 1)]
    first_stat = total_sum(
        out[8], [parameters, None, second_bands], [*order[1:], 1] if packed else None
    )
    norms, weight, bias, flip_weight, flip_bias = state["small"]
    second_taps = state["second"][:7] if packed else second_packs

    out = call(
        functools.partial(second_kernel, rows, counts),
        [meta, *firsts, first_stat, norms, *state["second"][-4:]],
        kept([*inner, eight]),
        wide + sides_of(wide),
        smem=1,
        cost=6,
    )
    seconds = out[0:4]
    unites = [*first_taps[4:7], *second_taps[4:7]]
    first_taps, second_taps = first_taps[:4], second_taps[:4]

    flip_firsts, flip_seconds = [None] * 4, [None] * 4

    def flip_first(branch):
        def work(start):
            (flip_firsts[branch],) = call(
                functools.partial(first_flip_kernel, rows, branch),
                [after(meta, start), tiles[branch], first_taps[3 - branch]],
                kept([wide[branch]]),
                [bands[branch], sides_of(wider)[branch]],
                smem=1,
                cost=2,
            )
            return [flip_firsts[branch].value]

        return work

    def flip_second(branch):
        def work(start):
            (flip_seconds[branch],) = call(
                functools.partial(second_flip_kernel, rows, counts, branch),
                [
                    after(meta, start),
                    flip_firsts[branch],
                    first_stat,
                    norms,
                    second_taps[3 - branch],
                ],
                kept([inner[branch]]),
                [wide[branch], bands[branch], sides_of(wide)[branch]],
                smem=1,
                cost=2,
            )
            return [flip_seconds[branch].value]

        return work

    second_stat = total_sum(out[4], [None] + [flip_first(branch) for branch in range(4)])

    out = call(
        functools.partial(third_kernel, rows, counts),
        [*seconds[1:], *tiles[1:], second_stat, norms, *unites],
        kept([*inner[1:], eight]),
    )
    mixes = out[0:3]
    mix_stat = total_sum(out[3], [None] + [flip_second(branch) for branch in range(4)])

    denominator = float(counts[0] * joints)
    out = call(
        functools.partial(loss_kernel, rows, counts, denominator),
        [
            seconds[0],
            tiles[0],
            second_stat,
            *mixes,
            mix_stat,
            norms,
            weight,
            bias,
            target_cells,
            loss_weight,
        ],
        kept([inner[0], *inner[1:], eight, inner[0], eight, inner[0], inner[0]]),
        cost=3,
    )
    heat, pre_sums, join_zero, zero_sums, united, heat_grad = out[0], out[1:4], *out[5:9]

    def head_grads(start):
        (state["head"],) = call(
            head_kernel, [after(meta, start), united, heat_grad], kept([eight]), smem=1
        )
        return [state["head"].value]

    head_sums = total_sum(out[4], [None, head_grads])

    out = call(
        functools.partial(join_kernel, rows, counts),
        [
            meta,
            *pre_sums,
            *mixes,
            *seconds,
            *tiles[1:],
            join_zero,
            zero_sums,
            state["head"],
            second_stat,
            mix_stat,
            head_sums,
            norms,
            *unites,
        ],
        kept([*inner[1:], *inner[1:], (16, 256), (256, 256), (256, 256)]),
        smem=1,
        cost=2,
    )
    join_grads = [join_zero, *out[0:3]]
    mixed_grads, edges = out[3:6], out[7:9]

    def mixers(start):
        state["mixers"] = call(
            functools.partial(mixer_kernel, rows, counts),
            [after(meta, start), *mixed_grads, *seconds[1:], *tiles[1:], second_stat, norms],
            kept([(CHANNELS[b] // 2, C0) for b in range(1, 4)] * 2),
            smem=1,
        )
        return [state["mixers"][0].value]

    def edge_rows(start):
        near, far = lax.optimization_barrier((edges[0].value, edges[1].value, start))[:2]
        state["edges"] = kept(swap_rows(near, far))
        return [part.value for part in state["edges"]]

    def turned_bands(start):
        state["turned"] = call(
            turned_kernel, [after(meta, start), *second_taps], kept(bands), smem=1, cost=2
        )
        return [state["turned"][0].value]

    second_sums = total_sum(out[6], [None, mixers, edge_rows, turned_bands])
    first_mixers, second_mixers = state["mixers"][:3], state["mixers"][3:]

    out = call(
        functools.partial(back_second_kernel, rows, counts),
        [
            meta,
            *join_grads,
            *seconds,
            *firsts,
            *state["turned"],
            *state["edges"],
            second_stat,
            second_sums,
            first_stat,
            norms,
        ],
        kept([*inner, eight, (128, 256), (128, 256)]),
        wide + sides_of(wide),
        smem=1,
        cost=6,
    )
    normed_grads, edges = out[0:4], out[5:7]
    stage = [None] * 4

    def second_grad(branch):
        def work(start):
            stage[3 - branch] = call(
                functools.partial(kernel_grad_second, rows, counts, branch),
                [
                    after(meta, start),
                    join_grads[branch],
                    seconds[branch],
                    firsts[branch],
                    second_stat,
                    second_sums,
                    first_stat,
                    norms,
                ],
                kept([TAPS_OUT[3 - branch]]),
                [wide[branch], sides_of(wide)[branch], bands[branch]],
                smem=1,
                cost=2,
            )[0]
            return [stage[3 - branch].value]

        return work

    grads_out = kept([(8, SHARD, 128)] * 2) if packed else list(TAPS_OUT[:4])

    def pack_second(start):
        state["packs"] = call(
            pack_kernel,
            [after(meta, start), *stage, *second_mixers],
            grads_out,
            [STAGE[4], *PACK_SCRATCH],
            smem=1,
        )
        return [state["packs"][0].value]

    works = [second_grad(branch) for branch in range(4)]
    first_sums = total_sum(
        out[4],
        [
            None,
            works[0],
            lambda start: works[1](start) + edge_rows(start),
            lambda start: works[2](start) + works[3](start),
            pack_second if packed else None,
        ],
    )
    if packed:
        add_second, received = scatter_start(state["packs"])
        second_parts = add_second(after(received, first_sums.value))
        first_meta = after(meta, second_parts[0].value)
    else:
        first_meta = meta

    first_kernels = call(
        functools.partial(kernel_grad_first, rows, counts, packed),
        [
            first_meta,
            *normed_grads,
            *firsts,
            *tiles,
            first_stat,
            first_sums,
            norms,
            *first_mixers,
        ],
        grads_out,
        [*STAGE, *PACK_SCRATCH] + wide + sides_of(wide) + bands,
        smem=1,
        cost=7,
    )

    def back_first(start):
        state["source"] = call(
            functools.partial(back_first_kernel, rows, counts),
            [
                after(meta, start),
                *normed_grads,
                *firsts,
                *join_grads,
                *first_taps,
                *state["edges"],
                first_stat,
                first_sums,
                norms,
            ],
            [value.shape for value in inputs],
            wide + sides_of(wide) + bands,
            smem=1,
            cost=7,
        )
        return [state["source"][0]]

    def flip_last(start):
        (state["heat"],) = call(
            functools.partial(flip_kernel, rows, counts),
            [
                *flip_seconds,
                *tiles,
                second_stat,
                *unites,
                mix_stat,
                norms,
                flip_weight,
                Kept(after(flip_bias.value, start)),
                heat,
            ],
            [targets.shape],
            [(cells[0], 128)] * 2,
            cost=5,
        )
        return [state["heat"]]

    def finish(start):
        state["finish"] = call(
            finish_kernel,
            [Kept(after(first_sums.value, start)), second_sums, head_sums],
            [(9, 128), (9, 128), (1, 1), (joints, C0), (1, joints)],
            limit=4,
        )
        return [state["finish"][0]]

    if packed:
        add_first, received = scatter_start(first_kernels)
        second_parts = scatter_step(second_parts, 0, [first_kernels[0].value])
        first_parts = add_first(after(received, second_parts[0].value))
        second_parts = scatter_step(second_parts, 1, [first_parts[0].value])
        start = second_parts[0].value
        received = swap(first_parts[3:], 0)
        (second_part,) = scatter_step(second_parts, 2)
        first_parts = scatter_step(first_parts, 0, back_first(start), received)
        start = second_part.value
        first_parts = scatter_step(first_parts, 1, flip_last(start))
        received = swap(first_parts[3:], 2)
        received[0] = Kept(after(received[0].value, *finish(first_parts[0].value)))
        keep, send = call(
            add_apart,
            [meta, *first_parts[:3], *received, second_part],
            kept([(SHARD, 128)] * 2),
            smem=1,
        )
        out = call(
            add_shard,
            [keep, Kept(exchange(send.value, 16))],
            [(ROWS_THREE, 128), (ROWS_TWO, 128), (ROWS_ONE, 128), (5, 128), (1, 64), (1, 128), (2, 128)],
        )
        shards = [part.reshape(-1)[:size] for part, size in zip(out, sizes)]
    else:
        for work in (back_first, flip_last, finish):
            work(first_sums.value)
        first_mixers, second_mixers = (
            [part.value for part in parts] for parts in (first_mixers, second_mixers)
        )
        stage = [part.value for part in stage]
        flat = [
            jnp.concatenate([one.reshape(-1), two.reshape(-1)])
            for one, two in zip([*first_kernels, *first_mixers], [*stage, *second_mixers])
        ]
        shards = [lax.psum_scatter(part, AXES, scatter_dimension=0, tiled=True) for part in flat]

    gain_grad, shift_grad, loss, head_grad, bias_grad = state["finish"]
    return (
        loss[0, 0],
        state["heat"],
        *state["source"],
        shards[3],
        shards[2],
        shards[1],
        shards[0],
        *shards[4:7],
        gain_grad.reshape(-1)[: norm_gain.shape[0]],
        shift_grad.reshape(-1)[: norm_shift.shape[0]],
        jnp.transpose(head_grad),
        bias_grad[0],
    )


def solution(mesh):
    rows = P("dp", "space", None)
    shard = P(("dp", "space"))
    heat = P("dp", None, "space", None)
    return jax.shard_map(
        body,
        mesh=mesh,
        in_specs=(*[rows] * 4, *[shard] * 7, *[P()] * 4, heat, rows, P("dp"), P()),
        out_specs=(P(), heat, *[rows] * 4, *[shard] * 7, *[P()] * 4),
        check_vma=False,
    )
```

```python
import functools

import jax
import jax.numpy as jnp
import numpy as np
from jax import lax
from jax.experimental import pallas as pl
from jax.experimental.pallas import tpu as pltpu
from jax.sharding import PartitionSpec as P

C0 = 32
CHANNELS = (32, 64, 128, 256)
SIDES = (128, 128, 256, 512)
AXES = ("dp", "space")
epsilon = 1e-05
f32 = jnp.float32
high = lax.Precision.HIGH


def dot_nn(left, right):
    return lax.dot_general(left, right, (((1,), (0,)), ((), ())), precision=high, preferred_element_type=f32)


def dot_nt(left, right):
    return lax.dot_general(left, right, (((1,), (1,)), ((), ())), precision=high, preferred_element_type=f32)


def dot_tn(left, right):
    return lax.dot_general(left, right, (((0,), (0,)), ((), ())), precision=high, preferred_element_type=f32)


def sigmoid(value):
    return 1.0 / (1.0 + jnp.exp(-value))


def silu(value):
    return value * sigmoid(value)


def silu_slope(value):
    sigma = sigmoid(value)
    return sigma * (1.0 + value * (1.0 - sigma))


def fold(row, channels):
    step = channels
    while step < 256:
        row = row + pltpu.roll(row, step, 1)
        step = 2 * step
    return row


def column_sum(value):
    return jnp.sum(value, axis=0, keepdims=True)


def moments(sums, channels, count):
    mean = fold(sums[0:1], channels) / count
    square = fold(sums[1:2], channels) / count
    return mean, lax.rsqrt(square - mean * mean + epsilon)


def affine(stats, gain, shift):
    scale = stats[1] * gain
    return scale, shift - stats[0] * scale


def load_rows(ref, first, count):
    lanes = ref.shape[2]
    return ref[:, first * 16 : (first + count) * 16, :].reshape(2 * count * 16, lanes)


def group_index(rows):
    return lax.broadcasted_iota(jnp.int32, (rows, 128), 0) % 16


def side_columns(value, channels):
    rows = value.shape[0]
    group = group_index(rows)
    lane = lax.broadcasted_iota(jnp.int32, (rows, 128), 1)

    def before(part):
        return jnp.where(group == 0, 0.0, pltpu.roll(part, 1, 0))

    def after(part):
        return jnp.where(group == 15, 0.0, pltpu.roll(part, rows - 1, 0))

    low, upper = value[:, :128], value[:, 128:]
    if channels == 256:
        return jnp.concatenate([before(low), before(upper), after(low), after(upper)], axis=1)
    if channels == 128:
        return jnp.concatenate([before(upper), after(low)], axis=1)
    return jnp.where(
        lane < channels, after(low), jnp.where(lane >= 128 - channels, before(upper), 0.0)
    )


def build_sides(source, side, channels):
    rows = source.shape[1]
    for image in range(2):
        side[image] = side_columns(source[image], channels)


def patches(source, side, count, offset=0):
    parts = []
    for tap_row in range(3):
        parts.append(load_rows(source, tap_row + offset, count))
        parts.append(load_rows(side, tap_row + offset, count))
    return jnp.concatenate(parts, axis=1)


def band_row(branch, tap_row, place):
    channels, side = CHANNELS[branch], SIDES[branch]
    base = tap_row * (256 + side)
    if place < 0:
        return base + 256 + (0 if channels >= 128 else 128 - channels)
    if place >= 256 // channels:
        return base + 256 + (side // 2 if channels >= 128 else 0)
    return base + place * channels


def build_band(band, tap, branch, offset):
    channels = CHANNELS[branch]
    groups = 256 // channels
    side = SIDES[branch]
    height = 256 + side
    if channels < 256:
        band[:, offset : offset + 256] = jnp.zeros((3 * height, 256), f32)
    for tap_row in range(3):
        for tap_col in range(3):
            matrix = tap(tap_row, tap_col)
            for out in range(groups):
                row = band_row(branch, tap_row, out + tap_col - 1)
                start = offset + out * channels
                band[row : row + channels, start : start + channels] = matrix


def collect_band(product, branch, emit):
    channels = CHANNELS[branch]
    for tap_row in range(3):
        for tap_col in range(3):
            total = None
            for out in range(256 // channels):
                row = band_row(branch, tap_row, out + tap_col - 1)
                start = out * channels
                if channels >= 128:
                    block = product[row : row + channels, start : start + channels]
                else:
                    tile = start // 128 * 128
                    block = product[row : row + channels, tile : tile + 128]
                    inner = start - tile
                    if inner:
                        block = pltpu.roll(block, 128 - inner, 1)
                total = block if total is None else total + block
            emit(tap_row, tap_col, total[:, :channels])


def tap_reader(ref, branch):
    channels = CHANNELS[branch]
    if channels == 256:

        def tap(tap_row, tap_col):
            first = (3 * tap_row + tap_col) * 512
            return jnp.concatenate(
                [ref[pl.ds(first, 256, stride=2), :], ref[pl.ds(first + 1, 256, stride=2), :]],
                axis=1,
            )

        return tap

    def tap(tap_row, tap_col):
        first = (3 * tap_row + tap_col) * channels
        return ref[first : first + channels, :]

    return tap


def tap_writer(ref, branch):
    channels = CHANNELS[branch]

    def emit(tap_row, tap_col, value):
        place = 3 * tap_row + tap_col
        if channels == 256:
            ref[pl.ds(place * 512, 256, stride=2), :] = value[:, :128]
            ref[pl.ds(place * 512 + 1, 256, stride=2), :] = value[:, 128:]
        else:
            ref[place * channels : (place + 1) * channels, :] = value

    return emit


SHARD = 392
ROWS_THREE, ROWS_TWO, ROWS_ONE = 288, 72, 18
PER_ZERO, PER_UNITE = 18, (2, 4, 8)
CHUNKS = ((0, 128), (128, 256), (256, 392))
STEPS = ((8, 4, 2), (4, 2, 8), (2, 8, 4))
TAPS_OUT = ((4608, 128), (1152, 128), (576, 64), (288, 32), (32, 32), (64, 32), (128, 32))
PACK_SCRATCH = ((16, 24, 128), (16, 8, 128), (288, 128))
STAGE = ((4608, 128), (1152, 128), (576, 64), (288, 32), (512, 32))


def partner(me, core, place, bits):
    return me ^ (core + sum(bit for i, bit in enumerate(bits) if place >> i & 1))


def shard_parts(device, three, two, one, zero):
    start = device * ROWS_THREE
    return (
        ((0, 128, three.at[pl.ds(pl.multiple_of(start, 8), 128), :]),),
        ((128, 256, three.at[pl.ds(pl.multiple_of(start + 128, 8), 128), :]),),
        (
            (256, 288, three.at[pl.ds(pl.multiple_of(start + 256, 8), 32), :]),
            (288, 360, two.at[pl.ds(pl.multiple_of(device * ROWS_TWO, 8), ROWS_TWO), :]),
            (360, 384, one.at[device]),
            (384, 392, zero.at[device]),
        ),
    )


def unpack_taps(me, packs, taps, scratch):
    three, two, one, zero = taps[:4]
    part_one, part_zero, flat_one = scratch
    for core in range(2):
        for place in range(8):
            for chunk in range(3):
                device = partner(me, core, place, STEPS[chunk])
                parts = shard_parts(device, three, two, part_one, part_zero)[chunk]
                for first, last, ref in parts:
                    ref[...] = packs[core][place, first:last]
    for device in range(16):
        flat_one[device * ROWS_ONE : (device + 1) * ROWS_ONE, :] = part_one[device, 0:ROWS_ONE]
    one[...] = flat_one[...].reshape(one.shape)
    narrow = part_zero[...].reshape(128, 128).reshape(512, 32)
    for device in range(16):
        first = device * 32
        for ref, height in zip(taps[3:7], (PER_ZERO, *PER_UNITE)):
            ref[device * height : (device + 1) * height, :] = narrow[first : first + height]
            first += height


def pack_grads(me, stage, unite_grads, packs, scratch):
    three, two, one, zero, narrow = stage
    part_one, part_zero, flat_one = scratch
    flat_one[...] = one[...].reshape(flat_one.shape)
    for device in range(16):
        part_one[device, 0:ROWS_ONE] = flat_one[device * ROWS_ONE : (device + 1) * ROWS_ONE, :]
        part_one[device, ROWS_ONE:24] = jnp.zeros((24 - ROWS_ONE, 128), f32)
        first = device * 32
        for ref, height in zip((zero, *unite_grads), (PER_ZERO, *PER_UNITE)):
            narrow[first : first + height, :] = ref[device * height : (device + 1) * height, :]
            first += height
    part_zero[...] = narrow[...].reshape(128, 128).reshape(16, 8, 128)
    for core in range(2):
        for place in range(8):
            for chunk in range(3):
                device = partner(me, core, place, STEPS[chunk][::-1])
                parts = shard_parts(device, three, two, part_one, part_zero)[chunk]
                for first, last, ref in parts:
                    packs[core][place, first:last] = ref[...]


def split_shard(meta, shard, other, *outs):
    second = meta[3] == 1
    for out, (first, last) in zip(outs, CHUNKS):
        own, far = shard[first:last], other[first:last]
        out[0, 0] = jnp.where(second, far, own)
        out[0, 1] = jnp.where(second, own, far)


def join_chunks(*refs):
    held, received, outs = split_refs(refs, 3, 3, 3)
    for chunk in range(3):
        count = held[chunk].shape[0]
        outs[chunk][0:count] = held[chunk][...]
        outs[chunk][count : 2 * count] = received[chunk][...]


def join_apart(*refs):
    held, received, first, second = split_refs(refs, 3, 3, 3, 3)
    for chunk in range(3):
        count = held[chunk].shape[0]
        for half, outs in ((0, first), (1, second)):
            outs[chunk][0:count] = held[chunk][:, half]
            outs[chunk][count : 2 * count] = received[chunk][:, half]


def join_whole(*refs):
    held, received, out = split_refs(refs, 3, 3, 1)
    for chunk, (first, last) in enumerate(CHUNKS):
        count = held[chunk].shape[0]
        out[0][0:count, first:last] = held[chunk][...]
        out[0][count : 2 * count, first:last] = received[chunk][...]


def add_received(*refs):
    held, received, low, high = split_refs(refs, 3, 3, 3, 3)
    for chunk in range(3):
        half = held[chunk].shape[0] // 2
        low[chunk][...] = held[chunk][0:half] + received[chunk][0:half]
        high[chunk][...] = held[chunk][half:] + received[chunk][half:]


def add_cores(*refs):
    keeps, received, low, high = split_refs(refs, 2, 2, 3, 3)
    for chunk, (first, last) in enumerate(CHUNKS):
        for half in range(2):
            low[chunk][:, half] = keeps[half][0:4, first:last] + received[half][0:4, first:last]
            high[chunk][:, half] = keeps[half][4:8, first:last] + received[half][4:8, first:last]


def add_last(meta, *refs):
    held, received, keep, send = split_refs(refs, 3, 3, 1, 1)
    second = meta[3] == 1
    for chunk, (first, last) in enumerate(CHUNKS):
        total = held[chunk][0] + received[chunk][0]
        keep[0][first:last, :] = jnp.where(second, total[1], total[0])
        send[0][first:last, :] = jnp.where(second, total[0], total[1])


def add_shard(keep, received, *outs):
    value = keep[...] + received[...]
    first = 0
    for ref in outs[:3]:
        last = first + ref.shape[0]
        ref[...] = value[first:last]
        first = last
    tail = SHARD - 8
    outs[3][...] = value[tail : tail + 5]
    outs[4][...] = value[tail + 4 : tail + 5, 64:]
    outs[5][...] = value[tail + 5 : tail + 6]
    outs[6][...] = value[tail + 6 : tail + 8]


def mirrored(tap):
    return lambda tap_row, tap_col: tap(tap_row, 2 - tap_col)


def turned(tap):
    return lambda tap_row, tap_col: jnp.transpose(tap(2 - tap_row, 2 - tap_col))


def mask_ends(value, rows, flags):
    place = lax.broadcasted_iota(jnp.int32, value.shape, 0) // 16 % (rows + 2)
    outside = ((place == 0) & (flags[0] == 0)) | ((place == rows + 1) & (flags[1] == 0))
    return jnp.where(outside, 0.0, value)


def mix_matrix(unite, branch):
    channels = CHANNELS[branch]
    groups = 256 // channels
    wide = jnp.concatenate([unite] * 8, axis=1)
    lane = lax.broadcasted_iota(jnp.int32, wide.shape, 1)
    span = 256 // groups
    return jnp.concatenate(
        [jnp.where(lane // span == place, wide, 0.0) for place in range(groups)], axis=0
    )


def split_refs(refs, *counts):
    out, first = [], 0
    for count in counts:
        out.append(refs[first : first + count])
        first += count
    assert first == len(refs)
    return out


class Kept:
    def __init__(self, value):
        self.value = value


def kept(values):
    return [Kept(value) for value in values]


def call(kernel, ins, outs, scratch=(), smem=0, limit=16, cost=1):
    specs = [pl.BlockSpec(memory_space=pltpu.SMEM)] * smem + [
        pl.BlockSpec(memory_space=pltpu.VMEM)
    ] * (len(ins) - smem)
    ins = ins[:smem] + [
        pltpu.with_memory_space_constraint(x.value, pltpu.VMEM)
        if isinstance(x, Kept)
        else pltpu.with_memory_space_constraint(x, pltpu.HBM)
        for x in ins[smem:]
    ]
    shapes = [pltpu.VMEM(x.value, f32) if isinstance(x, Kept) else pltpu.HBM(x, f32) for x in outs]
    results = pl.pallas_call(
        kernel,
        in_specs=specs,
        out_specs=[pl.BlockSpec(memory_space=pltpu.VMEM)] * len(outs),
        out_shape=shapes,
        scratch_shapes=[pltpu.VMEM(shape, f32) for shape in scratch],
        compiler_params=pltpu.CompilerParams(vmem_limit_bytes=limit * 2**20),
        cost_estimate=pl.CostEstimate(
            flops=int(cost * 1.1e9), bytes_accessed=int(cost * 3.0e6), transcendentals=0
        ),
    )(*ins)
    return [Kept(y) if isinstance(x, Kept) else y for x, y in zip(outs, results)]


def band_shape(branch, width):
    return (3 * (256 + SIDES[branch]), width)


def swap_blocks(parts):
    rows = parts[0].shape[0]
    group = lax.broadcasted_iota(jnp.int32, (rows, 128), 1) // 8
    step = 1
    while step < 16:
        high = (group & step) != 0
        parts = [
            jnp.where(high, parts[i], pltpu.roll(parts[i - step], 128 - 8 * step, 1))
            if i & step
            else jnp.where(high, pltpu.roll(parts[i + step], 8 * step, 1), parts[i])
            for i in range(16)
        ]
        step = 2 * step
    return parts


def joint_matrix():
    source = lax.broadcasted_iota(jnp.int32, (256, 256), 0)
    lane = lax.broadcasted_iota(jnp.int32, (256, 256), 1)
    matches = (source // 8 == lane % C0) & (source % 8 == lane // C0) & (source < 136)
    return jnp.where(matches, 1.0, 0.0)


def shift_group(value, group):
    return pltpu.roll(value, 128 - 8 * group, 1) if group else value


def parameter_kernel(gain, shift, weight, bias, flip, *outs):
    norms, weight_out, bias_out, flip_weight, flip_bias = outs
    weight = jnp.transpose(weight[...])
    for base, ref in ((0, gain), (11, shift)):
        offset = 0
        line = base
        sizes = [channels for channels in CHANNELS for _ in range(2)] + [C0] * 3
        for channels in sizes:
            part = ref[0:1, offset : offset + channels]
            norms[line : line + 1, :] = jnp.concatenate([part] * (256 // channels), axis=1)
            offset += channels
            line += 1
    joints = weight.shape[1]
    source = lax.broadcasted_iota(jnp.int32, (joints, joints), 0)
    moved = jnp.where(source == flip[...], 1.0, 0.0)
    for matrix, row, matrix_out, row_out in (
        (weight, bias[...], weight_out, bias_out),
        (
            jnp.dot(weight, moved, precision=lax.Precision.HIGHEST),
            jnp.dot(bias[...], moved, precision=lax.Precision.HIGHEST),
            flip_weight,
            flip_bias,
        ),
    ):
        matrix_out[...] = jnp.zeros((C0, C0), f32)
        matrix_out[:, 0:joints] = matrix
        row_out[...] = jnp.zeros((1, 256), f32)
        for place in range(8):
            row_out[0:1, C0 * place : C0 * place + joints] = row


def target_kernel(people, targets, mask, target_out, mask_out, scratch):
    lines = 2 * targets.shape[2]
    parts = swap_blocks([targets[:, j].reshape(lines, 128) for j in range(16)])
    last = targets[:, 16].reshape(lines, 128)
    cells = mask[...].reshape(lines, 128).astype(f32)
    lane = lax.broadcasted_iota(jnp.int32, (lines, 128), 1)
    tails = [
        jnp.where(lane < 8, shift_group(last, group), pltpu.roll(shift_group(cells, group), 8, 1))
        for group in range(16)
    ]
    whole = jnp.concatenate(
        [jnp.concatenate([part, tail], axis=1) for part, tail in zip(parts, tails)], axis=0
    )
    source = lax.broadcasted_iota(jnp.int32, (256, 256), 0)
    target_lane = lax.broadcasted_iota(jnp.int32, (256, 256), 1)
    spread = jnp.where((source >= 136) & (source < 144) & (source - 136 == target_lane // C0), 1.0, 0.0)
    target_rows = dot_nn(whole, joint_matrix())
    mask_rows = dot_nn(whole, spread)
    first_image = lax.broadcasted_iota(jnp.int32, (lines, 256), 0) < lines // 2
    share = jnp.where(first_image, people[0].astype(f32), people[1].astype(f32))
    for value, ref in ((target_rows, target_out), (mask_rows, mask_out)):
        for part in range(2):
            for group in range(16):
                span = slice(group * lines, (group + 1) * lines)
                block = value[span, 128 * part : 128 * part + 128]
                if ref is mask_out:
                    block = block / share[:, :128]
                scratch[pl.ds(group, lines, stride=16), :] = block
            ref[:, 128 * part : 128 * part + 128] = scratch[...]


def first_kernel(rows, packed, meta, *refs):
    xs, near, far, packs, tiles, mains, sums, taps, bands, sides, scratch = split_refs(
        refs, 4, 1, 1, 2 if packed else 4, 4, 4, 1, 7 * packed, 4, 4, 3 * packed
    )
    sums = sums[0]
    if packed:
        unpack_taps(meta[2], packs, taps, scratch)
    else:
        taps = packs
    odd = meta[4] == 1
    for branch in range(4):
        count = rows[branch]
        tile, side, band = tiles[branch], sides[branch], bands[branch]
        for image in range(2):
            one, two = (ref[0][image, 2 * branch : 2 * branch + 2, :] for ref in (near, far))
            for value, first, extent in (
                (jnp.where(odd, one, two), 0, 2),
                (xs[branch][image], 2, count),
                (jnp.where(odd, two, one), count + 2, 2),
            ):
                tile[image, first * 16 : (first + extent) * 16, :] = value.reshape(extent * 16, 256)
        build_sides(tile, side, CHANNELS[branch])
        build_band(band, tap_reader(taps[3 - branch], branch), branch, 0)
        out = dot_nn(patches(tile, side, count + 2), band[...])
        mains[branch][...] = out.reshape(2, (count + 2) * 16, 256)
        inner = load_rows(mains[branch], 1, count)
        sums[2 * branch : 2 * branch + 1, :] = column_sum(inner)
        sums[2 * branch + 1 : 2 * branch + 2, :] = column_sum(inner * inner)


def first_flip_kernel(rows, branch, meta, tile, taps, out, band, side):
    count = rows[branch]
    build_sides(tile, side, CHANNELS[branch])
    build_band(band, mirrored(tap_reader(taps, branch)), branch, 0)
    value = dot_nn(patches(tile, side, count + 2), band[...])
    out[...] = value.reshape(2, (count + 2) * 16, 256)


def fill_hidden(meta, firsts, stat, norms, hidden, branch, count, total):
    stats = moments(stat[2 * branch : 2 * branch + 2, :], CHANNELS[branch], total)
    scale, offset = affine(
        stats,
        norms[2 * branch : 2 * branch + 1, :],
        norms[11 + 2 * branch : 12 + 2 * branch, :],
    )
    value = load_rows(firsts[branch], 0, count + 2) * scale + offset
    value = mask_ends(silu(value), count, meta)
    hidden[branch][...] = value.reshape(2, (count + 2) * 16, 256)


def band_kernel(packed, meta, *refs):
    packs, taps, bands, scratch = split_refs(refs, 2 if packed else 4, 7 * packed, 4, 3 * packed)
    if packed:
        unpack_taps(meta[2], packs, taps, scratch)
    else:
        taps = packs
    for branch in range(4):
        build_band(bands[branch], tap_reader(taps[3 - branch], branch), branch, 0)


def turned_kernel(meta, *refs):
    taps, bands = split_refs(refs, 4, 4)
    for branch in range(4):
        build_band(bands[branch], turned(tap_reader(taps[3 - branch], branch)), branch, 0)


def second_kernel(rows, counts, meta, *refs):
    firsts, stat, norms, bands, outs, sums, hidden, sides = split_refs(refs, 4, 1, 1, 4, 4, 1, 4, 4)
    sums = sums[0]
    for branch in range(4):
        count, channels = rows[branch], CHANNELS[branch]
        fill_hidden(meta, firsts, stat[0], norms[0], hidden, branch, count, counts[branch])
        build_sides(hidden[branch], sides[branch], channels)
        out = dot_nn(patches(hidden[branch], sides[branch], count), bands[branch][...])
        outs[branch][...] = out
        sums[2 * branch : 2 * branch + 1, :] = column_sum(out)
        sums[2 * branch + 1 : 2 * branch + 2, :] = column_sum(out * out)


def second_flip_kernel(rows, counts, branch, meta, first, stat, norms, taps, out, hidden, band, side):
    count, channels = rows[branch], CHANNELS[branch]
    fill_hidden(meta, {branch: first}, stat, norms, {branch: hidden}, branch, count, counts[branch])
    build_sides(hidden, side, channels)
    build_band(band, mirrored(tap_reader(taps, branch)), branch, 0)
    out[...] = dot_nn(patches(hidden, side, count), band[...])


def joined(second, tile, stat, norms, branch, count, total):
    stats = moments(stat[2 * branch : 2 * branch + 2, :], CHANNELS[branch], total)
    gain = norms[2 * branch + 1 : 2 * branch + 2, :]
    shift = norms[12 + 2 * branch : 13 + 2 * branch, :]
    scaled = (second - stats[0]) * stats[1]
    return scaled * gain + shift + load_rows(tile, 2, count), scaled, stats


def third_kernel(rows, counts, *refs):
    seconds, tiles, stat, norms, unites, mixes, sums = split_refs(refs, 3, 3, 1, 1, 6, 3, 1)
    stat, norms, sums = stat[0], norms[0], sums[0]
    for level in range(3):
        branch = level + 1
        value, _, _ = joined(
            seconds[level][...], tiles[level], stat, norms, branch, rows[branch], counts[branch]
        )
        unite = jnp.concatenate([unites[level][...], unites[3 + level][...]], axis=0)
        mixed = dot_nn(silu(value), mix_matrix(unite, branch))
        mixes[level][...] = mixed
        sums[2 * level : 2 * level + 1, :] = column_sum(mixed)
        sums[2 * level + 1 : 2 * level + 2, :] = column_sum(mixed * mixed)
    sums[6:8, :] = jnp.zeros((2, 256), f32)


def spread_rows(value, rows, factor):
    value = value.reshape(2 * rows, 1, 16, 256)
    return jnp.broadcast_to(value, (2 * rows, factor, 16, 256)).reshape(2 * rows * factor * 16, 256)


def gather_rows(value, rows, factor):
    value = value.reshape(2 * rows // factor, factor, 16, 256)
    return jnp.sum(value, axis=1).reshape(2 * rows // factor * 16, 256)


def uniting_stats(stat, level, total):
    return moments(stat[2 * level : 2 * level + 2, :], C0, total * 2.0 ** (level + 1))


def united_sum(base, mixes, stat, norms, rows, counts):
    for level in range(3):
        stats = uniting_stats(stat, level, counts[level + 1])
        scale, offset = affine(
            stats, norms[8 + level : 9 + level, :], norms[19 + level : 20 + level, :]
        )
        base = base + spread_rows(mixes[level] * scale + offset, rows[level + 1], 2 ** (level + 1))
    return base


def head_matrix(weight):
    wide = jnp.concatenate([weight] * 8, axis=1)
    lane = lax.broadcasted_iota(jnp.int32, wide.shape, 1)
    return jnp.concatenate([jnp.where(lane // C0 == place, wide, 0.0) for place in range(8)], axis=0)


def loss_kernel(rows, counts, denominator, *refs):
    ins, outs = split_refs(refs, 12, 9)
    second, tile, stat, mix_one, mix_two, mix_three, mix_stat, norms, weight, bias, targets, mask = ins
    heat_out, sum_one, sum_two, sum_three, sums, join_grad, zero_sums, united_out, grad_out = outs
    count = rows[0]
    join, scaled, _ = joined(second[...], tile, stat, norms, 0, count, counts[0])
    mixes = (mix_one[...], mix_two[...], mix_three[...])
    pre = united_sum(silu(join), mixes, mix_stat, norms, rows, counts)
    united = silu(pre)
    head = head_matrix(weight[...])
    heat = dot_nn(united, head) + bias[...]
    heat_out[...] = heat
    error = heat - targets[...]
    weighted = mask[...] * error
    sums[6:7, :] = column_sum(weighted * error) / denominator
    heat_grad = weighted * (2.0 / denominator)
    sums[7:8, :] = column_sum(heat_grad)
    united_out[...] = united
    grad_out[...] = heat_grad
    grad = dot_nt(heat_grad, head) * silu_slope(pre)
    join_part = grad * silu_slope(join)
    join_grad[...] = join_part
    zero_sums[0:1, :] = column_sum(join_part)
    zero_sums[1:2, :] = column_sum(join_part * scaled)
    for level, out in enumerate((sum_one, sum_two, sum_three)):
        part = gather_rows(grad, count, 2 ** (level + 1))
        out[...] = part
        stats = uniting_stats(mix_stat, level, counts[level + 1])
        normed = (mixes[level] - stats[0]) * stats[1]
        sums[2 * level : 2 * level + 1, :] = column_sum(part)
        sums[2 * level + 1 : 2 * level + 2, :] = column_sum(part * normed)


def head_kernel(meta, united, heat_grad, out):
    product = dot_tn(united[...], heat_grad[...])
    total = None
    for place in range(8):
        first = place * C0
        tile_first = first // 128 * 128
        block = product[first : first + C0, tile_first : tile_first + 128]
        if first - tile_first:
            block = pltpu.roll(block, 128 - (first - tile_first), 1)
        total = block if total is None else total + block
    out[...] = jnp.zeros(out.shape, f32)
    out[:, 0:128] = jnp.concatenate(
        [total[8 * part : 8 * part + 8, :C0] for part in range(4)], axis=1
    )


def flip_kernel(rows, counts, *refs):
    seconds, tiles, stat, unites, mix_stat, norms, weight, bias, heat, out, scratch = split_refs(
        refs, 4, 4, 1, 6, 1, 1, 1, 1, 1, 1, 2
    )
    stat, norms = stat[0], norms[0]
    mixes = []
    for branch in range(4):
        value, _, _ = joined(
            seconds[branch][...], tiles[branch], stat, norms, branch, rows[branch], counts[branch]
        )
        if branch == 0:
            base = silu(value)
        else:
            unite = jnp.concatenate([unites[branch - 1][...], unites[branch + 2][...]], axis=0)
            mixes.append(dot_nn(silu(value), mix_matrix(unite, branch)))
    pre = united_sum(base, mixes, mix_stat[0], norms, rows, counts)
    back = dot_nn(silu(pre), head_matrix(weight[0][...])) + bias[0][...]
    moved = dot_nt(0.5 * (heat[0][...] + back), joint_matrix())
    scratch[0][...] = moved[:, :128]
    scratch[1][...] = moved[:, 128:]
    lines = 2 * rows[0]
    parts = [scratch[0][pl.ds(group, lines, stride=16), :] for group in range(16)]
    lane = lax.broadcasted_iota(jnp.int32, (lines, 128), 1)
    last = None
    for group in range(16):
        tail = scratch[1][pl.ds(group, lines, stride=16), :]
        tail = pltpu.roll(tail, 8 * group, 1) if group else tail
        last = tail if last is None else jnp.where(lane // 8 == group, tail, last)
    for joint, value in enumerate([*swap_blocks(parts), last]):
        out[0][:, joint] = value.reshape(2, rows[0], 128)


def edge_place(branch, image):
    return (2 * branch + image) * 16


def write_edges(odd, near, far, value, branch, count, base):
    for image in range(2):
        place = base + edge_place(branch, image)
        start = image * count * 16
        first = value[start : start + 16]
        last = value[start + (count - 1) * 16 : start + count * 16]
        near[place : place + 16, :] = jnp.where(odd, first, last)
        far[place : place + 16, :] = jnp.where(odd, last, first)


def join_kernel(rows, counts, meta, *refs):
    sums_in, mixes, seconds, tiles, join_zero, small, unites, outs = split_refs(
        refs, 3, 3, 4, 3, 1, 6, 6, 9
    )
    zero_sums, head_grad, stat, mix_stat, head_sums, norms = small
    grads, mixed_grads, sums, near, far = outs[0:3], outs[3:6], outs[6], outs[7], outs[8]
    odd = meta[4] == 1
    sums[0:2, :] = zero_sums[0:2, :]
    sums[8:16, :] = head_grad[...]
    write_edges(odd, near, far, join_zero[0][...], 0, rows[0], 0)
    write_edges(odd, near, far, seconds[0][...], 0, rows[0], 128)
    for level in range(3):
        branch = level + 1
        channels, count = CHANNELS[branch], rows[branch]
        total = counts[branch]
        stats = uniting_stats(mix_stat, level, total)
        gain = norms[8 + level : 9 + level, :]
        shift_sum = fold(head_sums[2 * level : 2 * level + 1, :], C0)
        gain_sum = fold(head_sums[2 * level + 1 : 2 * level + 2, :], C0)
        normed = (mixes[level][...] - stats[0]) * stats[1]
        share = 1.0 / (total * 2.0 ** (level + 1))
        mixed_grad = (gain * stats[1]) * (
            sums_in[level][...] - shift_sum * share - normed * (gain_sum * share)
        )
        mixed_grads[level][...] = mixed_grad
        value, scaled, _ = joined(
            seconds[branch][...], tiles[level], stat, norms, branch, count, total
        )
        unite = jnp.concatenate([unites[level][...], unites[3 + level][...]], axis=0)
        grad = dot_nt(mixed_grad, mix_matrix(unite, branch)) * silu_slope(value)
        grads[level][...] = grad
        sums[2 * branch : 2 * branch + 1, :] = column_sum(grad)
        sums[2 * branch + 1 : 2 * branch + 2, :] = column_sum(grad * scaled)
        write_edges(odd, near, far, grad, branch, count, 0)
        write_edges(odd, near, far, seconds[branch][...], branch, count, 128)


def mixer_kernel(rows, counts, meta, *refs):
    mixed_grads, seconds, tiles, stat, norms, outs = split_refs(refs, 3, 3, 3, 1, 1, 6)
    for level in range(3):
        branch = level + 1
        channels = CHANNELS[branch]
        value, _, _ = joined(
            seconds[level][...], tiles[level], stat[0], norms[0], branch, rows[branch], counts[branch]
        )
        product = dot_tn(silu(value), mixed_grads[level][...])
        mixer = None
        for place in range(8):
            row = place // (8 * channels // 256) * channels
            tile_first = place * C0 // 128 * 128
            block = product[row : row + channels, tile_first : tile_first + 128]
            inner = place * C0 - tile_first
            if inner:
                block = pltpu.roll(block, 128 - inner, 1)
            mixer = block if mixer is None else mixer + block
        outs[level][...] = mixer[: channels // 2, :C0]
        outs[3 + level][...] = mixer[channels // 2 :, :C0]


def norm_input_grad(grad, scaled, stats, gain, sums, channels, total):
    shift_sum = fold(sums[0:1, :], channels) / total
    gain_sum = fold(sums[1:2, :], channels) / total
    return (gain * stats[1]) * (grad - shift_sum - scaled * gain_sum)


def back_second_kernel(rows, counts, flags, *refs):
    ins, outs, wide, sides = split_refs(refs, 22, 7, 4, 4)
    grads, seconds, firsts, bands = ins[0:4], ins[4:8], ins[8:12], ins[12:16]
    near_in, far_in, stat, stat_sums, first_stat, norms = ins[16:22]
    normed_grads = outs[0:4]
    sums, near, far = outs[4:7]
    odd = flags[4] == 1
    for branch in range(4):
        count, channels, total = rows[branch], CHANNELS[branch], counts[branch]
        stats = moments(stat[2 * branch : 2 * branch + 2, :], channels, total)
        gain = norms[2 * branch + 1 : 2 * branch + 2, :]
        shift_sum = fold(stat_sums[2 * branch : 2 * branch + 1, :], channels) / total
        gain_sum = fold(stat_sums[2 * branch + 1 : 2 * branch + 2, :], channels) / total

        def input_grad(grad, value):
            scaled = (value - stats[0]) * stats[1]
            return (gain * stats[1]) * (grad - shift_sum - scaled * gain_sum)

        inner = input_grad(grads[branch][...], seconds[branch][...])
        wide[branch][:, 16 : (count + 1) * 16, :] = inner.reshape(2, count * 16, 256)
        for image in range(2):
            place = edge_place(branch, image)
            parts = [
                input_grad(ref[place : place + 16, :], ref[128 + place : 144 + place, :])
                for ref in (near_in, far_in)
            ]
            for value, start, flag in (
                (jnp.where(odd, parts[0], parts[1]), 0, flags[0]),
                (jnp.where(odd, parts[1], parts[0]), (count + 1) * 16, flags[1]),
            ):
                wide[branch][image, start : start + 16, :] = jnp.where(flag == 0, 0.0, value)
        build_sides(wide[branch], sides[branch], channels)
        hidden_grad = dot_nn(patches(wide[branch], sides[branch], count), bands[branch][...])
        first_stats = moments(first_stat[2 * branch : 2 * branch + 2, :], channels, total)
        scaled = (load_rows(firsts[branch], 1, count) - first_stats[0]) * first_stats[1]
        value = (
            scaled * norms[2 * branch : 2 * branch + 1, :]
            + norms[11 + 2 * branch : 12 + 2 * branch, :]
        )
        grad = hidden_grad * silu_slope(value)
        normed_grads[branch][...] = grad
        sums[2 * branch : 2 * branch + 1, :] = column_sum(grad)
        sums[2 * branch + 1 : 2 * branch + 2, :] = column_sum(grad * scaled)
        write_edges(odd, near, far, grad, branch, count, 0)


def cross_products(rows, branch, offset, source, value, out, side, product):
    count, channels = rows[branch], CHANNELS[branch]
    build_sides(source, side, channels)
    product[...] = dot_tn(patches(source, side, count, offset), value)

    def emit(tap_row, tap_col, block):
        place = (3 * tap_row + tap_col) * channels
        out[place : place + channels, :] = block

    collect_band(product, branch, emit)


def normalized(raw, stat, rows, counts, branch, inner):
    stats = moments(stat[2 * branch : 2 * branch + 2, :], CHANNELS[branch], counts[branch])
    value = raw[...] if inner else load_rows(raw, 1, rows[branch])
    return (value - stats[0]) * stats[1]


def sum_means(sums, branch, total):
    channels = CHANNELS[branch]
    return [fold(sums[2 * branch + i : 2 * branch + i + 1, :], channels) / total for i in range(2)]


def cross_kernel(rows, counts, devices, branch, offset, inner, meta, *refs):
    source, value, raw, stat, sums, out, side, product = refs
    shift_mean, gain_mean = sum_means(sums, branch, counts[branch] / devices)
    scaled = normalized(raw, stat, rows, counts, branch, inner)
    rest = value[...] - shift_mean - scaled * gain_mean
    cross_products(rows, branch, offset, source, rest, out, side, product)


def cross_norm_kernel(rows, counts, branch, offset, inner, meta, *refs):
    source, raw, stat, out, sums, side, product = refs
    count, channels = rows[branch], CHANNELS[branch]
    scaled = normalized(raw, stat, rows, counts, branch, inner)
    cross_products(rows, branch, offset, source, scaled, out, side, product)
    total = column_sum(patches(source, side, count, offset))
    column = jnp.transpose(jnp.broadcast_to(total, (8, total.shape[1])))
    for tap_row in range(3):
        for tap_col in range(3):
            block = None
            for place in range(256 // channels):
                row = band_row(branch, tap_row, place + tap_col - 1)
                part = column[row : row + channels]
                block = part if block is None else block + part
            start = (3 * tap_row + tap_col) * channels
            sums[start : start + channels, :] = block


def combine_kernel(counts, devices, packed, which, meta, *refs):
    crosses, norm_crosses, patch_sums, ins, unite_grads, outs, stage, scratch = split_refs(
        refs, 4, 4, 4, 4, 3, 2 if packed else 4, 5, 3
    )
    stat, own_sums, grad_sums, norms = ins
    for branch in range(4):
        channels, total = CHANNELS[branch], counts[branch]
        stats = moments(stat[2 * branch : 2 * branch + 2, :], channels, total)
        line = 2 * branch + which
        scale = (norms[line : line + 1, :] * stats[1])[:, :channels]
        shift_rest, gain_rest = (
            (whole - own)[:, :channels]
            for whole, own in zip(
                sum_means(grad_sums, branch, total), sum_means(own_sums, branch, total / devices)
            )
        )
        emit = tap_writer(stage[3 - branch], branch)
        for place in range(9):
            span = slice(place * channels, (place + 1) * channels)
            value = (
                crosses[branch][span, :]
                - patch_sums[branch][span, 0:1] * shift_rest
                - norm_crosses[branch][span, :] * gain_rest
            )
            emit(place // 3, place % 3, scale * value)
    if packed:
        pack_grads(meta[2], stage, unite_grads, outs, scratch)
    else:
        for ref, value in zip(outs, stage):
            ref[...] = value[...]


def back_first_kernel(rows, counts, flags, *refs):
    ins, source_grads, wide, sides, bands = split_refs(refs, 21, 4, 4, 4, 4)
    normed_grads, firsts, join_grads, taps = ins[0:4], ins[4:8], ins[8:12], ins[12:16]
    near, far, first_stat, first_sums, norms = ins[16:21]
    odd = flags[4] == 1
    for branch in range(4):
        count, channels, total = rows[branch], CHANNELS[branch], counts[branch]
        stats = moments(first_stat[2 * branch : 2 * branch + 2, :], channels, total)
        gain = norms[2 * branch : 2 * branch + 1, :]
        shift_sum = fold(first_sums[2 * branch : 2 * branch + 1, :], channels) / total
        gain_sum = fold(first_sums[2 * branch + 1 : 2 * branch + 2, :], channels) / total

        def input_grad(grad, value):
            scaled = (value - stats[0]) * stats[1]
            return (gain * stats[1]) * (grad - shift_sum - scaled * gain_sum)

        inner = input_grad(normed_grads[branch][...], load_rows(firsts[branch], 1, count))
        wide[branch][:, 16 : (count + 1) * 16, :] = inner.reshape(2, count * 16, 256)
        for image in range(2):
            place = edge_place(branch, image)
            one, two = (ref[place : place + 16, :] for ref in (near, far))
            for grad, start, flag in (
                (jnp.where(odd, one, two), 0, flags[0]),
                (jnp.where(odd, two, one), (count + 1) * 16, flags[1]),
            ):
                value = input_grad(grad, firsts[branch][image, start : start + 16, :])
                wide[branch][image, start : start + 16, :] = jnp.where(flag == 0, 0.0, value)
        build_sides(wide[branch], sides[branch], channels)
        build_band(bands[branch], turned(tap_reader(taps[3 - branch], branch)), branch, 0)
        grad = dot_nn(patches(wide[branch], sides[branch], count), bands[branch][...])
        grad = (grad + join_grads[branch][...]).reshape(2, count * 16, 256)
        for image in range(2):
            source_grads[branch][image] = grad[image].reshape(count, 4096)


def finish_kernel(first_sums, second_sums, head_sums, gain, shift, loss, head_weight, head_bias):
    offset = 0

    def put(sums, line, channels):
        nonlocal offset
        for ref, row in ((shift, line), (gain, line + 1)):
            value = fold(sums[row : row + 1, :], channels)
            done = 0
            while done < channels:
                place = offset + done
                width = min(channels - done, 128 - place % 128)
                ref[place // 128 : place // 128 + 1, place % 128 : place % 128 + width] = value[
                    :, done : done + width
                ]
                done += width
        offset += channels

    for branch in range(4):
        for sums in (first_sums, second_sums):
            put(sums, 2 * branch, CHANNELS[branch])
    for level in range(3):
        put(head_sums, 2 * level, C0)
    loss[...] = jnp.sum(head_sums[6:7, :], axis=1, keepdims=True)
    joints = head_bias.shape[1]
    head_bias[...] = fold(head_sums[7:8, :], C0)[:, :joints]
    total = jnp.concatenate(
        [second_sums[8:16, C0 * part : C0 * part + C0] for part in range(4)], axis=0
    )
    head_weight[...] = jnp.transpose(total)[:joints]


def device_count():
    return lax.axis_size("dp") * lax.axis_size("space")


def exchange(value, bit):
    return lax.ppermute(value, AXES, [(i, i ^ bit) for i in range(device_count())])


def total_sum(value, beside=(), order=None):
    value = value.value
    for step, bit in enumerate(order or [1 << i for i in range(device_count().bit_length() - 1)]):
        other = exchange(value, bit)
        if step < len(beside) and beside[step]:
            other = after(other, *beside[step](value))
        value = value + other
    return Kept(value)


def swap_rows(near, far):
    devices = lax.axis_size("space")
    pairs = [(i, i ^ 1) for i in range(devices)]
    others = [(i, i + 1) for i in range(1, devices - 1, 2)]
    others += [(j, i) for i, j in others]
    return lax.ppermute(near, "space", pairs), lax.ppermute(far, "space", others)


def device_index():
    return lax.axis_index("dp") * lax.axis_size("space") + lax.axis_index("space")


def after(value, *others):
    return lax.optimization_barrier((value, *others))[0]


def swap(parts, step):
    return [Kept(exchange(part.value, STEPS[chunk][step])) for chunk, part in enumerate(parts)]


def gather_shards(meta, flat, beside):
    other = exchange(flat, 16)
    other = after(other, *beside(flat))
    shapes = [(1, 2, last - first, 128) for first, last in CHUNKS]
    parts = call(split_shard, [meta, flat, Kept(other)], kept(shapes), smem=1)
    shapes = [(2, *shape[1:]) for shape in shapes]
    parts = call(join_chunks, [*parts, *swap(parts, 0)], kept(shapes))
    shapes = [(4, *shape[2:]) for shape in shapes]
    parts = call(join_apart, [*parts, *swap(parts, 1)], kept(shapes * 2))
    first, second = parts[:3], parts[3:]
    (whole,) = call(join_whole, [*first, *swap(first, 2)], kept([(8, SHARD, 128)]))
    second[0] = Kept(after(second[0].value, whole.value))
    received = swap(second, 2)

    def rest(start):
        received[0] = Kept(after(received[0].value, start))
        (whole,) = call(join_whole, [*second, *received], kept([(8, SHARD, 128)]))
        return [whole, Kept(exchange(whole.value, 1))]

    return [whole, Kept(exchange(whole.value, 1))], rest


def scatter_step(parts, step, beside, meta=None):
    received = swap(parts[3:], step)
    received[0] = Kept(after(received[0].value, *beside(parts[3].value)))
    if step == 2:
        return call(add_last, [meta, *parts[:3], *received], kept([(SHARD, 128)] * 2), smem=1)
    shapes = [(2 - step, 2, last - first, 128) for first, last in CHUNKS]
    return call(add_received, [*parts[:3], *received], kept(shapes * 2))


def body(
    branch_zero,
    branch_one,
    branch_two,
    branch_three,
    convs_zero,
    convs_one,
    convs_two,
    convs_three,
    unite_one,
    unite_two,
    unite_three,
    norm_gain,
    norm_shift,
    head_weight,
    head_bias,
    targets,
    crowd_mask,
    person_count,
    flip_order,
):
    inputs = (branch_zero, branch_one, branch_two, branch_three)
    devices = device_count()
    spaces = lax.axis_size("space")
    place = lax.axis_index("space")
    rows = tuple(value.shape[1] for value in inputs)
    counts = tuple(
        float(2 * rows[b] * 16 * (256 // CHANNELS[b]) * devices) for b in range(4)
    )
    joints = head_bias.shape[0]
    cells = [2 * rows[b] * 16 for b in range(4)]
    packed = devices == 32
    shards_in = (convs_three, convs_two, convs_one, convs_zero, unite_one, unite_two, unite_three)
    sizes = [part.shape[0] for part in shards_in]

    meta = jnp.stack(
        [
            place > 0,
            place < spaces - 1,
            device_index() & 15,
            (device_index() & 16) // 16,
            place % 2,
        ]
    ).astype(jnp.int32)

    state = {}

    def prepare(start):
        parts = lax.optimization_barrier((*inputs, start))[:4]
        last_rows = jnp.concatenate([value[:, -2:] for value in parts], axis=1)
        first_rows = jnp.concatenate([value[:, :2] for value in parts], axis=1)
        odd = place % 2 == 1
        state["halo"] = swap_rows(
            jnp.where(odd, first_rows, last_rows), jnp.where(odd, last_rows, first_rows)
        )
        state["targets"] = call(
            target_kernel,
            [after(person_count, start), targets, crowd_mask],
            kept([(cells[0], 256)] * 2),
            [(cells[0], 128)],
            smem=1,
            cost=4,
        )
        return [state["targets"][0].value, *state["halo"]]

    def parameters(start):
        state["small"] = call(
            parameter_kernel,
            [
                after(norm_gain, start)[None],
                norm_shift[None],
                jnp.transpose(head_weight),
                head_bias[None],
                flip_order[None],
            ],
            kept([(22, 256), (C0, C0), (1, 256), (C0, C0), (1, 256)]),
        )
        return [state["small"][0].value]

    if packed:
        gap = jnp.zeros(((24 - ROWS_ONE) * 128,), f32)
        flat = jnp.concatenate([*shards_in[:3], gap, *shards_in[3:]]).reshape(SHARD, 128)
        first_packs, rest = gather_shards(meta, flat, prepare)
    else:
        prepare(meta)
        whole = [lax.all_gather(part, AXES, axis=0, tiled=True) for part in shards_in]
        whole = [
            part.reshape(-1, width)
            for part, width in zip(whole, (128, 128, 64, 32, 32, 32, 32))
        ]
        first_packs = [part[: part.shape[0] // 2] for part in whole]
        second_packs = [part[part.shape[0] // 2 :] for part in whole]
    near, far = state["halo"]
    target_cells, loss_weight = state["targets"]

    bands = [band_shape(b, 256) for b in range(4)]
    inner = [(cells[b], 256) for b in range(4)]
    wide = [(2, (rows[b] + 2) * 16, 256) for b in range(4)]
    wider = [(2, (rows[b] + 4) * 16, 256) for b in range(4)]

    def sides_of(shapes):
        return [shape[:2] + (SIDES[b],) for b, shape in enumerate(shapes)]

    eight = (8, 256)
    taps_out = kept(TAPS_OUT) if packed else []
    unpack_scratch = list(PACK_SCRATCH) if packed else []

    out = call(
        functools.partial(first_kernel, rows, packed),
        [meta, *inputs, near, far, *first_packs[:4]],
        kept([*wider, *wide, eight]) + taps_out,
        bands + sides_of(wider) + unpack_scratch,
        smem=1,
        cost=7,
    )
    tiles, firsts = out[0:4], out[4:8]
    first_taps = out[9:] if packed else first_packs
    if packed:
        second_packs = rest(tiles[0].value)

    crosses = [[None] * 4, [None] * 4]
    norm_crosses = [[None] * 4, [None] * 4]
    natural = [(9 * CHANNELS[b], CHANNELS[b]) for b in range(4)]

    def cross(which, branch):
        def work(start):
            values = (
                (tiles[branch], normed_grads[branch], firsts[branch], first_stat, own_first)
                if which == 0
                else (hidden[branch], join_grads[branch], seconds[branch], second_stat, own_second)
            )
            (crosses[which][branch],) = call(
                functools.partial(cross_kernel, rows, counts, devices, branch, 1 - which, which),
                [after(meta, start), *values],
                kept([natural[branch]]),
                [sides_of(wide if which else wider)[branch], bands[branch]],
                smem=1,
                cost=2,
            )
            return [crosses[which][branch].value]

        return work

    def norm_cross(which, branch):
        def work(start):
            source, value, stat = (
                (tiles[branch], firsts[branch], first_stat)
                if which == 0
                else (hidden[branch], seconds[branch], second_stat)
            )
            norm_crosses[which][branch] = call(
                functools.partial(cross_norm_kernel, rows, counts, branch, 1 - which, which),
                [after(meta, start), source, value, stat],
                kept([natural[branch], (9 * CHANNELS[branch], 8)]),
                [sides_of(wide if which else wider)[branch], bands[branch]],
                smem=1,
                cost=2,
            )
            return [norm_crosses[which][branch][0].value]

        return work

    def combine(which, sums, mixers, start):
        return call(
            functools.partial(combine_kernel, counts, devices, packed, which),
            [
                after(meta, start),
                *crosses[which],
                *[part[0] for part in norm_crosses[which]],
                *[part[1] for part in norm_crosses[which]],
                (first_stat, second_stat)[which],
                (own_first, own_second)[which],
                sums,
                norms,
                *mixers,
            ],
            kept([(8, SHARD, 128)] * 2) if packed else list(TAPS_OUT[:4]),
            [*STAGE, *PACK_SCRATCH],
            smem=1,
            cost=2,
        )

    def works(*parts):
        return lambda start: sum((part(start) for part in parts), [])

    flip_firsts, flip_seconds = [None] * 4, [None] * 4

    def flip_first(branch):
        def work(start):
            (flip_firsts[branch],) = call(
                functools.partial(first_flip_kernel, rows, branch),
                [after(meta, start), tiles[branch], first_taps[3 - branch]],
                kept([wide[branch]]),
                [bands[branch], sides_of(wider)[branch]],
                smem=1,
                cost=2,
            )
            return [flip_firsts[branch].value]

        return work

    def second_bands(start):
        state["second"] = call(
            functools.partial(band_kernel, packed),
            [after(meta, start), *second_packs[:4]],
            taps_out + kept(bands),
            unpack_scratch,
            smem=1,
            cost=2,
        )
        return [state["second"][-1].value]

    order = [1 << i for i in range(devices.bit_length() - 1)]
    first_stat = total_sum(
        out[8],
        [parameters, flip_first(1), second_bands, flip_first(0)],
        [*order[1:], 1] if packed else None,
    )
    norms, weight, bias, flip_weight, flip_bias = state["small"]
    second_taps = state["second"][:7] if packed else second_packs

    out = call(
        functools.partial(second_kernel, rows, counts),
        [meta, *firsts, first_stat, norms, *state["second"][-4:]],
        kept([*inner, eight, *wide]),
        sides_of(wide),
        smem=1,
        cost=6,
    )
    seconds, hidden = out[0:4], out[5:9]
    unites = [*first_taps[4:7], *second_taps[4:7]]
    first_taps, second_taps = first_taps[:4], second_taps[:4]

    def flip_second(branch):
        def work(start):
            (flip_seconds[branch],) = call(
                functools.partial(second_flip_kernel, rows, counts, branch),
                [
                    after(meta, start),
                    flip_firsts[branch],
                    first_stat,
                    norms,
                    second_taps[3 - branch],
                ],
                kept([inner[branch]]),
                [wide[branch], bands[branch], sides_of(wide)[branch]],
                smem=1,
                cost=2,
            )
            return [flip_seconds[branch].value]

        return work

    second_stat = total_sum(
        out[4],
        [
            None,
            norm_cross(0, 0),
            norm_cross(0, 1),
            works(norm_cross(0, 2), flip_first(2)),
            works(norm_cross(0, 3), flip_first(3)),
        ],
    )

    out = call(
        functools.partial(third_kernel, rows, counts),
        [*seconds[1:], *tiles[1:], second_stat, norms, *unites],
        kept([*inner[1:], eight]),
    )
    mixes = out[0:3]
    mix_stat = total_sum(
        out[3],
        [
            None,
            flip_second(0),
            flip_second(1),
            works(flip_second(2), flip_second(3)),
            norm_cross(1, 3),
        ],
    )

    denominator = float(counts[0] * joints)
    out = call(
        functools.partial(loss_kernel, rows, counts, denominator),
        [
            seconds[0],
            tiles[0],
            second_stat,
            *mixes,
            mix_stat,
            norms,
            weight,
            bias,
            target_cells,
            loss_weight,
        ],
        kept([inner[0], *inner[1:], eight, inner[0], eight, inner[0], inner[0]]),
        cost=3,
    )
    heat, pre_sums, join_zero, zero_sums, united, heat_grad = out[0], out[1:4], *out[5:9]

    def head_grads(start):
        (state["head"],) = call(
            head_kernel, [after(meta, start), united, heat_grad], kept([eight]), smem=1
        )
        return [state["head"].value]

    def turned_bands(start):
        state["turned"] = call(
            turned_kernel, [after(meta, start), *second_taps], kept(bands), smem=1, cost=2
        )
        return [state["turned"][0].value]

    head_sums = total_sum(
        out[4],
        [
            None,
            norm_cross(1, 0),
            works(norm_cross(1, 1), head_grads),
            works(norm_cross(1, 2), turned_bands),
        ],
    )

    out = call(
        functools.partial(join_kernel, rows, counts),
        [
            meta,
            *pre_sums,
            *mixes,
            *seconds,
            *tiles[1:],
            join_zero,
            zero_sums,
            state["head"],
            second_stat,
            mix_stat,
            head_sums,
            norms,
            *unites,
        ],
        kept([*inner[1:], *inner[1:], (16, 256), (256, 256), (256, 256)]),
        smem=1,
        cost=2,
    )
    join_grads = [join_zero, *out[0:3]]
    mixed_grads, edges = out[3:6], out[7:9]

    def mixers(start):
        state["mixers"] = call(
            functools.partial(mixer_kernel, rows, counts),
            [after(meta, start), *mixed_grads, *seconds[1:], *tiles[1:], second_stat, norms],
            kept([(CHANNELS[b] // 2, C0) for b in range(1, 4)] * 2),
            smem=1,
        )
        return [state["mixers"][0].value]

    def edge_rows(start):
        near, far = lax.optimization_barrier((edges[0].value, edges[1].value, start))[:2]
        state["edges"] = kept(swap_rows(near, far))
        return [part.value for part in state["edges"]]

    own_second = out[6]
    second_sums = total_sum(
        own_second,
        [
            None,
            cross(1, 0),
            works(edge_rows, cross(1, 2)),
            cross(1, 1),
            works(cross(1, 3), mixers),
        ],
    )
    first_mixers, second_mixers = state["mixers"][:3], state["mixers"][3:]

    out = call(
        functools.partial(back_second_kernel, rows, counts),
        [
            meta,
            *join_grads,
            *seconds,
            *firsts,
            *state["turned"],
            *state["edges"],
            second_stat,
            second_sums,
            first_stat,
            norms,
        ],
        kept([*inner, eight, (128, 256), (128, 256)]),
        wide + sides_of(wide),
        smem=1,
        cost=6,
    )
    normed_grads, edges = out[0:4], out[5:7]

    def second_packs_work(start):
        state["packs"] = combine(1, second_sums, second_mixers, start)
        return [state["packs"][0].value] if packed else [state["packs"][0]]

    own_first = out[4]
    first_sums = total_sum(
        own_first,
        [
            None,
            second_packs_work,
            cross(0, 0),
            cross(0, 1),
            works(cross(0, 2), cross(0, 3)),
        ],
    )
    if packed:
        far_second = exchange(after(state["packs"][1].value, first_sums.value), 1)
        first_kernels = combine(0, first_sums, first_mixers, first_sums.value)
    else:
        second_kernels = state["packs"]
        first_kernels = combine(0, first_sums, first_mixers, first_sums.value)
        edge_rows(first_sums.value)

    def back_first(start):
        state["source"] = call(
            functools.partial(back_first_kernel, rows, counts),
            [
                after(meta, start),
                *normed_grads,
                *firsts,
                *join_grads,
                *first_taps,
                *state["edges"],
                first_stat,
                first_sums,
                norms,
            ],
            [value.shape for value in inputs],
            wide + sides_of(wide) + bands,
            smem=1,
            cost=7,
        )
        return [state["source"][0]]

    def flip_last(start):
        (state["heat"],) = call(
            functools.partial(flip_kernel, rows, counts),
            [
                *flip_seconds,
                *tiles,
                second_stat,
                *unites,
                mix_stat,
                norms,
                flip_weight,
                Kept(after(flip_bias.value, start)),
                heat,
            ],
            [targets.shape],
            [(cells[0], 128)] * 2,
            cost=5,
        )
        return [state["heat"]]

    def finish(start):
        state["finish"] = call(
            finish_kernel,
            [Kept(after(first_sums.value, start)), second_sums, head_sums],
            [(9, 128), (9, 128), (1, 1), (joints, C0), (1, joints)],
            limit=4,
        )
        return [state["finish"][0]]

    if packed:
        far_first = exchange(first_kernels[1].value, 1)
        far_first = after(far_first, *edge_rows(first_kernels[1].value))
        shapes = [(4, 2, last - first, 128) for first, last in CHUNKS]
        parts = call(
            add_cores,
            [first_kernels[0], state["packs"][0], Kept(far_first), Kept(far_second)],
            kept(shapes * 2),
            cost=2,
        )
        parts = scatter_step(parts, 0, back_first)
        parts = scatter_step(parts, 1, flip_last)
        keep, send = scatter_step(parts, 2, finish, meta)
        out = call(
            add_shard,
            [keep, Kept(exchange(send.value, 16))],
            [(ROWS_THREE, 128), (ROWS_TWO, 128), (ROWS_ONE, 128), (5, 128), (1, 64), (1, 128), (2, 128)],
        )
        shards = [part.reshape(-1)[:size] for part, size in zip(out, sizes)]
    else:
        for work in (back_first, flip_last, finish):
            work(first_sums.value)
        first_mixers, second_mixers = (
            [part.value for part in parts] for parts in (first_mixers, second_mixers)
        )
        flat = [
            jnp.concatenate([one.reshape(-1), two.reshape(-1)])
            for one, two in zip([*first_kernels, *first_mixers], [*second_kernels, *second_mixers])
        ]
        shards = [lax.psum_scatter(part, AXES, scatter_dimension=0, tiled=True) for part in flat]

    gain_grad, shift_grad, loss, head_grad, bias_grad = state["finish"]
    return (
        loss[0, 0],
        state["heat"],
        *state["source"],
        shards[3],
        shards[2],
        shards[1],
        shards[0],
        *shards[4:7],
        gain_grad.reshape(-1)[: norm_gain.shape[0]],
        shift_grad.reshape(-1)[: norm_shift.shape[0]],
        jnp.transpose(head_grad),
        bias_grad[0],
    )


def solution(mesh):
    rows = P("dp", "space", None)
    shard = P(("dp", "space"))
    heat = P("dp", None, "space", None)
    return jax.shard_map(
        body,
        mesh=mesh,
        in_specs=(*[rows] * 4, *[shard] * 7, *[P()] * 4, heat, rows, P("dp"), P()),
        out_specs=(P(), heat, *[rows] * 4, *[shard] * 7, *[P()] * 4),
        check_vma=False,
    )
```

```python
import functools

import jax
import jax.numpy as jnp
import numpy as np
from jax import lax
from jax.experimental import pallas as pl
from jax.experimental.pallas import tpu as pltpu
from jax.sharding import PartitionSpec as P

C0 = 32
CHANNELS = (32, 64, 128, 256)
SIDES = (128, 128, 256, 512)
AXES = ("dp", "space")
epsilon = 1e-05
f32 = jnp.float32
high = lax.Precision.HIGH


def dot_nn(left, right):
    return lax.dot_general(left, right, (((1,), (0,)), ((), ())), precision=high, preferred_element_type=f32)


def dot_nt(left, right):
    return lax.dot_general(left, right, (((1,), (1,)), ((), ())), precision=high, preferred_element_type=f32)


def dot_tn(left, right):
    return lax.dot_general(left, right, (((0,), (0,)), ((), ())), precision=high, preferred_element_type=f32)


def sigmoid(value):
    return 1.0 / (1.0 + jnp.exp(-value))


def silu(value):
    return value * sigmoid(value)


def silu_slope(value):
    sigma = sigmoid(value)
    return sigma * (1.0 + value * (1.0 - sigma))


def fold(row, channels):
    step = channels
    while step < 256:
        row = row + pltpu.roll(row, step, 1)
        step = 2 * step
    return row


def column_sum(value):
    return jnp.sum(value, axis=0, keepdims=True)


def moments(sums, channels, count):
    mean = fold(sums[0:1], channels) / count
    square = fold(sums[1:2], channels) / count
    return mean, lax.rsqrt(square - mean * mean + epsilon)


def affine(stats, gain, shift):
    scale = stats[1] * gain
    return scale, shift - stats[0] * scale


def load_rows(ref, first, count):
    lanes = ref.shape[2]
    return ref[:, first * 16 : (first + count) * 16, :].reshape(2 * count * 16, lanes)


def group_index(rows):
    return lax.broadcasted_iota(jnp.int32, (rows, 128), 0) % 16


def side_columns(value, channels):
    rows = value.shape[0]
    group = group_index(rows)
    lane = lax.broadcasted_iota(jnp.int32, (rows, 128), 1)

    def before(part):
        return jnp.where(group == 0, 0.0, pltpu.roll(part, 1, 0))

    def after(part):
        return jnp.where(group == 15, 0.0, pltpu.roll(part, rows - 1, 0))

    low, upper = value[:, :128], value[:, 128:]
    if channels == 256:
        return jnp.concatenate([before(low), before(upper), after(low), after(upper)], axis=1)
    if channels == 128:
        return jnp.concatenate([before(upper), after(low)], axis=1)
    return jnp.where(
        lane < channels, after(low), jnp.where(lane >= 128 - channels, before(upper), 0.0)
    )


def build_sides(source, side, channels):
    rows = source.shape[1]
    for image in range(2):
        side[image] = side_columns(source[image], channels)


def patches(source, side, count, offset=0):
    parts = []
    for tap_row in range(3):
        parts.append(load_rows(source, tap_row + offset, count))
        parts.append(load_rows(side, tap_row + offset, count))
    return jnp.concatenate(parts, axis=1)


def band_row(branch, tap_row, place):
    channels, side = CHANNELS[branch], SIDES[branch]
    base = tap_row * (256 + side)
    if place < 0:
        return base + 256 + (0 if channels >= 128 else 128 - channels)
    if place >= 256 // channels:
        return base + 256 + (side // 2 if channels >= 128 else 0)
    return base + place * channels


def build_band(band, tap, branch, offset):
    channels = CHANNELS[branch]
    groups = 256 // channels
    side = SIDES[branch]
    height = 256 + side
    if channels < 256:
        band[:, offset : offset + 256] = jnp.zeros((3 * height, 256), f32)
    for tap_row in range(3):
        for tap_col in range(3):
            matrix = tap(tap_row, tap_col)
            for out in range(groups):
                row = band_row(branch, tap_row, out + tap_col - 1)
                start = offset + out * channels
                band[row : row + channels, start : start + channels] = matrix


def collect_band(product, branch, emit):
    channels = CHANNELS[branch]
    for tap_row in range(3):
        for tap_col in range(3):
            total = None
            for out in range(256 // channels):
                row = band_row(branch, tap_row, out + tap_col - 1)
                start = out * channels
                if channels >= 128:
                    block = product[row : row + channels, start : start + channels]
                else:
                    tile = start // 128 * 128
                    block = product[row : row + channels, tile : tile + 128]
                    inner = start - tile
                    if inner:
                        block = pltpu.roll(block, 128 - inner, 1)
                total = block if total is None else total + block
            emit(tap_row, tap_col, total[:, :channels])


def tap_reader(ref, branch):
    channels = CHANNELS[branch]
    if channels == 256:

        def tap(tap_row, tap_col):
            first = (3 * tap_row + tap_col) * 512
            return jnp.concatenate(
                [ref[pl.ds(first, 256, stride=2), :], ref[pl.ds(first + 1, 256, stride=2), :]],
                axis=1,
            )

        return tap

    def tap(tap_row, tap_col):
        first = (3 * tap_row + tap_col) * channels
        return ref[first : first + channels, :]

    return tap


def tap_writer(ref, branch):
    channels = CHANNELS[branch]

    def emit(tap_row, tap_col, value):
        place = 3 * tap_row + tap_col
        if channels == 256:
            ref[pl.ds(place * 512, 256, stride=2), :] = value[:, :128]
            ref[pl.ds(place * 512 + 1, 256, stride=2), :] = value[:, 128:]
        else:
            ref[place * channels : (place + 1) * channels, :] = value

    return emit


SHARD = 392
ROWS_THREE, ROWS_TWO, ROWS_ONE = 288, 72, 18
PER_ZERO, PER_UNITE = 18, (2, 4, 8)
CHUNKS = ((0, 152), (152, 272), (272, 392))
STEPS = ((8, 4, 2), (4, 2, 8), (2, 8, 4))
TAPS_OUT = ((4608, 128), (1152, 128), (576, 64), (288, 32), (32, 32), (64, 32), (128, 32))
PACK_SCRATCH = ((16, 24, 128), (16, 8, 128), (288, 128))
STAGE = ((4608, 128), (1152, 128), (576, 64), (288, 32), (512, 32))


def partner(me, core, place, bits):
    return me ^ (core + sum(bit for i, bit in enumerate(bits) if place >> i & 1))


def shard_parts(device, three, two, one, zero):
    start = device * ROWS_THREE
    return (
        ((0, 152, three.at[pl.ds(pl.multiple_of(start, 8), 152), :]),),
        ((152, 272, three.at[pl.ds(pl.multiple_of(start + 152, 8), 120), :]),),
        (
            (272, 288, three.at[pl.ds(pl.multiple_of(start + 272, 8), 16), :]),
            (288, 360, two.at[pl.ds(pl.multiple_of(device * ROWS_TWO, 8), ROWS_TWO), :]),
            (360, 384, one.at[device]),
            (384, 392, zero.at[device]),
        ),
    )


def unpack_taps(me, packs, taps, scratch):
    three, two, one, zero = taps[:4]
    part_one, part_zero, flat_one = scratch
    for core in range(2):
        for place in range(8):
            for chunk in range(3):
                device = partner(me, core, place, STEPS[chunk])
                parts = shard_parts(device, three, two, part_one, part_zero)[chunk]
                for first, last, ref in parts:
                    ref[...] = packs[core][place, first:last]
    for device in range(16):
        flat_one[device * ROWS_ONE : (device + 1) * ROWS_ONE, :] = part_one[device, 0:ROWS_ONE]
    one[...] = flat_one[...].reshape(one.shape)
    narrow = part_zero[...].reshape(128, 128).reshape(512, 32)
    for device in range(16):
        first = device * 32
        for ref, height in zip(taps[3:7], (PER_ZERO, *PER_UNITE)):
            ref[device * height : (device + 1) * height, :] = narrow[first : first + height]
            first += height


def pack_grads(me, stage, unite_grads, packs, scratch):
    three, two, one, zero, narrow = stage
    part_one, part_zero, flat_one = scratch
    flat_one[...] = one[...].reshape(flat_one.shape)
    for device in range(16):
        part_one[device, 0:ROWS_ONE] = flat_one[device * ROWS_ONE : (device + 1) * ROWS_ONE, :]
        part_one[device, ROWS_ONE:24] = jnp.zeros((24 - ROWS_ONE, 128), f32)
        first = device * 32
        for ref, height in zip((zero, *unite_grads), (PER_ZERO, *PER_UNITE)):
            narrow[first : first + height, :] = ref[device * height : (device + 1) * height, :]
            first += height
    part_zero[...] = narrow[...].reshape(128, 128).reshape(16, 8, 128)
    for core in range(2):
        for place in range(8):
            for chunk in range(3):
                device = partner(me, core, place, STEPS[chunk][::-1])
                parts = shard_parts(device, three, two, part_one, part_zero)[chunk]
                for first, last, ref in parts:
                    packs[core][place, first:last] = ref[...]


def split_shard(meta, shard, other, *outs):
    second = meta[3] == 1
    for out, (first, last) in zip(outs, CHUNKS):
        own, far = shard[first:last], other[first:last]
        out[0, 0] = jnp.where(second, far, own)
        out[0, 1] = jnp.where(second, own, far)


def join_chunks(*refs):
    held, received, outs = split_refs(refs, 3, 3, 3)
    for chunk in range(3):
        count = held[chunk].shape[0]
        outs[chunk][0:count] = held[chunk][...]
        outs[chunk][count : 2 * count] = received[chunk][...]


def join_apart(*refs):
    held, received, first, second = split_refs(refs, 3, 3, 3, 3)
    for chunk in range(3):
        count = held[chunk].shape[0]
        for half, outs in ((0, first), (1, second)):
            outs[chunk][0:count] = held[chunk][:, half]
            outs[chunk][count : 2 * count] = received[chunk][:, half]


def join_whole(*refs):
    held, received, out = split_refs(refs, 3, 3, 1)
    for chunk, (first, last) in enumerate(CHUNKS):
        count = held[chunk].shape[0]
        out[0][0:count, first:last] = held[chunk][...]
        out[0][count : 2 * count, first:last] = received[chunk][...]


def add_received(*refs):
    held, received, low, high = split_refs(refs, 3, 3, 3, 3)
    for chunk in range(3):
        half = held[chunk].shape[0] // 2
        low[chunk][...] = held[chunk][0:half] + received[chunk][0:half]
        high[chunk][...] = held[chunk][half:] + received[chunk][half:]


def add_cores(*refs):
    keeps, received, low, high = split_refs(refs, 2, 2, 3, 3)
    for chunk, (first, last) in enumerate(CHUNKS):
        for half in range(2):
            low[chunk][:, half] = keeps[half][0:4, first:last] + received[half][0:4, first:last]
            high[chunk][:, half] = keeps[half][4:8, first:last] + received[half][4:8, first:last]


def add_last(meta, *refs):
    held, received, keep, send = split_refs(refs, 3, 3, 1, 1)
    second = meta[3] == 1
    for chunk, (first, last) in enumerate(CHUNKS):
        total = held[chunk][0] + received[chunk][0]
        keep[0][first:last, :] = jnp.where(second, total[1], total[0])
        send[0][first:last, :] = jnp.where(second, total[0], total[1])


def add_shard(keep, received, *outs):
    value = keep[...] + received[...]
    first = 0
    for ref in outs[:3]:
        last = first + ref.shape[0]
        ref[...] = value[first:last]
        first = last
    tail = SHARD - 8
    outs[3][...] = value[tail : tail + 5]
    outs[4][...] = value[tail + 4 : tail + 5, 64:]
    outs[5][...] = value[tail + 5 : tail + 6]
    outs[6][...] = value[tail + 6 : tail + 8]


def mirrored(tap):
    return lambda tap_row, tap_col: tap(tap_row, 2 - tap_col)


def turned(tap):
    return lambda tap_row, tap_col: jnp.transpose(tap(2 - tap_row, 2 - tap_col))


def mask_ends(value, rows, flags):
    place = lax.broadcasted_iota(jnp.int32, value.shape, 0) // 16 % (rows + 2)
    outside = ((place == 0) & (flags[0] == 0)) | ((place == rows + 1) & (flags[1] == 0))
    return jnp.where(outside, 0.0, value)


def mix_matrix(unite, branch):
    channels = CHANNELS[branch]
    groups = 256 // channels
    wide = jnp.concatenate([unite] * 8, axis=1)
    lane = lax.broadcasted_iota(jnp.int32, wide.shape, 1)
    span = 256 // groups
    return jnp.concatenate(
        [jnp.where(lane // span == place, wide, 0.0) for place in range(groups)], axis=0
    )


def split_refs(refs, *counts):
    out, first = [], 0
    for count in counts:
        out.append(refs[first : first + count])
        first += count
    assert first == len(refs)
    return out


class Kept:
    def __init__(self, value):
        self.value = value


def kept(values):
    return [Kept(value) for value in values]


def call(kernel, ins, outs, scratch=(), smem=0, limit=16, cost=0.01):
    specs = [pl.BlockSpec(memory_space=pltpu.SMEM)] * smem + [
        pl.BlockSpec(memory_space=pltpu.VMEM)
    ] * (len(ins) - smem)
    ins = ins[:smem] + [
        pltpu.with_memory_space_constraint(x.value, pltpu.VMEM)
        if isinstance(x, Kept)
        else pltpu.with_memory_space_constraint(x, pltpu.HBM)
        for x in ins[smem:]
    ]
    shapes = [pltpu.VMEM(x.value, f32) if isinstance(x, Kept) else pltpu.HBM(x, f32) for x in outs]
    results = pl.pallas_call(
        kernel,
        in_specs=specs,
        out_specs=[pl.BlockSpec(memory_space=pltpu.VMEM)] * len(outs),
        out_shape=shapes,
        scratch_shapes=[pltpu.VMEM(shape, f32) for shape in scratch],
        compiler_params=pltpu.CompilerParams(vmem_limit_bytes=limit * 2**20),
        cost_estimate=pl.CostEstimate(
            flops=int(cost * 1.1e9), bytes_accessed=int(cost * 3.0e6), transcendentals=0
        ),
    )(*ins)
    return [Kept(y) if isinstance(x, Kept) else y for x, y in zip(outs, results)]


def band_shape(branch, width):
    return (3 * (256 + SIDES[branch]), width)


def swap_blocks(parts):
    rows = parts[0].shape[0]
    group = lax.broadcasted_iota(jnp.int32, (rows, 128), 1) // 8
    step = 1
    while step < 16:
        high = (group & step) != 0
        parts = [
            jnp.where(high, parts[i], pltpu.roll(parts[i - step], 128 - 8 * step, 1))
            if i & step
            else jnp.where(high, pltpu.roll(parts[i + step], 8 * step, 1), parts[i])
            for i in range(16)
        ]
        step = 2 * step
    return parts


def joint_matrix():
    source = lax.broadcasted_iota(jnp.int32, (256, 256), 0)
    lane = lax.broadcasted_iota(jnp.int32, (256, 256), 1)
    matches = (source // 8 == lane % C0) & (source % 8 == lane // C0) & (source < 136)
    return jnp.where(matches, 1.0, 0.0)


def shift_group(value, group):
    return pltpu.roll(value, 128 - 8 * group, 1) if group else value


def parameter_kernel(gain, shift, weight, bias, flip, *outs):
    norms, weight_out, bias_out, flip_weight, flip_bias = outs
    weight = jnp.transpose(weight[...])
    for base, ref in ((0, gain), (11, shift)):
        offset = 0
        line = base
        sizes = [channels for channels in CHANNELS for _ in range(2)] + [C0] * 3
        for channels in sizes:
            part = ref[0:1, offset : offset + channels]
            norms[line : line + 1, :] = jnp.concatenate([part] * (256 // channels), axis=1)
            offset += channels
            line += 1
    joints = weight.shape[1]
    source = lax.broadcasted_iota(jnp.int32, (joints, joints), 0)
    moved = jnp.where(source == flip[...], 1.0, 0.0)
    for matrix, row, matrix_out, row_out in (
        (weight, bias[...], weight_out, bias_out),
        (
            jnp.dot(weight, moved, precision=lax.Precision.HIGHEST),
            jnp.dot(bias[...], moved, precision=lax.Precision.HIGHEST),
            flip_weight,
            flip_bias,
        ),
    ):
        matrix_out[...] = jnp.zeros((C0, C0), f32)
        matrix_out[:, 0:joints] = matrix
        row_out[...] = jnp.zeros((1, 256), f32)
        for place in range(8):
            row_out[0:1, C0 * place : C0 * place + joints] = row


def target_kernel(people, targets, mask, target_out, mask_out, scratch):
    lines = 2 * targets.shape[2]
    parts = swap_blocks([targets[:, j].reshape(lines, 128) for j in range(16)])
    last = targets[:, 16].reshape(lines, 128)
    cells = mask[...].reshape(lines, 128).astype(f32)
    lane = lax.broadcasted_iota(jnp.int32, (lines, 128), 1)
    tails = [
        jnp.where(lane < 8, shift_group(last, group), pltpu.roll(shift_group(cells, group), 8, 1))
        for group in range(16)
    ]
    whole = jnp.concatenate(
        [jnp.concatenate([part, tail], axis=1) for part, tail in zip(parts, tails)], axis=0
    )
    source = lax.broadcasted_iota(jnp.int32, (256, 256), 0)
    target_lane = lax.broadcasted_iota(jnp.int32, (256, 256), 1)
    spread = jnp.where((source >= 136) & (source < 144) & (source - 136 == target_lane // C0), 1.0, 0.0)
    target_rows = dot_nn(whole, joint_matrix())
    mask_rows = dot_nn(whole, spread)
    first_image = lax.broadcasted_iota(jnp.int32, (lines, 256), 0) < lines // 2
    share = jnp.where(first_image, people[0].astype(f32), people[1].astype(f32))
    for value, ref in ((target_rows, target_out), (mask_rows, mask_out)):
        for part in range(2):
            for group in range(16):
                span = slice(group * lines, (group + 1) * lines)
                block = value[span, 128 * part : 128 * part + 128]
                if ref is mask_out:
                    block = block / share[:, :128]
                scratch[pl.ds(group, lines, stride=16), :] = block
            ref[:, 128 * part : 128 * part + 128] = scratch[...]


def tile_kernel(rows, meta, *refs):
    xs, near, far, tiles, sides = split_refs(refs, 4, 1, 1, 4, 4)
    odd = meta[4] == 1
    for branch in range(4):
        count = rows[branch]
        tile = tiles[branch]
        for image in range(2):
            one, two = (ref[0][image, 2 * branch : 2 * branch + 2, :] for ref in (near, far))
            for value, first, extent in (
                (jnp.where(odd, one, two), 0, 2),
                (xs[branch][image], 2, count),
                (jnp.where(odd, two, one), count + 2, 2),
            ):
                tile[image, first * 16 : (first + extent) * 16, :] = value.reshape(extent * 16, 256)
        build_sides(tile, sides[branch], CHANNELS[branch])


def first_kernel(rows, packed, meta, *refs):
    tiles, sides, packs, mains, sums, taps, bands, scratch = split_refs(
        refs, 4, 4, 2 if packed else 4, 4, 1, 7 * packed, 4, 3 * packed
    )
    sums = sums[0]
    if packed:
        unpack_taps(meta[2], packs, taps, scratch)
    else:
        taps = packs
    for branch in range(4):
        count, band = rows[branch], bands[branch]
        build_band(band, tap_reader(taps[3 - branch], branch), branch, 0)
        out = dot_nn(patches(tiles[branch], sides[branch], count + 2), band[...])
        mains[branch][...] = out.reshape(2, (count + 2) * 16, 256)
        inner = load_rows(mains[branch], 1, count)
        sums[2 * branch : 2 * branch + 1, :] = column_sum(inner)
        sums[2 * branch + 1 : 2 * branch + 2, :] = column_sum(inner * inner)


def first_flip_kernel(rows, branch, meta, tile, side, taps, out, band):
    count = rows[branch]
    build_band(band, mirrored(tap_reader(taps, branch)), branch, 0)
    value = dot_nn(patches(tile, side, count + 2), band[...])
    out[...] = value.reshape(2, (count + 2) * 16, 256)


def fill_hidden(meta, firsts, stat, norms, hidden, branch, count, total):
    stats = moments(stat[2 * branch : 2 * branch + 2, :], CHANNELS[branch], total)
    scale, offset = affine(
        stats,
        norms[2 * branch : 2 * branch + 1, :],
        norms[11 + 2 * branch : 12 + 2 * branch, :],
    )
    value = load_rows(firsts[branch], 0, count + 2) * scale + offset
    value = mask_ends(silu(value), count, meta)
    hidden[branch][...] = value.reshape(2, (count + 2) * 16, 256)


def band_kernel(packed, meta, *refs):
    packs, taps, bands, scratch = split_refs(refs, 2 if packed else 4, 7 * packed, 4, 3 * packed)
    if packed:
        unpack_taps(meta[2], packs, taps, scratch)
    else:
        taps = packs
    for branch in range(4):
        build_band(bands[branch], tap_reader(taps[3 - branch], branch), branch, 0)


def turned_kernel(meta, *refs):
    taps, bands = split_refs(refs, 4, 4)
    for branch in range(4):
        build_band(bands[branch], turned(tap_reader(taps[3 - branch], branch)), branch, 0)


def second_kernel(rows, counts, meta, *refs):
    firsts, stat, norms, bands, outs, sums, hidden, sides = split_refs(refs, 4, 1, 1, 4, 4, 1, 4, 4)
    sums = sums[0]
    for branch in range(4):
        count, channels = rows[branch], CHANNELS[branch]
        fill_hidden(meta, firsts, stat[0], norms[0], hidden, branch, count, counts[branch])
        build_sides(hidden[branch], sides[branch], channels)
        out = dot_nn(patches(hidden[branch], sides[branch], count), bands[branch][...])
        outs[branch][...] = out
        sums[2 * branch : 2 * branch + 1, :] = column_sum(out)
        sums[2 * branch + 1 : 2 * branch + 2, :] = column_sum(out * out)


def second_flip_kernel(rows, counts, branch, meta, first, stat, norms, taps, out, hidden, band, side):
    count, channels = rows[branch], CHANNELS[branch]
    fill_hidden(meta, {branch: first}, stat, norms, {branch: hidden}, branch, count, counts[branch])
    build_sides(hidden, side, channels)
    build_band(band, mirrored(tap_reader(taps, branch)), branch, 0)
    out[...] = dot_nn(patches(hidden, side, count), band[...])


def joined(second, tile, stat, norms, branch, count, total):
    stats = moments(stat[2 * branch : 2 * branch + 2, :], CHANNELS[branch], total)
    gain = norms[2 * branch + 1 : 2 * branch + 2, :]
    shift = norms[12 + 2 * branch : 13 + 2 * branch, :]
    scaled = (second - stats[0]) * stats[1]
    return scaled * gain + shift + load_rows(tile, 2, count), scaled, stats


def third_kernel(rows, counts, *refs):
    seconds, tiles, stat, norms, unites, mixes, sums = split_refs(refs, 3, 3, 1, 1, 6, 3, 1)
    stat, norms, sums = stat[0], norms[0], sums[0]
    for level in range(3):
        branch = level + 1
        value, _, _ = joined(
            seconds[level][...], tiles[level], stat, norms, branch, rows[branch], counts[branch]
        )
        unite = jnp.concatenate([unites[level][...], unites[3 + level][...]], axis=0)
        mixed = dot_nn(silu(value), mix_matrix(unite, branch))
        mixes[level][...] = mixed
        sums[2 * level : 2 * level + 1, :] = column_sum(mixed)
        sums[2 * level + 1 : 2 * level + 2, :] = column_sum(mixed * mixed)
    sums[6:8, :] = jnp.zeros((2, 256), f32)


def spread_rows(value, rows, factor):
    value = value.reshape(2 * rows, 1, 16, 256)
    return jnp.broadcast_to(value, (2 * rows, factor, 16, 256)).reshape(2 * rows * factor * 16, 256)


def gather_rows(value, rows, factor):
    value = value.reshape(2 * rows // factor, factor, 16, 256)
    return jnp.sum(value, axis=1).reshape(2 * rows // factor * 16, 256)


def uniting_stats(stat, level, total):
    return moments(stat[2 * level : 2 * level + 2, :], C0, total * 2.0 ** (level + 1))


def united_sum(base, mixes, stat, norms, rows, counts):
    for level in range(3):
        stats = uniting_stats(stat, level, counts[level + 1])
        scale, offset = affine(
            stats, norms[8 + level : 9 + level, :], norms[19 + level : 20 + level, :]
        )
        base = base + spread_rows(mixes[level] * scale + offset, rows[level + 1], 2 ** (level + 1))
    return base


def head_matrix(weight):
    wide = jnp.concatenate([weight] * 8, axis=1)
    lane = lax.broadcasted_iota(jnp.int32, wide.shape, 1)
    return jnp.concatenate([jnp.where(lane // C0 == place, wide, 0.0) for place in range(8)], axis=0)


def loss_kernel(rows, counts, denominator, *refs):
    ins, outs = split_refs(refs, 12, 9)
    second, tile, stat, mix_one, mix_two, mix_three, mix_stat, norms, weight, bias, targets, mask = ins
    heat_out, sum_one, sum_two, sum_three, sums, join_grad, zero_sums, united_out, grad_out = outs
    count = rows[0]
    join, scaled, _ = joined(second[...], tile, stat, norms, 0, count, counts[0])
    mixes = (mix_one[...], mix_two[...], mix_three[...])
    pre = united_sum(silu(join), mixes, mix_stat, norms, rows, counts)
    united = silu(pre)
    head = head_matrix(weight[...])
    heat = dot_nn(united, head) + bias[...]
    heat_out[...] = heat
    error = heat - targets[...]
    weighted = mask[...] * error
    sums[6:7, :] = column_sum(weighted * error) / denominator
    heat_grad = weighted * (2.0 / denominator)
    sums[7:8, :] = column_sum(heat_grad)
    united_out[...] = united
    grad_out[...] = heat_grad
    grad = dot_nt(heat_grad, head) * silu_slope(pre)
    join_part = grad * silu_slope(join)
    join_grad[...] = join_part
    zero_sums[0:1, :] = column_sum(join_part)
    zero_sums[1:2, :] = column_sum(join_part * scaled)
    for level, out in enumerate((sum_one, sum_two, sum_three)):
        part = gather_rows(grad, count, 2 ** (level + 1))
        out[...] = part
        stats = uniting_stats(mix_stat, level, counts[level + 1])
        normed = (mixes[level] - stats[0]) * stats[1]
        sums[2 * level : 2 * level + 1, :] = column_sum(part)
        sums[2 * level + 1 : 2 * level + 2, :] = column_sum(part * normed)


def head_kernel(meta, united, heat_grad, out):
    product = dot_tn(united[...], heat_grad[...])
    total = None
    for place in range(8):
        first = place * C0
        tile_first = first // 128 * 128
        block = product[first : first + C0, tile_first : tile_first + 128]
        if first - tile_first:
            block = pltpu.roll(block, 128 - (first - tile_first), 1)
        total = block if total is None else total + block
    out[...] = jnp.zeros(out.shape, f32)
    out[:, 0:128] = jnp.concatenate(
        [total[8 * part : 8 * part + 8, :C0] for part in range(4)], axis=1
    )


def flip_kernel(rows, counts, *refs):
    seconds, tiles, stat, unites, mix_stat, norms, weight, bias, heat, out, scratch = split_refs(
        refs, 4, 4, 1, 6, 1, 1, 1, 1, 1, 1, 2
    )
    stat, norms = stat[0], norms[0]
    mixes = []
    for branch in range(4):
        value, _, _ = joined(
            seconds[branch][...], tiles[branch], stat, norms, branch, rows[branch], counts[branch]
        )
        if branch == 0:
            base = silu(value)
        else:
            unite = jnp.concatenate([unites[branch - 1][...], unites[branch + 2][...]], axis=0)
            mixes.append(dot_nn(silu(value), mix_matrix(unite, branch)))
    pre = united_sum(base, mixes, mix_stat[0], norms, rows, counts)
    back = dot_nn(silu(pre), head_matrix(weight[0][...])) + bias[0][...]
    moved = dot_nt(0.5 * (heat[0][...] + back), joint_matrix())
    scratch[0][...] = moved[:, :128]
    scratch[1][...] = moved[:, 128:]
    lines = 2 * rows[0]
    parts = [scratch[0][pl.ds(group, lines, stride=16), :] for group in range(16)]
    lane = lax.broadcasted_iota(jnp.int32, (lines, 128), 1)
    last = None
    for group in range(16):
        tail = scratch[1][pl.ds(group, lines, stride=16), :]
        tail = pltpu.roll(tail, 8 * group, 1) if group else tail
        last = tail if last is None else jnp.where(lane // 8 == group, tail, last)
    for joint, value in enumerate([*swap_blocks(parts), last]):
        out[0][:, joint] = value.reshape(2, rows[0], 128)


def edge_place(branch, image):
    return (2 * branch + image) * 16


def write_edges(odd, near, far, value, branch, count, base):
    for image in range(2):
        place = base + edge_place(branch, image)
        start = image * count * 16
        first = value[start : start + 16]
        last = value[start + (count - 1) * 16 : start + count * 16]
        near[place : place + 16, :] = jnp.where(odd, first, last)
        far[place : place + 16, :] = jnp.where(odd, last, first)


def join_kernel(rows, counts, meta, *refs):
    sums_in, mixes, seconds, tiles, join_zero, small, unites, outs = split_refs(
        refs, 3, 3, 4, 3, 1, 6, 6, 9
    )
    zero_sums, head_grad, stat, mix_stat, head_sums, norms = small
    grads, mixed_grads, sums, near, far = outs[0:3], outs[3:6], outs[6], outs[7], outs[8]
    odd = meta[4] == 1
    sums[0:2, :] = zero_sums[0:2, :]
    sums[8:16, :] = head_grad[...]
    write_edges(odd, near, far, join_zero[0][...], 0, rows[0], 0)
    write_edges(odd, near, far, seconds[0][...], 0, rows[0], 128)
    for level in range(3):
        branch = level + 1
        channels, count = CHANNELS[branch], rows[branch]
        total = counts[branch]
        stats = uniting_stats(mix_stat, level, total)
        gain = norms[8 + level : 9 + level, :]
        shift_sum = fold(head_sums[2 * level : 2 * level + 1, :], C0)
        gain_sum = fold(head_sums[2 * level + 1 : 2 * level + 2, :], C0)
        normed = (mixes[level][...] - stats[0]) * stats[1]
        share = 1.0 / (total * 2.0 ** (level + 1))
        mixed_grad = (gain * stats[1]) * (
            sums_in[level][...] - shift_sum * share - normed * (gain_sum * share)
        )
        mixed_grads[level][...] = mixed_grad
        value, scaled, _ = joined(
            seconds[branch][...], tiles[level], stat, norms, branch, count, total
        )
        unite = jnp.concatenate([unites[level][...], unites[3 + level][...]], axis=0)
        grad = dot_nt(mixed_grad, mix_matrix(unite, branch)) * silu_slope(value)
        grads[level][...] = grad
        sums[2 * branch : 2 * branch + 1, :] = column_sum(grad)
        sums[2 * branch + 1 : 2 * branch + 2, :] = column_sum(grad * scaled)
        write_edges(odd, near, far, grad, branch, count, 0)
        write_edges(odd, near, far, seconds[branch][...], branch, count, 128)


def mixer_kernel(rows, counts, meta, *refs):
    mixed_grads, seconds, tiles, stat, norms, outs = split_refs(refs, 3, 3, 3, 1, 1, 6)
    for level in range(3):
        branch = level + 1
        channels = CHANNELS[branch]
        value, _, _ = joined(
            seconds[level][...], tiles[level], stat[0], norms[0], branch, rows[branch], counts[branch]
        )
        product = dot_tn(silu(value), mixed_grads[level][...])
        mixer = None
        for place in range(8):
            row = place // (8 * channels // 256) * channels
            tile_first = place * C0 // 128 * 128
            block = product[row : row + channels, tile_first : tile_first + 128]
            inner = place * C0 - tile_first
            if inner:
                block = pltpu.roll(block, 128 - inner, 1)
            mixer = block if mixer is None else mixer + block
        outs[level][...] = mixer[: channels // 2, :C0]
        outs[3 + level][...] = mixer[channels // 2 :, :C0]


def norm_input_grad(grad, scaled, stats, gain, sums, channels, total):
    shift_sum = fold(sums[0:1, :], channels) / total
    gain_sum = fold(sums[1:2, :], channels) / total
    return (gain * stats[1]) * (grad - shift_sum - scaled * gain_sum)


def back_second_kernel(rows, counts, flags, *refs):
    ins, outs, wide, sides = split_refs(refs, 22, 7, 4, 4)
    grads, seconds, firsts, bands = ins[0:4], ins[4:8], ins[8:12], ins[12:16]
    near_in, far_in, stat, stat_sums, first_stat, norms = ins[16:22]
    normed_grads = outs[0:4]
    sums, near, far = outs[4:7]
    odd = flags[4] == 1
    for branch in range(4):
        count, channels, total = rows[branch], CHANNELS[branch], counts[branch]
        stats = moments(stat[2 * branch : 2 * branch + 2, :], channels, total)
        gain = norms[2 * branch + 1 : 2 * branch + 2, :]
        shift_sum = fold(stat_sums[2 * branch : 2 * branch + 1, :], channels) / total
        gain_sum = fold(stat_sums[2 * branch + 1 : 2 * branch + 2, :], channels) / total

        def input_grad(grad, value):
            scaled = (value - stats[0]) * stats[1]
            return (gain * stats[1]) * (grad - shift_sum - scaled * gain_sum)

        inner = input_grad(grads[branch][...], seconds[branch][...])
        wide[branch][:, 16 : (count + 1) * 16, :] = inner.reshape(2, count * 16, 256)
        for image in range(2):
            place = edge_place(branch, image)
            parts = [
                input_grad(ref[place : place + 16, :], ref[128 + place : 144 + place, :])
                for ref in (near_in, far_in)
            ]
            for value, start, flag in (
                (jnp.where(odd, parts[0], parts[1]), 0, flags[0]),
                (jnp.where(odd, parts[1], parts[0]), (count + 1) * 16, flags[1]),
            ):
                wide[branch][image, start : start + 16, :] = jnp.where(flag == 0, 0.0, value)
        build_sides(wide[branch], sides[branch], channels)
        hidden_grad = dot_nn(patches(wide[branch], sides[branch], count), bands[branch][...])
        first_stats = moments(first_stat[2 * branch : 2 * branch + 2, :], channels, total)
        scaled = (load_rows(firsts[branch], 1, count) - first_stats[0]) * first_stats[1]
        value = (
            scaled * norms[2 * branch : 2 * branch + 1, :]
            + norms[11 + 2 * branch : 12 + 2 * branch, :]
        )
        grad = hidden_grad * silu_slope(value)
        normed_grads[branch][...] = grad
        sums[2 * branch : 2 * branch + 1, :] = column_sum(grad)
        sums[2 * branch + 1 : 2 * branch + 2, :] = column_sum(grad * scaled)
        write_edges(odd, near, far, grad, branch, count, 0)


def cross_products(rows, branch, offset, source, value, out, side, product):
    count, channels = rows[branch], CHANNELS[branch]
    product[...] = dot_tn(patches(source, side, count, offset), value)

    def emit(tap_row, tap_col, block):
        place = (3 * tap_row + tap_col) * channels
        out[place : place + channels, :] = block

    collect_band(product, branch, emit)


def normalized(raw, stat, rows, counts, branch, inner):
    stats = moments(stat[2 * branch : 2 * branch + 2, :], CHANNELS[branch], counts[branch])
    value = raw[...] if inner else load_rows(raw, 1, rows[branch])
    return (value - stats[0]) * stats[1]


def sum_means(sums, branch, total):
    channels = CHANNELS[branch]
    return [fold(sums[2 * branch + i : 2 * branch + i + 1, :], channels) / total for i in range(2)]


def cross_kernel(rows, counts, devices, branch, offset, inner, meta, *refs):
    source, side, value, raw, stat, sums, out, product = refs
    shift_mean, gain_mean = sum_means(sums, branch, counts[branch] / devices)
    scaled = normalized(raw, stat, rows, counts, branch, inner)
    rest = value[...] - shift_mean - scaled * gain_mean
    cross_products(rows, branch, offset, source, rest, out, side, product)


def cross_norm_kernel(rows, counts, branch, offset, inner, meta, *refs):
    source, side, raw, stat, out, sums, product = refs
    count, channels = rows[branch], CHANNELS[branch]
    scaled = normalized(raw, stat, rows, counts, branch, inner)
    cross_products(rows, branch, offset, source, scaled, out, side, product)
    total = column_sum(patches(source, side, count, offset))
    column = jnp.transpose(jnp.broadcast_to(total, (8, total.shape[1])))
    for tap_row in range(3):
        for tap_col in range(3):
            block = None
            for place in range(256 // channels):
                row = band_row(branch, tap_row, place + tap_col - 1)
                part = column[row : row + channels]
                block = part if block is None else block + part
            start = (3 * tap_row + tap_col) * channels
            sums[start : start + channels, :] = block


def combine_kernel(counts, devices, packed, which, meta, *refs):
    crosses, norm_crosses, patch_sums, ins, unite_grads, outs, stage, scratch = split_refs(
        refs, 4, 4, 4, 4, 3, 2 if packed else 4, 5, 3
    )
    stat, own_sums, grad_sums, norms = ins
    for branch in range(4):
        channels, total = CHANNELS[branch], counts[branch]
        stats = moments(stat[2 * branch : 2 * branch + 2, :], channels, total)
        line = 2 * branch + which
        scale = (norms[line : line + 1, :] * stats[1])[:, :channels]
        shift_rest, gain_rest = (
            (whole - own)[:, :channels]
            for whole, own in zip(
                sum_means(grad_sums, branch, total), sum_means(own_sums, branch, total / devices)
            )
        )
        emit = tap_writer(stage[3 - branch], branch)
        for place in range(9):
            span = slice(place * channels, (place + 1) * channels)
            value = (
                crosses[branch][span, :]
                - patch_sums[branch][span, 0:1] * shift_rest
                - norm_crosses[branch][span, :] * gain_rest
            )
            emit(place // 3, place % 3, scale * value)
    if packed:
        pack_grads(meta[2], stage, unite_grads, outs, scratch)
    else:
        for ref, value in zip(outs, stage):
            ref[...] = value[...]


def back_first_kernel(rows, counts, flags, *refs):
    ins, source_grads, wide, sides, bands = split_refs(refs, 21, 4, 4, 4, 4)
    normed_grads, firsts, join_grads, taps = ins[0:4], ins[4:8], ins[8:12], ins[12:16]
    near, far, first_stat, first_sums, norms = ins[16:21]
    odd = flags[4] == 1
    for branch in range(4):
        count, channels, total = rows[branch], CHANNELS[branch], counts[branch]
        stats = moments(first_stat[2 * branch : 2 * branch + 2, :], channels, total)
        gain = norms[2 * branch : 2 * branch + 1, :]
        shift_sum = fold(first_sums[2 * branch : 2 * branch + 1, :], channels) / total
        gain_sum = fold(first_sums[2 * branch + 1 : 2 * branch + 2, :], channels) / total

        def input_grad(grad, value):
            scaled = (value - stats[0]) * stats[1]
            return (gain * stats[1]) * (grad - shift_sum - scaled * gain_sum)

        inner = input_grad(normed_grads[branch][...], load_rows(firsts[branch], 1, count))
        wide[branch][:, 16 : (count + 1) * 16, :] = inner.reshape(2, count * 16, 256)
        for image in range(2):
            place = edge_place(branch, image)
            one, two = (ref[place : place + 16, :] for ref in (near, far))
            for grad, start, flag in (
                (jnp.where(odd, one, two), 0, flags[0]),
                (jnp.where(odd, two, one), (count + 1) * 16, flags[1]),
            ):
                value = input_grad(grad, firsts[branch][image, start : start + 16, :])
                wide[branch][image, start : start + 16, :] = jnp.where(flag == 0, 0.0, value)
        build_sides(wide[branch], sides[branch], channels)
        build_band(bands[branch], turned(tap_reader(taps[3 - branch], branch)), branch, 0)
        grad = dot_nn(patches(wide[branch], sides[branch], count), bands[branch][...])
        grad = (grad + join_grads[branch][...]).reshape(2, count * 16, 256)
        for image in range(2):
            source_grads[branch][image] = grad[image].reshape(count, 4096)


def finish_kernel(first_sums, second_sums, head_sums, gain, shift, loss, head_weight, head_bias):
    offset = 0

    def put(sums, line, channels):
        nonlocal offset
        for ref, row in ((shift, line), (gain, line + 1)):
            value = fold(sums[row : row + 1, :], channels)
            done = 0
            while done < channels:
                place = offset + done
                width = min(channels - done, 128 - place % 128)
                ref[place // 128 : place // 128 + 1, place % 128 : place % 128 + width] = value[
                    :, done : done + width
                ]
                done += width
        offset += channels

    for branch in range(4):
        for sums in (first_sums, second_sums):
            put(sums, 2 * branch, CHANNELS[branch])
    for level in range(3):
        put(head_sums, 2 * level, C0)
    loss[...] = jnp.sum(head_sums[6:7, :], axis=1, keepdims=True)
    joints = head_bias.shape[1]
    head_bias[...] = fold(head_sums[7:8, :], C0)[:, :joints]
    total = jnp.concatenate(
        [second_sums[8:16, C0 * part : C0 * part + C0] for part in range(4)], axis=0
    )
    head_weight[...] = jnp.transpose(total)[:joints]


def device_count():
    return lax.axis_size("dp") * lax.axis_size("space")


def exchange(value, bit):
    return lax.ppermute(value, AXES, [(i, i ^ bit) for i in range(device_count())])


def total_sum(value, beside=(), order=None):
    value = value.value
    for step, bit in enumerate(order or [1 << i for i in range(device_count().bit_length() - 1)]):
        other = exchange(value, bit)
        if step < len(beside) and beside[step]:
            other = after(other, *beside[step](value))
        value = value + other
    return Kept(value)


def swap_rows(near, far):
    devices = lax.axis_size("space")
    pairs = [(i, i ^ 1) for i in range(devices)]
    others = [(i, i + 1) for i in range(1, devices - 1, 2)]
    others += [(j, i) for i, j in others]
    return lax.ppermute(near, "space", pairs), lax.ppermute(far, "space", others)


def swap_near(near, far):
    pairs = [(i, i ^ 1) for i in range(lax.axis_size("space"))]
    return lax.ppermute(near, "space", pairs), lax.ppermute(far, "space", pairs)


def pass_on(relay):
    devices = lax.axis_size("space")
    return lax.ppermute(relay, "space", [(i, (i + 2 - i % 2 * 4) % devices) for i in range(devices)])


def device_index():
    return lax.axis_index("dp") * lax.axis_size("space") + lax.axis_index("space")


def after(value, *others):
    return lax.optimization_barrier((value, *others))[0]


def swap(parts, step):
    return [Kept(exchange(part.value, STEPS[chunk][step])) for chunk, part in enumerate(parts)]


def gather_shards(meta, flat, beside):
    other = exchange(flat, 16)
    other = after(other, *beside[0](flat))
    shapes = [(1, 2, last - first, 128) for first, last in CHUNKS]
    parts = call(split_shard, [meta, flat, Kept(other)], kept(shapes), smem=1)
    shapes = [(2, *shape[1:]) for shape in shapes]
    received = swap(parts, 0)
    received[0] = Kept(after(received[0].value, *beside[1](parts[0].value)))
    parts = call(join_chunks, [*parts, *received], kept(shapes))
    shapes = [(4, *shape[2:]) for shape in shapes]
    received = swap(parts, 1)
    received[0] = Kept(after(received[0].value, *beside[2](parts[0].value)))
    parts = call(join_apart, [*parts, *received], kept(shapes * 2))
    first, second = parts[:3], parts[3:]
    received = swap(first, 2)
    received[0] = Kept(after(received[0].value, *beside[3](first[0].value)))
    (whole,) = call(join_whole, [*first, *received], kept([(8, SHARD, 128)]))
    second[0] = Kept(after(second[0].value, whole.value))
    received = swap(second, 2)

    def rest(start):
        received[0] = Kept(after(received[0].value, start))
        (whole,) = call(join_whole, [*second, *received], kept([(8, SHARD, 128)]))
        return [whole, Kept(exchange(whole.value, 1))]

    return [whole, Kept(exchange(whole.value, 1))], rest


def scatter_step(parts, step, beside, meta=None):
    received = swap(parts[3:], step)
    received[0] = Kept(after(received[0].value, *beside(parts[3].value)))
    if step == 2:
        return call(add_last, [meta, *parts[:3], *received], kept([(SHARD, 128)] * 2), smem=1)
    shapes = [(2 - step, 2, last - first, 128) for first, last in CHUNKS]
    return call(add_received, [*parts[:3], *received], kept(shapes * 2))


def body(
    branch_zero,
    branch_one,
    branch_two,
    branch_three,
    convs_zero,
    convs_one,
    convs_two,
    convs_three,
    unite_one,
    unite_two,
    unite_three,
    norm_gain,
    norm_shift,
    head_weight,
    head_bias,
    targets,
    crowd_mask,
    person_count,
    flip_order,
):
    inputs = (branch_zero, branch_one, branch_two, branch_three)
    devices = device_count()
    spaces = lax.axis_size("space")
    place = lax.axis_index("space")
    rows = tuple(value.shape[1] for value in inputs)
    counts = tuple(
        float(2 * rows[b] * 16 * (256 // CHANNELS[b]) * devices) for b in range(4)
    )
    joints = head_bias.shape[0]
    cells = [2 * rows[b] * 16 for b in range(4)]
    packed = devices == 32
    shards_in = (convs_three, convs_two, convs_one, convs_zero, unite_one, unite_two, unite_three)
    sizes = [part.shape[0] for part in shards_in]

    meta = jnp.stack(
        [
            place > 0,
            place < spaces - 1,
            device_index() & 15,
            (device_index() & 16) // 16,
            place % 2,
        ]
    ).astype(jnp.int32)

    bands = [band_shape(b, 256) for b in range(4)]
    inner = [(cells[b], 256) for b in range(4)]
    wide = [(2, (rows[b] + 2) * 16, 256) for b in range(4)]
    wider = [(2, (rows[b] + 4) * 16, 256) for b in range(4)]

    def sides_of(shapes):
        return [shape[:2] + (SIDES[b],) for b, shape in enumerate(shapes)]

    def works(*parts):
        return lambda start: sum((list(part(start)) for part in parts), [])

    state = {}

    def prepare(start):
        parts = lax.optimization_barrier((*inputs, start))[:4]
        last_rows = jnp.concatenate([value[:, -2:] for value in parts], axis=1)
        first_rows = jnp.concatenate([value[:, :2] for value in parts], axis=1)
        odd = place % 2 == 1
        state["halo"] = swap_rows(
            jnp.where(odd, first_rows, last_rows), jnp.where(odd, last_rows, first_rows)
        )
        return state["halo"]

    def prepare_targets(start):
        state["targets"] = call(
            target_kernel,
            [after(person_count, start), targets, crowd_mask],
            kept([(cells[0], 256)] * 2),
            [(cells[0], 128)],
            smem=1,
            cost=4,
        )
        return [state["targets"][0].value]

    def make_tiles(start):
        state["tiles"] = call(
            functools.partial(tile_kernel, rows),
            [after(meta, start), *inputs, *state["halo"]],
            kept([*wider, *sides_of(wider)]),
            smem=1,
        )
        return [state["tiles"][0].value]

    def parameters(start):
        state["small"] = call(
            parameter_kernel,
            [
                after(norm_gain, start)[None],
                norm_shift[None],
                jnp.transpose(head_weight),
                head_bias[None],
                flip_order[None],
            ],
            kept([(22, 256), (C0, C0), (1, 256), (C0, C0), (1, 256)]),
        )
        return [state["small"][0].value]

    if packed:
        gap = jnp.zeros(((24 - ROWS_ONE) * 128,), f32)
        flat = jnp.concatenate([*shards_in[:3], gap, *shards_in[3:]]).reshape(SHARD, 128)
        first_packs, rest = gather_shards(meta, flat, (works(prepare, prepare_targets), parameters, make_tiles, lambda start: []))
    else:
        for work in (prepare, parameters, make_tiles, prepare_targets):
            work(meta)
        whole = [lax.all_gather(part, AXES, axis=0, tiled=True) for part in shards_in]
        whole = [
            part.reshape(-1, width)
            for part, width in zip(whole, (128, 128, 64, 32, 32, 32, 32))
        ]
        first_packs = [part[: part.shape[0] // 2] for part in whole]
        second_packs = [part[part.shape[0] // 2 :] for part in whole]
    target_cells, loss_weight = state["targets"]
    tiles, tile_sides = state["tiles"][:4], state["tiles"][4:]
    norms, weight, bias, flip_weight, flip_bias = state["small"]

    eight = (8, 256)
    taps_out = kept(TAPS_OUT) if packed else []
    unpack_scratch = list(PACK_SCRATCH) if packed else []

    out = call(
        functools.partial(first_kernel, rows, packed),
        [meta, *tiles, *tile_sides, *first_packs[:4]],
        kept([*wide, eight]) + taps_out,
        bands + unpack_scratch,
        smem=1,
    )
    firsts = out[0:4]
    first_taps = out[5:] if packed else first_packs
    if packed:
        second_packs = rest(firsts[0].value)

    crosses = [[None] * 4, [None] * 4]
    norm_crosses = [[None] * 4, [None] * 4]
    natural = [(9 * CHANNELS[b], CHANNELS[b]) for b in range(4)]

    def cross(which, branch):
        def work(start):
            values = (
                (
                    tiles[branch],
                    tile_sides[branch],
                    normed_grads[branch],
                    firsts[branch],
                    first_stat,
                    own_first,
                )
                if which == 0
                else (
                    hidden[branch],
                    hidden_sides[branch],
                    join_grads[branch],
                    seconds[branch],
                    second_stat,
                    own_second,
                )
            )
            (crosses[which][branch],) = call(
                functools.partial(cross_kernel, rows, counts, devices, branch, 1 - which, which),
                [after(meta, start), *values],
                kept([natural[branch]]),
                [bands[branch]],
                smem=1,
            )
            return [crosses[which][branch].value]

        return work

    def norm_cross(which, branch):
        def work(start):
            values = (
                (tiles[branch], tile_sides[branch], firsts[branch], first_stat)
                if which == 0
                else (hidden[branch], hidden_sides[branch], seconds[branch], second_stat)
            )
            norm_crosses[which][branch] = call(
                functools.partial(cross_norm_kernel, rows, counts, branch, 1 - which, which),
                [after(meta, start), *values],
                kept([natural[branch], (9 * CHANNELS[branch], 8)]),
                [bands[branch]],
                smem=1,
            )
            return [norm_crosses[which][branch][0].value]

        return work

    def combine(which, sums, mixers, start):
        return call(
            functools.partial(combine_kernel, counts, devices, packed, which),
            [
                after(meta, start),
                *crosses[which],
                *[part[0] for part in norm_crosses[which]],
                *[part[1] for part in norm_crosses[which]],
                (first_stat, second_stat)[which],
                (own_first, own_second)[which],
                sums,
                norms,
                *mixers,
            ],
            kept([(8, SHARD, 128)] * 2) if packed else list(TAPS_OUT[:4]),
            [*STAGE, *PACK_SCRATCH],
            smem=1,
        )

    flip_firsts, flip_seconds = [None] * 4, [None] * 4

    def flip_first(branch):
        def work(start):
            (flip_firsts[branch],) = call(
                functools.partial(first_flip_kernel, rows, branch),
                [after(meta, start), tiles[branch], tile_sides[branch], first_taps[3 - branch]],
                kept([wide[branch]]),
                [bands[branch]],
                smem=1,
            )
            return [flip_firsts[branch].value]

        return work

    def second_bands(start):
        state["second"] = call(
            functools.partial(band_kernel, packed),
            [after(meta, start), *second_packs[:4]],
            taps_out + kept(bands),
            unpack_scratch,
            smem=1,
        )
        return [state["second"][-1].value]

    order = [1 << i for i in range(devices.bit_length() - 1)]
    first_stat = total_sum(
        out[4],
        [flip_first(1), None, second_bands],
        [*order[1:], 1] if packed else None,
    )
    second_taps = state["second"][:7] if packed else second_packs

    out = call(
        functools.partial(second_kernel, rows, counts),
        [meta, *firsts, first_stat, norms, *state["second"][-4:]],
        kept([*inner, eight, *wide, *sides_of(wide)]),
        smem=1,
    )
    seconds, hidden, hidden_sides = out[0:4], out[5:9], out[9:13]
    unites = [*first_taps[4:7], *second_taps[4:7]]
    first_taps, second_taps = first_taps[:4], second_taps[:4]

    def flip_second(branch):
        def work(start):
            (flip_seconds[branch],) = call(
                functools.partial(second_flip_kernel, rows, counts, branch),
                [
                    after(meta, start),
                    flip_firsts[branch],
                    first_stat,
                    norms,
                    second_taps[3 - branch],
                ],
                kept([inner[branch]]),
                [wide[branch], bands[branch], sides_of(wide)[branch]],
                smem=1,
            )
            return [flip_seconds[branch].value]

        return work

    second_stat = total_sum(
        out[4],
        [
            None,
            norm_cross(0, 0),
            norm_cross(0, 1),
            norm_cross(0, 2),
            norm_cross(0, 3),
        ],
    )

    out = call(
        functools.partial(third_kernel, rows, counts),
        [*seconds[1:], *tiles[1:], second_stat, norms, *unites],
        kept([*inner[1:], eight]),
    )
    mixes = out[0:3]
    mix_stat = total_sum(
        out[3],
        [
            None,
            norm_cross(1, 0),
            norm_cross(1, 1),
            norm_cross(1, 2),
            norm_cross(1, 3),
        ],
    )

    denominator = float(counts[0] * joints)
    out = call(
        functools.partial(loss_kernel, rows, counts, denominator),
        [
            seconds[0],
            tiles[0],
            second_stat,
            *mixes,
            mix_stat,
            norms,
            weight,
            bias,
            target_cells,
            loss_weight,
        ],
        kept([inner[0], *inner[1:], eight, inner[0], eight, inner[0], inner[0]]),
    )
    heat, pre_sums, join_zero, zero_sums, united, heat_grad = out[0], out[1:4], *out[5:9]

    def head_grads(start):
        (state["head"],) = call(
            head_kernel, [after(meta, start), united, heat_grad], kept([eight]), smem=1
        )
        return [state["head"].value]

    def turned_bands(start):
        state["turned"] = call(
            turned_kernel, [after(meta, start), *second_taps], kept(bands), smem=1, cost=2
        )
        return [state["turned"][0].value]

    head_sums = total_sum(
        out[4],
        [
            None,
            works(head_grads, turned_bands),
            flip_first(0),
            flip_second(1),
        ],
    )

    out = call(
        functools.partial(join_kernel, rows, counts),
        [
            meta,
            *pre_sums,
            *mixes,
            *seconds,
            *tiles[1:],
            join_zero,
            zero_sums,
            state["head"],
            second_stat,
            mix_stat,
            head_sums,
            norms,
            *unites,
        ],
        kept([*inner[1:], *inner[1:], (16, 256), (256, 256), (256, 256)]),
        smem=1,
    )
    join_grads = [join_zero, *out[0:3]]
    mixed_grads, edges = out[3:6], out[7:9]

    def mixers(start):
        state["mixers"] = call(
            functools.partial(mixer_kernel, rows, counts),
            [after(meta, start), *mixed_grads, *seconds[1:], *tiles[1:], second_stat, norms],
            kept([(CHANNELS[b] // 2, C0) for b in range(1, 4)] * 2),
            smem=1,
        )
        return [state["mixers"][0].value]

    def edge_near(start):
        near, far = lax.optimization_barrier((edges[0].value, edges[1].value, start))[:2]
        state["edges"] = swap_near(near, far)
        return [state["edges"][1]]

    def edge_far(start):
        near, relay = state["edges"]
        state["edges"] = kept([near, pass_on(after(relay, start))])
        return []

    def edge_done(start):
        return [part.value for part in state["edges"]]

    own_second = out[6]
    second_sums = total_sum(
        own_second,
        [
            None,
            works(edge_near, cross(1, 0)),
            works(edge_far, cross(1, 2), cross(1, 3)),
            cross(1, 1),
            works(edge_done, mixers),
        ],
    )
    first_mixers, second_mixers = state["mixers"][:3], state["mixers"][3:]

    out = call(
        functools.partial(back_second_kernel, rows, counts),
        [
            meta,
            *join_grads,
            *seconds,
            *firsts,
            *state["turned"],
            *state["edges"],
            second_stat,
            second_sums,
            first_stat,
            norms,
        ],
        kept([*inner, eight, (128, 256), (128, 256)]),
        wide + sides_of(wide),
        smem=1,
    )
    normed_grads, edges = out[0:4], out[5:7]

    def second_packs_work(start):
        state["packs"] = combine(1, second_sums, second_mixers, start)
        return [state["packs"][0].value] if packed else [state["packs"][0]]

    def swap_second(start):
        state["far"] = exchange(after(state["packs"][1].value, start), 1)
        return [state["far"]]

    own_first = out[4]
    first_sums = total_sum(
        own_first,
        [
            None,
            second_packs_work,
            cross(0, 0),
            cross(0, 1),
            works(*[swap_second] * packed, cross(0, 2), cross(0, 3)),
        ],
    )
    if packed:
        far_second = state["far"]
        first_kernels = combine(0, first_sums, first_mixers, first_sums.value)
    else:
        second_kernels = state["packs"]
        first_kernels = combine(0, first_sums, first_mixers, first_sums.value)
        for work in (edge_near, edge_far):
            work(first_sums.value)

    def back_first(start):
        state["source"] = call(
            functools.partial(back_first_kernel, rows, counts),
            [
                after(meta, start),
                *normed_grads,
                *firsts,
                *join_grads,
                *first_taps,
                *state["edges"],
                first_stat,
                first_sums,
                norms,
            ],
            [value.shape for value in inputs],
            wide + sides_of(wide) + bands,
            smem=1,
        )
        return [state["source"][0]]

    def flip_last(start):
        (state["heat"],) = call(
            functools.partial(flip_kernel, rows, counts),
            [
                *flip_seconds,
                *tiles,
                second_stat,
                *unites,
                mix_stat,
                norms,
                flip_weight,
                Kept(after(flip_bias.value, start)),
                heat,
            ],
            [targets.shape],
            [(cells[0], 128)] * 2,
        )
        return [state["heat"]]

    def finish(start):
        state["finish"] = call(
            finish_kernel,
            [Kept(after(first_sums.value, start)), second_sums, head_sums],
            [(9, 128), (9, 128), (1, 1), (joints, C0), (1, joints)],
            limit=4,
        )
        return [state["finish"][0]]

    if packed:
        far_first = exchange(first_kernels[1].value, 1)
        far_first = after(far_first, *edge_near(first_kernels[1].value))
        shapes = [(4, 2, last - first, 128) for first, last in CHUNKS]
        parts = call(
            add_cores,
            [first_kernels[0], state["packs"][0], Kept(far_first), Kept(far_second)],
            kept(shapes * 2),
        )
        first_flips = works(flip_first(2), flip_first(3), flip_second(0), flip_second(2))
        parts = scatter_step(parts, 0, works(edge_far, first_flips))
        parts = scatter_step(parts, 1, works(edge_done, flip_second(3), flip_last))
        keep, send = scatter_step(parts, 2, finish, meta)
        far = Kept(after(exchange(send.value, 16), *back_first(send.value)))
        out = call(
            add_shard,
            [keep, far],
            [(ROWS_THREE, 128), (ROWS_TWO, 128), (ROWS_ONE, 128), (5, 128), (1, 64), (1, 128), (2, 128)],
        )
        shards = [part.reshape(-1)[:size] for part, size in zip(out, sizes)]
    else:
        rest_first = [flip_first(branch) for branch in (2, 3)]
        rest_second = [flip_second(branch) for branch in (0, 2, 3)]
        for work in (back_first, *rest_first, *rest_second, flip_last, finish):
            work(first_sums.value)
        first_mixers, second_mixers = (
            [part.value for part in parts] for parts in (first_mixers, second_mixers)
        )
        flat = [
            jnp.concatenate([one.reshape(-1), two.reshape(-1)])
            for one, two in zip([*first_kernels, *first_mixers], [*second_kernels, *second_mixers])
        ]
        shards = [lax.psum_scatter(part, AXES, scatter_dimension=0, tiled=True) for part in flat]

    gain_grad, shift_grad, loss, head_grad, bias_grad = state["finish"]
    return (
        loss[0, 0],
        state["heat"],
        *state["source"],
        shards[3],
        shards[2],
        shards[1],
        shards[0],
        *shards[4:7],
        gain_grad.reshape(-1)[: norm_gain.shape[0]],
        shift_grad.reshape(-1)[: norm_shift.shape[0]],
        jnp.transpose(head_grad),
        bias_grad[0],
    )


def solution(mesh):
    rows = P("dp", "space", None)
    shard = P(("dp", "space"))
    heat = P("dp", None, "space", None)
    return jax.shard_map(
        body,
        mesh=mesh,
        in_specs=(*[rows] * 4, *[shard] * 7, *[P()] * 4, heat, rows, P("dp"), P()),
        out_specs=(P(), heat, *[rows] * 4, *[shard] * 7, *[P()] * 4),
        check_vma=False,
    )
```

```python
import functools

import jax
import jax.numpy as jnp
import numpy as np
from jax import lax
from jax.experimental import pallas as pl
from jax.experimental.pallas import tpu as pltpu
from jax.sharding import PartitionSpec as P

C0 = 32
CHANNELS = (32, 64, 128, 256)
SIDES = (128, 128, 256, 512)
AXES = ("dp", "space")
epsilon = 1e-05
f32 = jnp.float32
high = lax.Precision.HIGH


def dot_nn(left, right):
    return lax.dot_general(left, right, (((1,), (0,)), ((), ())), precision=high, preferred_element_type=f32)


def dot_nt(left, right):
    return lax.dot_general(left, right, (((1,), (1,)), ((), ())), precision=high, preferred_element_type=f32)


def dot_tn(left, right):
    return lax.dot_general(left, right, (((0,), (0,)), ((), ())), precision=high, preferred_element_type=f32)


def sigmoid(value):
    return 1.0 / (1.0 + jnp.exp(-value))


def silu(value):
    return value * sigmoid(value)


def silu_slope(value):
    sigma = sigmoid(value)
    return sigma * (1.0 + value * (1.0 - sigma))


def fold(row, channels):
    step = channels
    while step < 256:
        row = row + pltpu.roll(row, step, 1)
        step = 2 * step
    return row


def column_sum(value):
    return jnp.sum(value, axis=0, keepdims=True)


def moments(sums, channels, count):
    mean = fold(sums[0:1], channels) / count
    square = fold(sums[1:2], channels) / count
    return mean, lax.rsqrt(square - mean * mean + epsilon)


def affine(stats, gain, shift):
    scale = stats[1] * gain
    return scale, shift - stats[0] * scale


def load_rows(ref, first, count):
    lanes = ref.shape[2]
    return ref[:, first * 16 : (first + count) * 16, :].reshape(2 * count * 16, lanes)


def group_index(rows):
    return lax.broadcasted_iota(jnp.int32, (rows, 128), 0) % 16


def side_columns(value, channels):
    rows = value.shape[0]
    group = group_index(rows)
    lane = lax.broadcasted_iota(jnp.int32, (rows, 128), 1)

    def before(part):
        return jnp.where(group == 0, 0.0, pltpu.roll(part, 1, 0))

    def after(part):
        return jnp.where(group == 15, 0.0, pltpu.roll(part, rows - 1, 0))

    low, upper = value[:, :128], value[:, 128:]
    if channels == 256:
        return jnp.concatenate([before(low), before(upper), after(low), after(upper)], axis=1)
    if channels == 128:
        return jnp.concatenate([before(upper), after(low)], axis=1)
    return jnp.where(
        lane < channels, after(low), jnp.where(lane >= 128 - channels, before(upper), 0.0)
    )


def build_sides(source, side, channels):
    rows = source.shape[1]
    for image in range(2):
        side[image] = side_columns(source[image], channels)


def patches(source, side, count, offset=0):
    parts = []
    for tap_row in range(3):
        parts.append(load_rows(source, tap_row + offset, count))
        parts.append(load_rows(side, tap_row + offset, count))
    return jnp.concatenate(parts, axis=1)


def band_row(branch, tap_row, place):
    channels, side = CHANNELS[branch], SIDES[branch]
    base = tap_row * (256 + side)
    if place < 0:
        return base + 256 + (0 if channels >= 128 else 128 - channels)
    if place >= 256 // channels:
        return base + 256 + (side // 2 if channels >= 128 else 0)
    return base + place * channels


def build_band(band, tap, branch, offset):
    channels = CHANNELS[branch]
    groups = 256 // channels
    side = SIDES[branch]
    height = 256 + side
    if channels < 256:
        band[:, offset : offset + 256] = jnp.zeros((3 * height, 256), f32)
    for tap_row in range(3):
        for tap_col in range(3):
            matrix = tap(tap_row, tap_col)
            for out in range(groups):
                row = band_row(branch, tap_row, out + tap_col - 1)
                start = offset + out * channels
                band[row : row + channels, start : start + channels] = matrix


def collect_band(product, branch, emit):
    channels = CHANNELS[branch]
    for tap_row in range(3):
        for tap_col in range(3):
            total = None
            for out in range(256 // channels):
                row = band_row(branch, tap_row, out + tap_col - 1)
                start = out * channels
                if channels >= 128:
                    block = product[row : row + channels, start : start + channels]
                else:
                    tile = start // 128 * 128
                    block = product[row : row + channels, tile : tile + 128]
                    inner = start - tile
                    if inner:
                        block = pltpu.roll(block, 128 - inner, 1)
                total = block if total is None else total + block
            emit(tap_row, tap_col, total[:, :channels])


def tap_reader(ref, branch):
    channels = CHANNELS[branch]
    if channels == 256:

        def tap(tap_row, tap_col):
            first = (3 * tap_row + tap_col) * 512
            return jnp.concatenate(
                [ref[pl.ds(first, 256, stride=2), :], ref[pl.ds(first + 1, 256, stride=2), :]],
                axis=1,
            )

        return tap

    def tap(tap_row, tap_col):
        first = (3 * tap_row + tap_col) * channels
        return ref[first : first + channels, :]

    return tap


def tap_writer(ref, branch):
    channels = CHANNELS[branch]

    def emit(tap_row, tap_col, value):
        place = 3 * tap_row + tap_col
        if channels == 256:
            ref[pl.ds(place * 512, 256, stride=2), :] = value[:, :128]
            ref[pl.ds(place * 512 + 1, 256, stride=2), :] = value[:, 128:]
        else:
            ref[place * channels : (place + 1) * channels, :] = value

    return emit


SHARD = 392
ROWS_THREE, ROWS_TWO, ROWS_ONE = 288, 72, 18
PER_ZERO, PER_UNITE = 18, (2, 4, 8)
CHUNKS = ((0, 152), (152, 272), (272, 392))
STEPS = ((8, 4, 2), (4, 2, 8), (2, 8, 4))
TAPS_OUT = ((4608, 128), (1152, 128), (576, 64), (288, 32), (32, 32), (64, 32), (128, 32))
PACK_SCRATCH = ((16, 24, 128), (16, 8, 128), (288, 128))
STAGE = ((4608, 128), (1152, 128), (576, 64), (288, 32), (512, 32))


def partner(me, core, place, bits):
    return me ^ (core + sum(bit for i, bit in enumerate(bits) if place >> i & 1))


def shard_parts(device, three, two, one, zero):
    start = device * ROWS_THREE
    return (
        ((0, 152, three.at[pl.ds(pl.multiple_of(start, 8), 152), :]),),
        ((152, 272, three.at[pl.ds(pl.multiple_of(start + 152, 8), 120), :]),),
        (
            (272, 288, three.at[pl.ds(pl.multiple_of(start + 272, 8), 16), :]),
            (288, 360, two.at[pl.ds(pl.multiple_of(device * ROWS_TWO, 8), ROWS_TWO), :]),
            (360, 384, one.at[device]),
            (384, 392, zero.at[device]),
        ),
    )


def unpack_taps(me, packs, taps, scratch):
    three, two, one, zero = taps[:4]
    part_one, part_zero, flat_one = scratch
    for core in range(2):
        for place in range(8):
            for chunk in range(3):
                device = partner(me, core, place, STEPS[chunk])
                parts = shard_parts(device, three, two, part_one, part_zero)[chunk]
                for first, last, ref in parts:
                    ref[...] = packs[core][place, first:last]
    for device in range(16):
        flat_one[device * ROWS_ONE : (device + 1) * ROWS_ONE, :] = part_one[device, 0:ROWS_ONE]
    one[...] = flat_one[...].reshape(one.shape)
    narrow = part_zero[...].reshape(128, 128).reshape(512, 32)
    for device in range(16):
        first = device * 32
        for ref, height in zip(taps[3:7], (PER_ZERO, *PER_UNITE)):
            ref[device * height : (device + 1) * height, :] = narrow[first : first + height]
            first += height


def pack_grads(me, stage, unite_grads, packs, scratch):
    three, two, one, zero, narrow = stage
    part_one, part_zero, flat_one = scratch
    flat_one[...] = one[...].reshape(flat_one.shape)
    for device in range(16):
        part_one[device, 0:ROWS_ONE] = flat_one[device * ROWS_ONE : (device + 1) * ROWS_ONE, :]
        part_one[device, ROWS_ONE:24] = jnp.zeros((24 - ROWS_ONE, 128), f32)
        first = device * 32
        for ref, height in zip((zero, *unite_grads), (PER_ZERO, *PER_UNITE)):
            narrow[first : first + height, :] = ref[device * height : (device + 1) * height, :]
            first += height
    part_zero[...] = narrow[...].reshape(128, 128).reshape(16, 8, 128)
    for core in range(2):
        for place in range(8):
            for chunk in range(3):
                device = partner(me, core, place, STEPS[chunk][::-1])
                parts = shard_parts(device, three, two, part_one, part_zero)[chunk]
                for first, last, ref in parts:
                    packs[core][place, first:last] = ref[...]


def split_shard(meta, shard, other, *outs):
    second = meta[3] == 1
    for out, (first, last) in zip(outs, CHUNKS):
        own, far = shard[first:last], other[first:last]
        out[0, 0] = jnp.where(second, far, own)
        out[0, 1] = jnp.where(second, own, far)


def join_chunks(*refs):
    held, received, outs = split_refs(refs, 3, 3, 3)
    for chunk in range(3):
        count = held[chunk].shape[0]
        outs[chunk][0:count] = held[chunk][...]
        outs[chunk][count : 2 * count] = received[chunk][...]


def join_apart(*refs):
    held, received, first, second = split_refs(refs, 3, 3, 3, 3)
    for chunk in range(3):
        count = held[chunk].shape[0]
        for half, outs in ((0, first), (1, second)):
            outs[chunk][0:count] = held[chunk][:, half]
            outs[chunk][count : 2 * count] = received[chunk][:, half]


def join_whole(*refs):
    held, received, out = split_refs(refs, 3, 3, 1)
    for chunk, (first, last) in enumerate(CHUNKS):
        count = held[chunk].shape[0]
        out[0][0:count, first:last] = held[chunk][...]
        out[0][count : 2 * count, first:last] = received[chunk][...]


def add_received(*refs):
    held, received, low, high = split_refs(refs, 3, 3, 3, 3)
    for chunk in range(3):
        half = held[chunk].shape[0] // 2
        low[chunk][...] = held[chunk][0:half] + received[chunk][0:half]
        high[chunk][...] = held[chunk][half:] + received[chunk][half:]


def add_cores(*refs):
    keeps, received, low, high = split_refs(refs, 2, 2, 3, 3)
    for chunk, (first, last) in enumerate(CHUNKS):
        for half in range(2):
            low[chunk][:, half] = keeps[half][0:4, first:last] + received[half][0:4, first:last]
            high[chunk][:, half] = keeps[half][4:8, first:last] + received[half][4:8, first:last]


def add_last(meta, *refs):
    held, received, keep, send = split_refs(refs, 3, 3, 1, 1)
    second = meta[3] == 1
    for chunk, (first, last) in enumerate(CHUNKS):
        total = held[chunk][0] + received[chunk][0]
        keep[0][first:last, :] = jnp.where(second, total[1], total[0])
        send[0][first:last, :] = jnp.where(second, total[0], total[1])


def add_shard(keep, received, *outs):
    value = keep[...] + received[...]
    first = 0
    for ref in outs[:3]:
        last = first + ref.shape[0]
        ref[...] = value[first:last]
        first = last
    tail = SHARD - 8
    outs[3][...] = value[tail : tail + 5]
    outs[4][...] = value[tail + 4 : tail + 5, 64:]
    outs[5][...] = value[tail + 5 : tail + 6]
    outs[6][...] = value[tail + 6 : tail + 8]


def mirrored(tap):
    return lambda tap_row, tap_col: tap(tap_row, 2 - tap_col)


def turned(tap):
    return lambda tap_row, tap_col: jnp.transpose(tap(2 - tap_row, 2 - tap_col))


def mask_ends(value, rows, flags):
    place = lax.broadcasted_iota(jnp.int32, value.shape, 0) // 16 % (rows + 2)
    outside = ((place == 0) & (flags[0] == 0)) | ((place == rows + 1) & (flags[1] == 0))
    return jnp.where(outside, 0.0, value)


def mix_matrix(unite, branch):
    channels = CHANNELS[branch]
    groups = 256 // channels
    wide = jnp.concatenate([unite] * 8, axis=1)
    lane = lax.broadcasted_iota(jnp.int32, wide.shape, 1)
    span = 256 // groups
    return jnp.concatenate(
        [jnp.where(lane // span == place, wide, 0.0) for place in range(groups)], axis=0
    )


def split_refs(refs, *counts):
    out, first = [], 0
    for count in counts:
        out.append(refs[first : first + count])
        first += count
    assert first == len(refs)
    return out


class Kept:
    def __init__(self, value):
        self.value = value


def kept(values):
    return [Kept(value) for value in values]


def call(kernel, ins, outs, scratch=(), smem=0, limit=16, cost=0.01):
    specs = [pl.BlockSpec(memory_space=pltpu.SMEM)] * smem + [
        pl.BlockSpec(memory_space=pltpu.VMEM)
    ] * (len(ins) - smem)
    ins = ins[:smem] + [
        pltpu.with_memory_space_constraint(x.value, pltpu.VMEM)
        if isinstance(x, Kept)
        else pltpu.with_memory_space_constraint(x, pltpu.HBM)
        for x in ins[smem:]
    ]
    shapes = [pltpu.VMEM(x.value, f32) if isinstance(x, Kept) else pltpu.HBM(x, f32) for x in outs]
    results = pl.pallas_call(
        kernel,
        in_specs=specs,
        out_specs=[pl.BlockSpec(memory_space=pltpu.VMEM)] * len(outs),
        out_shape=shapes,
        scratch_shapes=[pltpu.VMEM(shape, f32) for shape in scratch],
        compiler_params=pltpu.CompilerParams(vmem_limit_bytes=limit * 2**20),
        cost_estimate=pl.CostEstimate(
            flops=int(cost * 1.1e9), bytes_accessed=int(cost * 3.0e6), transcendentals=0
        ),
    )(*ins)
    return [Kept(y) if isinstance(x, Kept) else y for x, y in zip(outs, results)]


def band_shape(branch, width):
    return (3 * (256 + SIDES[branch]), width)


def swap_blocks(parts):
    rows = parts[0].shape[0]
    group = lax.broadcasted_iota(jnp.int32, (rows, 128), 1) // 8
    step = 1
    while step < 16:
        high = (group & step) != 0
        parts = [
            jnp.where(high, parts[i], pltpu.roll(parts[i - step], 128 - 8 * step, 1))
            if i & step
            else jnp.where(high, pltpu.roll(parts[i + step], 8 * step, 1), parts[i])
            for i in range(16)
        ]
        step = 2 * step
    return parts


def joint_matrix():
    source = lax.broadcasted_iota(jnp.int32, (256, 256), 0)
    lane = lax.broadcasted_iota(jnp.int32, (256, 256), 1)
    matches = (source // 8 == lane % C0) & (source % 8 == lane // C0) & (source < 136)
    return jnp.where(matches, 1.0, 0.0)


def shift_group(value, group):
    return pltpu.roll(value, 128 - 8 * group, 1) if group else value


def parameter_kernel(gain, shift, weight, bias, flip, *outs):
    norms, weight_out, bias_out, flip_weight, flip_bias = outs
    weight = jnp.transpose(weight[...])
    for base, ref in ((0, gain), (11, shift)):
        offset = 0
        line = base
        sizes = [channels for channels in CHANNELS for _ in range(2)] + [C0] * 3
        for channels in sizes:
            part = ref[0:1, offset : offset + channels]
            norms[line : line + 1, :] = jnp.concatenate([part] * (256 // channels), axis=1)
            offset += channels
            line += 1
    joints = weight.shape[1]
    source = lax.broadcasted_iota(jnp.int32, (joints, joints), 0)
    moved = jnp.where(source == flip[...], 1.0, 0.0)
    for matrix, row, matrix_out, row_out in (
        (weight, bias[...], weight_out, bias_out),
        (
            jnp.dot(weight, moved, precision=lax.Precision.HIGHEST),
            jnp.dot(bias[...], moved, precision=lax.Precision.HIGHEST),
            flip_weight,
            flip_bias,
        ),
    ):
        matrix_out[...] = jnp.zeros((C0, C0), f32)
        matrix_out[:, 0:joints] = matrix
        row_out[...] = jnp.zeros((1, 256), f32)
        for place in range(8):
            row_out[0:1, C0 * place : C0 * place + joints] = row


def target_kernel(people, targets, mask, target_out, mask_out, scratch):
    lines = 2 * targets.shape[2]
    parts = swap_blocks([targets[:, j].reshape(lines, 128) for j in range(16)])
    last = targets[:, 16].reshape(lines, 128)
    cells = mask[...].reshape(lines, 128).astype(f32)
    lane = lax.broadcasted_iota(jnp.int32, (lines, 128), 1)
    tails = [
        jnp.where(lane < 8, shift_group(last, group), pltpu.roll(shift_group(cells, group), 8, 1))
        for group in range(16)
    ]
    whole = jnp.concatenate(
        [jnp.concatenate([part, tail], axis=1) for part, tail in zip(parts, tails)], axis=0
    )
    source = lax.broadcasted_iota(jnp.int32, (256, 256), 0)
    target_lane = lax.broadcasted_iota(jnp.int32, (256, 256), 1)
    spread = jnp.where((source >= 136) & (source < 144) & (source - 136 == target_lane // C0), 1.0, 0.0)
    target_rows = dot_nn(whole, joint_matrix())
    mask_rows = dot_nn(whole, spread)
    first_image = lax.broadcasted_iota(jnp.int32, (lines, 256), 0) < lines // 2
    share = jnp.where(first_image, people[0].astype(f32), people[1].astype(f32))
    for value, ref in ((target_rows, target_out), (mask_rows, mask_out)):
        for part in range(2):
            for group in range(16):
                span = slice(group * lines, (group + 1) * lines)
                block = value[span, 128 * part : 128 * part + 128]
                if ref is mask_out:
                    block = block / share[:, :128]
                scratch[pl.ds(group, lines, stride=16), :] = block
            ref[:, 128 * part : 128 * part + 128] = scratch[...]


def tile_kernel(rows, meta, *refs):
    xs, near, far, tiles, sides = split_refs(refs, 4, 1, 1, 4, 4)
    odd = meta[4] == 1
    for branch in range(4):
        count = rows[branch]
        tile = tiles[branch]
        for image in range(2):
            one, two = (ref[0][image, 2 * branch : 2 * branch + 2, :] for ref in (near, far))
            for value, first, extent in (
                (jnp.where(odd, one, two), 0, 2),
                (xs[branch][image], 2, count),
                (jnp.where(odd, two, one), count + 2, 2),
            ):
                tile[image, first * 16 : (first + extent) * 16, :] = value.reshape(extent * 16, 256)
        build_sides(tile, sides[branch], CHANNELS[branch])


def first_kernel(rows, packed, meta, *refs):
    tiles, sides, packs, mains, sums, taps, bands, scratch = split_refs(
        refs, 4, 4, 2 if packed else 4, 4, 1, 7 * packed, 4, 3 * packed
    )
    sums = sums[0]
    if packed:
        unpack_taps(meta[2], packs, taps, scratch)
    else:
        taps = packs
    for branch in range(4):
        count, band = rows[branch], bands[branch]
        build_band(band, tap_reader(taps[3 - branch], branch), branch, 0)
        out = dot_nn(patches(tiles[branch], sides[branch], count + 2), band[...])
        mains[branch][...] = out.reshape(2, (count + 2) * 16, 256)
        inner = load_rows(mains[branch], 1, count)
        sums[2 * branch : 2 * branch + 1, :] = column_sum(inner)
        sums[2 * branch + 1 : 2 * branch + 2, :] = column_sum(inner * inner)


def first_flip_kernel(rows, branch, meta, tile, side, taps, out, band):
    count = rows[branch]
    build_band(band, mirrored(tap_reader(taps, branch)), branch, 0)
    value = dot_nn(patches(tile, side, count + 2), band[...])
    out[...] = value.reshape(2, (count + 2) * 16, 256)


def fill_hidden(meta, firsts, stat, norms, hidden, branch, count, total):
    stats = moments(stat[2 * branch : 2 * branch + 2, :], CHANNELS[branch], total)
    scale, offset = affine(
        stats,
        norms[2 * branch : 2 * branch + 1, :],
        norms[11 + 2 * branch : 12 + 2 * branch, :],
    )
    value = load_rows(firsts[branch], 0, count + 2) * scale + offset
    value = mask_ends(silu(value), count, meta)
    hidden[branch][...] = value.reshape(2, (count + 2) * 16, 256)


def band_kernel(packed, meta, *refs):
    packs, taps, bands, scratch = split_refs(refs, 2 if packed else 4, 7 * packed, 4, 3 * packed)
    if packed:
        unpack_taps(meta[2], packs, taps, scratch)
    else:
        taps = packs
    for branch in range(4):
        build_band(bands[branch], tap_reader(taps[3 - branch], branch), branch, 0)


def turned_kernel(meta, *refs):
    taps, bands = split_refs(refs, 4, 4)
    for branch in range(4):
        build_band(bands[branch], turned(tap_reader(taps[3 - branch], branch)), branch, 0)


def second_kernel(rows, counts, meta, *refs):
    firsts, stat, norms, bands, outs, sums, hidden, sides = split_refs(refs, 4, 1, 1, 4, 4, 1, 4, 4)
    sums = sums[0]
    for branch in range(4):
        count, channels = rows[branch], CHANNELS[branch]
        fill_hidden(meta, firsts, stat[0], norms[0], hidden, branch, count, counts[branch])
        build_sides(hidden[branch], sides[branch], channels)
        out = dot_nn(patches(hidden[branch], sides[branch], count), bands[branch][...])
        outs[branch][...] = out
        sums[2 * branch : 2 * branch + 1, :] = column_sum(out)
        sums[2 * branch + 1 : 2 * branch + 2, :] = column_sum(out * out)


def second_flip_kernel(rows, counts, branch, meta, first, stat, norms, taps, out, hidden, band, side):
    count, channels = rows[branch], CHANNELS[branch]
    fill_hidden(meta, {branch: first}, stat, norms, {branch: hidden}, branch, count, counts[branch])
    build_sides(hidden, side, channels)
    build_band(band, mirrored(tap_reader(taps, branch)), branch, 0)
    out[...] = dot_nn(patches(hidden, side, count), band[...])


def joined(second, tile, stat, norms, branch, count, total):
    stats = moments(stat[2 * branch : 2 * branch + 2, :], CHANNELS[branch], total)
    gain = norms[2 * branch + 1 : 2 * branch + 2, :]
    shift = norms[12 + 2 * branch : 13 + 2 * branch, :]
    scaled = (second - stats[0]) * stats[1]
    return scaled * gain + shift + load_rows(tile, 2, count), scaled, stats


def third_kernel(rows, counts, *refs):
    seconds, tiles, stat, norms, unites, mixes, sums = split_refs(refs, 3, 3, 1, 1, 6, 3, 1)
    stat, norms, sums = stat[0], norms[0], sums[0]
    for level in range(3):
        branch = level + 1
        value, _, _ = joined(
            seconds[level][...], tiles[level], stat, norms, branch, rows[branch], counts[branch]
        )
        unite = jnp.concatenate([unites[level][...], unites[3 + level][...]], axis=0)
        mixed = dot_nn(silu(value), mix_matrix(unite, branch))
        mixes[level][...] = mixed
        sums[2 * level : 2 * level + 1, :] = column_sum(mixed)
        sums[2 * level + 1 : 2 * level + 2, :] = column_sum(mixed * mixed)
    sums[6:8, :] = jnp.zeros((2, 256), f32)


def spread_rows(value, rows, factor):
    value = value.reshape(2 * rows, 1, 16, 256)
    return jnp.broadcast_to(value, (2 * rows, factor, 16, 256)).reshape(2 * rows * factor * 16, 256)


def gather_rows(value, rows, factor):
    value = value.reshape(2 * rows // factor, factor, 16, 256)
    return jnp.sum(value, axis=1).reshape(2 * rows // factor * 16, 256)


def uniting_stats(stat, level, total):
    return moments(stat[2 * level : 2 * level + 2, :], C0, total * 2.0 ** (level + 1))


def united_sum(base, mixes, stat, norms, rows, counts):
    for level in range(3):
        stats = uniting_stats(stat, level, counts[level + 1])
        scale, offset = affine(
            stats, norms[8 + level : 9 + level, :], norms[19 + level : 20 + level, :]
        )
        base = base + spread_rows(mixes[level] * scale + offset, rows[level + 1], 2 ** (level + 1))
    return base


def head_matrix(weight):
    wide = jnp.concatenate([weight] * 8, axis=1)
    lane = lax.broadcasted_iota(jnp.int32, wide.shape, 1)
    return jnp.concatenate([jnp.where(lane // C0 == place, wide, 0.0) for place in range(8)], axis=0)


def loss_kernel(rows, counts, denominator, *refs):
    ins, outs = split_refs(refs, 12, 9)
    second, tile, stat, mix_one, mix_two, mix_three, mix_stat, norms, weight, bias, targets, mask = ins
    heat_out, sum_one, sum_two, sum_three, sums, join_grad, zero_sums, united_out, grad_out = outs
    count = rows[0]
    join, scaled, _ = joined(second[...], tile, stat, norms, 0, count, counts[0])
    mixes = (mix_one[...], mix_two[...], mix_three[...])
    pre = united_sum(silu(join), mixes, mix_stat, norms, rows, counts)
    united = silu(pre)
    head = head_matrix(weight[...])
    heat = dot_nn(united, head) + bias[...]
    heat_out[...] = heat
    error = heat - targets[...]
    weighted = mask[...] * error
    sums[6:7, :] = column_sum(weighted * error) / denominator
    heat_grad = weighted * (2.0 / denominator)
    sums[7:8, :] = column_sum(heat_grad)
    united_out[...] = united
    grad_out[...] = heat_grad
    grad = dot_nt(heat_grad, head) * silu_slope(pre)
    join_part = grad * silu_slope(join)
    join_grad[...] = join_part
    zero_sums[0:1, :] = column_sum(join_part)
    zero_sums[1:2, :] = column_sum(join_part * scaled)
    for level, out in enumerate((sum_one, sum_two, sum_three)):
        part = gather_rows(grad, count, 2 ** (level + 1))
        out[...] = part
        stats = uniting_stats(mix_stat, level, counts[level + 1])
        normed = (mixes[level] - stats[0]) * stats[1]
        sums[2 * level : 2 * level + 1, :] = column_sum(part)
        sums[2 * level + 1 : 2 * level + 2, :] = column_sum(part * normed)


def head_kernel(meta, united, heat_grad, out):
    product = dot_tn(united[...], heat_grad[...])
    total = None
    for place in range(8):
        first = place * C0
        tile_first = first // 128 * 128
        block = product[first : first + C0, tile_first : tile_first + 128]
        if first - tile_first:
            block = pltpu.roll(block, 128 - (first - tile_first), 1)
        total = block if total is None else total + block
    out[...] = jnp.zeros(out.shape, f32)
    out[:, 0:128] = jnp.concatenate(
        [total[8 * part : 8 * part + 8, :C0] for part in range(4)], axis=1
    )


def flip_kernel(rows, counts, *refs):
    seconds, tiles, stat, unites, mix_stat, norms, weight, bias, heat, out, scratch = split_refs(
        refs, 4, 4, 1, 6, 1, 1, 1, 1, 1, 1, 2
    )
    stat, norms = stat[0], norms[0]
    mixes = []
    for branch in range(4):
        value, _, _ = joined(
            seconds[branch][...], tiles[branch], stat, norms, branch, rows[branch], counts[branch]
        )
        if branch == 0:
            base = silu(value)
        else:
            unite = jnp.concatenate([unites[branch - 1][...], unites[branch + 2][...]], axis=0)
            mixes.append(dot_nn(silu(value), mix_matrix(unite, branch)))
    pre = united_sum(base, mixes, mix_stat[0], norms, rows, counts)
    back = dot_nn(silu(pre), head_matrix(weight[0][...])) + bias[0][...]
    moved = dot_nt(0.5 * (heat[0][...] + back), joint_matrix())
    scratch[0][...] = moved[:, :128]
    scratch[1][...] = moved[:, 128:]
    lines = 2 * rows[0]
    parts = [scratch[0][pl.ds(group, lines, stride=16), :] for group in range(16)]
    lane = lax.broadcasted_iota(jnp.int32, (lines, 128), 1)
    last = None
    for group in range(16):
        tail = scratch[1][pl.ds(group, lines, stride=16), :]
        tail = pltpu.roll(tail, 8 * group, 1) if group else tail
        last = tail if last is None else jnp.where(lane // 8 == group, tail, last)
    for joint, value in enumerate([*swap_blocks(parts), last]):
        out[0][:, joint] = value.reshape(2, rows[0], 128)


def edge_place(branch, image):
    return (2 * branch + image) * 16


def write_edges(odd, near, far, value, branch, count, base):
    for image in range(2):
        place = base + edge_place(branch, image)
        start = image * count * 16
        first = value[start : start + 16]
        last = value[start + (count - 1) * 16 : start + count * 16]
        near[place : place + 16, :] = jnp.where(odd, first, last)
        far[place : place + 16, :] = jnp.where(odd, last, first)


def join_kernel(rows, counts, meta, *refs):
    sums_in, mixes, seconds, tiles, join_zero, small, unites, outs = split_refs(
        refs, 3, 3, 4, 3, 1, 6, 6, 9
    )
    zero_sums, head_grad, stat, mix_stat, head_sums, norms = small
    grads, mixed_grads, sums, near, far = outs[0:3], outs[3:6], outs[6], outs[7], outs[8]
    odd = meta[4] == 1
    sums[0:2, :] = zero_sums[0:2, :]
    sums[8:16, :] = head_grad[...]
    write_edges(odd, near, far, join_zero[0][...], 0, rows[0], 0)
    write_edges(odd, near, far, seconds[0][...], 0, rows[0], 128)
    for level in range(3):
        branch = level + 1
        channels, count = CHANNELS[branch], rows[branch]
        total = counts[branch]
        stats = uniting_stats(mix_stat, level, total)
        gain = norms[8 + level : 9 + level, :]
        shift_sum = fold(head_sums[2 * level : 2 * level + 1, :], C0)
        gain_sum = fold(head_sums[2 * level + 1 : 2 * level + 2, :], C0)
        normed = (mixes[level][...] - stats[0]) * stats[1]
        share = 1.0 / (total * 2.0 ** (level + 1))
        mixed_grad = (gain * stats[1]) * (
            sums_in[level][...] - shift_sum * share - normed * (gain_sum * share)
        )
        mixed_grads[level][...] = mixed_grad
        value, scaled, _ = joined(
            seconds[branch][...], tiles[level], stat, norms, branch, count, total
        )
        unite = jnp.concatenate([unites[level][...], unites[3 + level][...]], axis=0)
        grad = dot_nt(mixed_grad, mix_matrix(unite, branch)) * silu_slope(value)
        grads[level][...] = grad
        sums[2 * branch : 2 * branch + 1, :] = column_sum(grad)
        sums[2 * branch + 1 : 2 * branch + 2, :] = column_sum(grad * scaled)
        write_edges(odd, near, far, grad, branch, count, 0)
        write_edges(odd, near, far, seconds[branch][...], branch, count, 128)


def mixer_kernel(rows, counts, meta, *refs):
    mixed_grads, seconds, tiles, stat, norms, outs = split_refs(refs, 3, 3, 3, 1, 1, 6)
    for level in range(3):
        branch = level + 1
        channels = CHANNELS[branch]
        value, _, _ = joined(
            seconds[level][...], tiles[level], stat[0], norms[0], branch, rows[branch], counts[branch]
        )
        product = dot_tn(silu(value), mixed_grads[level][...])
        mixer = None
        for place in range(8):
            row = place // (8 * channels // 256) * channels
            tile_first = place * C0 // 128 * 128
            block = product[row : row + channels, tile_first : tile_first + 128]
            inner = place * C0 - tile_first
            if inner:
                block = pltpu.roll(block, 128 - inner, 1)
            mixer = block if mixer is None else mixer + block
        outs[level][...] = mixer[: channels // 2, :C0]
        outs[3 + level][...] = mixer[channels // 2 :, :C0]


def norm_input_grad(grad, scaled, stats, gain, sums, channels, total):
    shift_sum = fold(sums[0:1, :], channels) / total
    gain_sum = fold(sums[1:2, :], channels) / total
    return (gain * stats[1]) * (grad - shift_sum - scaled * gain_sum)


def back_second_kernel(rows, counts, flags, *refs):
    ins, outs, wide, sides = split_refs(refs, 22, 7, 4, 4)
    grads, seconds, firsts, bands = ins[0:4], ins[4:8], ins[8:12], ins[12:16]
    near_in, far_in, stat, stat_sums, first_stat, norms = ins[16:22]
    normed_grads = outs[0:4]
    sums, near, far = outs[4:7]
    odd = flags[4] == 1
    for branch in range(4):
        count, channels, total = rows[branch], CHANNELS[branch], counts[branch]
        stats = moments(stat[2 * branch : 2 * branch + 2, :], channels, total)
        gain = norms[2 * branch + 1 : 2 * branch + 2, :]
        shift_sum = fold(stat_sums[2 * branch : 2 * branch + 1, :], channels) / total
        gain_sum = fold(stat_sums[2 * branch + 1 : 2 * branch + 2, :], channels) / total

        def input_grad(grad, value):
            scaled = (value - stats[0]) * stats[1]
            return (gain * stats[1]) * (grad - shift_sum - scaled * gain_sum)

        inner = input_grad(grads[branch][...], seconds[branch][...])
        wide[branch][:, 16 : (count + 1) * 16, :] = inner.reshape(2, count * 16, 256)
        for image in range(2):
            place = edge_place(branch, image)
            parts = [
                input_grad(ref[place : place + 16, :], ref[128 + place : 144 + place, :])
                for ref in (near_in, far_in)
            ]
            for value, start, flag in (
                (jnp.where(odd, parts[0], parts[1]), 0, flags[0]),
                (jnp.where(odd, parts[1], parts[0]), (count + 1) * 16, flags[1]),
            ):
                wide[branch][image, start : start + 16, :] = jnp.where(flag == 0, 0.0, value)
        build_sides(wide[branch], sides[branch], channels)
        hidden_grad = dot_nn(patches(wide[branch], sides[branch], count), bands[branch][...])
        first_stats = moments(first_stat[2 * branch : 2 * branch + 2, :], channels, total)
        scaled = (load_rows(firsts[branch], 1, count) - first_stats[0]) * first_stats[1]
        value = (
            scaled * norms[2 * branch : 2 * branch + 1, :]
            + norms[11 + 2 * branch : 12 + 2 * branch, :]
        )
        grad = hidden_grad * silu_slope(value)
        normed_grads[branch][...] = grad
        sums[2 * branch : 2 * branch + 1, :] = column_sum(grad)
        sums[2 * branch + 1 : 2 * branch + 2, :] = column_sum(grad * scaled)
        write_edges(odd, near, far, grad, branch, count, 0)


def cross_products(rows, branch, offset, source, value, out, side, product):
    count, channels = rows[branch], CHANNELS[branch]
    product[...] = dot_tn(patches(source, side, count, offset), value)

    def emit(tap_row, tap_col, block):
        place = (3 * tap_row + tap_col) * channels
        out[place : place + channels, :] = block

    collect_band(product, branch, emit)


def normalized(raw, stat, rows, counts, branch, inner):
    stats = moments(stat[2 * branch : 2 * branch + 2, :], CHANNELS[branch], counts[branch])
    value = raw[...] if inner else load_rows(raw, 1, rows[branch])
    return (value - stats[0]) * stats[1]


def sum_means(sums, branch, total):
    channels = CHANNELS[branch]
    return [fold(sums[2 * branch + i : 2 * branch + i + 1, :], channels) / total for i in range(2)]


def cross_kernel(rows, counts, devices, branch, offset, inner, meta, *refs):
    source, side, value, raw, stat, sums, out, product = refs
    shift_mean, gain_mean = sum_means(sums, branch, counts[branch] / devices)
    scaled = normalized(raw, stat, rows, counts, branch, inner)
    rest = value[...] - shift_mean - scaled * gain_mean
    cross_products(rows, branch, offset, source, rest, out, side, product)


def cross_norm_kernel(rows, counts, branch, offset, inner, meta, *refs):
    source, side, raw, stat, out, sums, product = refs
    count, channels = rows[branch], CHANNELS[branch]
    scaled = normalized(raw, stat, rows, counts, branch, inner)
    cross_products(rows, branch, offset, source, scaled, out, side, product)
    total = column_sum(patches(source, side, count, offset))
    column = jnp.transpose(jnp.broadcast_to(total, (8, total.shape[1])))
    for tap_row in range(3):
        for tap_col in range(3):
            block = None
            for place in range(256 // channels):
                row = band_row(branch, tap_row, place + tap_col - 1)
                part = column[row : row + channels]
                block = part if block is None else block + part
            start = (3 * tap_row + tap_col) * channels
            sums[start : start + channels, :] = block


def combine_kernel(counts, devices, packed, which, meta, *refs):
    crosses, norm_crosses, patch_sums, ins, unite_grads, outs, stage, scratch = split_refs(
        refs, 4, 4, 4, 4, 3, 2 if packed else 4, 5, 3
    )
    stat, own_sums, grad_sums, norms = ins
    for branch in range(4):
        channels, total = CHANNELS[branch], counts[branch]
        stats = moments(stat[2 * branch : 2 * branch + 2, :], channels, total)
        line = 2 * branch + which
        scale = (norms[line : line + 1, :] * stats[1])[:, :channels]
        shift_rest, gain_rest = (
            (whole - own)[:, :channels]
            for whole, own in zip(
                sum_means(grad_sums, branch, total), sum_means(own_sums, branch, total / devices)
            )
        )
        emit = tap_writer(stage[3 - branch], branch)
        for place in range(9):
            span = slice(place * channels, (place + 1) * channels)
            value = (
                crosses[branch][span, :]
                - patch_sums[branch][span, 0:1] * shift_rest
                - norm_crosses[branch][span, :] * gain_rest
            )
            emit(place // 3, place % 3, scale * value)
    if packed:
        pack_grads(meta[2], stage, unite_grads, outs, scratch)
    else:
        for ref, value in zip(outs, stage):
            ref[...] = value[...]


def back_first_kernel(rows, counts, flags, *refs):
    ins, source_grads, wide, sides, bands = split_refs(refs, 21, 4, 4, 4, 4)
    normed_grads, firsts, join_grads, taps = ins[0:4], ins[4:8], ins[8:12], ins[12:16]
    near, far, first_stat, first_sums, norms = ins[16:21]
    odd = flags[4] == 1
    for branch in range(4):
        count, channels, total = rows[branch], CHANNELS[branch], counts[branch]
        stats = moments(first_stat[2 * branch : 2 * branch + 2, :], channels, total)
        gain = norms[2 * branch : 2 * branch + 1, :]
        shift_sum = fold(first_sums[2 * branch : 2 * branch + 1, :], channels) / total
        gain_sum = fold(first_sums[2 * branch + 1 : 2 * branch + 2, :], channels) / total

        def input_grad(grad, value):
            scaled = (value - stats[0]) * stats[1]
            return (gain * stats[1]) * (grad - shift_sum - scaled * gain_sum)

        inner = input_grad(normed_grads[branch][...], load_rows(firsts[branch], 1, count))
        wide[branch][:, 16 : (count + 1) * 16, :] = inner.reshape(2, count * 16, 256)
        for image in range(2):
            place = edge_place(branch, image)
            one, two = (ref[place : place + 16, :] for ref in (near, far))
            for grad, start, flag in (
                (jnp.where(odd, one, two), 0, flags[0]),
                (jnp.where(odd, two, one), (count + 1) * 16, flags[1]),
            ):
                value = input_grad(grad, firsts[branch][image, start : start + 16, :])
                wide[branch][image, start : start + 16, :] = jnp.where(flag == 0, 0.0, value)
        build_sides(wide[branch], sides[branch], channels)
        build_band(bands[branch], turned(tap_reader(taps[3 - branch], branch)), branch, 0)
        grad = dot_nn(patches(wide[branch], sides[branch], count), bands[branch][...])
        grad = (grad + join_grads[branch][...]).reshape(2, count * 16, 256)
        for image in range(2):
            source_grads[branch][image] = grad[image].reshape(count, 4096)


def finish_kernel(first_sums, second_sums, head_sums, gain, shift, loss, head_weight, head_bias):
    offset = 0

    def put(sums, line, channels):
        nonlocal offset
        for ref, row in ((shift, line), (gain, line + 1)):
            value = fold(sums[row : row + 1, :], channels)
            done = 0
            while done < channels:
                place = offset + done
                width = min(channels - done, 128 - place % 128)
                ref[place // 128 : place // 128 + 1, place % 128 : place % 128 + width] = value[
                    :, done : done + width
                ]
                done += width
        offset += channels

    for branch in range(4):
        for sums in (first_sums, second_sums):
            put(sums, 2 * branch, CHANNELS[branch])
    for level in range(3):
        put(head_sums, 2 * level, C0)
    loss[...] = jnp.sum(head_sums[6:7, :], axis=1, keepdims=True)
    joints = head_bias.shape[1]
    head_bias[...] = fold(head_sums[7:8, :], C0)[:, :joints]
    total = jnp.concatenate(
        [second_sums[8:16, C0 * part : C0 * part + C0] for part in range(4)], axis=0
    )
    head_weight[...] = jnp.transpose(total)[:joints]


def device_count():
    return lax.axis_size("dp") * lax.axis_size("space")


def exchange(value, bit):
    return lax.ppermute(value, AXES, [(i, i ^ bit) for i in range(device_count())])


def total_sum(value, beside=(), order=None):
    value = value.value
    for step, bit in enumerate(order or [1 << i for i in range(device_count().bit_length() - 1)]):
        other = exchange(value, bit)
        if step < len(beside) and beside[step]:
            other = after(other, *beside[step](value))
        value = value + other
    return Kept(value)


def swap_rows(near, far):
    devices = lax.axis_size("space")
    pairs = [(i, i ^ 1) for i in range(devices)]
    others = [(i, i + 1) for i in range(1, devices - 1, 2)]
    others += [(j, i) for i, j in others]
    return lax.ppermute(near, "space", pairs), lax.ppermute(far, "space", others)


def swap_near(near, far):
    pairs = [(i, i ^ 1) for i in range(lax.axis_size("space"))]
    return lax.ppermute(near, "space", pairs), lax.ppermute(far, "space", pairs)


def pass_on(relay):
    devices = lax.axis_size("space")
    return lax.ppermute(relay, "space", [(i, (i + 2 - i % 2 * 4) % devices) for i in range(devices)])


def device_index():
    return lax.axis_index("dp") * lax.axis_size("space") + lax.axis_index("space")


def after(value, *others):
    return lax.optimization_barrier((value, *others))[0]


def swap(parts, step):
    return [Kept(exchange(part.value, STEPS[chunk][step])) for chunk, part in enumerate(parts)]


def gather_shards(meta, flat, beside):
    other = exchange(flat, 16)
    other = after(other, *beside[0](flat))
    shapes = [(1, 2, last - first, 128) for first, last in CHUNKS]
    parts = call(split_shard, [meta, flat, Kept(other)], kept(shapes), smem=1)
    shapes = [(2, *shape[1:]) for shape in shapes]
    received = swap(parts, 0)
    received[0] = Kept(after(received[0].value, *beside[1](parts[0].value)))
    parts = call(join_chunks, [*parts, *received], kept(shapes))
    shapes = [(4, *shape[2:]) for shape in shapes]
    received = swap(parts, 1)
    received[0] = Kept(after(received[0].value, *beside[2](parts[0].value)))
    parts = call(join_apart, [*parts, *received], kept(shapes * 2))
    first, second = parts[:3], parts[3:]
    received = swap(first, 2)
    received[0] = Kept(after(received[0].value, *beside[3](first[0].value)))
    (whole,) = call(join_whole, [*first, *received], kept([(8, SHARD, 128)]))
    second[0] = Kept(after(second[0].value, whole.value))
    received = swap(second, 2)

    def rest(start):
        received[0] = Kept(after(received[0].value, start))
        (whole,) = call(join_whole, [*second, *received], kept([(8, SHARD, 128)]))
        return [whole, Kept(exchange(whole.value, 1))]

    return [whole, Kept(exchange(whole.value, 1))], rest


def scatter_step(parts, step, beside, meta=None):
    received = swap(parts[3:], step)
    received[0] = Kept(after(received[0].value, *beside(parts[3].value)))
    if step == 2:
        return call(add_last, [meta, *parts[:3], *received], kept([(SHARD, 128)] * 2), smem=1)
    shapes = [(2 - step, 2, last - first, 128) for first, last in CHUNKS]
    return call(add_received, [*parts[:3], *received], kept(shapes * 2))


def body(
    branch_zero,
    branch_one,
    branch_two,
    branch_three,
    convs_zero,
    convs_one,
    convs_two,
    convs_three,
    unite_one,
    unite_two,
    unite_three,
    norm_gain,
    norm_shift,
    head_weight,
    head_bias,
    targets,
    crowd_mask,
    person_count,
    flip_order,
):
    inputs = (branch_zero, branch_one, branch_two, branch_three)
    devices = device_count()
    spaces = lax.axis_size("space")
    place = lax.axis_index("space")
    rows = tuple(value.shape[1] for value in inputs)
    counts = tuple(
        float(2 * rows[b] * 16 * (256 // CHANNELS[b]) * devices) for b in range(4)
    )
    joints = head_bias.shape[0]
    cells = [2 * rows[b] * 16 for b in range(4)]
    packed = devices == 32
    shards_in = (convs_three, convs_two, convs_one, convs_zero, unite_one, unite_two, unite_three)
    sizes = [part.shape[0] for part in shards_in]

    meta = jnp.stack(
        [
            place > 0,
            place < spaces - 1,
            device_index() & 15,
            (device_index() & 16) // 16,
            place % 2,
        ]
    ).astype(jnp.int32)

    bands = [band_shape(b, 256) for b in range(4)]
    inner = [(cells[b], 256) for b in range(4)]
    wide = [(2, (rows[b] + 2) * 16, 256) for b in range(4)]
    wider = [(2, (rows[b] + 4) * 16, 256) for b in range(4)]

    def sides_of(shapes):
        return [shape[:2] + (SIDES[b],) for b, shape in enumerate(shapes)]

    def works(*parts):
        return lambda start: sum((list(part(start)) for part in parts), [])

    state = {}

    def prepare(start):
        parts = lax.optimization_barrier((*inputs, start))[:4]
        last_rows = jnp.concatenate([value[:, -2:] for value in parts], axis=1)
        first_rows = jnp.concatenate([value[:, :2] for value in parts], axis=1)
        odd = place % 2 == 1
        state["halo"] = swap_rows(
            jnp.where(odd, first_rows, last_rows), jnp.where(odd, last_rows, first_rows)
        )
        return state["halo"]

    def prepare_targets(start):
        state["targets"] = call(
            target_kernel,
            [after(person_count, start), targets, crowd_mask],
            kept([(cells[0], 256)] * 2),
            [(cells[0], 128)],
            smem=1,
            cost=4,
        )
        return [state["targets"][0].value]

    def make_tiles(start):
        state["tiles"] = call(
            functools.partial(tile_kernel, rows),
            [after(meta, start), *inputs, *state["halo"]],
            kept([*wider, *sides_of(wider)]),
            smem=1,
        )
        return [state["tiles"][0].value]

    def parameters(start):
        state["small"] = call(
            parameter_kernel,
            [
                after(norm_gain, start)[None],
                norm_shift[None],
                jnp.transpose(head_weight),
                head_bias[None],
                flip_order[None],
            ],
            kept([(22, 256), (C0, C0), (1, 256), (C0, C0), (1, 256)]),
        )
        return [state["small"][0].value]

    if packed:
        gap = jnp.zeros(((24 - ROWS_ONE) * 128,), f32)
        flat = jnp.concatenate([*shards_in[:3], gap, *shards_in[3:]]).reshape(SHARD, 128)
        first_packs, rest = gather_shards(meta, flat, (works(prepare, prepare_targets), parameters, make_tiles, lambda start: []))
    else:
        for work in (prepare, parameters, make_tiles, prepare_targets):
            work(meta)
        whole = [lax.all_gather(part, AXES, axis=0, tiled=True) for part in shards_in]
        whole = [
            part.reshape(-1, width)
            for part, width in zip(whole, (128, 128, 64, 32, 32, 32, 32))
        ]
        first_packs = [part[: part.shape[0] // 2] for part in whole]
        second_packs = [part[part.shape[0] // 2 :] for part in whole]
    target_cells, loss_weight = state["targets"]
    tiles, tile_sides = state["tiles"][:4], state["tiles"][4:]
    norms, weight, bias, flip_weight, flip_bias = state["small"]

    eight = (8, 256)
    taps_out = kept(TAPS_OUT) if packed else []
    unpack_scratch = list(PACK_SCRATCH) if packed else []

    out = call(
        functools.partial(first_kernel, rows, packed),
        [meta, *tiles, *tile_sides, *first_packs[:4]],
        kept([*wide, eight]) + taps_out,
        bands + unpack_scratch,
        smem=1,
    )
    firsts = out[0:4]
    first_taps = out[5:] if packed else first_packs
    if packed:
        second_packs = rest(firsts[0].value)

    crosses = [[None] * 4, [None] * 4]
    norm_crosses = [[None] * 4, [None] * 4]
    natural = [(9 * CHANNELS[b], CHANNELS[b]) for b in range(4)]

    def cross(which, branch):
        def work(start):
            values = (
                (
                    tiles[branch],
                    tile_sides[branch],
                    normed_grads[branch],
                    firsts[branch],
                    first_stat,
                    own_first,
                )
                if which == 0
                else (
                    hidden[branch],
                    hidden_sides[branch],
                    join_grads[branch],
                    seconds[branch],
                    second_stat,
                    own_second,
                )
            )
            (crosses[which][branch],) = call(
                functools.partial(cross_kernel, rows, counts, devices, branch, 1 - which, which),
                [after(meta, start), *values],
                kept([natural[branch]]),
                [bands[branch]],
                smem=1,
            )
            return [crosses[which][branch].value]

        return work

    def norm_cross(which, branch):
        def work(start):
            values = (
                (tiles[branch], tile_sides[branch], firsts[branch], first_stat)
                if which == 0
                else (hidden[branch], hidden_sides[branch], seconds[branch], second_stat)
            )
            norm_crosses[which][branch] = call(
                functools.partial(cross_norm_kernel, rows, counts, branch, 1 - which, which),
                [after(meta, start), *values],
                kept([natural[branch], (9 * CHANNELS[branch], 8)]),
                [bands[branch]],
                smem=1,
            )
            return [norm_crosses[which][branch][0].value]

        return work

    def combine(which, sums, mixers, start):
        return call(
            functools.partial(combine_kernel, counts, devices, packed, which),
            [
                after(meta, start),
                *crosses[which],
                *[part[0] for part in norm_crosses[which]],
                *[part[1] for part in norm_crosses[which]],
                (first_stat, second_stat)[which],
                (own_first, own_second)[which],
                sums,
                norms,
                *mixers,
            ],
            kept([(8, SHARD, 128)] * 2) if packed else list(TAPS_OUT[:4]),
            [*STAGE, *PACK_SCRATCH],
            smem=1,
        )

    flip_firsts, flip_seconds = [None] * 4, [None] * 4

    def flip_first(branch):
        def work(start):
            (flip_firsts[branch],) = call(
                functools.partial(first_flip_kernel, rows, branch),
                [after(meta, start), tiles[branch], tile_sides[branch], first_taps[3 - branch]],
                kept([wide[branch]]),
                [bands[branch]],
                smem=1,
            )
            return [flip_firsts[branch].value]

        return work

    def second_bands(start):
        state["second"] = call(
            functools.partial(band_kernel, packed),
            [after(meta, start), *second_packs[:4]],
            taps_out + kept(bands),
            unpack_scratch,
            smem=1,
        )
        return [state["second"][-1].value]

    order = [1 << i for i in range(devices.bit_length() - 1)]
    first_stat = total_sum(
        out[4],
        [flip_first(1), None, second_bands, flip_first(0)],
        [*order[1:], 1] if packed else None,
    )
    second_taps = state["second"][:7] if packed else second_packs

    out = call(
        functools.partial(second_kernel, rows, counts),
        [meta, *firsts, first_stat, norms, *state["second"][-4:]],
        kept([*inner, eight, *wide, *sides_of(wide)]),
        smem=1,
    )
    seconds, hidden, hidden_sides = out[0:4], out[5:9], out[9:13]
    unites = [*first_taps[4:7], *second_taps[4:7]]
    first_taps, second_taps = first_taps[:4], second_taps[:4]

    def flip_second(branch):
        def work(start):
            (flip_seconds[branch],) = call(
                functools.partial(second_flip_kernel, rows, counts, branch),
                [
                    after(meta, start),
                    flip_firsts[branch],
                    first_stat,
                    norms,
                    second_taps[3 - branch],
                ],
                kept([inner[branch]]),
                [wide[branch], bands[branch], sides_of(wide)[branch]],
                smem=1,
            )
            return [flip_seconds[branch].value]

        return work

    second_stat = total_sum(
        out[4],
        [
            None,
            norm_cross(0, 1),
            norm_cross(0, 2),
            norm_cross(0, 3),
            norm_cross(0, 0),
        ],
    )

    out = call(
        functools.partial(third_kernel, rows, counts),
        [*seconds[1:], *tiles[1:], second_stat, norms, *unites],
        kept([*inner[1:], eight]),
    )
    mixes = out[0:3]
    mix_stat = total_sum(
        out[3],
        [
            None,
            norm_cross(1, 1),
            norm_cross(1, 2),
            norm_cross(1, 3),
            norm_cross(1, 0),
        ],
    )

    denominator = float(counts[0] * joints)
    out = call(
        functools.partial(loss_kernel, rows, counts, denominator),
        [
            seconds[0],
            tiles[0],
            second_stat,
            *mixes,
            mix_stat,
            norms,
            weight,
            bias,
            target_cells,
            loss_weight,
        ],
        kept([inner[0], *inner[1:], eight, inner[0], eight, inner[0], inner[0]]),
    )
    heat, pre_sums, join_zero, zero_sums, united, heat_grad = out[0], out[1:4], *out[5:9]

    def head_grads(start):
        (state["head"],) = call(
            head_kernel, [after(meta, start), united, heat_grad], kept([eight]), smem=1
        )
        return [state["head"].value]

    def turned_bands(start):
        state["turned"] = call(
            turned_kernel, [after(meta, start), *second_taps], kept(bands), smem=1, cost=2
        )
        return [state["turned"][0].value]

    head_sums = total_sum(
        out[4],
        [
            None,
            turned_bands,
            head_grads,
            flip_second(1),
        ],
    )

    out = call(
        functools.partial(join_kernel, rows, counts),
        [
            meta,
            *pre_sums,
            *mixes,
            *seconds,
            *tiles[1:],
            join_zero,
            zero_sums,
            state["head"],
            second_stat,
            mix_stat,
            head_sums,
            norms,
            *unites,
        ],
        kept([*inner[1:], *inner[1:], (16, 256), (256, 256), (256, 256)]),
        smem=1,
    )
    join_grads = [join_zero, *out[0:3]]
    mixed_grads, edges = out[3:6], out[7:9]

    def mixers(start):
        state["mixers"] = call(
            functools.partial(mixer_kernel, rows, counts),
            [after(meta, start), *mixed_grads, *seconds[1:], *tiles[1:], second_stat, norms],
            kept([(CHANNELS[b] // 2, C0) for b in range(1, 4)] * 2),
            smem=1,
        )
        return [state["mixers"][0].value]

    def edge_near(start):
        near, far = lax.optimization_barrier((edges[0].value, edges[1].value, start))[:2]
        state["edges"] = swap_near(near, far)
        return [state["edges"][1]]

    def edge_far(start):
        near, relay = state["edges"]
        state["edges"] = kept([near, pass_on(after(relay, start))])
        return []

    def edge_done(start):
        return [part.value for part in state["edges"]]

    own_second = out[6]
    second_sums = total_sum(
        own_second,
        [
            None,
            works(edge_near, mixers, cross(1, 2)),
            works(edge_far, cross(1, 3)),
            cross(1, 1),
            works(edge_done, cross(1, 0)),
        ],
    )
    first_mixers, second_mixers = state["mixers"][:3], state["mixers"][3:]

    out = call(
        functools.partial(back_second_kernel, rows, counts),
        [
            meta,
            *join_grads,
            *seconds,
            *firsts,
            *state["turned"],
            *state["edges"],
            second_stat,
            second_sums,
            first_stat,
            norms,
        ],
        kept([*inner, eight, (128, 256), (128, 256)]),
        wide + sides_of(wide),
        smem=1,
    )
    normed_grads, edges = out[0:4], out[5:7]

    def second_packs_work(start):
        state["packs"] = combine(1, second_sums, second_mixers, start)
        return [state["packs"][0].value] if packed else [state["packs"][0]]

    def swap_second(start):
        state["far"] = exchange(after(state["packs"][1].value, start), 1)
        return [state["far"]]

    own_first = out[4]
    first_sums = total_sum(
        own_first,
        [
            None,
            second_packs_work,
            cross(0, 0),
            works(edge_near, cross(0, 1)),
            works(*[swap_second] * packed, cross(0, 2), cross(0, 3)),
        ],
    )
    if packed:
        far_second = state["far"]
        first_kernels = combine(0, first_sums, first_mixers, first_sums.value)
    else:
        second_kernels = state["packs"]
        first_kernels = combine(0, first_sums, first_mixers, first_sums.value)
        edge_far(first_sums.value)

    def back_first(start):
        state["source"] = call(
            functools.partial(back_first_kernel, rows, counts),
            [
                after(meta, start),
                *normed_grads,
                *firsts,
                *join_grads,
                *first_taps,
                *state["edges"],
                first_stat,
                first_sums,
                norms,
            ],
            [value.shape for value in inputs],
            wide + sides_of(wide) + bands,
            smem=1,
        )
        return [state["source"][0]]

    def flip_last(start):
        (state["heat"],) = call(
            functools.partial(flip_kernel, rows, counts),
            [
                *flip_seconds,
                *tiles,
                second_stat,
                *unites,
                mix_stat,
                norms,
                flip_weight,
                Kept(after(flip_bias.value, start)),
                heat,
            ],
            [targets.shape],
            [(cells[0], 128)] * 2,
        )
        return [state["heat"]]

    def finish(start):
        state["finish"] = call(
            finish_kernel,
            [Kept(after(first_sums.value, start)), second_sums, head_sums],
            [(9, 128), (9, 128), (1, 1), (joints, C0), (1, joints)],
            limit=4,
        )
        return [state["finish"][0]]

    if packed:
        far_first = exchange(first_kernels[1].value, 1)
        edge_far(first_kernels[1].value)
        shapes = [(4, 2, last - first, 128) for first, last in CHUNKS]
        parts = call(
            add_cores,
            [first_kernels[0], state["packs"][0], Kept(far_first), Kept(far_second)],
            kept(shapes * 2),
        )
        first_flips = works(flip_first(2), flip_first(3), flip_second(0), flip_second(2))
        parts = scatter_step(parts, 0, works(first_flips, edge_done))
        parts = scatter_step(parts, 1, works(flip_second(3), flip_last))
        keep, send = scatter_step(parts, 2, finish, meta)
        far = Kept(after(exchange(send.value, 16), *back_first(send.value)))
        out = call(
            add_shard,
            [keep, far],
            [(ROWS_THREE, 128), (ROWS_TWO, 128), (ROWS_ONE, 128), (5, 128), (1, 64), (1, 128), (2, 128)],
        )
        shards = [part.reshape(-1)[:size] for part, size in zip(out, sizes)]
    else:
        rest_first = [flip_first(branch) for branch in (2, 3)]
        rest_second = [flip_second(branch) for branch in (0, 2, 3)]
        for work in (back_first, *rest_first, *rest_second, flip_last, finish):
            work(first_sums.value)
        first_mixers, second_mixers = (
            [part.value for part in parts] for parts in (first_mixers, second_mixers)
        )
        flat = [
            jnp.concatenate([one.reshape(-1), two.reshape(-1)])
            for one, two in zip([*first_kernels, *first_mixers], [*second_kernels, *second_mixers])
        ]
        shards = [lax.psum_scatter(part, AXES, scatter_dimension=0, tiled=True) for part in flat]

    gain_grad, shift_grad, loss, head_grad, bias_grad = state["finish"]
    return (
        loss[0, 0],
        state["heat"],
        *state["source"],
        shards[3],
        shards[2],
        shards[1],
        shards[0],
        *shards[4:7],
        gain_grad.reshape(-1)[: norm_gain.shape[0]],
        shift_grad.reshape(-1)[: norm_shift.shape[0]],
        jnp.transpose(head_grad),
        bias_grad[0],
    )


def solution(mesh):
    rows = P("dp", "space", None)
    shard = P(("dp", "space"))
    heat = P("dp", None, "space", None)
    return jax.shard_map(
        body,
        mesh=mesh,
        in_specs=(*[rows] * 4, *[shard] * 7, *[P()] * 4, heat, rows, P("dp"), P()),
        out_specs=(P(), heat, *[rows] * 4, *[shard] * 7, *[P()] * 4),
        check_vma=False,
    )
```

```python
import functools

import jax
import jax.numpy as jnp
import numpy as np
from jax import lax
from jax.experimental import pallas as pl
from jax.experimental.pallas import tpu as pltpu
from jax.sharding import PartitionSpec as P

C0 = 32
CHANNELS = (32, 64, 128, 256)
SIDES = (256, 128, 256, 512)
AXES = ("dp", "space")
epsilon = 1e-05
f32 = jnp.float32
high = lax.Precision.HIGH


def dot_nn(left, right):
    return lax.dot_general(left, right, (((1,), (0,)), ((), ())), precision=high, preferred_element_type=f32)


def dot_nt(left, right):
    return lax.dot_general(left, right, (((1,), (1,)), ((), ())), precision=high, preferred_element_type=f32)


def dot_tn(left, right):
    return lax.dot_general(left, right, (((0,), (0,)), ((), ())), precision=high, preferred_element_type=f32)


def sigmoid(value):
    return 1.0 / (1.0 + jnp.exp(-value))


def silu(value):
    return value * sigmoid(value)


def silu_slope(value):
    sigma = sigmoid(value)
    return sigma * (1.0 + value * (1.0 - sigma))


def fold(row, channels):
    step = channels
    while step < 256:
        row = row + pltpu.roll(row, step, 1)
        step = 2 * step
    return row


def column_sum(value):
    return jnp.sum(value, axis=0, keepdims=True)


def moments(sums, channels, count):
    mean = fold(sums[0:1], channels) / count
    square = fold(sums[1:2], channels) / count
    return mean, lax.rsqrt(square - mean * mean + epsilon)


def affine(stats, gain, shift):
    scale = stats[1] * gain
    return scale, shift - stats[0] * scale


def load_rows(ref, first, count):
    lanes = ref.shape[2]
    return ref[:, first * 16 : (first + count) * 16, :].reshape(2 * count * 16, lanes)


def group_index(rows):
    return lax.broadcasted_iota(jnp.int32, (rows, 128), 0) % 16


def side_columns(value, channels):
    rows = value.shape[0]
    group = group_index(rows)
    lane = lax.broadcasted_iota(jnp.int32, (rows, 128), 1)

    def before(part):
        return jnp.where(group == 0, 0.0, pltpu.roll(part, 1, 0))

    def after(part):
        return jnp.where(group == 15, 0.0, pltpu.roll(part, rows - 1, 0))

    low, upper = value[:, :128], value[:, 128:]
    if channels == 256:
        return jnp.concatenate([before(low), before(upper), after(low), after(upper)], axis=1)
    if channels == 128:
        return jnp.concatenate([before(upper), after(low)], axis=1)
    first, last = after(low), before(upper)
    ends = jnp.where(lane < channels, first, jnp.where(lane >= 128 - channels, last, 0.0))
    if channels == 64:
        return ends
    first, last = pltpu.roll(first, channels, 1), pltpu.roll(last, 128 - channels, 1)
    middle = jnp.where(lane // channels == 1, first, jnp.where(lane // channels == 2, last, 0.0))
    return jnp.concatenate([ends, middle], axis=1)


def build_sides(source, side, channels):
    rows = source.shape[1]
    for image in range(2):
        side[image] = side_columns(source[image], channels)


def patches(branch, source, side, count, offset=0):
    parts = []
    for tap_row in range(3):
        parts.append(load_rows(source, tap_row + offset, count))
        if branch:
            parts.append(load_rows(side, tap_row + offset, count))
    if branch == 0:
        sides = [load_rows(side, tap_row + offset, count) for tap_row in range(3)]
        parts += [sides[0][:, :128] + sides[1][:, 128:], sides[2][:, :128]]
    return jnp.concatenate(parts, axis=1)


def band_row(branch, tap_row, place):
    channels, side = CHANNELS[branch], SIDES[branch]
    if branch == 0:
        if 0 <= place < 8:
            return tap_row * 256 + place * channels
        return ((768, 864), (800, 832), (896, 992))[tap_row][place < 0]
    base = tap_row * (256 + side)
    if place < 0:
        return base + 256 + (0 if channels >= 128 else 128 - channels)
    if place >= 256 // channels:
        return base + 256 + (side // 2 if channels >= 128 else 0)
    return base + place * channels


def build_band(band, tap, branch, offset):
    channels = CHANNELS[branch]
    groups = 256 // channels
    side = SIDES[branch]
    height = 256 + side
    if channels < 256:
        band[:, offset : offset + 256] = jnp.zeros((band.shape[0], 256), f32)
    for tap_row in range(3):
        for tap_col in range(3):
            matrix = tap(tap_row, tap_col)
            for out in range(groups):
                row = band_row(branch, tap_row, out + tap_col - 1)
                start = offset + out * channels
                band[row : row + channels, start : start + channels] = matrix


def collect_band(product, branch, emit):
    channels = CHANNELS[branch]
    for tap_row in range(3):
        for tap_col in range(3):
            total = None
            for out in range(256 // channels):
                row = band_row(branch, tap_row, out + tap_col - 1)
                start = out * channels
                if channels >= 128:
                    block = product[row : row + channels, start : start + channels]
                else:
                    tile = start // 128 * 128
                    block = product[row : row + channels, tile : tile + 128]
                    inner = start - tile
                    if inner:
                        block = pltpu.roll(block, 128 - inner, 1)
                total = block if total is None else total + block
            emit(tap_row, tap_col, total[:, :channels])


def tap_reader(ref, branch):
    channels = CHANNELS[branch]
    if channels == 256:

        def tap(tap_row, tap_col):
            first = (3 * tap_row + tap_col) * 512
            return jnp.concatenate(
                [ref[pl.ds(first, 256, stride=2), :], ref[pl.ds(first + 1, 256, stride=2), :]],
                axis=1,
            )

        return tap

    def tap(tap_row, tap_col):
        first = (3 * tap_row + tap_col) * channels
        return ref[first : first + channels, :]

    return tap


def tap_writer(ref, branch):
    channels = CHANNELS[branch]

    def emit(tap_row, tap_col, value):
        place = 3 * tap_row + tap_col
        if channels == 256:
            ref[pl.ds(place * 512, 256, stride=2), :] = value[:, :128]
            ref[pl.ds(place * 512 + 1, 256, stride=2), :] = value[:, 128:]
        else:
            ref[place * channels : (place + 1) * channels, :] = value

    return emit


SHARD = 392
ROWS_THREE, ROWS_TWO, ROWS_ONE = 288, 72, 18
PER_ZERO, PER_UNITE = 18, (2, 4, 8)
CHUNKS = ((0, 152), (152, 272), (272, 392))
STEPS = ((8, 4, 2), (4, 2, 8), (2, 8, 4))
TAPS_OUT = ((4608, 128), (1152, 128), (576, 64), (288, 32), (32, 32), (64, 32), (128, 32))
PACK_SCRATCH = ((16, 24, 128), (16, 8, 128), (288, 128))
STAGE = ((4608, 128), (1152, 128), (576, 64), (288, 32), (512, 32))


def partner(me, core, place, bits):
    return me ^ (core + sum(bit for i, bit in enumerate(bits) if place >> i & 1))


def shard_parts(device, three, two, one, zero):
    start = device * ROWS_THREE
    return (
        ((0, 152, three.at[pl.ds(pl.multiple_of(start, 8), 152), :]),),
        ((152, 272, three.at[pl.ds(pl.multiple_of(start + 152, 8), 120), :]),),
        (
            (272, 288, three.at[pl.ds(pl.multiple_of(start + 272, 8), 16), :]),
            (288, 360, two.at[pl.ds(pl.multiple_of(device * ROWS_TWO, 8), ROWS_TWO), :]),
            (360, 384, one.at[device]),
            (384, 392, zero.at[device]),
        ),
    )


def unpack_taps(me, packs, taps, scratch):
    three, two, one, zero = taps[:4]
    part_one, part_zero, flat_one = scratch
    for core in range(2):
        for place in range(8):
            for chunk in range(3):
                device = partner(me, core, place, STEPS[chunk])
                parts = shard_parts(device, three, two, part_one, part_zero)[chunk]
                for first, last, ref in parts:
                    ref[...] = packs[core][place, first:last]
    for device in range(16):
        flat_one[device * ROWS_ONE : (device + 1) * ROWS_ONE, :] = part_one[device, 0:ROWS_ONE]
    one[...] = flat_one[...].reshape(one.shape)
    narrow = part_zero[...].reshape(128, 128).reshape(512, 32)
    for device in range(16):
        first = device * 32
        for ref, height in zip(taps[3:7], (PER_ZERO, *PER_UNITE)):
            ref[device * height : (device + 1) * height, :] = narrow[first : first + height]
            first += height


def pack_grads(me, stage, unite_grads, packs, scratch):
    three, two, one, zero, narrow = stage
    part_one, part_zero, flat_one = scratch
    flat_one[...] = one[...].reshape(flat_one.shape)
    for device in range(16):
        part_one[device, 0:ROWS_ONE] = flat_one[device * ROWS_ONE : (device + 1) * ROWS_ONE, :]
        part_one[device, ROWS_ONE:24] = jnp.zeros((24 - ROWS_ONE, 128), f32)
        first = device * 32
        for ref, height in zip((zero, *unite_grads), (PER_ZERO, *PER_UNITE)):
            narrow[first : first + height, :] = ref[device * height : (device + 1) * height, :]
            first += height
    part_zero[...] = narrow[...].reshape(128, 128).reshape(16, 8, 128)
    for core in range(2):
        for place in range(8):
            for chunk in range(3):
                device = partner(me, core, place, STEPS[chunk][::-1])
                parts = shard_parts(device, three, two, part_one, part_zero)[chunk]
                for first, last, ref in parts:
                    packs[core][place, first:last] = ref[...]


def split_shard(meta, shard, other, *outs):
    second = meta[3] == 1
    for out, (first, last) in zip(outs, CHUNKS):
        own, far = shard[first:last], other[first:last]
        out[0, 0] = jnp.where(second, far, own)
        out[0, 1] = jnp.where(second, own, far)


def join_chunks(*refs):
    held, received, outs = split_refs(refs, 3, 3, 3)
    for chunk in range(3):
        count = held[chunk].shape[0]
        outs[chunk][0:count] = held[chunk][...]
        outs[chunk][count : 2 * count] = received[chunk][...]


def join_apart(*refs):
    held, received, first, second = split_refs(refs, 3, 3, 3, 3)
    for chunk in range(3):
        count = held[chunk].shape[0]
        for half, outs in ((0, first), (1, second)):
            outs[chunk][0:count] = held[chunk][:, half]
            outs[chunk][count : 2 * count] = received[chunk][:, half]


def join_whole(*refs):
    held, received, out = split_refs(refs, 3, 3, 1)
    for chunk, (first, last) in enumerate(CHUNKS):
        count = held[chunk].shape[0]
        out[0][0:count, first:last] = held[chunk][...]
        out[0][count : 2 * count, first:last] = received[chunk][...]


def add_received(*refs):
    held, received, low, high = split_refs(refs, 3, 3, 3, 3)
    for chunk in range(3):
        half = held[chunk].shape[0] // 2
        low[chunk][...] = held[chunk][0:half] + received[chunk][0:half]
        high[chunk][...] = held[chunk][half:] + received[chunk][half:]


def add_cores(*refs):
    keeps, received, low, high = split_refs(refs, 2, 2, 3, 3)
    for chunk, (first, last) in enumerate(CHUNKS):
        for half in range(2):
            low[chunk][:, half] = keeps[half][0:4, first:last] + received[half][0:4, first:last]
            high[chunk][:, half] = keeps[half][4:8, first:last] + received[half][4:8, first:last]


def add_last(meta, *refs):
    held, received, keep, send = split_refs(refs, 3, 3, 1, 1)
    second = meta[3] == 1
    for chunk, (first, last) in enumerate(CHUNKS):
        total = held[chunk][0] + received[chunk][0]
        keep[0][first:last, :] = jnp.where(second, total[1], total[0])
        send[0][first:last, :] = jnp.where(second, total[0], total[1])


def add_shard(keep, received, *outs):
    value = keep[...] + received[...]
    first = 0
    for ref in outs[:3]:
        last = first + ref.shape[0]
        ref[...] = value[first:last]
        first = last
    tail = SHARD - 8
    outs[3][...] = value[tail : tail + 5]
    outs[4][...] = value[tail + 4 : tail + 5, 64:]
    outs[5][...] = value[tail + 5 : tail + 6]
    outs[6][...] = value[tail + 6 : tail + 8]


def mirrored(tap):
    return lambda tap_row, tap_col: tap(tap_row, 2 - tap_col)


def turned(tap):
    return lambda tap_row, tap_col: jnp.transpose(tap(2 - tap_row, 2 - tap_col))


def mask_ends(value, rows, flags):
    place = lax.broadcasted_iota(jnp.int32, value.shape, 0) // 16 % (rows + 2)
    outside = ((place == 0) & (flags[0] == 0)) | ((place == rows + 1) & (flags[1] == 0))
    return jnp.where(outside, 0.0, value)


def mix_matrix(unite, branch):
    channels = CHANNELS[branch]
    groups = 256 // channels
    wide = jnp.concatenate([unite] * 8, axis=1)
    lane = lax.broadcasted_iota(jnp.int32, wide.shape, 1)
    span = 256 // groups
    return jnp.concatenate(
        [jnp.where(lane // span == place, wide, 0.0) for place in range(groups)], axis=0
    )


def split_refs(refs, *counts):
    out, first = [], 0
    for count in counts:
        out.append(refs[first : first + count])
        first += count
    assert first == len(refs)
    return out


class Kept:
    def __init__(self, value):
        self.value = value


def kept(values):
    return [Kept(value) for value in values]


def call(kernel, ins, outs, scratch=(), smem=0, limit=10, cost=0.01):
    specs = [pl.BlockSpec(memory_space=pltpu.SMEM)] * smem + [
        pl.BlockSpec(memory_space=pltpu.VMEM)
    ] * (len(ins) - smem)
    ins = ins[:smem] + [
        pltpu.with_memory_space_constraint(x.value, pltpu.VMEM)
        if isinstance(x, Kept)
        else pltpu.with_memory_space_constraint(x, pltpu.HBM)
        for x in ins[smem:]
    ]
    shapes = [pltpu.VMEM(x.value, f32) if isinstance(x, Kept) else pltpu.HBM(x, f32) for x in outs]
    results = pl.pallas_call(
        kernel,
        in_specs=specs,
        out_specs=[pl.BlockSpec(memory_space=pltpu.VMEM)] * len(outs),
        out_shape=shapes,
        scratch_shapes=[pltpu.VMEM(shape, f32) for shape in scratch],
        compiler_params=pltpu.CompilerParams(vmem_limit_bytes=limit * 2**20),
        cost_estimate=pl.CostEstimate(
            flops=int(cost * 1.1e9), bytes_accessed=int(cost * 3.0e6), transcendentals=0
        ),
    )(*ins)
    return [Kept(y) if isinstance(x, Kept) else y for x, y in zip(outs, results)]


def band_shape(branch, width):
    return (1024 if branch == 0 else 3 * (256 + SIDES[branch]), width)


def swap_blocks(parts):
    rows = parts[0].shape[0]
    group = lax.broadcasted_iota(jnp.int32, (rows, 128), 1) // 8
    step = 1
    while step < 16:
        high = (group & step) != 0
        parts = [
            jnp.where(high, parts[i], pltpu.roll(parts[i - step], 128 - 8 * step, 1))
            if i & step
            else jnp.where(high, pltpu.roll(parts[i + step], 8 * step, 1), parts[i])
            for i in range(16)
        ]
        step = 2 * step
    return parts


def joint_matrix():
    source = lax.broadcasted_iota(jnp.int32, (256, 256), 0)
    lane = lax.broadcasted_iota(jnp.int32, (256, 256), 1)
    matches = (source // 8 == lane % C0) & (source % 8 == lane // C0) & (source < 136)
    return jnp.where(matches, 1.0, 0.0)


def shift_group(value, group):
    return pltpu.roll(value, 128 - 8 * group, 1) if group else value


def parameter_kernel(gain, shift, weight, bias, flip, *outs):
    norms, weight_out, bias_out, flip_weight, flip_bias = outs
    weight = jnp.transpose(weight[...])
    for base, ref in ((0, gain), (11, shift)):
        offset = 0
        line = base
        sizes = [channels for channels in CHANNELS for _ in range(2)] + [C0] * 3
        for channels in sizes:
            part = ref[0:1, offset : offset + channels]
            norms[line : line + 1, :] = jnp.concatenate([part] * (256 // channels), axis=1)
            offset += channels
            line += 1
    joints = weight.shape[1]
    source = lax.broadcasted_iota(jnp.int32, (joints, joints), 0)
    moved = jnp.where(source == flip[...], 1.0, 0.0)
    for matrix, row, matrix_out, row_out in (
        (weight, bias[...], weight_out, bias_out),
        (
            jnp.dot(weight, moved, precision=lax.Precision.HIGHEST),
            jnp.dot(bias[...], moved, precision=lax.Precision.HIGHEST),
            flip_weight,
            flip_bias,
        ),
    ):
        matrix_out[...] = jnp.zeros((C0, C0), f32)
        matrix_out[:, 0:joints] = matrix
        row_out[...] = jnp.zeros((1, 256), f32)
        for place in range(8):
            row_out[0:1, C0 * place : C0 * place + joints] = row


def target_kernel(people, targets, mask, target_out, mask_out, scratch):
    lines = 2 * targets.shape[2]
    parts = swap_blocks([targets[:, j].reshape(lines, 128) for j in range(16)])
    last = targets[:, 16].reshape(lines, 128)
    cells = mask[...].reshape(lines, 128).astype(f32)
    lane = lax.broadcasted_iota(jnp.int32, (lines, 128), 1)
    tails = [
        jnp.where(lane < 8, shift_group(last, group), pltpu.roll(shift_group(cells, group), 8, 1))
        for group in range(16)
    ]
    whole = jnp.concatenate(
        [jnp.concatenate([part, tail], axis=1) for part, tail in zip(parts, tails)], axis=0
    )
    source = lax.broadcasted_iota(jnp.int32, (256, 256), 0)
    target_lane = lax.broadcasted_iota(jnp.int32, (256, 256), 1)
    spread = jnp.where((source >= 136) & (source < 144) & (source - 136 == target_lane // C0), 1.0, 0.0)
    target_rows = dot_nn(whole, joint_matrix())
    mask_rows = dot_nn(whole, spread)
    first_image = lax.broadcasted_iota(jnp.int32, (lines, 256), 0) < lines // 2
    share = jnp.where(first_image, people[0].astype(f32), people[1].astype(f32))
    for value, ref in ((target_rows, target_out), (mask_rows, mask_out)):
        for part in range(2):
            for group in range(16):
                span = slice(group * lines, (group + 1) * lines)
                block = value[span, 128 * part : 128 * part + 128]
                if ref is mask_out:
                    block = block / share[:, :128]
                scratch[pl.ds(group, lines, stride=16), :] = block
            ref[:, 128 * part : 128 * part + 128] = scratch[...]


def tile_kernel(rows, meta, *refs):
    xs, near, far, tiles, sides = split_refs(refs, 4, 1, 1, 4, 4)
    odd = meta[4] == 1
    for branch in range(4):
        count = rows[branch]
        tile = tiles[branch]
        for image in range(2):
            one, two = (ref[0][image, 2 * branch : 2 * branch + 2, :] for ref in (near, far))
            for value, first, extent in (
                (jnp.where(odd, one, two), 0, 2),
                (xs[branch][image], 2, count),
                (jnp.where(odd, two, one), count + 2, 2),
            ):
                tile[image, first * 16 : (first + extent) * 16, :] = value.reshape(extent * 16, 256)
        build_sides(tile, sides[branch], CHANNELS[branch])


def first_kernel(rows, packed, meta, *refs):
    tiles, sides, packs, mains, sums, taps, bands, scratch = split_refs(
        refs, 4, 4, 2 if packed else 4, 4, 1, 7 * packed, 4, 3 * packed
    )
    sums = sums[0]
    if packed:
        unpack_taps(meta[2], packs, taps, scratch)
    else:
        taps = packs
    for branch in range(4):
        count, band = rows[branch], bands[branch]
        build_band(band, tap_reader(taps[3 - branch], branch), branch, 0)
        out = dot_nn(patches(branch, tiles[branch], sides[branch], count + 2), band[...])
        mains[branch][...] = out.reshape(2, (count + 2) * 16, 256)
        inner = load_rows(mains[branch], 1, count)
        sums[2 * branch : 2 * branch + 1, :] = column_sum(inner)
        sums[2 * branch + 1 : 2 * branch + 2, :] = column_sum(inner * inner)


def first_flip_kernel(rows, branch, meta, tile, side, taps, out, band):
    count = rows[branch]
    build_band(band, mirrored(tap_reader(taps, branch)), branch, 0)
    value = dot_nn(patches(branch, tile, side, count + 2), band[...])
    out[...] = value.reshape(2, (count + 2) * 16, 256)


def fill_hidden(meta, firsts, stat, norms, hidden, branch, count, total):
    stats = moments(stat[2 * branch : 2 * branch + 2, :], CHANNELS[branch], total)
    scale, offset = affine(
        stats,
        norms[2 * branch : 2 * branch + 1, :],
        norms[11 + 2 * branch : 12 + 2 * branch, :],
    )
    value = load_rows(firsts[branch], 0, count + 2) * scale + offset
    value = mask_ends(silu(value), count, meta)
    hidden[branch][...] = value.reshape(2, (count + 2) * 16, 256)


def band_kernel(packed, meta, *refs):
    packs, taps, bands, scratch = split_refs(refs, 2 if packed else 4, 7 * packed, 4, 3 * packed)
    if packed:
        unpack_taps(meta[2], packs, taps, scratch)
    else:
        taps = packs
    for branch in range(4):
        build_band(bands[branch], tap_reader(taps[3 - branch], branch), branch, 0)


def turned_kernel(meta, *refs):
    taps, bands = split_refs(refs, 4, 4)
    for branch in range(4):
        build_band(bands[branch], turned(tap_reader(taps[3 - branch], branch)), branch, 0)


def second_kernel(rows, counts, branches, meta, *refs):
    each = len(branches)
    firsts, stat, norms, bands, outs, sums, hidden, sides = split_refs(
        refs, each, 1, 1, each, each, 1, each, each
    )
    sums = sums[0]
    sums[...] = jnp.zeros(sums.shape, f32)
    for i, branch in enumerate(branches):
        count, channels = rows[branch], CHANNELS[branch]
        fill_hidden(
            meta, {branch: firsts[i]}, stat[0], norms[0], {branch: hidden[i]}, branch, count, counts[branch]
        )
        build_sides(hidden[i], sides[i], channels)
        out = dot_nn(patches(branch, hidden[i], sides[i], count), bands[i][...])
        outs[i][...] = out
        sums[2 * branch : 2 * branch + 1, :] = column_sum(out)
        sums[2 * branch + 1 : 2 * branch + 2, :] = column_sum(out * out)


def second_flip_kernel(rows, counts, branch, meta, first, stat, norms, taps, out, hidden, band, side):
    count, channels = rows[branch], CHANNELS[branch]
    fill_hidden(meta, {branch: first}, stat, norms, {branch: hidden}, branch, count, counts[branch])
    build_sides(hidden, side, channels)
    build_band(band, mirrored(tap_reader(taps, branch)), branch, 0)
    out[...] = dot_nn(patches(branch, hidden, side, count), band[...])


def joined(second, tile, stat, norms, branch, count, total):
    stats = moments(stat[2 * branch : 2 * branch + 2, :], CHANNELS[branch], total)
    gain = norms[2 * branch + 1 : 2 * branch + 2, :]
    shift = norms[12 + 2 * branch : 13 + 2 * branch, :]
    scaled = (second - stats[0]) * stats[1]
    return scaled * gain + shift + load_rows(tile, 2, count), scaled, stats


def third_kernel(rows, counts, *refs):
    seconds, tiles, stat, norms, unites, top_sums, mixes, sums = split_refs(
        refs, 3, 3, 1, 1, 6, 1, 3, 1
    )
    stat, norms, sums = stat[0], norms[0], sums[0]
    for level in range(3):
        branch = level + 1
        value, _, _ = joined(
            seconds[level][...], tiles[level], stat, norms, branch, rows[branch], counts[branch]
        )
        unite = jnp.concatenate([unites[level][...], unites[3 + level][...]], axis=0)
        mixed = dot_nn(silu(value), mix_matrix(unite, branch))
        mixes[level][...] = mixed
        sums[2 * level : 2 * level + 1, :] = column_sum(mixed)
        sums[2 * level + 1 : 2 * level + 2, :] = column_sum(mixed * mixed)
    sums[6:8, :] = top_sums[0][0:2, :]


def spread_rows(value, rows, factor):
    value = value.reshape(2 * rows, 1, 16, 256)
    return jnp.broadcast_to(value, (2 * rows, factor, 16, 256)).reshape(2 * rows * factor * 16, 256)


def gather_rows(value, rows, factor):
    value = value.reshape(2 * rows // factor, factor, 16, 256)
    return jnp.sum(value, axis=1).reshape(2 * rows // factor * 16, 256)


def uniting_stats(stat, level, total):
    return moments(stat[2 * level : 2 * level + 2, :], C0, total * 2.0 ** (level + 1))


def united_sum(base, mixes, stat, norms, rows, counts):
    for level in range(3):
        stats = uniting_stats(stat, level, counts[level + 1])
        scale, offset = affine(
            stats, norms[8 + level : 9 + level, :], norms[19 + level : 20 + level, :]
        )
        base = base + spread_rows(mixes[level] * scale + offset, rows[level + 1], 2 ** (level + 1))
    return base


def head_matrix(weight):
    wide = jnp.concatenate([weight] * 8, axis=1)
    lane = lax.broadcasted_iota(jnp.int32, wide.shape, 1)
    return jnp.concatenate([jnp.where(lane // C0 == place, wide, 0.0) for place in range(8)], axis=0)


def top_edge_kernel(rows, meta, grad, second, near, far):
    odd = meta[4] == 1
    write_edges(odd, near, far, grad, 0, rows[0], 0)
    write_edges(odd, near, far, second, 0, rows[0], 32)


def loss_kernel(rows, counts, denominator, *refs):
    ins, outs = split_refs(refs, 12, 10)
    second, tile, low_stat, mix_one, mix_two, mix_three, mix_stat, norms, weight, bias, targets, mask = ins
    heat_out, sum_one, sum_two, sum_three, sums, join_grad, zero_sums, united_out, grad_out = outs[:9]
    stat = outs[9]
    stat[0:2, :] = mix_stat[6:8, :]
    stat[2:8, :] = low_stat[2:8, :]
    sums[8:16, :] = jnp.zeros((8, 256), f32)
    count = rows[0]
    join, scaled, _ = joined(second[...], tile, stat, norms, 0, count, counts[0])
    mixes = (mix_one[...], mix_two[...], mix_three[...])
    pre = united_sum(silu(join), mixes, mix_stat, norms, rows, counts)
    united = silu(pre)
    head = head_matrix(weight[...])
    heat = dot_nn(united, head) + bias[...]
    heat_out[...] = heat
    error = heat - targets[...]
    weighted = mask[...] * error
    sums[6:7, :] = column_sum(weighted * error) / denominator
    heat_grad = weighted * (2.0 / denominator)
    sums[7:8, :] = column_sum(heat_grad)
    united_out[...] = united
    grad_out[...] = heat_grad
    grad = dot_nt(heat_grad, head) * silu_slope(pre)
    join_part = grad * silu_slope(join)
    join_grad[...] = join_part
    zero_sums[0:1, :] = column_sum(join_part)
    zero_sums[1:2, :] = column_sum(join_part * scaled)
    sums[8:10, :] = zero_sums[0:2, :]
    for level, out in enumerate((sum_one, sum_two, sum_three)):
        part = gather_rows(grad, count, 2 ** (level + 1))
        out[...] = part
        stats = uniting_stats(mix_stat, level, counts[level + 1])
        normed = (mixes[level] - stats[0]) * stats[1]
        sums[2 * level : 2 * level + 1, :] = column_sum(part)
        sums[2 * level + 1 : 2 * level + 2, :] = column_sum(part * normed)


def head_kernel(meta, united, heat_grad, out):
    product = dot_tn(united[...], heat_grad[...])
    total = None
    for place in range(8):
        first = place * C0
        tile_first = first // 128 * 128
        block = product[first : first + C0, tile_first : tile_first + 128]
        if first - tile_first:
            block = pltpu.roll(block, 128 - (first - tile_first), 1)
        total = block if total is None else total + block
    out[...] = jnp.zeros(out.shape, f32)
    out[:, 0:128] = jnp.concatenate(
        [total[8 * part : 8 * part + 8, :C0] for part in range(4)], axis=1
    )


def flip_kernel(rows, counts, *refs):
    seconds, tiles, stat, unites, mix_stat, norms, weight, bias, heat, out, scratch = split_refs(
        refs, 4, 4, 1, 6, 1, 1, 1, 1, 1, 1, 2
    )
    stat, norms = stat[0], norms[0]
    mixes = []
    for branch in range(4):
        value, _, _ = joined(
            seconds[branch][...], tiles[branch], stat, norms, branch, rows[branch], counts[branch]
        )
        if branch == 0:
            base = silu(value)
        else:
            unite = jnp.concatenate([unites[branch - 1][...], unites[branch + 2][...]], axis=0)
            mixes.append(dot_nn(silu(value), mix_matrix(unite, branch)))
    pre = united_sum(base, mixes, mix_stat[0], norms, rows, counts)
    back = dot_nn(silu(pre), head_matrix(weight[0][...])) + bias[0][...]
    moved = dot_nt(0.5 * (heat[0][...] + back), joint_matrix())
    scratch[0][...] = moved[:, :128]
    scratch[1][...] = moved[:, 128:]
    lines = 2 * rows[0]
    parts = [scratch[0][pl.ds(group, lines, stride=16), :] for group in range(16)]
    lane = lax.broadcasted_iota(jnp.int32, (lines, 128), 1)
    last = None
    for group in range(16):
        tail = scratch[1][pl.ds(group, lines, stride=16), :]
        tail = pltpu.roll(tail, 8 * group, 1) if group else tail
        last = tail if last is None else jnp.where(lane // 8 == group, tail, last)
    for joint, value in enumerate([*swap_blocks(parts), last]):
        out[0][:, joint] = value.reshape(2, rows[0], 128)


def edge_place(branch, image):
    return (2 * branch + image) * 16


def write_edges(odd, near, far, value, branch, count, base):
    for image in range(2):
        place = base + edge_place(branch, image)
        start = image * count * 16
        first = value[start : start + 16]
        last = value[start + (count - 1) * 16 : start + count * 16]
        near[place : place + 16, :] = jnp.where(odd, first, last)
        far[place : place + 16, :] = jnp.where(odd, last, first)


def join_kernel(rows, counts, meta, *refs):
    sums_in, mixes, seconds, tiles, small, unites, outs = split_refs(refs, 3, 3, 3, 3, 6, 6, 9)
    zero_sums, head_grad, stat, mix_stat, head_sums, norms = small
    grads, mixed_grads, sums, near, far = outs[0:3], outs[3:6], outs[6], outs[7], outs[8]
    odd = meta[4] == 1
    sums[0:2, :] = zero_sums[0:2, :]
    sums[8:16, :] = head_grad[...]
    for level in range(3):
        branch = level + 1
        channels, count = CHANNELS[branch], rows[branch]
        total = counts[branch]
        stats = uniting_stats(mix_stat, level, total)
        gain = norms[8 + level : 9 + level, :]
        shift_sum = fold(head_sums[2 * level : 2 * level + 1, :], C0)
        gain_sum = fold(head_sums[2 * level + 1 : 2 * level + 2, :], C0)
        normed = (mixes[level][...] - stats[0]) * stats[1]
        share = 1.0 / (total * 2.0 ** (level + 1))
        mixed_grad = (gain * stats[1]) * (
            sums_in[level][...] - shift_sum * share - normed * (gain_sum * share)
        )
        mixed_grads[level][...] = mixed_grad
        value, scaled, _ = joined(
            seconds[level][...], tiles[level], stat, norms, branch, count, total
        )
        unite = jnp.concatenate([unites[level][...], unites[3 + level][...]], axis=0)
        grad = dot_nt(mixed_grad, mix_matrix(unite, branch)) * silu_slope(value)
        grads[level][...] = grad
        sums[2 * branch : 2 * branch + 1, :] = column_sum(grad)
        sums[2 * branch + 1 : 2 * branch + 2, :] = column_sum(grad * scaled)
        write_edges(odd, near, far, grad, branch, count, 0)
        write_edges(odd, near, far, seconds[level][...], branch, count, 128)


def mixer_kernel(rows, counts, meta, *refs):
    mixed_grads, seconds, tiles, stat, norms, outs = split_refs(refs, 3, 3, 3, 1, 1, 6)
    for level in range(3):
        branch = level + 1
        channels = CHANNELS[branch]
        value, _, _ = joined(
            seconds[level][...], tiles[level], stat[0], norms[0], branch, rows[branch], counts[branch]
        )
        product = dot_tn(silu(value), mixed_grads[level][...])
        mixer = None
        for place in range(8):
            row = place // (8 * channels // 256) * channels
            tile_first = place * C0 // 128 * 128
            block = product[row : row + channels, tile_first : tile_first + 128]
            inner = place * C0 - tile_first
            if inner:
                block = pltpu.roll(block, 128 - inner, 1)
            mixer = block if mixer is None else mixer + block
        outs[level][...] = mixer[: channels // 2, :C0]
        outs[3 + level][...] = mixer[channels // 2 :, :C0]


def norm_input_grad(grad, scaled, stats, gain, sums, channels, total):
    shift_sum = fold(sums[0:1, :], channels) / total
    gain_sum = fold(sums[1:2, :], channels) / total
    return (gain * stats[1]) * (grad - shift_sum - scaled * gain_sum)


def back_second_branch(
    rows, counts, branch, meta, grad, second, first, band, edges, stats_in, out, sums, wide, side
):
    stat, own, first_stat, norms = stats_in
    count, channels, total = rows[branch], CHANNELS[branch], counts[branch]
    odd = meta[4] == 1
    stats = moments(stat[2 * branch : 2 * branch + 2, :], channels, total)
    gain = norms[2 * branch + 1 : 2 * branch + 2, :]
    shift_sum = fold(own[0:1], channels) / total
    gain_sum = fold(own[1:2], channels) / total

    def input_grad(part, value):
        scaled = (value - stats[0]) * stats[1]
        return (gain * stats[1]) * (part - shift_sum - scaled * gain_sum)

    inner = input_grad(grad[...], second[...])
    wide[:, 16 : (count + 1) * 16, :] = inner.reshape(2, count * 16, 256)
    for image in range(2):
        parts = [input_grad(*edge) for edge in edges[image]]
        for value, start, flag in (
            (jnp.where(odd, parts[0], parts[1]), 0, meta[0]),
            (jnp.where(odd, parts[1], parts[0]), (count + 1) * 16, meta[1]),
        ):
            wide[image, start : start + 16, :] = jnp.where(flag == 0, 0.0, value)
    build_sides(wide, side, channels)
    hidden_grad = dot_nn(patches(branch, wide, side, count), band[...])
    first_stats = moments(first_stat[2 * branch : 2 * branch + 2, :], channels, total)
    scaled = (load_rows(first, 1, count) - first_stats[0]) * first_stats[1]
    value = (
        scaled * norms[2 * branch : 2 * branch + 1, :]
        + norms[11 + 2 * branch : 12 + 2 * branch, :]
    )
    result = hidden_grad * silu_slope(value)
    out[...] = result
    sums[2 * branch : 2 * branch + 1, :] = column_sum(result)
    sums[2 * branch + 1 : 2 * branch + 2, :] = column_sum(result * scaled)
    return result


def back_top_kernel(rows, counts, meta, *refs):
    grad, second, first, band, near, far, stat, head_sums, first_stat, norms, out, sums, wide, side = refs
    edges = [
        [(ref[at : at + 16, :], ref[32 + at : 48 + at, :]) for ref in (near, far)]
        for at in (0, 16)
    ]
    stats_in = (stat, head_sums[8:10, :], first_stat, norms)
    back_second_branch(
        rows, counts, 0, meta, grad, second, first, band, edges, stats_in, out, sums, wide, side
    )


def back_second_kernel(rows, counts, meta, *refs):
    ins, outs, wide, sides = split_refs(refs, 20, 6, 3, 3)
    grads, seconds, firsts, bands = ins[0:3], ins[3:6], ins[6:9], ins[9:12]
    near_in, far_in, stat, stat_sums, first_stat, norms, top, top_sums = ins[12:20]
    sums, near, far = outs[3:6]
    odd = meta[4] == 1
    sums[0:2, :] = top_sums[0:2, :]
    write_edges(odd, near, far, top[...], 0, rows[0], 0)
    for level in range(3):
        branch = level + 1
        places = [edge_place(branch, image) for image in range(2)]
        edges = [
            [(ref[at : at + 16, :], ref[128 + at : 144 + at, :]) for ref in (near_in, far_in)]
            for at in places
        ]
        stats_in = (stat, stat_sums[2 * branch : 2 * branch + 2, :], first_stat, norms)
        result = back_second_branch(
            rows,
            counts,
            branch,
            meta,
            grads[level],
            seconds[level],
            firsts[level],
            bands[level],
            edges,
            stats_in,
            outs[level],
            sums,
            wide[level],
            sides[level],
        )
        write_edges(odd, near, far, result, branch, rows[branch], 0)


def cross_products(rows, branch, offset, source, value, out, side, product):
    count, channels = rows[branch], CHANNELS[branch]
    product[...] = dot_tn(patches(branch, source, side, count, offset), value)

    def emit(tap_row, tap_col, block):
        place = (3 * tap_row + tap_col) * channels
        out[place : place + channels, :] = block

    collect_band(product, branch, emit)


def normalized(raw, stat, rows, counts, branch, inner):
    stats = moments(stat[2 * branch : 2 * branch + 2, :], CHANNELS[branch], counts[branch])
    value = raw[...] if inner else load_rows(raw, 1, rows[branch])
    return (value - stats[0]) * stats[1]


def sum_means(sums, branch, total):
    channels = CHANNELS[branch]
    return [fold(sums[2 * branch + i : 2 * branch + i + 1, :], channels) / total for i in range(2)]


def cross_kernel(rows, counts, devices, branch, offset, inner, meta, *refs):
    source, side, value, raw, stat, sums, out, product = refs
    shift_mean, gain_mean = sum_means(sums, branch, counts[branch] / devices)
    scaled = normalized(raw, stat, rows, counts, branch, inner)
    rest = value[...] - shift_mean - scaled * gain_mean
    cross_products(rows, branch, offset, source, rest, out, side, product)


def cross_norm_kernel(rows, counts, branch, offset, inner, meta, *refs):
    source, side, raw, stat, out, sums, product = refs
    count, channels = rows[branch], CHANNELS[branch]
    scaled = normalized(raw, stat, rows, counts, branch, inner)
    cross_products(rows, branch, offset, source, scaled, out, side, product)
    total = column_sum(patches(branch, source, side, count, offset))
    column = jnp.transpose(jnp.broadcast_to(total, (8, total.shape[1])))
    for tap_row in range(3):
        for tap_col in range(3):
            block = None
            for place in range(256 // channels):
                row = band_row(branch, tap_row, place + tap_col - 1)
                part = column[row : row + channels]
                block = part if block is None else block + part
            start = (3 * tap_row + tap_col) * channels
            sums[start : start + channels, :] = block


def combine_kernel(counts, devices, packed, which, meta, *refs):
    crosses, norm_crosses, patch_sums, ins, unite_grads, outs, stage, scratch = split_refs(
        refs, 4, 4, 4, 4, 3, 2 if packed else 4, 5, 3
    )
    stat, own_sums, grad_sums, norms = ins
    for branch in range(4):
        channels, total = CHANNELS[branch], counts[branch]
        stats = moments(stat[2 * branch : 2 * branch + 2, :], channels, total)
        line = 2 * branch + which
        scale = (norms[line : line + 1, :] * stats[1])[:, :channels]
        shift_rest, gain_rest = (
            (whole - own)[:, :channels]
            for whole, own in zip(
                sum_means(grad_sums, branch, total), sum_means(own_sums, branch, total / devices)
            )
        )
        emit = tap_writer(stage[3 - branch], branch)
        for place in range(9):
            span = slice(place * channels, (place + 1) * channels)
            value = (
                crosses[branch][span, :]
                - patch_sums[branch][span, 0:1] * shift_rest
                - norm_crosses[branch][span, :] * gain_rest
            )
            emit(place // 3, place % 3, scale * value)
    if packed:
        pack_grads(meta[2], stage, unite_grads, outs, scratch)
    else:
        for ref, value in zip(outs, stage):
            ref[...] = value[...]


def back_first_kernel(rows, counts, flags, *refs):
    ins, source_grads, wide, sides, bands = split_refs(refs, 21, 4, 4, 4, 4)
    normed_grads, firsts, join_grads, taps = ins[0:4], ins[4:8], ins[8:12], ins[12:16]
    near, far, first_stat, first_sums, norms = ins[16:21]
    odd = flags[4] == 1
    for branch in range(4):
        count, channels, total = rows[branch], CHANNELS[branch], counts[branch]
        stats = moments(first_stat[2 * branch : 2 * branch + 2, :], channels, total)
        gain = norms[2 * branch : 2 * branch + 1, :]
        shift_sum = fold(first_sums[2 * branch : 2 * branch + 1, :], channels) / total
        gain_sum = fold(first_sums[2 * branch + 1 : 2 * branch + 2, :], channels) / total

        def input_grad(grad, value):
            scaled = (value - stats[0]) * stats[1]
            return (gain * stats[1]) * (grad - shift_sum - scaled * gain_sum)

        inner = input_grad(normed_grads[branch][...], load_rows(firsts[branch], 1, count))
        wide[branch][:, 16 : (count + 1) * 16, :] = inner.reshape(2, count * 16, 256)
        for image in range(2):
            place = edge_place(branch, image)
            one, two = (ref[place : place + 16, :] for ref in (near, far))
            for grad, start, flag in (
                (jnp.where(odd, one, two), 0, flags[0]),
                (jnp.where(odd, two, one), (count + 1) * 16, flags[1]),
            ):
                value = input_grad(grad, firsts[branch][image, start : start + 16, :])
                wide[branch][image, start : start + 16, :] = jnp.where(flag == 0, 0.0, value)
        build_sides(wide[branch], sides[branch], channels)
        build_band(bands[branch], turned(tap_reader(taps[3 - branch], branch)), branch, 0)
        grad = dot_nn(patches(branch, wide[branch], sides[branch], count), bands[branch][...])
        grad = (grad + join_grads[branch][...]).reshape(2, count * 16, 256)
        for image in range(2):
            source_grads[branch][image] = grad[image].reshape(count, 4096)


def finish_kernel(first_sums, second_sums, head_sums, gain, shift, loss, head_weight, head_bias):
    offset = 0

    def put(sums, line, channels):
        nonlocal offset
        for ref, row in ((shift, line), (gain, line + 1)):
            value = fold(sums[row : row + 1, :], channels)
            done = 0
            while done < channels:
                place = offset + done
                width = min(channels - done, 128 - place % 128)
                ref[place // 128 : place // 128 + 1, place % 128 : place % 128 + width] = value[
                    :, done : done + width
                ]
                done += width
        offset += channels

    for branch in range(4):
        for sums in (first_sums, second_sums):
            put(sums, 2 * branch, CHANNELS[branch])
    for level in range(3):
        put(head_sums, 2 * level, C0)
    loss[...] = jnp.sum(head_sums[6:7, :], axis=1, keepdims=True)
    joints = head_bias.shape[1]
    head_bias[...] = fold(head_sums[7:8, :], C0)[:, :joints]
    total = jnp.concatenate(
        [second_sums[8:16, C0 * part : C0 * part + C0] for part in range(4)], axis=0
    )
    head_weight[...] = jnp.transpose(total)[:joints]


def device_count():
    return lax.axis_size("dp") * lax.axis_size("space")


def exchange(value, bit):
    return lax.ppermute(value, AXES, [(i, i ^ bit) for i in range(device_count())])


def total_sum(value, beside=(), order=None):
    value = value.value
    for step, bit in enumerate(order or [1 << i for i in range(device_count().bit_length() - 1)]):
        other = exchange(value, bit)
        if step < len(beside) and beside[step]:
            other = after(other, *beside[step](value))
        value = value + other
    return Kept(value)


def swap_rows(near, far):
    devices = lax.axis_size("space")
    pairs = [(i, i ^ 1) for i in range(devices)]
    others = [(i, i + 1) for i in range(1, devices - 1, 2)]
    others += [(j, i) for i, j in others]
    return lax.ppermute(near, "space", pairs), lax.ppermute(far, "space", others)


def swap_near(near, far):
    pairs = [(i, i ^ 1) for i in range(lax.axis_size("space"))]
    return lax.ppermute(near, "space", pairs), lax.ppermute(far, "space", pairs)


def pass_on(relay):
    devices = lax.axis_size("space")
    return lax.ppermute(relay, "space", [(i, (i + 2 - i % 2 * 4) % devices) for i in range(devices)])


def device_index():
    return lax.axis_index("dp") * lax.axis_size("space") + lax.axis_index("space")


def after(value, *others):
    return lax.optimization_barrier((value, *others))[0]


def swap(parts, step):
    return [Kept(exchange(part.value, STEPS[chunk][step])) for chunk, part in enumerate(parts)]


def gather_shards(meta, flat, beside):
    other = exchange(flat, 16)
    other = after(other, *beside[0](flat))
    shapes = [(1, 2, last - first, 128) for first, last in CHUNKS]
    parts = call(split_shard, [meta, flat, Kept(other)], kept(shapes), smem=1)
    shapes = [(2, *shape[1:]) for shape in shapes]
    received = swap(parts, 0)
    received[0] = Kept(after(received[0].value, *beside[1](parts[0].value)))
    parts = call(join_chunks, [*parts, *received], kept(shapes))
    shapes = [(4, *shape[2:]) for shape in shapes]
    received = swap(parts, 1)
    received[0] = Kept(after(received[0].value, *beside[2](parts[0].value)))
    parts = call(join_apart, [*parts, *received], kept(shapes * 2))
    first, second = parts[:3], parts[3:]
    received = swap(first, 2)
    received[0] = Kept(after(received[0].value, *beside[3](first[0].value)))
    (whole,) = call(join_whole, [*first, *received], kept([(8, SHARD, 128)]))
    second[0] = Kept(after(second[0].value, whole.value))
    received = swap(second, 2)

    def rest(start):
        received[0] = Kept(after(received[0].value, start))
        (whole,) = call(join_whole, [*second, *received], kept([(8, SHARD, 128)]))
        return [whole, Kept(exchange(whole.value, 1))]

    return [whole, Kept(exchange(whole.value, 1))], rest


def scatter_step(parts, step, beside, meta=None):
    received = swap(parts[3:], step)
    received[0] = Kept(after(received[0].value, *beside(parts[3].value)))
    if step == 2:
        return call(add_last, [meta, *parts[:3], *received], kept([(SHARD, 128)] * 2), smem=1)
    shapes = [(2 - step, 2, last - first, 128) for first, last in CHUNKS]
    return call(add_received, [*parts[:3], *received], kept(shapes * 2))


def body(
    branch_zero,
    branch_one,
    branch_two,
    branch_three,
    convs_zero,
    convs_one,
    convs_two,
    convs_three,
    unite_one,
    unite_two,
    unite_three,
    norm_gain,
    norm_shift,
    head_weight,
    head_bias,
    targets,
    crowd_mask,
    person_count,
    flip_order,
):
    inputs = (branch_zero, branch_one, branch_two, branch_three)
    devices = device_count()
    spaces = lax.axis_size("space")
    place = lax.axis_index("space")
    rows = tuple(value.shape[1] for value in inputs)
    counts = tuple(
        float(2 * rows[b] * 16 * (256 // CHANNELS[b]) * devices) for b in range(4)
    )
    joints = head_bias.shape[0]
    cells = [2 * rows[b] * 16 for b in range(4)]
    packed = devices == 32
    shards_in = (convs_three, convs_two, convs_one, convs_zero, unite_one, unite_two, unite_three)
    sizes = [part.shape[0] for part in shards_in]

    meta = jnp.stack(
        [
            place > 0,
            place < spaces - 1,
            device_index() & 15,
            (device_index() & 16) // 16,
            place % 2,
        ]
    ).astype(jnp.int32)

    bands = [band_shape(b, 256) for b in range(4)]
    inner = [(cells[b], 256) for b in range(4)]
    wide = [(2, (rows[b] + 2) * 16, 256) for b in range(4)]
    wider = [(2, (rows[b] + 4) * 16, 256) for b in range(4)]

    def sides_of(shapes):
        return [shape[:2] + (SIDES[b],) for b, shape in enumerate(shapes)]

    def works(*parts):
        return lambda start: sum((list(part(start)) for part in parts), [])

    state = {}

    def prepare(start):
        parts = lax.optimization_barrier((*inputs, start))[:4]
        last_rows = jnp.concatenate([value[:, -2:] for value in parts], axis=1)
        first_rows = jnp.concatenate([value[:, :2] for value in parts], axis=1)
        odd = place % 2 == 1
        state["halo"] = swap_rows(
            jnp.where(odd, first_rows, last_rows), jnp.where(odd, last_rows, first_rows)
        )
        return state["halo"]

    def prepare_targets(start):
        state["targets"] = call(
            target_kernel,
            [after(person_count, start), targets, crowd_mask],
            kept([(cells[0], 256)] * 2),
            [(cells[0], 128)],
            smem=1,
            cost=4,
        )
        return [state["targets"][0].value]

    def make_tiles(start):
        state["tiles"] = call(
            functools.partial(tile_kernel, rows),
            [after(meta, start), *inputs, *state["halo"]],
            kept([*wider, *sides_of(wider)]),
            smem=1,
        )
        return [state["tiles"][0].value]

    def parameters(start):
        state["small"] = call(
            parameter_kernel,
            [
                after(norm_gain, start)[None],
                norm_shift[None],
                jnp.transpose(head_weight),
                head_bias[None],
                flip_order[None],
            ],
            kept([(22, 256), (C0, C0), (1, 256), (C0, C0), (1, 256)]),
        )
        return [state["small"][0].value]

    if packed:
        gap = jnp.zeros(((24 - ROWS_ONE) * 128,), f32)
        flat = jnp.concatenate([*shards_in[:3], gap, *shards_in[3:]]).reshape(SHARD, 128)
        first_packs, rest = gather_shards(meta, flat, (works(prepare, prepare_targets), parameters, make_tiles, lambda start: []))
    else:
        for work in (prepare, parameters, make_tiles, prepare_targets):
            work(meta)
        whole = [lax.all_gather(part, AXES, axis=0, tiled=True) for part in shards_in]
        whole = [
            part.reshape(-1, width)
            for part, width in zip(whole, (128, 128, 64, 32, 32, 32, 32))
        ]
        first_packs = [part[: part.shape[0] // 2] for part in whole]
        second_packs = [part[part.shape[0] // 2 :] for part in whole]
    target_cells, loss_weight = state["targets"]
    tiles, tile_sides = state["tiles"][:4], state["tiles"][4:]
    norms, weight, bias, flip_weight, flip_bias = state["small"]

    eight = (8, 256)
    taps_out = kept(TAPS_OUT) if packed else []
    unpack_scratch = list(PACK_SCRATCH) if packed else []

    out = call(
        functools.partial(first_kernel, rows, packed),
        [meta, *tiles, *tile_sides, *first_packs[:4]],
        kept([*wide, eight]) + taps_out,
        bands + unpack_scratch,
        smem=1,
    )
    firsts = out[0:4]
    first_taps = out[5:] if packed else first_packs
    if packed:
        second_packs = rest(firsts[0].value)

    crosses = [[None] * 4, [None] * 4]
    norm_crosses = [[None] * 4, [None] * 4]
    natural = [(9 * CHANNELS[b], CHANNELS[b]) for b in range(4)]

    def cross(which, branch):
        def work(start):
            values = (
                (
                    tiles[branch],
                    tile_sides[branch],
                    normed_grads[branch],
                    firsts[branch],
                    first_stat,
                    own_first,
                )
                if which == 0
                else (
                    hidden[branch],
                    hidden_sides[branch],
                    join_grads[branch],
                    seconds[branch],
                    second_stat,
                    own_second,
                )
            )
            (crosses[which][branch],) = call(
                functools.partial(cross_kernel, rows, counts, devices, branch, 1 - which, which),
                [after(meta, start), *values],
                kept([natural[branch]]),
                [bands[branch]],
                smem=1,
            )
            return [crosses[which][branch].value]

        return work

    def norm_cross(which, branch):
        def work(start):
            values = (
                (tiles[branch], tile_sides[branch], firsts[branch], first_stat)
                if which == 0
                else (hidden[branch], hidden_sides[branch], seconds[branch], second_stat)
            )
            norm_crosses[which][branch] = call(
                functools.partial(cross_norm_kernel, rows, counts, branch, 1 - which, which),
                [after(meta, start), *values],
                kept([natural[branch], (9 * CHANNELS[branch], 8)]),
                [bands[branch]],
                smem=1,
            )
            return [norm_crosses[which][branch][0].value]

        return work

    def combine(which, sums, mixers, start):
        return call(
            functools.partial(combine_kernel, counts, devices, packed, which),
            [
                after(meta, start),
                *crosses[which],
                *[part[0] for part in norm_crosses[which]],
                *[part[1] for part in norm_crosses[which]],
                (first_stat, second_stat)[which],
                (own_first, own_second)[which],
                sums,
                norms,
                *mixers,
            ],
            kept([(8, SHARD, 128)] * 2) if packed else list(TAPS_OUT[:4]),
            [*STAGE, *PACK_SCRATCH],
            smem=1,
        )

    flip_firsts, flip_seconds = [None] * 4, [None] * 4

    def flip_first(branch):
        def work(start):
            (flip_firsts[branch],) = call(
                functools.partial(first_flip_kernel, rows, branch),
                [after(meta, start), tiles[branch], tile_sides[branch], first_taps[3 - branch]],
                kept([wide[branch]]),
                [bands[branch]],
                smem=1,
            )
            return [flip_firsts[branch].value]

        return work

    def second_bands(start):
        state["second"] = call(
            functools.partial(band_kernel, packed),
            [after(meta, start), *second_packs[:4]],
            taps_out + kept(bands),
            unpack_scratch,
            smem=1,
        )
        return [state["second"][-1].value]

    def turned_bands(start):
        state["turned"] = call(
            turned_kernel, [after(meta, start), *(state["second"] if packed else second_packs)[:4]], kept(bands), smem=1, cost=2
        )
        return [state["turned"][0].value]

    order = [1 << i for i in range(devices.bit_length() - 1)]
    first_stat = total_sum(
        out[4],
        [flip_first(1), second_bands, None, flip_first(0)],
        [*order[1:], 1] if packed else None,
    )
    second_taps = state["second"][:7] if packed else second_packs

    out = call(
        functools.partial(second_kernel, rows, counts, (1, 2, 3)),
        [meta, *firsts[1:], first_stat, norms, *state["second"][-3:]],
        kept([*inner[1:], eight, *wide[1:], *sides_of(wide)[1:]]),
        smem=1,
    )
    seconds, hidden, hidden_sides = ([None, *part] for part in (out[0:3], out[4:7], out[7:10]))
    low_sums = out[3]

    def second_top(start):
        seconds[0], state["top"], hidden[0], hidden_sides[0] = call(
            functools.partial(second_kernel, rows, counts, (0,)),
            [after(meta, start), firsts[0], first_stat, norms, state["second"][-4]],
            kept([inner[0], eight, wide[0], sides_of(wide)[0]]),
            smem=1,
        )
        return [seconds[0].value]

    unites = [*first_taps[4:7], *second_taps[4:7]]
    first_taps, second_taps = first_taps[:4], second_taps[:4]

    def flip_second(branch):
        def work(start):
            (flip_seconds[branch],) = call(
                functools.partial(second_flip_kernel, rows, counts, branch),
                [
                    after(meta, start),
                    flip_firsts[branch],
                    first_stat,
                    norms,
                    second_taps[3 - branch],
                ],
                kept([inner[branch]]),
                [wide[branch], bands[branch], sides_of(wide)[branch]],
                smem=1,
            )
            return [flip_seconds[branch].value]

        return work

    second_stat = total_sum(
        low_sums,
        [
            None,
            norm_cross(0, 1),
            norm_cross(0, 2),
            norm_cross(0, 3),
            second_top,
        ],
    )

    out = call(
        functools.partial(third_kernel, rows, counts),
        [*seconds[1:], *tiles[1:], second_stat, norms, *unites, state["top"]],
        kept([*inner[1:], eight]),
    )
    mixes = out[0:3]
    mix_stat = total_sum(
        out[3],
        [
            None,
            norm_cross(1, 1),
            norm_cross(1, 2),
            norm_cross(1, 3),
            norm_cross(0, 0),
        ],
    )

    denominator = float(counts[0] * joints)
    out = call(
        functools.partial(loss_kernel, rows, counts, denominator),
        [
            seconds[0],
            tiles[0],
            second_stat,
            *mixes,
            mix_stat,
            norms,
            weight,
            bias,
            target_cells,
            loss_weight,
        ],
        kept(
            [inner[0], *inner[1:], (16, 256), inner[0], eight, inner[0], inner[0], eight]
        ),
    )
    heat, pre_sums, head_part = out[0], out[1:4], out[4]
    join_zero, zero_sums, united, heat_grad, second_stat = out[5:10]
    own_second, edges = zero_sums, None
    join_grads = [join_zero]

    def top_edges_out(start):
        nonlocal edges
        edges = call(
            functools.partial(top_edge_kernel, rows),
            [after(meta, start), join_zero, seconds[0]],
            kept([(64, 256)] * 2),
            smem=1,
        )
        return [edges[0].value]

    def edge_near(start):
        near, far = lax.optimization_barrier((edges[0].value, edges[1].value, start))[:2]
        state["edges"] = swap_near(near, far)
        return [state["edges"][1]]

    def edge_far(start):
        near, relay = state["edges"]
        state["edges"] = kept([near, pass_on(after(relay, start))])
        return []

    def edge_done(start):
        return [part.value for part in state["edges"]]

    def head_grads(start):
        (state["head"],) = call(
            head_kernel, [after(meta, start), united, heat_grad], kept([eight]), smem=1
        )
        return [state["head"].value]

    head_sums = total_sum(
        head_part,
        [
            top_edges_out,
            works(edge_near, head_grads),
            works(edge_far, norm_cross(1, 0)),
            turned_bands,
            works(edge_done, cross(1, 0)),
        ],
    )
    top_edges = state["edges"]

    def back_top(start):
        state["back"] = call(
            functools.partial(back_top_kernel, rows, counts),
            [
                after(meta, start),
                join_zero,
                seconds[0],
                firsts[0],
                state["turned"][0],
                *top_edges,
                second_stat,
                head_sums,
                first_stat,
                norms,
            ],
            kept([inner[0], eight]),
            [wide[0], sides_of(wide)[0]],
            smem=1,
        )
        return [state["back"][0].value]

    out = call(
        functools.partial(join_kernel, rows, counts),
        [
            meta,
            *pre_sums,
            *mixes,
            *seconds[1:],
            *tiles[1:],
            zero_sums,
            state["head"],
            second_stat,
            mix_stat,
            head_sums,
            norms,
            *unites,
        ],
        kept([*inner[1:], *inner[1:], (16, 256), (256, 256), (256, 256)]),
        smem=1,
    )
    join_grads = [join_zero, *out[0:3]]
    mixed_grads, edges = out[3:6], out[7:9]

    def mixers(start):
        state["mixers"] = call(
            functools.partial(mixer_kernel, rows, counts),
            [after(meta, start), *mixed_grads, *seconds[1:], *tiles[1:], second_stat, norms],
            kept([(CHANNELS[b] // 2, C0) for b in range(1, 4)] * 2),
            smem=1,
        )
        return [state["mixers"][0].value]

    own_second = out[6]
    second_sums = total_sum(
        own_second,
        [
            None,
            works(edge_near, mixers, cross(1, 2)),
            works(edge_far, cross(1, 3)),
            cross(1, 1),
            works(edge_done, back_top),
        ],
    )
    first_mixers, second_mixers = state["mixers"][:3], state["mixers"][3:]

    out = call(
        functools.partial(back_second_kernel, rows, counts),
        [
            meta,
            *join_grads[1:],
            *seconds[1:],
            *firsts[1:],
            *state["turned"][1:],
            *state["edges"],
            second_stat,
            second_sums,
            first_stat,
            norms,
            *state["back"],
        ],
        kept([*inner[1:], eight, (128, 256), (128, 256)]),
        wide[1:] + sides_of(wide)[1:],
        smem=1,
    )
    normed_grads, edges = [state["back"][0], *out[0:3]], out[4:6]

    def second_packs_work(start):
        state["packs"] = combine(1, second_sums, second_mixers, start)
        return [state["packs"][0].value] if packed else [state["packs"][0]]

    def swap_second(start):
        state["far"] = exchange(after(state["packs"][1].value, start), 1)
        return [state["far"]]

    own_first = out[3]
    first_sums = total_sum(
        own_first,
        [
            None,
            second_packs_work,
            cross(0, 0),
            works(edge_near, cross(0, 1)),
            works(*[swap_second] * packed, cross(0, 2), cross(0, 3)),
        ],
    )
    if packed:
        far_second = state["far"]
        first_kernels = combine(0, first_sums, first_mixers, first_sums.value)
    else:
        second_kernels = state["packs"]
        first_kernels = combine(0, first_sums, first_mixers, first_sums.value)
        edge_far(first_sums.value)

    def back_first(start):
        state["source"] = call(
            functools.partial(back_first_kernel, rows, counts),
            [
                after(meta, start),
                *normed_grads,
                *firsts,
                *join_grads,
                *first_taps,
                *state["edges"],
                first_stat,
                first_sums,
                norms,
            ],
            [value.shape for value in inputs],
            wide + sides_of(wide) + bands,
            limit=14,
            smem=1,
        )
        return [state["source"][0]]

    def flip_last(start):
        (state["heat"],) = call(
            functools.partial(flip_kernel, rows, counts),
            [
                *flip_seconds,
                *tiles,
                second_stat,
                *unites,
                mix_stat,
                norms,
                flip_weight,
                Kept(after(flip_bias.value, start)),
                heat,
            ],
            [targets.shape],
            [(cells[0], 128)] * 2,
        )
        return [state["heat"]]

    def finish(start):
        state["finish"] = call(
            finish_kernel,
            [Kept(after(first_sums.value, start)), second_sums, head_sums],
            [(9, 128), (9, 128), (1, 1), (joints, C0), (1, joints)],
            limit=4,
        )
        return [state["finish"][0]]

    if packed:
        far_first = exchange(first_kernels[1].value, 1)
        edge_far(first_kernels[1].value)
        shapes = [(4, 2, last - first, 128) for first, last in CHUNKS]
        parts = call(
            add_cores,
            [first_kernels[0], state["packs"][0], Kept(far_first), Kept(far_second)],
            kept(shapes * 2),
        )
        first_flips = works(
            flip_first(2), flip_first(3), flip_second(0), flip_second(1), flip_second(2)
        )
        parts = scatter_step(parts, 0, works(first_flips, edge_done))
        parts = scatter_step(parts, 1, works(flip_second(3), flip_last))
        keep, send = scatter_step(parts, 2, finish, meta)
        far = Kept(after(exchange(send.value, 16), *back_first(send.value)))
        out = call(
            add_shard,
            [keep, far],
            [(ROWS_THREE, 128), (ROWS_TWO, 128), (ROWS_ONE, 128), (5, 128), (1, 64), (1, 128), (2, 128)],
        )
        shards = [part.reshape(-1)[:size] for part, size in zip(out, sizes)]
    else:
        rest_first = [flip_first(branch) for branch in (2, 3)]
        rest_second = [flip_second(branch) for branch in range(4)]
        for work in (back_first, *rest_first, *rest_second, flip_last, finish):
            work(first_sums.value)
        first_mixers, second_mixers = (
            [part.value for part in parts] for parts in (first_mixers, second_mixers)
        )
        flat = [
            jnp.concatenate([one.reshape(-1), two.reshape(-1)])
            for one, two in zip([*first_kernels, *first_mixers], [*second_kernels, *second_mixers])
        ]
        shards = [lax.psum_scatter(part, AXES, scatter_dimension=0, tiled=True) for part in flat]

    gain_grad, shift_grad, loss, head_grad, bias_grad = state["finish"]
    return (
        loss[0, 0],
        state["heat"],
        *state["source"],
        shards[3],
        shards[2],
        shards[1],
        shards[0],
        *shards[4:7],
        gain_grad.reshape(-1)[: norm_gain.shape[0]],
        shift_grad.reshape(-1)[: norm_shift.shape[0]],
        jnp.transpose(head_grad),
        bias_grad[0],
    )


def solution(mesh):
    rows = P("dp", "space", None)
    shard = P(("dp", "space"))
    heat = P("dp", None, "space", None)
    return jax.shard_map(
        body,
        mesh=mesh,
        in_specs=(*[rows] * 4, *[shard] * 7, *[P()] * 4, heat, rows, P("dp"), P()),
        out_specs=(P(), heat, *[rows] * 4, *[shard] * 7, *[P()] * 4),
        check_vma=False,
    )
```

```python
import functools

import jax
import jax.numpy as jnp
import numpy as np
from jax import lax
from jax.experimental import pallas as pl
from jax.experimental.pallas import tpu as pltpu
from jax.sharding import PartitionSpec as P

C0 = 32
CHANNELS = (32, 64, 128, 256)
SIDES = (256, 128, 256, 512)
AXES = ("dp", "space")
epsilon = 1e-05
f32 = jnp.float32
high = lax.Precision.HIGH


def dot_nn(left, right):
    return lax.dot_general(left, right, (((1,), (0,)), ((), ())), precision=high, preferred_element_type=f32)


def dot_nt(left, right):
    return lax.dot_general(left, right, (((1,), (1,)), ((), ())), precision=high, preferred_element_type=f32)


def dot_tn(left, right):
    return lax.dot_general(left, right, (((0,), (0,)), ((), ())), precision=high, preferred_element_type=f32)


def sigmoid(value):
    return 1.0 / (1.0 + jnp.exp(-value))


def silu(value):
    return value * sigmoid(value)


def silu_slope(value):
    sigma = sigmoid(value)
    return sigma * (1.0 + value * (1.0 - sigma))


def fold(row, channels):
    step = channels
    while step < 256:
        row = row + pltpu.roll(row, step, 1)
        step = 2 * step
    return row


def column_sum(value):
    return jnp.sum(value, axis=0, keepdims=True)


def moments(sums, channels, count):
    mean = fold(sums[0:1], channels) / count
    square = fold(sums[1:2], channels) / count
    return mean, lax.rsqrt(square - mean * mean + epsilon)


def affine(stats, gain, shift):
    scale = stats[1] * gain
    return scale, shift - stats[0] * scale


def load_rows(ref, first, count):
    lanes = ref.shape[2]
    return ref[:, first * 16 : (first + count) * 16, :].reshape(2 * count * 16, lanes)


def group_index(rows):
    return lax.broadcasted_iota(jnp.int32, (rows, 128), 0) % 16


def side_columns(value, channels):
    rows = value.shape[0]
    group = group_index(rows)
    lane = lax.broadcasted_iota(jnp.int32, (rows, 128), 1)

    def before(part):
        return jnp.where(group == 0, 0.0, pltpu.roll(part, 1, 0))

    def after(part):
        return jnp.where(group == 15, 0.0, pltpu.roll(part, rows - 1, 0))

    low, upper = value[:, :128], value[:, 128:]
    if channels == 256:
        return jnp.concatenate([before(low), before(upper), after(low), after(upper)], axis=1)
    if channels == 128:
        return jnp.concatenate([before(upper), after(low)], axis=1)
    first, last = after(low), before(upper)
    ends = jnp.where(lane < channels, first, jnp.where(lane >= 128 - channels, last, 0.0))
    if channels == 64:
        return ends
    first, last = pltpu.roll(first, channels, 1), pltpu.roll(last, 128 - channels, 1)
    middle = jnp.where(lane // channels == 1, first, jnp.where(lane // channels == 2, last, 0.0))
    return jnp.concatenate([ends, middle], axis=1)


def build_sides(source, side, channels):
    rows = source.shape[1]
    for image in range(2):
        side[image] = side_columns(source[image], channels)


def patches(branch, source, side, count, offset=0):
    parts = []
    for tap_row in range(3):
        parts.append(load_rows(source, tap_row + offset, count))
        if branch:
            parts.append(load_rows(side, tap_row + offset, count))
    if branch == 0:
        sides = [load_rows(side, tap_row + offset, count) for tap_row in range(3)]
        parts += [sides[0][:, :128] + sides[1][:, 128:], sides[2][:, :128]]
    return jnp.concatenate(parts, axis=1)


def band_row(branch, tap_row, place):
    channels, side = CHANNELS[branch], SIDES[branch]
    if branch == 0:
        if 0 <= place < 8:
            return tap_row * 256 + place * channels
        return ((768, 864), (800, 832), (896, 992))[tap_row][place < 0]
    base = tap_row * (256 + side)
    if place < 0:
        return base + 256 + (0 if channels >= 128 else 128 - channels)
    if place >= 256 // channels:
        return base + 256 + (side // 2 if channels >= 128 else 0)
    return base + place * channels


def build_band(band, tap, branch, offset):
    channels = CHANNELS[branch]
    groups = 256 // channels
    side = SIDES[branch]
    height = 256 + side
    if channels < 256:
        band[:, offset : offset + 256] = jnp.zeros((band.shape[0], 256), f32)
    for tap_row in range(3):
        for tap_col in range(3):
            matrix = tap(tap_row, tap_col)
            for out in range(groups):
                row = band_row(branch, tap_row, out + tap_col - 1)
                start = offset + out * channels
                band[row : row + channels, start : start + channels] = matrix


def collect_band(product, branch, emit):
    channels = CHANNELS[branch]
    for tap_row in range(3):
        for tap_col in range(3):
            total = None
            for out in range(256 // channels):
                row = band_row(branch, tap_row, out + tap_col - 1)
                start = out * channels
                if channels >= 128:
                    block = product[row : row + channels, start : start + channels]
                else:
                    tile = start // 128 * 128
                    block = product[row : row + channels, tile : tile + 128]
                    inner = start - tile
                    if inner:
                        block = pltpu.roll(block, 128 - inner, 1)
                total = block if total is None else total + block
            emit(tap_row, tap_col, total[:, :channels])


def tap_reader(ref, branch):
    channels = CHANNELS[branch]
    if channels == 256:

        def tap(tap_row, tap_col):
            first = (3 * tap_row + tap_col) * 512
            return jnp.concatenate(
                [ref[pl.ds(first, 256, stride=2), :], ref[pl.ds(first + 1, 256, stride=2), :]],
                axis=1,
            )

        return tap

    def tap(tap_row, tap_col):
        first = (3 * tap_row + tap_col) * channels
        return ref[first : first + channels, :]

    return tap


def tap_writer(ref, branch):
    channels = CHANNELS[branch]

    def emit(tap_row, tap_col, value):
        place = 3 * tap_row + tap_col
        if channels == 256:
            ref[pl.ds(place * 512, 256, stride=2), :] = value[:, :128]
            ref[pl.ds(place * 512 + 1, 256, stride=2), :] = value[:, 128:]
        else:
            ref[place * channels : (place + 1) * channels, :] = value

    return emit


SHARD = 392
ROWS_THREE, ROWS_TWO, ROWS_ONE = 288, 72, 18
PER_ZERO, PER_UNITE = 18, (2, 4, 8)
CHUNKS = ((0, 152), (152, 272), (272, 392))
STEPS = ((8, 4, 2), (4, 2, 8), (2, 8, 4))
TAPS_OUT = ((4624, 128), (1152, 128), (576, 64), (288, 32), (32, 32), (64, 32), (128, 32))
PACK_SCRATCH = ((16, 24, 128), (16, 8, 128), (288, 128))
STAGE = ((4624, 128), (1152, 128), (576, 64), (288, 32), (512, 32))


def partner(me, core, place, bits):
    return me ^ (core + sum(bit for i, bit in enumerate(bits) if place >> i & 1))


def shard_parts(device, three, two, one, zero):
    start = device * ROWS_THREE
    return (
        ((0, 152, three.at[pl.ds(pl.multiple_of(start, 8), 152), :]),),
        ((152, 272, three.at[pl.ds(pl.multiple_of(start + 152, 8), 120), :]),),
        (
            (272, 288, three.at[pl.ds(pl.multiple_of(start + 272, 8), 16), :]),
            (288, 360, two.at[pl.ds(pl.multiple_of(device * ROWS_TWO, 8), ROWS_TWO), :]),
            (360, 384, one.at[device]),
            (384, 392, zero.at[device]),
        ),
    )


def unpack_taps(me, packs, taps, scratch):
    three, two, one, zero = taps[:4]
    part_one, part_zero, flat_one = scratch
    for core in range(2):
        for place in range(8):
            for chunk in range(3):
                device = partner(me, core, place, STEPS[chunk])
                parts = shard_parts(device, three, two, part_one, part_zero)[chunk]
                for first, last, ref in parts:
                    ref[...] = packs[core][place, first:last]
    for device in range(16):
        flat_one[device * ROWS_ONE : (device + 1) * ROWS_ONE, :] = part_one[device, 0:ROWS_ONE]
    one[...] = flat_one[...].reshape(one.shape)
    narrow = part_zero[...].reshape(128, 128).reshape(512, 32)
    for device in range(16):
        first = device * 32
        for ref, height in zip(taps[3:7], (PER_ZERO, *PER_UNITE)):
            ref[device * height : (device + 1) * height, :] = narrow[first : first + height]
            first += height


def pack_grads(me, stage, unite_grads, packs, scratch):
    three, two, one, zero, narrow = stage
    part_one, part_zero, flat_one = scratch
    flat_one[...] = one[...].reshape(flat_one.shape)
    for device in range(16):
        part_one[device, 0:ROWS_ONE] = flat_one[device * ROWS_ONE : (device + 1) * ROWS_ONE, :]
        part_one[device, ROWS_ONE:24] = jnp.zeros((24 - ROWS_ONE, 128), f32)
        first = device * 32
        for ref, height in zip((zero, *unite_grads), (PER_ZERO, *PER_UNITE)):
            narrow[first : first + height, :] = ref[device * height : (device + 1) * height, :]
            first += height
    part_zero[...] = narrow[...].reshape(128, 128).reshape(16, 8, 128)
    for core in range(2):
        for place in range(8):
            for chunk in range(3):
                device = partner(me, core, place, STEPS[chunk][::-1])
                parts = shard_parts(device, three, two, part_one, part_zero)[chunk]
                for first, last, ref in parts:
                    packs[core][place, first:last] = ref[...]


def split_shard(meta, shard, other, *outs):
    second = meta[3] == 1
    for out, (first, last) in zip(outs, CHUNKS):
        own, far = shard[first:last], other[first:last]
        out[0, 0] = jnp.where(second, far, own)
        out[0, 1] = jnp.where(second, own, far)


def join_chunks(*refs):
    held, received, outs = split_refs(refs, 3, 3, 3)
    for chunk in range(3):
        count = held[chunk].shape[0]
        outs[chunk][0:count] = held[chunk][...]
        outs[chunk][count : 2 * count] = received[chunk][...]


def join_apart(*refs):
    held, received, first, second = split_refs(refs, 3, 3, 3, 3)
    for chunk in range(3):
        count = held[chunk].shape[0]
        for half, outs in ((0, first), (1, second)):
            outs[chunk][0:count] = held[chunk][:, half]
            outs[chunk][count : 2 * count] = received[chunk][:, half]


def join_whole(*refs):
    held, received, out = split_refs(refs, 3, 3, 1)
    for chunk, (first, last) in enumerate(CHUNKS):
        count = held[chunk].shape[0]
        out[0][0:count, first:last] = held[chunk][...]
        out[0][count : 2 * count, first:last] = received[chunk][...]


def add_received(*refs):
    held, received, low, high = split_refs(refs, 3, 3, 3, 3)
    for chunk in range(3):
        half = held[chunk].shape[0] // 2
        low[chunk][...] = held[chunk][0:half] + received[chunk][0:half]
        high[chunk][...] = held[chunk][half:] + received[chunk][half:]


def add_cores(*refs):
    keeps, received, low, high = split_refs(refs, 2, 2, 3, 3)
    for chunk, (first, last) in enumerate(CHUNKS):
        for half in range(2):
            low[chunk][:, half] = keeps[half][0:4, first:last] + received[half][0:4, first:last]
            high[chunk][:, half] = keeps[half][4:8, first:last] + received[half][4:8, first:last]


def add_last(meta, *refs):
    held, received, keep, send = split_refs(refs, 3, 3, 1, 1)
    second = meta[3] == 1
    for chunk, (first, last) in enumerate(CHUNKS):
        total = held[chunk][0] + received[chunk][0]
        keep[0][first:last, :] = jnp.where(second, total[1], total[0])
        send[0][first:last, :] = jnp.where(second, total[0], total[1])


def add_shard(keep, received, *outs):
    value = keep[...] + received[...]
    first = 0
    for ref in outs[:3]:
        last = first + ref.shape[0]
        ref[...] = value[first:last]
        first = last
    tail = SHARD - 8
    outs[3][...] = value[tail : tail + 5]
    outs[4][...] = value[tail + 4 : tail + 5, 64:]
    outs[5][...] = value[tail + 5 : tail + 6]
    outs[6][...] = value[tail + 6 : tail + 8]


def mirrored(tap):
    return lambda tap_row, tap_col: tap(tap_row, 2 - tap_col)


def turned(tap):
    return lambda tap_row, tap_col: jnp.transpose(tap(2 - tap_row, 2 - tap_col))


def mask_ends(value, rows, flags):
    place = lax.broadcasted_iota(jnp.int32, value.shape, 0) // 16 % (rows + 2)
    outside = ((place == 0) & (flags[0] == 0)) | ((place == rows + 1) & (flags[1] == 0))
    return jnp.where(outside, 0.0, value)


def mix_matrix(unite, branch):
    channels = CHANNELS[branch]
    groups = 256 // channels
    wide = jnp.concatenate([unite] * 8, axis=1)
    lane = lax.broadcasted_iota(jnp.int32, wide.shape, 1)
    span = 256 // groups
    return jnp.concatenate(
        [jnp.where(lane // span == place, wide, 0.0) for place in range(groups)], axis=0
    )


def split_refs(refs, *counts):
    out, first = [], 0
    for count in counts:
        out.append(refs[first : first + count])
        first += count
    assert first == len(refs)
    return out


class Kept:
    def __init__(self, value):
        self.value = value


def kept(values):
    return [Kept(value) for value in values]


def call(kernel, ins, outs, scratch=(), smem=0, limit=10, cost=0.01):
    specs = [pl.BlockSpec(memory_space=pltpu.SMEM)] * smem + [
        pl.BlockSpec(memory_space=pltpu.VMEM)
    ] * (len(ins) - smem)
    ins = ins[:smem] + [
        pltpu.with_memory_space_constraint(x.value, pltpu.VMEM)
        if isinstance(x, Kept)
        else pltpu.with_memory_space_constraint(x, pltpu.HBM)
        for x in ins[smem:]
    ]
    shapes = [pltpu.VMEM(x.value, f32) if isinstance(x, Kept) else pltpu.HBM(x, f32) for x in outs]
    results = pl.pallas_call(
        kernel,
        in_specs=specs,
        out_specs=[pl.BlockSpec(memory_space=pltpu.VMEM)] * len(outs),
        out_shape=shapes,
        scratch_shapes=[pltpu.VMEM(shape, f32) for shape in scratch],
        compiler_params=pltpu.CompilerParams(vmem_limit_bytes=limit * 2**20),
        cost_estimate=pl.CostEstimate(
            flops=int(cost * 1.1e9), bytes_accessed=int(cost * 3.0e6), transcendentals=0
        ),
    )(*ins)
    return [Kept(y) if isinstance(x, Kept) else y for x, y in zip(outs, results)]


def band_shape(branch, width):
    return (1024 if branch == 0 else 3 * (256 + SIDES[branch]), width)


def swap_blocks(parts):
    rows = parts[0].shape[0]
    group = lax.broadcasted_iota(jnp.int32, (rows, 128), 1) // 8
    step = 1
    while step < 16:
        high = (group & step) != 0
        parts = [
            jnp.where(high, parts[i], pltpu.roll(parts[i - step], 128 - 8 * step, 1))
            if i & step
            else jnp.where(high, pltpu.roll(parts[i + step], 8 * step, 1), parts[i])
            for i in range(16)
        ]
        step = 2 * step
    return parts


def joint_matrix():
    source = lax.broadcasted_iota(jnp.int32, (256, 256), 0)
    lane = lax.broadcasted_iota(jnp.int32, (256, 256), 1)
    matches = (source // 8 == lane % C0) & (source % 8 == lane // C0) & (source < 136)
    return jnp.where(matches, 1.0, 0.0)


def shift_group(value, group):
    return pltpu.roll(value, 128 - 8 * group, 1) if group else value


def parameter_kernel(gain, shift, weight, bias, flip, *outs):
    norms, weight_out, bias_out, flip_weight, flip_bias = outs
    weight = jnp.transpose(weight[...])
    for base, ref in ((0, gain), (11, shift)):
        offset = 0
        line = base
        sizes = [channels for channels in CHANNELS for _ in range(2)] + [C0] * 3
        for channels in sizes:
            part = ref[0:1, offset : offset + channels]
            norms[line : line + 1, :] = jnp.concatenate([part] * (256 // channels), axis=1)
            offset += channels
            line += 1
    joints = weight.shape[1]
    source = lax.broadcasted_iota(jnp.int32, (joints, joints), 0)
    moved = jnp.where(source == flip[...], 1.0, 0.0)
    for matrix, row, matrix_out, row_out in (
        (weight, bias[...], weight_out, bias_out),
        (
            jnp.dot(weight, moved, precision=lax.Precision.HIGHEST),
            jnp.dot(bias[...], moved, precision=lax.Precision.HIGHEST),
            flip_weight,
            flip_bias,
        ),
    ):
        matrix_out[...] = jnp.zeros((C0, C0), f32)
        matrix_out[:, 0:joints] = matrix
        row_out[...] = jnp.zeros((1, 256), f32)
        for place in range(8):
            row_out[0:1, C0 * place : C0 * place + joints] = row


def target_kernel(people, targets, mask, target_out, mask_out, scratch):
    lines = 2 * targets.shape[2]
    parts = swap_blocks([targets[:, j].reshape(lines, 128) for j in range(16)])
    last = targets[:, 16].reshape(lines, 128)
    cells = mask[...].reshape(lines, 128).astype(f32)
    lane = lax.broadcasted_iota(jnp.int32, (lines, 128), 1)
    tails = [
        jnp.where(lane < 8, shift_group(last, group), pltpu.roll(shift_group(cells, group), 8, 1))
        for group in range(16)
    ]
    whole = jnp.concatenate(
        [jnp.concatenate([part, tail], axis=1) for part, tail in zip(parts, tails)], axis=0
    )
    source = lax.broadcasted_iota(jnp.int32, (256, 256), 0)
    target_lane = lax.broadcasted_iota(jnp.int32, (256, 256), 1)
    spread = jnp.where((source >= 136) & (source < 144) & (source - 136 == target_lane // C0), 1.0, 0.0)
    target_rows = dot_nn(whole, joint_matrix())
    mask_rows = dot_nn(whole, spread)
    first_image = lax.broadcasted_iota(jnp.int32, (lines, 256), 0) < lines // 2
    share = jnp.where(first_image, people[0].astype(f32), people[1].astype(f32))
    for value, ref in ((target_rows, target_out), (mask_rows, mask_out)):
        for part in range(2):
            for group in range(16):
                span = slice(group * lines, (group + 1) * lines)
                block = value[span, 128 * part : 128 * part + 128]
                if ref is mask_out:
                    block = block / share[:, :128]
                scratch[pl.ds(group, lines, stride=16), :] = block
            ref[:, 128 * part : 128 * part + 128] = scratch[0 : ref.shape[0]]


def tile_kernel(rows, meta, *refs):
    xs, near, far, tiles, sides = split_refs(refs, 4, 1, 1, 4, 4)
    odd = meta[4] == 1
    for branch in range(4):
        count = rows[branch]
        tile = tiles[branch]
        for image in range(2):
            one, two = (ref[0][image, 2 * branch : 2 * branch + 2, :] for ref in (near, far))
            for value, first, extent in (
                (jnp.where(odd, one, two), 0, 2),
                (xs[branch][image], 2, count),
                (jnp.where(odd, two, one), count + 2, 2),
            ):
                tile[image, first * 16 : (first + extent) * 16, :] = value.reshape(extent * 16, 256)
        build_sides(tile, sides[branch], CHANNELS[branch])


def first_kernel(rows, packed, meta, *refs):
    tiles, sides, packs, mains, sums, taps, bands, scratch = split_refs(
        refs, 4, 4, 2 if packed else 4, 4, 1, 7 * packed, 4, 3 * packed
    )
    sums = sums[0]
    if packed:
        unpack_taps(meta[2], packs, taps, scratch)
    else:
        taps = packs
    for branch in range(4):
        count, band = rows[branch], bands[branch]
        build_band(band, tap_reader(taps[3 - branch], branch), branch, 0)
        out = dot_nn(patches(branch, tiles[branch], sides[branch], count + 2), band[...])
        mains[branch][...] = out.reshape(2, (count + 2) * 16, 256)
        inner = load_rows(mains[branch], 1, count)
        sums[2 * branch : 2 * branch + 1, :] = column_sum(inner)
        sums[2 * branch + 1 : 2 * branch + 2, :] = column_sum(inner * inner)


def first_flip_kernel(rows, branch, meta, tile, side, taps, out, band):
    count = rows[branch]
    build_band(band, mirrored(tap_reader(taps, branch)), branch, 0)
    value = dot_nn(patches(branch, tile, side, count + 2), band[...])
    out[...] = value.reshape(2, (count + 2) * 16, 256)


def fill_hidden(meta, firsts, stat, norms, hidden, branch, count, total):
    stats = moments(stat[2 * branch : 2 * branch + 2, :], CHANNELS[branch], total)
    scale, offset = affine(
        stats,
        norms[2 * branch : 2 * branch + 1, :],
        norms[11 + 2 * branch : 12 + 2 * branch, :],
    )
    value = load_rows(firsts[branch], 0, count + 2) * scale + offset
    value = mask_ends(silu(value), count, meta)
    hidden[branch][...] = value.reshape(2, (count + 2) * 16, 256)


def band_kernel(packed, meta, *refs):
    packs, taps, bands, scratch = split_refs(refs, 2 if packed else 4, 7 * packed, 4, 3 * packed)
    if packed:
        unpack_taps(meta[2], packs, taps, scratch)
    else:
        taps = packs
    for branch in range(4):
        build_band(bands[branch], tap_reader(taps[3 - branch], branch), branch, 0)


def turned_kernel(meta, *refs):
    taps, bands = split_refs(refs, 4, 4)
    for branch in range(4):
        build_band(bands[branch], turned(tap_reader(taps[3 - branch], branch)), branch, 0)


def second_kernel(rows, counts, branches, meta, *refs):
    each = len(branches)
    firsts, stat, norms, bands, outs, sums, hidden, sides = split_refs(
        refs, each, 1, 1, each, each, 1, each, each
    )
    sums = sums[0]
    sums[...] = jnp.zeros(sums.shape, f32)
    for i, branch in enumerate(branches):
        count, channels = rows[branch], CHANNELS[branch]
        fill_hidden(
            meta, {branch: firsts[i]}, stat[0], norms[0], {branch: hidden[i]}, branch, count, counts[branch]
        )
        build_sides(hidden[i], sides[i], channels)
        out = dot_nn(patches(branch, hidden[i], sides[i], count), bands[i][...])
        outs[i][...] = out
        sums[2 * branch : 2 * branch + 1, :] = column_sum(out)
        sums[2 * branch + 1 : 2 * branch + 2, :] = column_sum(out * out)


def second_flip_kernel(rows, counts, branch, meta, first, stat, norms, taps, out, hidden, band, side):
    count, channels = rows[branch], CHANNELS[branch]
    fill_hidden(meta, {branch: first}, stat, norms, {branch: hidden}, branch, count, counts[branch])
    build_sides(hidden, side, channels)
    build_band(band, mirrored(tap_reader(taps, branch)), branch, 0)
    out[...] = dot_nn(patches(branch, hidden, side, count), band[...])


def joined(second, tile, stat, norms, branch, count, total):
    stats = moments(stat[2 * branch : 2 * branch + 2, :], CHANNELS[branch], total)
    gain = norms[2 * branch + 1 : 2 * branch + 2, :]
    shift = norms[12 + 2 * branch : 13 + 2 * branch, :]
    scaled = (second - stats[0]) * stats[1]
    return scaled * gain + shift + load_rows(tile, 2, count), scaled, stats


def third_kernel(rows, counts, *refs):
    seconds, tiles, stat, norms, unites, top_sums, mixes, sums = split_refs(
        refs, 3, 3, 1, 1, 6, 1, 3, 1
    )
    stat, norms, sums = stat[0], norms[0], sums[0]
    for level in range(3):
        branch = level + 1
        value, _, _ = joined(
            seconds[level][...], tiles[level], stat, norms, branch, rows[branch], counts[branch]
        )
        unite = jnp.concatenate([unites[level][...], unites[3 + level][...]], axis=0)
        mixed = dot_nn(silu(value), mix_matrix(unite, branch))
        mixes[level][...] = mixed
        sums[2 * level : 2 * level + 1, :] = column_sum(mixed)
        sums[2 * level + 1 : 2 * level + 2, :] = column_sum(mixed * mixed)
    sums[6:8, :] = top_sums[0][0:2, :]


def spread_rows(value, rows, factor):
    value = value.reshape(2 * rows, 1, 16, 256)
    return jnp.broadcast_to(value, (2 * rows, factor, 16, 256)).reshape(2 * rows * factor * 16, 256)


def gather_rows(value, rows, factor):
    value = value.reshape(2 * rows // factor, factor, 16, 256)
    return jnp.sum(value, axis=1).reshape(2 * rows // factor * 16, 256)


def uniting_stats(stat, level, total):
    return moments(stat[2 * level : 2 * level + 2, :], C0, total * 2.0 ** (level + 1))


def united_sum(base, mixes, stat, norms, rows, counts):
    for level in range(3):
        stats = uniting_stats(stat, level, counts[level + 1])
        scale, offset = affine(
            stats, norms[8 + level : 9 + level, :], norms[19 + level : 20 + level, :]
        )
        base = base + spread_rows(mixes[level] * scale + offset, rows[level + 1], 2 ** (level + 1))
    return base


def head_matrix(weight):
    wide = jnp.concatenate([weight] * 8, axis=1)
    lane = lax.broadcasted_iota(jnp.int32, wide.shape, 1)
    return jnp.concatenate([jnp.where(lane // C0 == place, wide, 0.0) for place in range(8)], axis=0)


def top_edge_kernel(rows, meta, grad, second, near, far):
    odd = meta[4] == 1
    write_edges(odd, near, far, grad, 0, rows[0], 0)
    write_edges(odd, near, far, second, 0, rows[0], 32)


def loss_kernel(rows, counts, denominator, *refs):
    ins, outs = split_refs(refs, 12, 10)
    second, tile, low_stat, mix_one, mix_two, mix_three, mix_stat, norms, weight, bias, targets, mask = ins
    heat_out, sum_one, sum_two, sum_three, sums, join_grad, zero_sums, united_out, grad_out = outs[:9]
    stat = outs[9]
    stat[0:2, :] = mix_stat[6:8, :]
    stat[2:8, :] = low_stat[2:8, :]
    sums[8:16, :] = jnp.zeros((8, 256), f32)
    count = rows[0]
    join, scaled, _ = joined(second[...], tile, stat, norms, 0, count, counts[0])
    mixes = (mix_one[...], mix_two[...], mix_three[...])
    pre = united_sum(silu(join), mixes, mix_stat, norms, rows, counts)
    united = silu(pre)
    head = head_matrix(weight[...])
    heat = dot_nn(united, head) + bias[...]
    heat_out[...] = heat
    error = heat - targets[...]
    weighted = mask[...] * error
    sums[6:7, :] = column_sum(weighted * error) / denominator
    heat_grad = weighted * (2.0 / denominator)
    sums[7:8, :] = column_sum(heat_grad)
    united_out[...] = united
    grad_out[...] = heat_grad
    grad = dot_nt(heat_grad, head) * silu_slope(pre)
    join_part = grad * silu_slope(join)
    join_grad[...] = join_part
    zero_sums[0:1, :] = column_sum(join_part)
    zero_sums[1:2, :] = column_sum(join_part * scaled)
    sums[8:10, :] = zero_sums[0:2, :]
    for level, out in enumerate((sum_one, sum_two, sum_three)):
        part = gather_rows(grad, count, 2 ** (level + 1))
        out[...] = part
        stats = uniting_stats(mix_stat, level, counts[level + 1])
        normed = (mixes[level] - stats[0]) * stats[1]
        sums[2 * level : 2 * level + 1, :] = column_sum(part)
        sums[2 * level + 1 : 2 * level + 2, :] = column_sum(part * normed)


def head_kernel(meta, united, heat_grad, out):
    product = dot_tn(united[...], heat_grad[...])
    total = None
    for place in range(8):
        first = place * C0
        tile_first = first // 128 * 128
        block = product[first : first + C0, tile_first : tile_first + 128]
        if first - tile_first:
            block = pltpu.roll(block, 128 - (first - tile_first), 1)
        total = block if total is None else total + block
    out[...] = jnp.zeros(out.shape, f32)
    out[:, 0:128] = jnp.concatenate(
        [total[8 * part : 8 * part + 8, :C0] for part in range(4)], axis=1
    )


def flip_kernel(rows, counts, *refs):
    seconds, tiles, stat, unites, mix_stat, norms, weight, bias, heat, out, scratch = split_refs(
        refs, 4, 4, 1, 6, 1, 1, 1, 1, 1, 1, 2
    )
    stat, norms = stat[0], norms[0]
    mixes = []
    for branch in range(4):
        value, _, _ = joined(
            seconds[branch][...], tiles[branch], stat, norms, branch, rows[branch], counts[branch]
        )
        if branch == 0:
            base = silu(value)
        else:
            unite = jnp.concatenate([unites[branch - 1][...], unites[branch + 2][...]], axis=0)
            mixes.append(dot_nn(silu(value), mix_matrix(unite, branch)))
    pre = united_sum(base, mixes, mix_stat[0], norms, rows, counts)
    back = dot_nn(silu(pre), head_matrix(weight[0][...])) + bias[0][...]
    moved = dot_nt(0.5 * (heat[0][...] + back), joint_matrix())
    scratch[0][0 : moved.shape[0]] = moved[:, :128]
    scratch[1][0 : moved.shape[0]] = moved[:, 128:]
    lines = 2 * rows[0]
    parts = [scratch[0][pl.ds(group, lines, stride=16), :] for group in range(16)]
    lane = lax.broadcasted_iota(jnp.int32, (lines, 128), 1)
    last = None
    for group in range(16):
        tail = scratch[1][pl.ds(group, lines, stride=16), :]
        tail = pltpu.roll(tail, 8 * group, 1) if group else tail
        last = tail if last is None else jnp.where(lane // 8 == group, tail, last)
    for joint, value in enumerate([*swap_blocks(parts), last]):
        out[0][:, joint] = value.reshape(2, rows[0], 128)


def edge_place(branch, image):
    return (2 * branch + image) * 16


def write_edges(odd, near, far, value, branch, count, base):
    for image in range(2):
        place = base + edge_place(branch, image)
        start = image * count * 16
        first = value[start : start + 16]
        last = value[start + (count - 1) * 16 : start + count * 16]
        near[place : place + 16, :] = jnp.where(odd, first, last)
        far[place : place + 16, :] = jnp.where(odd, last, first)


def join_kernel(rows, counts, meta, *refs):
    sums_in, mixes, seconds, tiles, small, unites, outs = split_refs(refs, 3, 3, 3, 3, 6, 6, 9)
    zero_sums, head_grad, stat, mix_stat, head_sums, norms = small
    grads, mixed_grads, sums, near, far = outs[0:3], outs[3:6], outs[6], outs[7], outs[8]
    odd = meta[4] == 1
    sums[0:2, :] = zero_sums[0:2, :]
    sums[8:16, :] = head_grad[...]
    for level in range(3):
        branch = level + 1
        channels, count = CHANNELS[branch], rows[branch]
        total = counts[branch]
        stats = uniting_stats(mix_stat, level, total)
        gain = norms[8 + level : 9 + level, :]
        shift_sum = fold(head_sums[2 * level : 2 * level + 1, :], C0)
        gain_sum = fold(head_sums[2 * level + 1 : 2 * level + 2, :], C0)
        normed = (mixes[level][...] - stats[0]) * stats[1]
        share = 1.0 / (total * 2.0 ** (level + 1))
        mixed_grad = (gain * stats[1]) * (
            sums_in[level][...] - shift_sum * share - normed * (gain_sum * share)
        )
        mixed_grads[level][...] = mixed_grad
        value, scaled, _ = joined(
            seconds[level][...], tiles[level], stat, norms, branch, count, total
        )
        unite = jnp.concatenate([unites[level][...], unites[3 + level][...]], axis=0)
        grad = dot_nt(mixed_grad, mix_matrix(unite, branch)) * silu_slope(value)
        grads[level][...] = grad
        sums[2 * branch : 2 * branch + 1, :] = column_sum(grad)
        sums[2 * branch + 1 : 2 * branch + 2, :] = column_sum(grad * scaled)
        write_edges(odd, near, far, grad, branch, count, 0)
        write_edges(odd, near, far, seconds[level][...], branch, count, 128)


def mixer_kernel(rows, counts, meta, *refs):
    mixed_grads, seconds, tiles, stat, norms, outs = split_refs(refs, 3, 3, 3, 1, 1, 6)
    for level in range(3):
        branch = level + 1
        channels = CHANNELS[branch]
        value, _, _ = joined(
            seconds[level][...], tiles[level], stat[0], norms[0], branch, rows[branch], counts[branch]
        )
        product = dot_tn(silu(value), mixed_grads[level][...])
        mixer = None
        for place in range(8):
            row = place // (8 * channels // 256) * channels
            tile_first = place * C0 // 128 * 128
            block = product[row : row + channels, tile_first : tile_first + 128]
            inner = place * C0 - tile_first
            if inner:
                block = pltpu.roll(block, 128 - inner, 1)
            mixer = block if mixer is None else mixer + block
        outs[level][...] = mixer[: channels // 2, :C0]
        outs[3 + level][...] = mixer[channels // 2 :, :C0]


def norm_input_grad(grad, scaled, stats, gain, sums, channels, total):
    shift_sum = fold(sums[0:1, :], channels) / total
    gain_sum = fold(sums[1:2, :], channels) / total
    return (gain * stats[1]) * (grad - shift_sum - scaled * gain_sum)


def back_second_branch(
    rows, counts, branch, meta, grad, second, first, band, edges, stats_in, out, sums, wide, side
):
    stat, own, first_stat, norms = stats_in
    count, channels, total = rows[branch], CHANNELS[branch], counts[branch]
    odd = meta[4] == 1
    stats = moments(stat[2 * branch : 2 * branch + 2, :], channels, total)
    gain = norms[2 * branch + 1 : 2 * branch + 2, :]
    shift_sum = fold(own[0:1], channels) / total
    gain_sum = fold(own[1:2], channels) / total

    def input_grad(part, value):
        scaled = (value - stats[0]) * stats[1]
        return (gain * stats[1]) * (part - shift_sum - scaled * gain_sum)

    inner = input_grad(grad[...], second[...])
    wide[:, 16 : (count + 1) * 16, :] = inner.reshape(2, count * 16, 256)
    for image in range(2):
        parts = [input_grad(*edge) for edge in edges[image]]
        for value, start, flag in (
            (jnp.where(odd, parts[0], parts[1]), 0, meta[0]),
            (jnp.where(odd, parts[1], parts[0]), (count + 1) * 16, meta[1]),
        ):
            wide[image, start : start + 16, :] = jnp.where(flag == 0, 0.0, value)
    build_sides(wide, side, channels)
    hidden_grad = dot_nn(patches(branch, wide, side, count), band[...])
    first_stats = moments(first_stat[2 * branch : 2 * branch + 2, :], channels, total)
    scaled = (load_rows(first, 1, count) - first_stats[0]) * first_stats[1]
    value = (
        scaled * norms[2 * branch : 2 * branch + 1, :]
        + norms[11 + 2 * branch : 12 + 2 * branch, :]
    )
    result = hidden_grad * silu_slope(value)
    out[...] = result
    sums[2 * branch : 2 * branch + 1, :] = column_sum(result)
    sums[2 * branch + 1 : 2 * branch + 2, :] = column_sum(result * scaled)
    return result


def back_top_kernel(rows, counts, meta, *refs):
    grad, second, first, band, near, far, stat, head_sums, first_stat, norms, out, sums, wide, side = refs
    edges = [
        [(ref[at : at + 16, :], ref[32 + at : 48 + at, :]) for ref in (near, far)]
        for at in (0, 16)
    ]
    stats_in = (stat, head_sums[8:10, :], first_stat, norms)
    back_second_branch(
        rows, counts, 0, meta, grad, second, first, band, edges, stats_in, out, sums, wide, side
    )


def back_second_kernel(rows, counts, meta, *refs):
    ins, outs, wide, sides = split_refs(refs, 20, 6, 3, 3)
    grads, seconds, firsts, bands = ins[0:3], ins[3:6], ins[6:9], ins[9:12]
    near_in, far_in, stat, stat_sums, first_stat, norms, top, top_sums = ins[12:20]
    sums, near, far = outs[3:6]
    odd = meta[4] == 1
    sums[0:2, :] = top_sums[0:2, :]
    write_edges(odd, near, far, top[...], 0, rows[0], 0)
    for level in range(3):
        branch = level + 1
        places = [edge_place(branch, image) for image in range(2)]
        edges = [
            [(ref[at : at + 16, :], ref[128 + at : 144 + at, :]) for ref in (near_in, far_in)]
            for at in places
        ]
        stats_in = (stat, stat_sums[2 * branch : 2 * branch + 2, :], first_stat, norms)
        result = back_second_branch(
            rows,
            counts,
            branch,
            meta,
            grads[level],
            seconds[level],
            firsts[level],
            bands[level],
            edges,
            stats_in,
            outs[level],
            sums,
            wide[level],
            sides[level],
        )
        write_edges(odd, near, far, result, branch, rows[branch], 0)


def cross_products(rows, branch, offset, source, value, out, side, product):
    count, channels = rows[branch], CHANNELS[branch]
    product[...] = dot_tn(patches(branch, source, side, count, offset), value)

    def emit(tap_row, tap_col, block):
        place = (3 * tap_row + tap_col) * channels
        out[place : place + channels, :] = block

    collect_band(product, branch, emit)


def normalized(raw, stat, rows, counts, branch, inner):
    stats = moments(stat[2 * branch : 2 * branch + 2, :], CHANNELS[branch], counts[branch])
    value = raw[...] if inner else load_rows(raw, 1, rows[branch])
    return (value - stats[0]) * stats[1]


def sum_means(sums, branch, total):
    channels = CHANNELS[branch]
    return [fold(sums[2 * branch + i : 2 * branch + i + 1, :], channels) / total for i in range(2)]


def cross_kernel(rows, counts, devices, branch, offset, inner, meta, *refs):
    source, side, value, raw, stat, sums, out, product = refs
    shift_mean, gain_mean = sum_means(sums, branch, counts[branch] / devices)
    scaled = normalized(raw, stat, rows, counts, branch, inner)
    rest = value[...] - shift_mean - scaled * gain_mean
    cross_products(rows, branch, offset, source, rest, out, side, product)


def cross_norm_kernel(rows, counts, branch, offset, inner, meta, *refs):
    source, side, raw, stat, out, sums, product = refs
    count, channels = rows[branch], CHANNELS[branch]
    scaled = normalized(raw, stat, rows, counts, branch, inner)
    cross_products(rows, branch, offset, source, scaled, out, side, product)
    total = column_sum(patches(branch, source, side, count, offset))
    column = jnp.transpose(jnp.broadcast_to(total, (8, total.shape[1])))
    for tap_row in range(3):
        for tap_col in range(3):
            block = None
            for place in range(256 // channels):
                row = band_row(branch, tap_row, place + tap_col - 1)
                part = column[row : row + channels]
                block = part if block is None else block + part
            start = (3 * tap_row + tap_col) * channels
            sums[start : start + channels, :] = block


def combine_kernel(counts, devices, packed, which, meta, *refs):
    crosses, norm_crosses, patch_sums, ins, unite_grads, outs, stage, scratch = split_refs(
        refs, 4, 4, 4, 4, 3, 2 if packed else 4, 5, 3
    )
    stat, own_sums, grad_sums, norms = ins
    for branch in range(4):
        channels, total = CHANNELS[branch], counts[branch]
        stats = moments(stat[2 * branch : 2 * branch + 2, :], channels, total)
        line = 2 * branch + which
        scale = (norms[line : line + 1, :] * stats[1])[:, :channels]
        shift_rest, gain_rest = (
            (whole - own)[:, :channels]
            for whole, own in zip(
                sum_means(grad_sums, branch, total), sum_means(own_sums, branch, total / devices)
            )
        )
        emit = tap_writer(stage[3 - branch], branch)
        for place in range(9):
            span = slice(place * channels, (place + 1) * channels)
            value = (
                crosses[branch][span, :]
                - patch_sums[branch][span, 0:1] * shift_rest
                - norm_crosses[branch][span, :] * gain_rest
            )
            emit(place // 3, place % 3, scale * value)
    if packed:
        pack_grads(meta[2], stage, unite_grads, outs, scratch)
    else:
        for ref, value in zip(outs, stage):
            ref[...] = value[0 : ref.shape[0]]


def back_first_kernel(rows, counts, flags, *refs):
    ins, source_grads, wide, sides, bands = split_refs(refs, 21, 4, 4, 4, 4)
    normed_grads, firsts, join_grads, taps = ins[0:4], ins[4:8], ins[8:12], ins[12:16]
    near, far, first_stat, first_sums, norms = ins[16:21]
    odd = flags[4] == 1
    for branch in range(4):
        count, channels, total = rows[branch], CHANNELS[branch], counts[branch]
        stats = moments(first_stat[2 * branch : 2 * branch + 2, :], channels, total)
        gain = norms[2 * branch : 2 * branch + 1, :]
        shift_sum = fold(first_sums[2 * branch : 2 * branch + 1, :], channels) / total
        gain_sum = fold(first_sums[2 * branch + 1 : 2 * branch + 2, :], channels) / total

        def input_grad(grad, value):
            scaled = (value - stats[0]) * stats[1]
            return (gain * stats[1]) * (grad - shift_sum - scaled * gain_sum)

        inner = input_grad(normed_grads[branch][...], load_rows(firsts[branch], 1, count))
        wide[branch][:, 16 : (count + 1) * 16, :] = inner.reshape(2, count * 16, 256)
        for image in range(2):
            place = edge_place(branch, image)
            one, two = (ref[place : place + 16, :] for ref in (near, far))
            for grad, start, flag in (
                (jnp.where(odd, one, two), 0, flags[0]),
                (jnp.where(odd, two, one), (count + 1) * 16, flags[1]),
            ):
                value = input_grad(grad, firsts[branch][image, start : start + 16, :])
                wide[branch][image, start : start + 16, :] = jnp.where(flag == 0, 0.0, value)
        build_sides(wide[branch], sides[branch], channels)
        build_band(bands[branch], turned(tap_reader(taps[3 - branch], branch)), branch, 0)
        grad = dot_nn(patches(branch, wide[branch], sides[branch], count), bands[branch][...])
        grad = (grad + join_grads[branch][...]).reshape(2, count * 16, 256)
        for image in range(2):
            source_grads[branch][image] = grad[image].reshape(count, 4096)


def finish_kernel(first_sums, second_sums, head_sums, gain, shift, loss, head_weight, head_bias):
    offset = 0

    def put(sums, line, channels):
        nonlocal offset
        for ref, row in ((shift, line), (gain, line + 1)):
            value = fold(sums[row : row + 1, :], channels)
            done = 0
            while done < channels:
                place = offset + done
                width = min(channels - done, 128 - place % 128)
                ref[place // 128 : place // 128 + 1, place % 128 : place % 128 + width] = value[
                    :, done : done + width
                ]
                done += width
        offset += channels

    for branch in range(4):
        for sums in (first_sums, second_sums):
            put(sums, 2 * branch, CHANNELS[branch])
    for level in range(3):
        put(head_sums, 2 * level, C0)
    loss[...] = jnp.sum(head_sums[6:7, :], axis=1, keepdims=True)
    joints = head_bias.shape[1]
    head_bias[...] = fold(head_sums[7:8, :], C0)[:, :joints]
    total = jnp.concatenate(
        [second_sums[8:16, C0 * part : C0 * part + C0] for part in range(4)], axis=0
    )
    head_weight[...] = jnp.transpose(total)[:joints]


def device_count():
    return lax.axis_size("dp") * lax.axis_size("space")


def exchange(value, bit):
    return lax.ppermute(value, AXES, [(i, i ^ bit) for i in range(device_count())])


def total_sum(value, beside=(), order=None):
    value = value.value
    for step, bit in enumerate(order or [1 << i for i in range(device_count().bit_length() - 1)]):
        other = exchange(value, bit)
        if step < len(beside) and beside[step]:
            other = after(other, *beside[step](value))
        value = value + other
    return Kept(value)


def swap_rows(near, far):
    devices = lax.axis_size("space")
    pairs = [(i, i ^ 1) for i in range(devices)]
    others = [(i, i + 1) for i in range(1, devices - 1, 2)]
    others += [(j, i) for i, j in others]
    return lax.ppermute(near, "space", pairs), lax.ppermute(far, "space", others)


def swap_near(near, far):
    pairs = [(i, i ^ 1) for i in range(lax.axis_size("space"))]
    return lax.ppermute(near, "space", pairs), lax.ppermute(far, "space", pairs)


def pass_on(relay):
    devices = lax.axis_size("space")
    return lax.ppermute(relay, "space", [(i, (i + 2 - i % 2 * 4) % devices) for i in range(devices)])


def device_index():
    return lax.axis_index("dp") * lax.axis_size("space") + lax.axis_index("space")


def after(value, *others):
    return lax.optimization_barrier((value, *others))[0]


def swap(parts, step):
    return [Kept(exchange(part.value, STEPS[chunk][step])) for chunk, part in enumerate(parts)]


def gather_shards(meta, flat, beside):
    other = exchange(flat, 16)
    other = after(other, *beside[0](flat))
    shapes = [(1, 2, last - first, 128) for first, last in CHUNKS]
    parts = call(split_shard, [meta, flat, Kept(other)], kept(shapes), smem=1)
    shapes = [(2, *shape[1:]) for shape in shapes]
    received = swap(parts, 0)
    received[0] = Kept(after(received[0].value, *beside[1](parts[0].value)))
    parts = call(join_chunks, [*parts, *received], kept(shapes))
    shapes = [(4, *shape[2:]) for shape in shapes]
    received = swap(parts, 1)
    received[0] = Kept(after(received[0].value, *beside[2](parts[0].value)))
    parts = call(join_apart, [*parts, *received], kept(shapes * 2))
    first, second = parts[:3], parts[3:]
    received = swap(first, 2)
    received[0] = Kept(after(received[0].value, *beside[3](first[0].value)))
    (whole,) = call(join_whole, [*first, *received], kept([(8, SHARD, 128)]))
    second[0] = Kept(after(second[0].value, whole.value))
    received = swap(second, 2)

    def rest(start):
        received[0] = Kept(after(received[0].value, start))
        (whole,) = call(join_whole, [*second, *received], kept([(8, SHARD, 128)]))
        return [whole, Kept(exchange(whole.value, 1))]

    return [whole, Kept(exchange(whole.value, 1))], rest


def scatter_step(parts, step, beside, meta=None):
    received = swap(parts[3:], step)
    received[0] = Kept(after(received[0].value, *beside(parts[3].value)))
    if step == 2:
        return call(add_last, [meta, *parts[:3], *received], kept([(SHARD, 128)] * 2), smem=1)
    shapes = [(2 - step, 2, last - first, 128) for first, last in CHUNKS]
    return call(add_received, [*parts[:3], *received], kept(shapes * 2))


def body(
    branch_zero,
    branch_one,
    branch_two,
    branch_three,
    convs_zero,
    convs_one,
    convs_two,
    convs_three,
    unite_one,
    unite_two,
    unite_three,
    norm_gain,
    norm_shift,
    head_weight,
    head_bias,
    targets,
    crowd_mask,
    person_count,
    flip_order,
):
    inputs = (branch_zero, branch_one, branch_two, branch_three)
    devices = device_count()
    spaces = lax.axis_size("space")
    place = lax.axis_index("space")
    rows = tuple(value.shape[1] for value in inputs)
    counts = tuple(
        float(2 * rows[b] * 16 * (256 // CHANNELS[b]) * devices) for b in range(4)
    )
    joints = head_bias.shape[0]
    cells = [2 * rows[b] * 16 for b in range(4)]
    packed = devices == 32
    shards_in = (convs_three, convs_two, convs_one, convs_zero, unite_one, unite_two, unite_three)
    sizes = [part.shape[0] for part in shards_in]

    meta = jnp.stack(
        [
            place > 0,
            place < spaces - 1,
            device_index() & 15,
            (device_index() & 16) // 16,
            place % 2,
        ]
    ).astype(jnp.int32)

    bands = [band_shape(b, 256) for b in range(4)]
    inner = [(cells[b], 256) for b in range(4)]
    wide = [(2, (rows[b] + 2) * 16, 256) for b in range(4)]
    wider = [(2, (rows[b] + 4) * 16, 256) for b in range(4)]

    def sides_of(shapes):
        return [shape[:2] + (SIDES[b],) for b, shape in enumerate(shapes)]

    def works(*parts):
        return lambda start: sum((list(part(start)) for part in parts), [])

    state = {}

    def prepare(start):
        parts = lax.optimization_barrier((*inputs, start))[:4]
        last_rows = jnp.concatenate([value[:, -2:] for value in parts], axis=1)
        first_rows = jnp.concatenate([value[:, :2] for value in parts], axis=1)
        odd = place % 2 == 1
        state["halo"] = swap_rows(
            jnp.where(odd, first_rows, last_rows), jnp.where(odd, last_rows, first_rows)
        )
        return state["halo"]

    def prepare_targets(start):
        state["targets"] = call(
            target_kernel,
            [after(person_count, start), targets, crowd_mask],
            kept([(cells[0], 256)] * 2),
            [(cells[0] + 16, 128)],
            smem=1,
            cost=4,
        )
        return [state["targets"][0].value]

    def make_tiles(start):
        state["tiles"] = call(
            functools.partial(tile_kernel, rows),
            [after(meta, start), *inputs, *state["halo"]],
            kept([*wider, *sides_of(wider)]),
            smem=1,
        )
        return [state["tiles"][0].value]

    def parameters(start):
        state["small"] = call(
            parameter_kernel,
            [
                after(norm_gain, start)[None],
                norm_shift[None],
                jnp.transpose(head_weight),
                head_bias[None],
                flip_order[None],
            ],
            kept([(22, 256), (C0, C0), (1, 256), (C0, C0), (1, 256)]),
        )
        return [state["small"][0].value]

    if packed:
        gap = jnp.zeros(((24 - ROWS_ONE) * 128,), f32)
        flat = jnp.concatenate([*shards_in[:3], gap, *shards_in[3:]]).reshape(SHARD, 128)
        first_packs, rest = gather_shards(meta, flat, (works(prepare, prepare_targets), parameters, make_tiles, lambda start: []))
    else:
        for work in (prepare, parameters, make_tiles, prepare_targets):
            work(meta)
        whole = [lax.all_gather(part, AXES, axis=0, tiled=True) for part in shards_in]
        whole = [
            part.reshape(-1, width)
            for part, width in zip(whole, (128, 128, 64, 32, 32, 32, 32))
        ]
        first_packs = [part[: part.shape[0] // 2] for part in whole]
        second_packs = [part[part.shape[0] // 2 :] for part in whole]
    target_cells, loss_weight = state["targets"]
    tiles, tile_sides = state["tiles"][:4], state["tiles"][4:]
    norms, weight, bias, flip_weight, flip_bias = state["small"]

    eight = (8, 256)
    taps_out = kept(TAPS_OUT) if packed else []
    unpack_scratch = list(PACK_SCRATCH) if packed else []

    out = call(
        functools.partial(first_kernel, rows, packed),
        [meta, *tiles, *tile_sides, *first_packs[:4]],
        kept([*wide, eight]) + taps_out,
        bands + unpack_scratch,
        smem=1,
    )
    firsts = out[0:4]
    first_taps = out[5:] if packed else first_packs
    if packed:
        second_packs = rest(firsts[0].value)

    crosses = [[None] * 4, [None] * 4]
    norm_crosses = [[None] * 4, [None] * 4]
    natural = [(9 * CHANNELS[b], CHANNELS[b]) for b in range(4)]

    def cross(which, branch):
        def work(start):
            values = (
                (
                    tiles[branch],
                    tile_sides[branch],
                    normed_grads[branch],
                    firsts[branch],
                    first_stat,
                    own_first,
                )
                if which == 0
                else (
                    hidden[branch],
                    hidden_sides[branch],
                    join_grads[branch],
                    seconds[branch],
                    second_stat,
                    own_second,
                )
            )
            (crosses[which][branch],) = call(
                functools.partial(cross_kernel, rows, counts, devices, branch, 1 - which, which),
                [after(meta, start), *values],
                kept([natural[branch]]),
                [bands[branch]],
                smem=1,
            )
            return [crosses[which][branch].value]

        return work

    def norm_cross(which, branch):
        def work(start):
            values = (
                (tiles[branch], tile_sides[branch], firsts[branch], first_stat)
                if which == 0
                else (hidden[branch], hidden_sides[branch], seconds[branch], second_stat)
            )
            norm_crosses[which][branch] = call(
                functools.partial(cross_norm_kernel, rows, counts, branch, 1 - which, which),
                [after(meta, start), *values],
                kept([natural[branch], (9 * CHANNELS[branch], 8)]),
                [bands[branch]],
                smem=1,
            )
            return [norm_crosses[which][branch][0].value]

        return work

    def combine(which, sums, mixers, start):
        return call(
            functools.partial(combine_kernel, counts, devices, packed, which),
            [
                after(meta, start),
                *crosses[which],
                *[part[0] for part in norm_crosses[which]],
                *[part[1] for part in norm_crosses[which]],
                (first_stat, second_stat)[which],
                (own_first, own_second)[which],
                sums,
                norms,
                *mixers,
            ],
            kept([(8, SHARD, 128)] * 2) if packed else [(4608, 128), *TAPS_OUT[1:4]],
            [*STAGE, *PACK_SCRATCH],
            smem=1,
        )

    flip_firsts, flip_seconds = [None] * 4, [None] * 4

    def flip_first(branch):
        def work(start):
            (flip_firsts[branch],) = call(
                functools.partial(first_flip_kernel, rows, branch),
                [after(meta, start), tiles[branch], tile_sides[branch], first_taps[3 - branch]],
                kept([wide[branch]]),
                [bands[branch]],
                smem=1,
            )
            return [flip_firsts[branch].value]

        return work

    def second_bands(start):
        state["second"] = call(
            functools.partial(band_kernel, packed),
            [after(meta, start), *second_packs[:4]],
            taps_out + kept(bands),
            unpack_scratch,
            smem=1,
        )
        return [state["second"][-1].value]

    def turned_bands(start):
        state["turned"] = call(
            turned_kernel, [after(meta, start), *(state["second"] if packed else second_packs)[:4]], kept(bands), smem=1, cost=2
        )
        return [state["turned"][0].value]

    order = [1 << i for i in range(devices.bit_length() - 1)]
    first_stat = total_sum(
        out[4],
        [flip_first(1), second_bands, None, flip_first(0)],
        [*order[1:], 1] if packed else None,
    )
    second_taps = state["second"][:7] if packed else second_packs

    out = call(
        functools.partial(second_kernel, rows, counts, (1, 2, 3)),
        [meta, *firsts[1:], first_stat, norms, *state["second"][-3:]],
        kept([*inner[1:], eight, *wide[1:], *sides_of(wide)[1:]]),
        smem=1,
    )
    seconds, hidden, hidden_sides = ([None, *part] for part in (out[0:3], out[4:7], out[7:10]))
    low_sums = out[3]

    def second_top(start):
        seconds[0], state["top"], hidden[0], hidden_sides[0] = call(
            functools.partial(second_kernel, rows, counts, (0,)),
            [after(meta, start), firsts[0], first_stat, norms, state["second"][-4]],
            kept([inner[0], eight, wide[0], sides_of(wide)[0]]),
            smem=1,
        )
        return [seconds[0].value]

    unites = [*first_taps[4:7], *second_taps[4:7]]
    first_taps, second_taps = first_taps[:4], second_taps[:4]

    def flip_second(branch):
        def work(start):
            (flip_seconds[branch],) = call(
                functools.partial(second_flip_kernel, rows, counts, branch),
                [
                    after(meta, start),
                    flip_firsts[branch],
                    first_stat,
                    norms,
                    second_taps[3 - branch],
                ],
                kept([inner[branch]]),
                [wide[branch], bands[branch], sides_of(wide)[branch]],
                smem=1,
            )
            return [flip_seconds[branch].value]

        return work

    second_stat = total_sum(
        low_sums,
        [
            None,
            norm_cross(0, 1),
            norm_cross(0, 2),
            norm_cross(0, 3),
            second_top,
        ],
    )

    out = call(
        functools.partial(third_kernel, rows, counts),
        [*seconds[1:], *tiles[1:], second_stat, norms, *unites, state["top"]],
        kept([*inner[1:], eight]),
    )
    mixes = out[0:3]
    mix_stat = total_sum(
        out[3],
        [
            None,
            norm_cross(1, 1),
            norm_cross(1, 2),
            norm_cross(1, 3),
            norm_cross(0, 0),
        ],
    )

    denominator = float(counts[0] * joints)
    out = call(
        functools.partial(loss_kernel, rows, counts, denominator),
        [
            seconds[0],
            tiles[0],
            second_stat,
            *mixes,
            mix_stat,
            norms,
            weight,
            bias,
            target_cells,
            loss_weight,
        ],
        kept(
            [inner[0], *inner[1:], (16, 256), inner[0], eight, inner[0], inner[0], eight]
        ),
    )
    heat, pre_sums, head_part = out[0], out[1:4], out[4]
    join_zero, zero_sums, united, heat_grad, second_stat = out[5:10]
    own_second, edges = zero_sums, None
    join_grads = [join_zero]

    def top_edges_out(start):
        nonlocal edges
        edges = call(
            functools.partial(top_edge_kernel, rows),
            [after(meta, start), join_zero, seconds[0]],
            kept([(64, 256)] * 2),
            smem=1,
        )
        return [edges[0].value]

    def edge_near(start):
        near, far = lax.optimization_barrier((edges[0].value, edges[1].value, start))[:2]
        state["edges"] = swap_near(near, far)
        return [state["edges"][1]]

    def edge_far(start):
        near, relay = state["edges"]
        state["edges"] = kept([near, pass_on(after(relay, start))])
        return []

    def edge_done(start):
        return [part.value for part in state["edges"]]

    def head_grads(start):
        (state["head"],) = call(
            head_kernel, [after(meta, start), united, heat_grad], kept([eight]), smem=1
        )
        return [state["head"].value]

    head_sums = total_sum(
        head_part,
        [
            top_edges_out,
            works(edge_near, head_grads),
            works(edge_far, norm_cross(1, 0)),
            turned_bands,
            works(edge_done, cross(1, 0)),
        ],
    )
    top_edges = state["edges"]

    def back_top(start):
        state["back"] = call(
            functools.partial(back_top_kernel, rows, counts),
            [
                after(meta, start),
                join_zero,
                seconds[0],
                firsts[0],
                state["turned"][0],
                *top_edges,
                second_stat,
                head_sums,
                first_stat,
                norms,
            ],
            kept([inner[0], eight]),
            [wide[0], sides_of(wide)[0]],
            smem=1,
        )
        return [state["back"][0].value]

    out = call(
        functools.partial(join_kernel, rows, counts),
        [
            meta,
            *pre_sums,
            *mixes,
            *seconds[1:],
            *tiles[1:],
            zero_sums,
            state["head"],
            second_stat,
            mix_stat,
            head_sums,
            norms,
            *unites,
        ],
        kept([*inner[1:], *inner[1:], (16, 256), (256, 256), (256, 256)]),
        smem=1,
    )
    join_grads = [join_zero, *out[0:3]]
    mixed_grads, edges = out[3:6], out[7:9]

    def mixers(start):
        state["mixers"] = call(
            functools.partial(mixer_kernel, rows, counts),
            [after(meta, start), *mixed_grads, *seconds[1:], *tiles[1:], second_stat, norms],
            kept([(CHANNELS[b] // 2, C0) for b in range(1, 4)] * 2),
            smem=1,
        )
        return [state["mixers"][0].value]

    own_second = out[6]
    second_sums = total_sum(
        own_second,
        [
            None,
            works(edge_near, mixers, cross(1, 2)),
            works(edge_far, cross(1, 3)),
            cross(1, 1),
            works(edge_done, back_top),
        ],
    )
    first_mixers, second_mixers = state["mixers"][:3], state["mixers"][3:]

    out = call(
        functools.partial(back_second_kernel, rows, counts),
        [
            meta,
            *join_grads[1:],
            *seconds[1:],
            *firsts[1:],
            *state["turned"][1:],
            *state["edges"],
            second_stat,
            second_sums,
            first_stat,
            norms,
            *state["back"],
        ],
        kept([*inner[1:], eight, (128, 256), (128, 256)]),
        wide[1:] + sides_of(wide)[1:],
        smem=1,
    )
    normed_grads, edges = [state["back"][0], *out[0:3]], out[4:6]

    def second_packs_work(start):
        state["packs"] = combine(1, second_sums, second_mixers, start)
        return [state["packs"][0].value] if packed else [state["packs"][0]]

    def swap_second(start):
        state["far"] = exchange(after(state["packs"][1].value, start), 1)
        return [state["far"]]

    own_first = out[3]
    first_sums = total_sum(
        own_first,
        [
            None,
            second_packs_work,
            cross(0, 0),
            works(edge_near, cross(0, 1)),
            works(*[swap_second] * packed, cross(0, 2), cross(0, 3)),
        ],
    )
    if packed:
        far_second = state["far"]
        first_kernels = combine(0, first_sums, first_mixers, first_sums.value)
    else:
        second_kernels = state["packs"]
        first_kernels = combine(0, first_sums, first_mixers, first_sums.value)
        edge_far(first_sums.value)

    def back_first(start):
        state["source"] = call(
            functools.partial(back_first_kernel, rows, counts),
            [
                after(meta, start),
                *normed_grads,
                *firsts,
                *join_grads,
                *first_taps,
                *state["edges"],
                first_stat,
                first_sums,
                norms,
            ],
            [value.shape for value in inputs],
            wide + sides_of(wide) + bands,
            limit=14,
            smem=1,
        )
        return [state["source"][0]]

    def flip_last(start):
        (state["heat"],) = call(
            functools.partial(flip_kernel, rows, counts),
            [
                *flip_seconds,
                *tiles,
                second_stat,
                *unites,
                mix_stat,
                norms,
                flip_weight,
                Kept(after(flip_bias.value, start)),
                heat,
            ],
            [targets.shape],
            [(cells[0] + 16, 128)] * 2,
        )
        return [state["heat"]]

    def finish(start):
        state["finish"] = call(
            finish_kernel,
            [Kept(after(first_sums.value, start)), second_sums, head_sums],
            [(9, 128), (9, 128), (1, 1), (joints, C0), (1, joints)],
            limit=4,
        )
        return [state["finish"][0]]

    if packed:
        far_first = exchange(first_kernels[1].value, 1)
        edge_far(first_kernels[1].value)
        shapes = [(4, 2, last - first, 128) for first, last in CHUNKS]
        parts = call(
            add_cores,
            [first_kernels[0], state["packs"][0], Kept(far_first), Kept(far_second)],
            kept(shapes * 2),
        )
        first_flips = works(
            flip_first(2), flip_first(3), flip_second(0), flip_second(1), flip_second(2)
        )
        parts = scatter_step(parts, 0, works(first_flips, edge_done))
        parts = scatter_step(parts, 1, works(flip_second(3), flip_last))
        keep, send = scatter_step(parts, 2, finish, meta)
        far = Kept(after(exchange(send.value, 16), *back_first(send.value)))
        out = call(
            add_shard,
            [keep, far],
            [(ROWS_THREE, 128), (ROWS_TWO, 128), (ROWS_ONE, 128), (5, 128), (1, 64), (1, 128), (2, 128)],
        )
        shards = [part.reshape(-1)[:size] for part, size in zip(out, sizes)]
    else:
        rest_first = [flip_first(branch) for branch in (2, 3)]
        rest_second = [flip_second(branch) for branch in range(4)]
        for work in (back_first, *rest_first, *rest_second, flip_last, finish):
            work(first_sums.value)
        first_mixers, second_mixers = (
            [part.value for part in parts] for parts in (first_mixers, second_mixers)
        )
        flat = [
            jnp.concatenate([one.reshape(-1), two.reshape(-1)])
            for one, two in zip([*first_kernels, *first_mixers], [*second_kernels, *second_mixers])
        ]
        shards = [lax.psum_scatter(part, AXES, scatter_dimension=0, tiled=True) for part in flat]

    gain_grad, shift_grad, loss, head_grad, bias_grad = state["finish"]
    return (
        loss[0, 0],
        state["heat"],
        *state["source"],
        shards[3],
        shards[2],
        shards[1],
        shards[0],
        *shards[4:7],
        gain_grad.reshape(-1)[: norm_gain.shape[0]],
        shift_grad.reshape(-1)[: norm_shift.shape[0]],
        jnp.transpose(head_grad),
        bias_grad[0],
    )


def solution(mesh):
    rows = P("dp", "space", None)
    shard = P(("dp", "space"))
    heat = P("dp", None, "space", None)
    return jax.shard_map(
        body,
        mesh=mesh,
        in_specs=(*[rows] * 4, *[shard] * 7, *[P()] * 4, heat, rows, P("dp"), P()),
        out_specs=(P(), heat, *[rows] * 4, *[shard] * 7, *[P()] * 4),
        check_vma=False,
    )
```

```python
import functools

import jax
import jax.numpy as jnp
import numpy as np
from jax import lax
from jax.experimental import pallas as pl
from jax.experimental.pallas import tpu as pltpu
from jax.sharding import PartitionSpec as P

C0 = 32
CHANNELS = (32, 64, 128, 256)
SIDES = (256, 128, 256, 512)
AXES = ("dp", "space")
epsilon = 1e-05
f32 = jnp.float32
high = lax.Precision.HIGH


def dot_nn(left, right):
    return lax.dot_general(left, right, (((1,), (0,)), ((), ())), precision=high, preferred_element_type=f32)


def dot_nt(left, right):
    return lax.dot_general(left, right, (((1,), (1,)), ((), ())), precision=high, preferred_element_type=f32)


def dot_tn(left, right):
    return lax.dot_general(left, right, (((0,), (0,)), ((), ())), precision=high, preferred_element_type=f32)


def sigmoid(value):
    return 1.0 / (1.0 + jnp.exp(-value))


def silu(value):
    return value * sigmoid(value)


def silu_slope(value):
    sigma = sigmoid(value)
    return sigma * (1.0 + value * (1.0 - sigma))


def fold(row, channels):
    step = channels
    while step < 256:
        row = row + pltpu.roll(row, step, 1)
        step = 2 * step
    return row


def column_sum(value):
    return jnp.sum(value, axis=0, keepdims=True)


def moments(sums, channels, count):
    mean = fold(sums[0:1], channels) / count
    square = fold(sums[1:2], channels) / count
    return mean, lax.rsqrt(square - mean * mean + epsilon)


def affine(stats, gain, shift):
    scale = stats[1] * gain
    return scale, shift - stats[0] * scale


def load_rows(ref, first, count):
    lanes = ref.shape[2]
    return ref[:, first * 16 : (first + count) * 16, :].reshape(2 * count * 16, lanes)


def group_index(rows):
    return lax.broadcasted_iota(jnp.int32, (rows, 128), 0) % 16


def side_columns(value, channels):
    rows = value.shape[0]
    group = group_index(rows)
    lane = lax.broadcasted_iota(jnp.int32, (rows, 128), 1)

    def before(part):
        return jnp.where(group == 0, 0.0, pltpu.roll(part, 1, 0))

    def after(part):
        return jnp.where(group == 15, 0.0, pltpu.roll(part, rows - 1, 0))

    low, upper = value[:, :128], value[:, 128:]
    if channels == 256:
        return jnp.concatenate([before(low), before(upper), after(low), after(upper)], axis=1)
    if channels == 128:
        return jnp.concatenate([before(upper), after(low)], axis=1)
    first, last = after(low), before(upper)
    ends = jnp.where(lane < channels, first, jnp.where(lane >= 128 - channels, last, 0.0))
    if channels == 64:
        return ends
    first, last = pltpu.roll(first, channels, 1), pltpu.roll(last, 128 - channels, 1)
    middle = jnp.where(lane // channels == 1, first, jnp.where(lane // channels == 2, last, 0.0))
    return jnp.concatenate([ends, middle], axis=1)


def build_sides(source, side, channels):
    rows = source.shape[1]
    for image in range(2):
        side[image] = side_columns(source[image], channels)


def patches(branch, source, side, count, offset=0):
    parts = []
    for tap_row in range(3):
        parts.append(load_rows(source, tap_row + offset, count))
        if branch:
            parts.append(load_rows(side, tap_row + offset, count))
    if branch == 0:
        sides = [load_rows(side, tap_row + offset, count) for tap_row in range(3)]
        parts += [sides[0][:, :128] + sides[1][:, 128:], sides[2][:, :128]]
    return jnp.concatenate(parts, axis=1)


def band_row(branch, tap_row, place):
    channels, side = CHANNELS[branch], SIDES[branch]
    if branch == 0:
        if 0 <= place < 8:
            return tap_row * 256 + place * channels
        return ((768, 864), (800, 832), (896, 992))[tap_row][place < 0]
    base = tap_row * (256 + side)
    if place < 0:
        return base + 256 + (0 if channels >= 128 else 128 - channels)
    if place >= 256 // channels:
        return base + 256 + (side // 2 if channels >= 128 else 0)
    return base + place * channels


def build_band(band, tap, branch, offset):
    channels = CHANNELS[branch]
    groups = 256 // channels
    side = SIDES[branch]
    height = 256 + side
    if channels < 256:
        band[:, offset : offset + 256] = jnp.zeros((band.shape[0], 256), f32)
    for tap_row in range(3):
        for tap_col in range(3):
            matrix = tap(tap_row, tap_col)
            for out in range(groups):
                row = band_row(branch, tap_row, out + tap_col - 1)
                start = offset + out * channels
                band[row : row + channels, start : start + channels] = matrix


def collect_band(product, branch, emit):
    channels = CHANNELS[branch]
    for tap_row in range(3):
        for tap_col in range(3):
            total = None
            for out in range(256 // channels):
                row = band_row(branch, tap_row, out + tap_col - 1)
                start = out * channels
                if channels >= 128:
                    block = product[row : row + channels, start : start + channels]
                else:
                    tile = start // 128 * 128
                    block = product[row : row + channels, tile : tile + 128]
                    inner = start - tile
                    if inner:
                        block = pltpu.roll(block, 128 - inner, 1)
                total = block if total is None else total + block
            emit(tap_row, tap_col, total[:, :channels])


def tap_reader(ref, branch):
    channels = CHANNELS[branch]
    if channels == 256:

        def tap(tap_row, tap_col):
            first = (3 * tap_row + tap_col) * 512
            return jnp.concatenate(
                [ref[pl.ds(first, 256, stride=2), :], ref[pl.ds(first + 1, 256, stride=2), :]],
                axis=1,
            )

        return tap

    def tap(tap_row, tap_col):
        first = (3 * tap_row + tap_col) * channels
        return ref[first : first + channels, :]

    return tap


def tap_writer(ref, branch):
    channels = CHANNELS[branch]

    def emit(tap_row, tap_col, value):
        place = 3 * tap_row + tap_col
        if channels == 256:
            ref[pl.ds(place * 512, 256, stride=2), :] = value[:, :128]
            ref[pl.ds(place * 512 + 1, 256, stride=2), :] = value[:, 128:]
        else:
            ref[place * channels : (place + 1) * channels, :] = value

    return emit


SHARD = 392
ROWS_THREE, ROWS_TWO, ROWS_ONE = 288, 72, 18
PER_ZERO, PER_UNITE = 18, (2, 4, 8)
CHUNKS = ((0, 136), (136, 264), (264, 392))
STEPS = ((8, 4, 2), (4, 2, 8), (2, 8, 4))
TAPS_OUT = ((4624, 128), (1152, 128), (576, 64), (288, 32), (32, 32), (64, 32), (128, 32))
PACK_SCRATCH = ((16, 24, 128), (16, 8, 128), (288, 128))
STAGE = ((4624, 128), (1152, 128), (576, 64), (288, 32), (512, 32))


def partner(me, core, place, bits):
    return me ^ (core + sum(bit for i, bit in enumerate(bits) if place >> i & 1))


def shard_parts(device, three, two, one, zero):
    start = device * ROWS_THREE
    return (
        ((0, 136, three.at[pl.ds(pl.multiple_of(start, 8), 136), :]),),
        ((136, 264, three.at[pl.ds(pl.multiple_of(start + 136, 8), 128), :]),),
        (
            (264, 288, three.at[pl.ds(pl.multiple_of(start + 264, 8), 24), :]),
            (288, 360, two.at[pl.ds(pl.multiple_of(device * ROWS_TWO, 8), ROWS_TWO), :]),
            (360, 384, one.at[device]),
            (384, 392, zero.at[device]),
        ),
    )


def unpack_taps(me, packs, taps, scratch):
    three, two, one, zero = taps[:4]
    part_one, part_zero, flat_one = scratch
    for core in range(2):
        for place in range(8):
            for chunk in range(3):
                device = partner(me, core, place, STEPS[chunk])
                parts = shard_parts(device, three, two, part_one, part_zero)[chunk]
                for first, last, ref in parts:
                    ref[...] = packs[core][place, first:last]
    for device in range(16):
        flat_one[device * ROWS_ONE : (device + 1) * ROWS_ONE, :] = part_one[device, 0:ROWS_ONE]
    one[...] = flat_one[...].reshape(one.shape)
    narrow = part_zero[...].reshape(128, 128).reshape(512, 32)
    for device in range(16):
        first = device * 32
        for ref, height in zip(taps[3:7], (PER_ZERO, *PER_UNITE)):
            ref[device * height : (device + 1) * height, :] = narrow[first : first + height]
            first += height


def pack_grads(me, stage, unite_grads, packs, scratch):
    three, two, one, zero, narrow = stage
    part_one, part_zero, flat_one = scratch
    flat_one[...] = one[...].reshape(flat_one.shape)
    for device in range(16):
        part_one[device, 0:ROWS_ONE] = flat_one[device * ROWS_ONE : (device + 1) * ROWS_ONE, :]
        part_one[device, ROWS_ONE:24] = jnp.zeros((24 - ROWS_ONE, 128), f32)
        first = device * 32
        for ref, height in zip((zero, *unite_grads), (PER_ZERO, *PER_UNITE)):
            narrow[first : first + height, :] = ref[device * height : (device + 1) * height, :]
            first += height
    part_zero[...] = narrow[...].reshape(128, 128).reshape(16, 8, 128)
    for core in range(2):
        for place in range(8):
            for chunk in range(3):
                device = partner(me, core, place, STEPS[chunk][::-1])
                parts = shard_parts(device, three, two, part_one, part_zero)[chunk]
                for first, last, ref in parts:
                    packs[core][place, first:last] = ref[...]


def split_shard(meta, shard, other, *outs):
    second = meta[3] == 1
    for out, (first, last) in zip(outs, CHUNKS):
        own, far = shard[first:last], other[first:last]
        out[0, 0] = jnp.where(second, far, own)
        out[0, 1] = jnp.where(second, own, far)


def join_chunks(*refs):
    held, received, outs = split_refs(refs, 3, 3, 3)
    for chunk in range(3):
        count = held[chunk].shape[0]
        outs[chunk][0:count] = held[chunk][...]
        outs[chunk][count : 2 * count] = received[chunk][...]


def join_apart(*refs):
    held, received, first, second = split_refs(refs, 3, 3, 3, 3)
    for chunk in range(3):
        count = held[chunk].shape[0]
        for half, outs in ((0, first), (1, second)):
            outs[chunk][0:count] = held[chunk][:, half]
            outs[chunk][count : 2 * count] = received[chunk][:, half]


def join_whole(*refs):
    held, received, out = split_refs(refs, 3, 3, 1)
    for chunk, (first, last) in enumerate(CHUNKS):
        count = held[chunk].shape[0]
        out[0][0:count, first:last] = held[chunk][...]
        out[0][count : 2 * count, first:last] = received[chunk][...]


def add_received(*refs):
    held, received, low, high = split_refs(refs, 3, 3, 3, 3)
    for chunk in range(3):
        half = held[chunk].shape[0] // 2
        low[chunk][...] = held[chunk][0:half] + received[chunk][0:half]
        high[chunk][...] = held[chunk][half:] + received[chunk][half:]


def add_cores(*refs):
    keeps, received, low, high = split_refs(refs, 2, 2, 3, 3)
    for chunk, (first, last) in enumerate(CHUNKS):
        for half in range(2):
            low[chunk][:, half] = keeps[half][0:4, first:last] + received[half][0:4, first:last]
            high[chunk][:, half] = keeps[half][4:8, first:last] + received[half][4:8, first:last]


def add_last(meta, *refs):
    held, received, keep, send = split_refs(refs, 3, 3, 1, 1)
    second = meta[3] == 1
    for chunk, (first, last) in enumerate(CHUNKS):
        total = held[chunk][0] + received[chunk][0]
        keep[0][first:last, :] = jnp.where(second, total[1], total[0])
        send[0][first:last, :] = jnp.where(second, total[0], total[1])


def add_shard(keep, received, *outs):
    value = keep[...] + received[...]
    first = 0
    for ref in outs[:3]:
        last = first + ref.shape[0]
        ref[...] = value[first:last]
        first = last
    tail = SHARD - 8
    outs[3][...] = value[tail : tail + 5]
    outs[4][...] = value[tail + 4 : tail + 5, 64:]
    outs[5][...] = value[tail + 5 : tail + 6]
    outs[6][...] = value[tail + 6 : tail + 8]


def mirrored(tap):
    return lambda tap_row, tap_col: tap(tap_row, 2 - tap_col)


def turned(tap):
    return lambda tap_row, tap_col: jnp.transpose(tap(2 - tap_row, 2 - tap_col))


def mask_ends(value, rows, flags):
    place = lax.broadcasted_iota(jnp.int32, value.shape, 0) // 16 % (rows + 2)
    outside = ((place == 0) & (flags[0] == 0)) | ((place == rows + 1) & (flags[1] == 0))
    return jnp.where(outside, 0.0, value)


def mix_matrix(unite, branch):
    channels = CHANNELS[branch]
    groups = 256 // channels
    wide = jnp.concatenate([unite] * 8, axis=1)
    lane = lax.broadcasted_iota(jnp.int32, wide.shape, 1)
    span = 256 // groups
    return jnp.concatenate(
        [jnp.where(lane // span == place, wide, 0.0) for place in range(groups)], axis=0
    )


def split_refs(refs, *counts):
    out, first = [], 0
    for count in counts:
        out.append(refs[first : first + count])
        first += count
    assert first == len(refs)
    return out


class Kept:
    def __init__(self, value):
        self.value = value


def kept(values):
    return [Kept(value) for value in values]


def call(kernel, ins, outs, scratch=(), smem=0, limit=10, cost=0.01):
    specs = [pl.BlockSpec(memory_space=pltpu.SMEM)] * smem + [
        pl.BlockSpec(memory_space=pltpu.VMEM)
    ] * (len(ins) - smem)
    ins = ins[:smem] + [
        pltpu.with_memory_space_constraint(x.value, pltpu.VMEM)
        if isinstance(x, Kept)
        else pltpu.with_memory_space_constraint(x, pltpu.HBM)
        for x in ins[smem:]
    ]
    shapes = [pltpu.VMEM(x.value, f32) if isinstance(x, Kept) else pltpu.HBM(x, f32) for x in outs]
    results = pl.pallas_call(
        kernel,
        in_specs=specs,
        out_specs=[pl.BlockSpec(memory_space=pltpu.VMEM)] * len(outs),
        out_shape=shapes,
        scratch_shapes=[pltpu.VMEM(shape, f32) for shape in scratch],
        compiler_params=pltpu.CompilerParams(vmem_limit_bytes=limit * 2**20),
        cost_estimate=pl.CostEstimate(
            flops=int(cost * 1.1e9), bytes_accessed=int(cost * 3.0e6), transcendentals=0
        ),
    )(*ins)
    return [Kept(y) if isinstance(x, Kept) else y for x, y in zip(outs, results)]


def band_shape(branch, width):
    return (1024 if branch == 0 else 3 * (256 + SIDES[branch]), width)


def swap_blocks(parts):
    rows = parts[0].shape[0]
    group = lax.broadcasted_iota(jnp.int32, (rows, 128), 1) // 8
    step = 1
    while step < 16:
        high = (group & step) != 0
        parts = [
            jnp.where(high, parts[i], pltpu.roll(parts[i - step], 128 - 8 * step, 1))
            if i & step
            else jnp.where(high, pltpu.roll(parts[i + step], 8 * step, 1), parts[i])
            for i in range(16)
        ]
        step = 2 * step
    return parts


def joint_matrix():
    source = lax.broadcasted_iota(jnp.int32, (256, 256), 0)
    lane = lax.broadcasted_iota(jnp.int32, (256, 256), 1)
    matches = (source // 8 == lane % C0) & (source % 8 == lane // C0) & (source < 136)
    return jnp.where(matches, 1.0, 0.0)


def shift_group(value, group):
    return pltpu.roll(value, 128 - 8 * group, 1) if group else value


def parameter_kernel(gain, shift, weight, bias, flip, *outs):
    norms, weight_out, bias_out, flip_weight, flip_bias = outs
    weight = jnp.transpose(weight[...])
    for base, ref in ((0, gain), (11, shift)):
        offset = 0
        line = base
        sizes = [channels for channels in CHANNELS for _ in range(2)] + [C0] * 3
        for channels in sizes:
            part = ref[0:1, offset : offset + channels]
            norms[line : line + 1, :] = jnp.concatenate([part] * (256 // channels), axis=1)
            offset += channels
            line += 1
    joints = weight.shape[1]
    source = lax.broadcasted_iota(jnp.int32, (joints, joints), 0)
    moved = jnp.where(source == flip[...], 1.0, 0.0)
    for matrix, row, matrix_out, row_out in (
        (weight, bias[...], weight_out, bias_out),
        (
            jnp.dot(weight, moved, precision=lax.Precision.HIGHEST),
            jnp.dot(bias[...], moved, precision=lax.Precision.HIGHEST),
            flip_weight,
            flip_bias,
        ),
    ):
        matrix_out[...] = jnp.zeros((C0, C0), f32)
        matrix_out[:, 0:joints] = matrix
        row_out[...] = jnp.zeros((1, 256), f32)
        for place in range(8):
            row_out[0:1, C0 * place : C0 * place + joints] = row


def target_kernel(people, targets, mask, target_out, mask_out, scratch):
    lines = 2 * targets.shape[2]
    parts = swap_blocks([targets[:, j].reshape(lines, 128) for j in range(16)])
    last = targets[:, 16].reshape(lines, 128)
    cells = mask[...].reshape(lines, 128).astype(f32)
    lane = lax.broadcasted_iota(jnp.int32, (lines, 128), 1)
    tails = [
        jnp.where(lane < 8, shift_group(last, group), pltpu.roll(shift_group(cells, group), 8, 1))
        for group in range(16)
    ]
    whole = jnp.concatenate(
        [jnp.concatenate([part, tail], axis=1) for part, tail in zip(parts, tails)], axis=0
    )
    source = lax.broadcasted_iota(jnp.int32, (256, 256), 0)
    target_lane = lax.broadcasted_iota(jnp.int32, (256, 256), 1)
    spread = jnp.where((source >= 136) & (source < 144) & (source - 136 == target_lane // C0), 1.0, 0.0)
    target_rows = dot_nn(whole, joint_matrix())
    mask_rows = dot_nn(whole, spread)
    first_image = lax.broadcasted_iota(jnp.int32, (lines, 256), 0) < lines // 2
    share = jnp.where(first_image, people[0].astype(f32), people[1].astype(f32))
    for value, ref in ((target_rows, target_out), (mask_rows, mask_out)):
        for part in range(2):
            for group in range(16):
                span = slice(group * lines, (group + 1) * lines)
                block = value[span, 128 * part : 128 * part + 128]
                if ref is mask_out:
                    block = block / share[:, :128]
                scratch[pl.ds(group, lines, stride=16), :] = block
            ref[:, 128 * part : 128 * part + 128] = scratch[0 : ref.shape[0]]


def tile_kernel(rows, meta, *refs):
    xs, near, far, tiles, sides = split_refs(refs, 4, 1, 1, 4, 4)
    odd = meta[4] == 1
    for branch in range(4):
        count = rows[branch]
        tile = tiles[branch]
        for image in range(2):
            one, two = (ref[0][image, 2 * branch : 2 * branch + 2, :] for ref in (near, far))
            for value, first, extent in (
                (jnp.where(odd, one, two), 0, 2),
                (xs[branch][image], 2, count),
                (jnp.where(odd, two, one), count + 2, 2),
            ):
                tile[image, first * 16 : (first + extent) * 16, :] = value.reshape(extent * 16, 256)
        build_sides(tile, sides[branch], CHANNELS[branch])


def first_kernel(rows, packed, meta, *refs):
    tiles, sides, packs, mains, sums, taps, bands, scratch = split_refs(
        refs, 4, 4, 2 if packed else 4, 4, 1, 7 * packed, 4, 3 * packed
    )
    sums = sums[0]
    if packed:
        unpack_taps(meta[2], packs, taps, scratch)
    else:
        taps = packs
    for branch in range(4):
        count, band = rows[branch], bands[branch]
        build_band(band, tap_reader(taps[3 - branch], branch), branch, 0)
        out = dot_nn(patches(branch, tiles[branch], sides[branch], count + 2), band[...])
        mains[branch][...] = out.reshape(2, (count + 2) * 16, 256)
        inner = load_rows(mains[branch], 1, count)
        sums[2 * branch : 2 * branch + 1, :] = column_sum(inner)
        sums[2 * branch + 1 : 2 * branch + 2, :] = column_sum(inner * inner)


def first_flip_kernel(rows, branch, meta, tile, side, taps, out, band):
    count = rows[branch]
    build_band(band, mirrored(tap_reader(taps, branch)), branch, 0)
    value = dot_nn(patches(branch, tile, side, count + 2), band[...])
    out[...] = value.reshape(2, (count + 2) * 16, 256)


def fill_hidden(meta, firsts, stat, norms, hidden, branch, count, total):
    stats = moments(stat[2 * branch : 2 * branch + 2, :], CHANNELS[branch], total)
    scale, offset = affine(
        stats,
        norms[2 * branch : 2 * branch + 1, :],
        norms[11 + 2 * branch : 12 + 2 * branch, :],
    )
    value = load_rows(firsts[branch], 0, count + 2) * scale + offset
    value = mask_ends(silu(value), count, meta)
    hidden[branch][...] = value.reshape(2, (count + 2) * 16, 256)


def band_kernel(packed, meta, *refs):
    packs, taps, bands, scratch = split_refs(refs, 2 if packed else 4, 7 * packed, 4, 3 * packed)
    if packed:
        unpack_taps(meta[2], packs, taps, scratch)
    else:
        taps = packs
    for branch in range(4):
        build_band(bands[branch], tap_reader(taps[3 - branch], branch), branch, 0)


def turned_kernel(meta, *refs):
    taps, bands = split_refs(refs, 4, 4)
    for branch in range(4):
        build_band(bands[branch], turned(tap_reader(taps[3 - branch], branch)), branch, 0)


def second_kernel(rows, counts, branches, meta, *refs):
    each = len(branches)
    firsts, stat, norms, bands, outs, sums, hidden, sides = split_refs(
        refs, each, 1, 1, each, each, 1, each, each
    )
    sums = sums[0]
    sums[...] = jnp.zeros(sums.shape, f32)
    for i, branch in enumerate(branches):
        count, channels = rows[branch], CHANNELS[branch]
        fill_hidden(
            meta, {branch: firsts[i]}, stat[0], norms[0], {branch: hidden[i]}, branch, count, counts[branch]
        )
        build_sides(hidden[i], sides[i], channels)
        out = dot_nn(patches(branch, hidden[i], sides[i], count), bands[i][...])
        outs[i][...] = out
        sums[2 * branch : 2 * branch + 1, :] = column_sum(out)
        sums[2 * branch + 1 : 2 * branch + 2, :] = column_sum(out * out)


def second_flip_kernel(rows, counts, branch, meta, first, stat, norms, taps, out, hidden, band, side):
    count, channels = rows[branch], CHANNELS[branch]
    fill_hidden(meta, {branch: first}, stat, norms, {branch: hidden}, branch, count, counts[branch])
    build_sides(hidden, side, channels)
    build_band(band, mirrored(tap_reader(taps, branch)), branch, 0)
    out[...] = dot_nn(patches(branch, hidden, side, count), band[...])


def joined(second, tile, stat, norms, branch, count, total):
    stats = moments(stat[2 * branch : 2 * branch + 2, :], CHANNELS[branch], total)
    gain = norms[2 * branch + 1 : 2 * branch + 2, :]
    shift = norms[12 + 2 * branch : 13 + 2 * branch, :]
    scaled = (second - stats[0]) * stats[1]
    return scaled * gain + shift + load_rows(tile, 2, count), scaled, stats


def third_kernel(rows, counts, *refs):
    seconds, tiles, stat, norms, unites, top_sums, mixes, sums = split_refs(
        refs, 3, 3, 1, 1, 6, 1, 3, 1
    )
    stat, norms, sums = stat[0], norms[0], sums[0]
    for level in range(3):
        branch = level + 1
        value, _, _ = joined(
            seconds[level][...], tiles[level], stat, norms, branch, rows[branch], counts[branch]
        )
        unite = jnp.concatenate([unites[level][...], unites[3 + level][...]], axis=0)
        mixed = dot_nn(silu(value), mix_matrix(unite, branch))
        mixes[level][...] = mixed
        sums[2 * level : 2 * level + 1, :] = column_sum(mixed)
        sums[2 * level + 1 : 2 * level + 2, :] = column_sum(mixed * mixed)
    sums[6:8, :] = top_sums[0][0:2, :]


def spread_rows(value, rows, factor):
    value = value.reshape(2 * rows, 1, 16, 256)
    return jnp.broadcast_to(value, (2 * rows, factor, 16, 256)).reshape(2 * rows * factor * 16, 256)


def gather_rows(value, rows, factor):
    value = value.reshape(2 * rows // factor, factor, 16, 256)
    return jnp.sum(value, axis=1).reshape(2 * rows // factor * 16, 256)


def uniting_stats(stat, level, total):
    return moments(stat[2 * level : 2 * level + 2, :], C0, total * 2.0 ** (level + 1))


def united_sum(base, mixes, stat, norms, rows, counts):
    for level in range(3):
        stats = uniting_stats(stat, level, counts[level + 1])
        scale, offset = affine(
            stats, norms[8 + level : 9 + level, :], norms[19 + level : 20 + level, :]
        )
        base = base + spread_rows(mixes[level] * scale + offset, rows[level + 1], 2 ** (level + 1))
    return base


def head_matrix(weight):
    wide = jnp.concatenate([weight] * 8, axis=1)
    lane = lax.broadcasted_iota(jnp.int32, wide.shape, 1)
    return jnp.concatenate([jnp.where(lane // C0 == place, wide, 0.0) for place in range(8)], axis=0)


def top_edge_kernel(rows, meta, grad, second, near, far):
    odd = meta[4] == 1
    write_edges(odd, near, far, grad, 0, rows[0], 0)
    write_edges(odd, near, far, second, 0, rows[0], 32)


def loss_kernel(rows, counts, denominator, *refs):
    ins, outs = split_refs(refs, 12, 10)
    second, tile, low_stat, mix_one, mix_two, mix_three, mix_stat, norms, weight, bias, targets, mask = ins
    heat_out, sum_one, sum_two, sum_three, sums, join_grad, zero_sums, united_out, grad_out = outs[:9]
    stat = outs[9]
    stat[0:2, :] = mix_stat[6:8, :]
    stat[2:8, :] = low_stat[2:8, :]
    sums[8:16, :] = jnp.zeros((8, 256), f32)
    count = rows[0]
    join, scaled, _ = joined(second[...], tile, stat, norms, 0, count, counts[0])
    mixes = (mix_one[...], mix_two[...], mix_three[...])
    pre = united_sum(silu(join), mixes, mix_stat, norms, rows, counts)
    united = silu(pre)
    head = head_matrix(weight[...])
    heat = dot_nn(united, head) + bias[...]
    heat_out[...] = heat
    error = heat - targets[...]
    weighted = mask[...] * error
    sums[6:7, :] = column_sum(weighted * error) / denominator
    heat_grad = weighted * (2.0 / denominator)
    sums[7:8, :] = column_sum(heat_grad)
    united_out[...] = united
    grad_out[...] = heat_grad
    grad = dot_nt(heat_grad, head) * silu_slope(pre)
    join_part = grad * silu_slope(join)
    join_grad[...] = join_part
    zero_sums[0:1, :] = column_sum(join_part)
    zero_sums[1:2, :] = column_sum(join_part * scaled)
    sums[8:10, :] = zero_sums[0:2, :]
    for level, out in enumerate((sum_one, sum_two, sum_three)):
        part = gather_rows(grad, count, 2 ** (level + 1))
        out[...] = part
        stats = uniting_stats(mix_stat, level, counts[level + 1])
        normed = (mixes[level] - stats[0]) * stats[1]
        sums[2 * level : 2 * level + 1, :] = column_sum(part)
        sums[2 * level + 1 : 2 * level + 2, :] = column_sum(part * normed)


def head_kernel(meta, united, heat_grad, out):
    product = dot_tn(united[...], heat_grad[...])
    total = None
    for place in range(8):
        first = place * C0
        tile_first = first // 128 * 128
        block = product[first : first + C0, tile_first : tile_first + 128]
        if first - tile_first:
            block = pltpu.roll(block, 128 - (first - tile_first), 1)
        total = block if total is None else total + block
    out[...] = jnp.zeros(out.shape, f32)
    out[:, 0:128] = jnp.concatenate(
        [total[8 * part : 8 * part + 8, :C0] for part in range(4)], axis=1
    )


def flip_kernel(rows, counts, *refs):
    seconds, tiles, stat, unites, mix_stat, norms, weight, bias, heat, out, scratch = split_refs(
        refs, 4, 4, 1, 6, 1, 1, 1, 1, 1, 1, 2
    )
    stat, norms = stat[0], norms[0]
    mixes = []
    for branch in range(4):
        value, _, _ = joined(
            seconds[branch][...], tiles[branch], stat, norms, branch, rows[branch], counts[branch]
        )
        if branch == 0:
            base = silu(value)
        else:
            unite = jnp.concatenate([unites[branch - 1][...], unites[branch + 2][...]], axis=0)
            mixes.append(dot_nn(silu(value), mix_matrix(unite, branch)))
    pre = united_sum(base, mixes, mix_stat[0], norms, rows, counts)
    back = dot_nn(silu(pre), head_matrix(weight[0][...])) + bias[0][...]
    moved = dot_nt(0.5 * (heat[0][...] + back), joint_matrix())
    scratch[0][0 : moved.shape[0]] = moved[:, :128]
    scratch[1][0 : moved.shape[0]] = moved[:, 128:]
    lines = 2 * rows[0]
    parts = [scratch[0][pl.ds(group, lines, stride=16), :] for group in range(16)]
    lane = lax.broadcasted_iota(jnp.int32, (lines, 128), 1)
    last = None
    for group in range(16):
        tail = scratch[1][pl.ds(group, lines, stride=16), :]
        tail = pltpu.roll(tail, 8 * group, 1) if group else tail
        last = tail if last is None else jnp.where(lane // 8 == group, tail, last)
    for joint, value in enumerate([*swap_blocks(parts), last]):
        out[0][:, joint] = value.reshape(2, rows[0], 128)


def edge_place(branch, image):
    return (2 * branch + image) * 16


def write_edges(odd, near, far, value, branch, count, base):
    for image in range(2):
        place = base + edge_place(branch, image)
        start = image * count * 16
        first = value[start : start + 16]
        last = value[start + (count - 1) * 16 : start + count * 16]
        near[place : place + 16, :] = jnp.where(odd, first, last)
        far[place : place + 16, :] = jnp.where(odd, last, first)


def join_kernel(rows, counts, meta, *refs):
    sums_in, mixes, seconds, tiles, small, unites, outs = split_refs(refs, 3, 3, 3, 3, 6, 6, 9)
    zero_sums, head_grad, stat, mix_stat, head_sums, norms = small
    grads, mixed_grads, sums, near, far = outs[0:3], outs[3:6], outs[6], outs[7], outs[8]
    odd = meta[4] == 1
    sums[0:2, :] = zero_sums[0:2, :]
    sums[8:16, :] = head_grad[...]
    for level in range(3):
        branch = level + 1
        channels, count = CHANNELS[branch], rows[branch]
        total = counts[branch]
        stats = uniting_stats(mix_stat, level, total)
        gain = norms[8 + level : 9 + level, :]
        shift_sum = fold(head_sums[2 * level : 2 * level + 1, :], C0)
        gain_sum = fold(head_sums[2 * level + 1 : 2 * level + 2, :], C0)
        normed = (mixes[level][...] - stats[0]) * stats[1]
        share = 1.0 / (total * 2.0 ** (level + 1))
        mixed_grad = (gain * stats[1]) * (
            sums_in[level][...] - shift_sum * share - normed * (gain_sum * share)
        )
        mixed_grads[level][...] = mixed_grad
        value, scaled, _ = joined(
            seconds[level][...], tiles[level], stat, norms, branch, count, total
        )
        unite = jnp.concatenate([unites[level][...], unites[3 + level][...]], axis=0)
        grad = dot_nt(mixed_grad, mix_matrix(unite, branch)) * silu_slope(value)
        grads[level][...] = grad
        sums[2 * branch : 2 * branch + 1, :] = column_sum(grad)
        sums[2 * branch + 1 : 2 * branch + 2, :] = column_sum(grad * scaled)
        write_edges(odd, near, far, grad, branch, count, 0)
        write_edges(odd, near, far, seconds[level][...], branch, count, 128)


def mixer_kernel(rows, counts, meta, *refs):
    mixed_grads, seconds, tiles, stat, norms, outs = split_refs(refs, 3, 3, 3, 1, 1, 6)
    for level in range(3):
        branch = level + 1
        channels = CHANNELS[branch]
        value, _, _ = joined(
            seconds[level][...], tiles[level], stat[0], norms[0], branch, rows[branch], counts[branch]
        )
        product = dot_tn(silu(value), mixed_grads[level][...])
        mixer = None
        for place in range(8):
            row = place // (8 * channels // 256) * channels
            tile_first = place * C0 // 128 * 128
            block = product[row : row + channels, tile_first : tile_first + 128]
            inner = place * C0 - tile_first
            if inner:
                block = pltpu.roll(block, 128 - inner, 1)
            mixer = block if mixer is None else mixer + block
        outs[level][...] = mixer[: channels // 2, :C0]
        outs[3 + level][...] = mixer[channels // 2 :, :C0]


def norm_input_grad(grad, scaled, stats, gain, sums, channels, total):
    shift_sum = fold(sums[0:1, :], channels) / total
    gain_sum = fold(sums[1:2, :], channels) / total
    return (gain * stats[1]) * (grad - shift_sum - scaled * gain_sum)


def back_second_branch(
    rows, counts, branch, meta, grad, second, first, band, edges, stats_in, out, sums, wide, side
):
    stat, own, first_stat, norms = stats_in
    count, channels, total = rows[branch], CHANNELS[branch], counts[branch]
    odd = meta[4] == 1
    stats = moments(stat[2 * branch : 2 * branch + 2, :], channels, total)
    gain = norms[2 * branch + 1 : 2 * branch + 2, :]
    shift_sum = fold(own[0:1], channels) / total
    gain_sum = fold(own[1:2], channels) / total

    def input_grad(part, value):
        scaled = (value - stats[0]) * stats[1]
        return (gain * stats[1]) * (part - shift_sum - scaled * gain_sum)

    inner = input_grad(grad[...], second[...])
    wide[:, 16 : (count + 1) * 16, :] = inner.reshape(2, count * 16, 256)
    for image in range(2):
        parts = [input_grad(*edge) for edge in edges[image]]
        for value, start, flag in (
            (jnp.where(odd, parts[0], parts[1]), 0, meta[0]),
            (jnp.where(odd, parts[1], parts[0]), (count + 1) * 16, meta[1]),
        ):
            wide[image, start : start + 16, :] = jnp.where(flag == 0, 0.0, value)
    build_sides(wide, side, channels)
    hidden_grad = dot_nn(patches(branch, wide, side, count), band[...])
    first_stats = moments(first_stat[2 * branch : 2 * branch + 2, :], channels, total)
    scaled = (load_rows(first, 1, count) - first_stats[0]) * first_stats[1]
    value = (
        scaled * norms[2 * branch : 2 * branch + 1, :]
        + norms[11 + 2 * branch : 12 + 2 * branch, :]
    )
    result = hidden_grad * silu_slope(value)
    out[...] = result
    sums[2 * branch : 2 * branch + 1, :] = column_sum(result)
    sums[2 * branch + 1 : 2 * branch + 2, :] = column_sum(result * scaled)
    return result


def back_top_kernel(rows, counts, meta, *refs):
    grad, second, first, band, near, far, stat, head_sums, first_stat, norms, out, sums, wide, side = refs
    edges = [
        [(ref[at : at + 16, :], ref[32 + at : 48 + at, :]) for ref in (near, far)]
        for at in (0, 16)
    ]
    stats_in = (stat, head_sums[8:10, :], first_stat, norms)
    back_second_branch(
        rows, counts, 0, meta, grad, second, first, band, edges, stats_in, out, sums, wide, side
    )


def back_second_kernel(rows, counts, meta, *refs):
    ins, outs, wide, sides = split_refs(refs, 20, 6, 3, 3)
    grads, seconds, firsts, bands = ins[0:3], ins[3:6], ins[6:9], ins[9:12]
    near_in, far_in, stat, stat_sums, first_stat, norms, top, top_sums = ins[12:20]
    sums, near, far = outs[3:6]
    odd = meta[4] == 1
    sums[0:2, :] = top_sums[0:2, :]
    write_edges(odd, near, far, top[...], 0, rows[0], 0)
    for level in range(3):
        branch = level + 1
        places = [edge_place(branch, image) for image in range(2)]
        edges = [
            [(ref[at : at + 16, :], ref[128 + at : 144 + at, :]) for ref in (near_in, far_in)]
            for at in places
        ]
        stats_in = (stat, stat_sums[2 * branch : 2 * branch + 2, :], first_stat, norms)
        result = back_second_branch(
            rows,
            counts,
            branch,
            meta,
            grads[level],
            seconds[level],
            firsts[level],
            bands[level],
            edges,
            stats_in,
            outs[level],
            sums,
            wide[level],
            sides[level],
        )
        write_edges(odd, near, far, result, branch, rows[branch], 0)


def cross_products(rows, branch, offset, source, value, out, side, product):
    count, channels = rows[branch], CHANNELS[branch]
    product[...] = dot_tn(patches(branch, source, side, count, offset), value)

    def emit(tap_row, tap_col, block):
        place = (3 * tap_row + tap_col) * channels
        out[place : place + channels, :] = block

    collect_band(product, branch, emit)


def normalized(raw, stat, rows, counts, branch, inner):
    stats = moments(stat[2 * branch : 2 * branch + 2, :], CHANNELS[branch], counts[branch])
    value = raw[...] if inner else load_rows(raw, 1, rows[branch])
    return (value - stats[0]) * stats[1]


def sum_means(sums, branch, total):
    channels = CHANNELS[branch]
    return [fold(sums[2 * branch + i : 2 * branch + i + 1, :], channels) / total for i in range(2)]


def cross_kernel(rows, counts, devices, branch, offset, inner, meta, *refs):
    source, side, value, raw, stat, sums, out, product = refs
    shift_mean, gain_mean = sum_means(sums, branch, counts[branch] / devices)
    scaled = normalized(raw, stat, rows, counts, branch, inner)
    rest = value[...] - shift_mean - scaled * gain_mean
    cross_products(rows, branch, offset, source, rest, out, side, product)


def cross_norm_kernel(rows, counts, branch, offset, inner, meta, *refs):
    source, side, raw, stat, out, sums, product = refs
    count, channels = rows[branch], CHANNELS[branch]
    scaled = normalized(raw, stat, rows, counts, branch, inner)
    cross_products(rows, branch, offset, source, scaled, out, side, product)
    total = column_sum(patches(branch, source, side, count, offset))
    column = jnp.transpose(jnp.broadcast_to(total, (8, total.shape[1])))
    for tap_row in range(3):
        for tap_col in range(3):
            block = None
            for place in range(256 // channels):
                row = band_row(branch, tap_row, place + tap_col - 1)
                part = column[row : row + channels]
                block = part if block is None else block + part
            start = (3 * tap_row + tap_col) * channels
            sums[start : start + channels, :] = block


def combine_kernel(counts, devices, packed, which, meta, *refs):
    crosses, norm_crosses, patch_sums, ins, unite_grads, outs, stage, scratch = split_refs(
        refs, 4, 4, 4, 4, 3, 2 if packed else 4, 5, 3
    )
    stat, own_sums, grad_sums, norms = ins
    for branch in range(4):
        channels, total = CHANNELS[branch], counts[branch]
        stats = moments(stat[2 * branch : 2 * branch + 2, :], channels, total)
        line = 2 * branch + which
        scale = (norms[line : line + 1, :] * stats[1])[:, :channels]
        shift_rest, gain_rest = (
            (whole - own)[:, :channels]
            for whole, own in zip(
                sum_means(grad_sums, branch, total), sum_means(own_sums, branch, total / devices)
            )
        )
        emit = tap_writer(stage[3 - branch], branch)
        for place in range(9):
            span = slice(place * channels, (place + 1) * channels)
            value = (
                crosses[branch][span, :]
                - patch_sums[branch][span, 0:1] * shift_rest
                - norm_crosses[branch][span, :] * gain_rest
            )
            emit(place // 3, place % 3, scale * value)
    if packed:
        pack_grads(meta[2], stage, unite_grads, outs, scratch)
    else:
        for ref, value in zip(outs, stage):
            ref[...] = value[0 : ref.shape[0]]


def back_first_kernel(rows, counts, flags, *refs):
    ins, source_grads, wide, sides, bands = split_refs(refs, 21, 4, 4, 4, 4)
    normed_grads, firsts, join_grads, taps = ins[0:4], ins[4:8], ins[8:12], ins[12:16]
    near, far, first_stat, first_sums, norms = ins[16:21]
    odd = flags[4] == 1
    for branch in range(4):
        count, channels, total = rows[branch], CHANNELS[branch], counts[branch]
        stats = moments(first_stat[2 * branch : 2 * branch + 2, :], channels, total)
        gain = norms[2 * branch : 2 * branch + 1, :]
        shift_sum = fold(first_sums[2 * branch : 2 * branch + 1, :], channels) / total
        gain_sum = fold(first_sums[2 * branch + 1 : 2 * branch + 2, :], channels) / total

        def input_grad(grad, value):
            scaled = (value - stats[0]) * stats[1]
            return (gain * stats[1]) * (grad - shift_sum - scaled * gain_sum)

        inner = input_grad(normed_grads[branch][...], load_rows(firsts[branch], 1, count))
        wide[branch][:, 16 : (count + 1) * 16, :] = inner.reshape(2, count * 16, 256)
        for image in range(2):
            place = edge_place(branch, image)
            one, two = (ref[place : place + 16, :] for ref in (near, far))
            for grad, start, flag in (
                (jnp.where(odd, one, two), 0, flags[0]),
                (jnp.where(odd, two, one), (count + 1) * 16, flags[1]),
            ):
                value = input_grad(grad, firsts[branch][image, start : start + 16, :])
                wide[branch][image, start : start + 16, :] = jnp.where(flag == 0, 0.0, value)
        build_sides(wide[branch], sides[branch], channels)
        build_band(bands[branch], turned(tap_reader(taps[3 - branch], branch)), branch, 0)
        grad = dot_nn(patches(branch, wide[branch], sides[branch], count), bands[branch][...])
        grad = (grad + join_grads[branch][...]).reshape(2, count * 16, 256)
        for image in range(2):
            source_grads[branch][image] = grad[image].reshape(count, 4096)


def finish_kernel(first_sums, second_sums, head_sums, gain, shift, loss, head_weight, head_bias):
    offset = 0

    def put(sums, line, channels):
        nonlocal offset
        for ref, row in ((shift, line), (gain, line + 1)):
            value = fold(sums[row : row + 1, :], channels)
            done = 0
            while done < channels:
                place = offset + done
                width = min(channels - done, 128 - place % 128)
                ref[place // 128 : place // 128 + 1, place % 128 : place % 128 + width] = value[
                    :, done : done + width
                ]
                done += width
        offset += channels

    for branch in range(4):
        for sums in (first_sums, second_sums):
            put(sums, 2 * branch, CHANNELS[branch])
    for level in range(3):
        put(head_sums, 2 * level, C0)
    loss[...] = jnp.sum(head_sums[6:7, :], axis=1, keepdims=True)
    joints = head_bias.shape[1]
    head_bias[...] = fold(head_sums[7:8, :], C0)[:, :joints]
    total = jnp.concatenate(
        [second_sums[8:16, C0 * part : C0 * part + C0] for part in range(4)], axis=0
    )
    head_weight[...] = jnp.transpose(total)[:joints]


def device_count():
    return lax.axis_size("dp") * lax.axis_size("space")


def exchange(value, bit):
    return lax.ppermute(value, AXES, [(i, i ^ bit) for i in range(device_count())])


def total_sum(value, beside=(), order=None):
    value = value.value
    for step, bit in enumerate(order or [1 << i for i in range(device_count().bit_length() - 1)]):
        other = exchange(value, bit)
        if step < len(beside) and beside[step]:
            other = after(other, *beside[step](value))
        value = value + other
    return Kept(value)


def swap_rows(near, far):
    devices = lax.axis_size("space")
    pairs = [(i, i ^ 1) for i in range(devices)]
    others = [(i, i + 1) for i in range(1, devices - 1, 2)]
    others += [(j, i) for i, j in others]
    return lax.ppermute(near, "space", pairs), lax.ppermute(far, "space", others)


def swap_near(near, far):
    pairs = [(i, i ^ 1) for i in range(lax.axis_size("space"))]
    return lax.ppermute(near, "space", pairs), lax.ppermute(far, "space", pairs)


def pass_on(relay):
    devices = lax.axis_size("space")
    return lax.ppermute(relay, "space", [(i, (i + 2 - i % 2 * 4) % devices) for i in range(devices)])


def device_index():
    return lax.axis_index("dp") * lax.axis_size("space") + lax.axis_index("space")


def after(value, *others):
    return lax.optimization_barrier((value, *others))[0]


def swap(parts, step):
    return [Kept(exchange(part.value, STEPS[chunk][step])) for chunk, part in enumerate(parts)]


def gather_shards(meta, flat, beside):
    other = exchange(flat, 16)
    other = after(other, *beside[0](flat))
    shapes = [(1, 2, last - first, 128) for first, last in CHUNKS]
    parts = call(split_shard, [meta, flat, Kept(other)], kept(shapes), smem=1)
    shapes = [(2, *shape[1:]) for shape in shapes]
    received = swap(parts, 0)
    received[0] = Kept(after(received[0].value, *beside[1](parts[0].value)))
    parts = call(join_chunks, [*parts, *received], kept(shapes))
    shapes = [(4, *shape[2:]) for shape in shapes]
    received = swap(parts, 1)
    received[0] = Kept(after(received[0].value, *beside[2](parts[0].value)))
    parts = call(join_apart, [*parts, *received], kept(shapes * 2))
    first, second = parts[:3], parts[3:]
    received = swap(first, 2)
    received[0] = Kept(after(received[0].value, *beside[3](first[0].value)))
    (whole,) = call(join_whole, [*first, *received], kept([(8, SHARD, 128)]))
    second[0] = Kept(after(second[0].value, whole.value))
    received = swap(second, 2)

    def rest(start):
        received[0] = Kept(after(received[0].value, start))
        (whole,) = call(join_whole, [*second, *received], kept([(8, SHARD, 128)]))
        return [whole, Kept(exchange(whole.value, 1))]

    return [whole, Kept(exchange(whole.value, 1))], rest


def scatter_step(parts, step, beside, meta=None):
    received = swap(parts[3:], step)
    received[0] = Kept(after(received[0].value, *beside(parts[3].value)))
    if step == 2:
        return call(add_last, [meta, *parts[:3], *received], kept([(SHARD, 128)] * 2), smem=1)
    shapes = [(2 - step, 2, last - first, 128) for first, last in CHUNKS]
    return call(add_received, [*parts[:3], *received], kept(shapes * 2))


def body(
    branch_zero,
    branch_one,
    branch_two,
    branch_three,
    convs_zero,
    convs_one,
    convs_two,
    convs_three,
    unite_one,
    unite_two,
    unite_three,
    norm_gain,
    norm_shift,
    head_weight,
    head_bias,
    targets,
    crowd_mask,
    person_count,
    flip_order,
):
    inputs = (branch_zero, branch_one, branch_two, branch_three)
    devices = device_count()
    spaces = lax.axis_size("space")
    place = lax.axis_index("space")
    rows = tuple(value.shape[1] for value in inputs)
    counts = tuple(
        float(2 * rows[b] * 16 * (256 // CHANNELS[b]) * devices) for b in range(4)
    )
    joints = head_bias.shape[0]
    cells = [2 * rows[b] * 16 for b in range(4)]
    packed = devices == 32
    shards_in = (convs_three, convs_two, convs_one, convs_zero, unite_one, unite_two, unite_three)
    sizes = [part.shape[0] for part in shards_in]

    meta = jnp.stack(
        [
            place > 0,
            place < spaces - 1,
            device_index() & 15,
            (device_index() & 16) // 16,
            place % 2,
        ]
    ).astype(jnp.int32)

    bands = [band_shape(b, 256) for b in range(4)]
    inner = [(cells[b], 256) for b in range(4)]
    wide = [(2, (rows[b] + 2) * 16, 256) for b in range(4)]
    wider = [(2, (rows[b] + 4) * 16, 256) for b in range(4)]

    def sides_of(shapes):
        return [shape[:2] + (SIDES[b],) for b, shape in enumerate(shapes)]

    def works(*parts):
        return lambda start: sum((list(part(start)) for part in parts), [])

    state = {}

    def prepare(start):
        parts = lax.optimization_barrier((*inputs, start))[:4]
        last_rows = jnp.concatenate([value[:, -2:] for value in parts], axis=1)
        first_rows = jnp.concatenate([value[:, :2] for value in parts], axis=1)
        odd = place % 2 == 1
        state["halo"] = swap_rows(
            jnp.where(odd, first_rows, last_rows), jnp.where(odd, last_rows, first_rows)
        )
        return state["halo"]

    def prepare_targets(start):
        state["targets"] = call(
            target_kernel,
            [after(person_count, start), targets, crowd_mask],
            kept([(cells[0], 256)] * 2),
            [(cells[0] + 16, 128)],
            smem=1,
            cost=4,
        )
        return [state["targets"][0].value]

    def make_tiles(start):
        state["tiles"] = call(
            functools.partial(tile_kernel, rows),
            [after(meta, start), *inputs, *state["halo"]],
            kept([*wider, *sides_of(wider)]),
            smem=1,
        )
        return [state["tiles"][0].value]

    def parameters(start):
        state["small"] = call(
            parameter_kernel,
            [
                after(norm_gain, start)[None],
                norm_shift[None],
                jnp.transpose(head_weight),
                head_bias[None],
                flip_order[None],
            ],
            kept([(22, 256), (C0, C0), (1, 256), (C0, C0), (1, 256)]),
        )
        return [state["small"][0].value]

    if packed:
        gap = jnp.zeros(((24 - ROWS_ONE) * 128,), f32)
        flat = jnp.concatenate([*shards_in[:3], gap, *shards_in[3:]]).reshape(SHARD, 128)
        first_packs, rest = gather_shards(meta, flat, (works(prepare, prepare_targets), lambda start: [], make_tiles, parameters))
    else:
        for work in (prepare, parameters, make_tiles, prepare_targets):
            work(meta)
        whole = [lax.all_gather(part, AXES, axis=0, tiled=True) for part in shards_in]
        whole = [
            part.reshape(-1, width)
            for part, width in zip(whole, (128, 128, 64, 32, 32, 32, 32))
        ]
        first_packs = [part[: part.shape[0] // 2] for part in whole]
        second_packs = [part[part.shape[0] // 2 :] for part in whole]
    target_cells, loss_weight = state["targets"]
    tiles, tile_sides = state["tiles"][:4], state["tiles"][4:]
    norms, weight, bias, flip_weight, flip_bias = state["small"]

    eight = (8, 256)
    taps_out = kept(TAPS_OUT) if packed else []
    unpack_scratch = list(PACK_SCRATCH) if packed else []

    out = call(
        functools.partial(first_kernel, rows, packed),
        [meta, *tiles, *tile_sides, *first_packs[:4]],
        kept([*wide, eight]) + taps_out,
        bands + unpack_scratch,
        smem=1,
    )
    firsts = out[0:4]
    first_taps = out[5:] if packed else first_packs
    if packed:
        second_packs = rest(firsts[0].value)

    crosses = [[None] * 4, [None] * 4]
    norm_crosses = [[None] * 4, [None] * 4]
    natural = [(9 * CHANNELS[b], CHANNELS[b]) for b in range(4)]

    def cross(which, branch):
        def work(start):
            values = (
                (
                    tiles[branch],
                    tile_sides[branch],
                    normed_grads[branch],
                    firsts[branch],
                    first_stat,
                    own_first,
                )
                if which == 0
                else (
                    hidden[branch],
                    hidden_sides[branch],
                    join_grads[branch],
                    seconds[branch],
                    second_stat,
                    own_second,
                )
            )
            (crosses[which][branch],) = call(
                functools.partial(cross_kernel, rows, counts, devices, branch, 1 - which, which),
                [after(meta, start), *values],
                kept([natural[branch]]),
                [bands[branch]],
                smem=1,
            )
            return [crosses[which][branch].value]

        return work

    def norm_cross(which, branch):
        def work(start):
            values = (
                (tiles[branch], tile_sides[branch], firsts[branch], first_stat)
                if which == 0
                else (hidden[branch], hidden_sides[branch], seconds[branch], second_stat)
            )
            norm_crosses[which][branch] = call(
                functools.partial(cross_norm_kernel, rows, counts, branch, 1 - which, which),
                [after(meta, start), *values],
                kept([natural[branch], (9 * CHANNELS[branch], 8)]),
                [bands[branch]],
                smem=1,
            )
            return [norm_crosses[which][branch][0].value]

        return work

    def combine(which, sums, mixers, start):
        return call(
            functools.partial(combine_kernel, counts, devices, packed, which),
            [
                after(meta, start),
                *crosses[which],
                *[part[0] for part in norm_crosses[which]],
                *[part[1] for part in norm_crosses[which]],
                (first_stat, second_stat)[which],
                (own_first, own_second)[which],
                sums,
                norms,
                *mixers,
            ],
            kept([(8, SHARD, 128)] * 2) if packed else [(4608, 128), *TAPS_OUT[1:4]],
            [*STAGE, *PACK_SCRATCH],
            smem=1,
        )

    flip_firsts, flip_seconds = [None] * 4, [None] * 4

    def flip_first(branch):
        def work(start):
            (flip_firsts[branch],) = call(
                functools.partial(first_flip_kernel, rows, branch),
                [after(meta, start), tiles[branch], tile_sides[branch], first_taps[3 - branch]],
                kept([wide[branch]]),
                [bands[branch]],
                smem=1,
            )
            return [flip_firsts[branch].value]

        return work

    def second_bands(start):
        state["second"] = call(
            functools.partial(band_kernel, packed),
            [after(meta, start), *second_packs[:4]],
            taps_out + kept(bands),
            unpack_scratch,
            smem=1,
        )
        return [state["second"][-1].value]

    def turned_bands(start):
        state["turned"] = call(
            turned_kernel, [after(meta, start), *(state["second"] if packed else second_packs)[:4]], kept(bands), smem=1, cost=2
        )
        return [state["turned"][0].value]

    order = [1 << i for i in range(devices.bit_length() - 1)]
    first_stat = total_sum(
        out[4],
        [flip_first(1), second_bands, turned_bands, flip_first(0)],
        [*order[1:], 1] if packed else None,
    )
    second_taps = state["second"][:7] if packed else second_packs

    out = call(
        functools.partial(second_kernel, rows, counts, (1, 2, 3)),
        [meta, *firsts[1:], first_stat, norms, *state["second"][-3:]],
        kept([*inner[1:], eight, *wide[1:], *sides_of(wide)[1:]]),
        smem=1,
    )
    seconds, hidden, hidden_sides = ([None, *part] for part in (out[0:3], out[4:7], out[7:10]))
    low_sums = out[3]

    def second_top(start):
        seconds[0], state["top"], hidden[0], hidden_sides[0] = call(
            functools.partial(second_kernel, rows, counts, (0,)),
            [after(meta, start), firsts[0], first_stat, norms, state["second"][-4]],
            kept([inner[0], eight, wide[0], sides_of(wide)[0]]),
            smem=1,
        )
        return [seconds[0].value]

    unites = [*first_taps[4:7], *second_taps[4:7]]
    first_taps, second_taps = first_taps[:4], second_taps[:4]

    def flip_second(branch):
        def work(start):
            (flip_seconds[branch],) = call(
                functools.partial(second_flip_kernel, rows, counts, branch),
                [
                    after(meta, start),
                    flip_firsts[branch],
                    first_stat,
                    norms,
                    second_taps[3 - branch],
                ],
                kept([inner[branch]]),
                [wide[branch], bands[branch], sides_of(wide)[branch]],
                smem=1,
            )
            return [flip_seconds[branch].value]

        return work

    second_stat = total_sum(
        low_sums,
        [
            None,
            norm_cross(0, 1),
            norm_cross(0, 2),
            norm_cross(0, 3),
            second_top,
        ],
    )

    out = call(
        functools.partial(third_kernel, rows, counts),
        [*seconds[1:], *tiles[1:], second_stat, norms, *unites, state["top"]],
        kept([*inner[1:], eight]),
    )
    mixes = out[0:3]
    mix_stat = total_sum(
        out[3],
        [
            None,
            norm_cross(1, 1),
            norm_cross(1, 2),
            norm_cross(1, 3),
            norm_cross(0, 0),
        ],
    )

    denominator = float(counts[0] * joints)
    out = call(
        functools.partial(loss_kernel, rows, counts, denominator),
        [
            seconds[0],
            tiles[0],
            second_stat,
            *mixes,
            mix_stat,
            norms,
            weight,
            bias,
            target_cells,
            loss_weight,
        ],
        kept(
            [inner[0], *inner[1:], (16, 256), inner[0], eight, inner[0], inner[0], eight]
        ),
    )
    heat, pre_sums, head_part = out[0], out[1:4], out[4]
    join_zero, zero_sums, united, heat_grad, second_stat = out[5:10]
    own_second, edges = zero_sums, None
    join_grads = [join_zero]

    def top_edges_out(start):
        nonlocal edges
        edges = call(
            functools.partial(top_edge_kernel, rows),
            [after(meta, start), join_zero, seconds[0]],
            kept([(64, 256)] * 2),
            smem=1,
        )
        return [edges[0].value]

    def edge_near(start):
        near, far = lax.optimization_barrier((edges[0].value, edges[1].value, start))[:2]
        state["edges"] = swap_near(near, far)
        return [state["edges"][1]]

    def edge_far(start):
        near, relay = state["edges"]
        state["edges"] = kept([near, pass_on(after(relay, start))])
        return []

    def edge_done(start):
        return [part.value for part in state["edges"]]

    def head_grads(start):
        (state["head"],) = call(
            head_kernel, [after(meta, start), united, heat_grad], kept([eight]), smem=1
        )
        return [state["head"].value]

    head_sums = total_sum(
        head_part,
        [
            top_edges_out,
            works(edge_near, head_grads),
            edge_far,
            norm_cross(1, 0),
            works(edge_done, cross(1, 0)),
        ],
    )
    top_edges = state["edges"]

    def back_top(start):
        state["back"] = call(
            functools.partial(back_top_kernel, rows, counts),
            [
                after(meta, start),
                join_zero,
                seconds[0],
                firsts[0],
                state["turned"][0],
                *top_edges,
                second_stat,
                head_sums,
                first_stat,
                norms,
            ],
            kept([inner[0], eight]),
            [wide[0], sides_of(wide)[0]],
            smem=1,
        )
        return [state["back"][0].value]

    out = call(
        functools.partial(join_kernel, rows, counts),
        [
            meta,
            *pre_sums,
            *mixes,
            *seconds[1:],
            *tiles[1:],
            zero_sums,
            state["head"],
            second_stat,
            mix_stat,
            head_sums,
            norms,
            *unites,
        ],
        kept([*inner[1:], *inner[1:], (16, 256), (256, 256), (256, 256)]),
        smem=1,
    )
    join_grads = [join_zero, *out[0:3]]
    mixed_grads, edges = out[3:6], out[7:9]

    def mixers(start):
        state["mixers"] = call(
            functools.partial(mixer_kernel, rows, counts),
            [after(meta, start), *mixed_grads, *seconds[1:], *tiles[1:], second_stat, norms],
            kept([(CHANNELS[b] // 2, C0) for b in range(1, 4)] * 2),
            smem=1,
        )
        return [state["mixers"][0].value]

    own_second = out[6]
    second_sums = total_sum(
        own_second,
        [
            None,
            works(edge_near, mixers, cross(1, 2)),
            works(edge_far, cross(1, 3)),
            cross(1, 1),
            works(edge_done, back_top),
        ],
    )
    first_mixers, second_mixers = state["mixers"][:3], state["mixers"][3:]

    out = call(
        functools.partial(back_second_kernel, rows, counts),
        [
            meta,
            *join_grads[1:],
            *seconds[1:],
            *firsts[1:],
            *state["turned"][1:],
            *state["edges"],
            second_stat,
            second_sums,
            first_stat,
            norms,
            *state["back"],
        ],
        kept([*inner[1:], eight, (128, 256), (128, 256)]),
        wide[1:] + sides_of(wide)[1:],
        smem=1,
    )
    normed_grads, edges = [state["back"][0], *out[0:3]], out[4:6]

    def second_packs_work(start):
        state["packs"] = combine(1, second_sums, second_mixers, start)
        return [state["packs"][0].value] if packed else [state["packs"][0]]

    def swap_second(start):
        state["far"] = exchange(after(state["packs"][1].value, start), 1)
        return [state["far"]]

    own_first = out[3]
    first_sums = total_sum(
        own_first,
        [
            None,
            works(edge_near, second_packs_work),
            cross(0, 0),
            works(edge_far, cross(0, 1)),
            works(*[swap_second] * packed, edge_done, cross(0, 2), cross(0, 3)),
        ],
    )
    if packed:
        far_second = state["far"]
        first_kernels = combine(0, first_sums, first_mixers, first_sums.value)
    else:
        second_kernels = state["packs"]
        first_kernels = combine(0, first_sums, first_mixers, first_sums.value)

    def back_first(start):
        state["source"] = call(
            functools.partial(back_first_kernel, rows, counts),
            [
                after(meta, start),
                *normed_grads,
                *firsts,
                *join_grads,
                *first_taps,
                *state["edges"],
                first_stat,
                first_sums,
                norms,
            ],
            [value.shape for value in inputs],
            wide + sides_of(wide) + bands,
            limit=14,
            smem=1,
        )
        return [state["source"][0]]

    def flip_last(start):
        (state["heat"],) = call(
            functools.partial(flip_kernel, rows, counts),
            [
                *flip_seconds,
                *tiles,
                second_stat,
                *unites,
                mix_stat,
                norms,
                flip_weight,
                Kept(after(flip_bias.value, start)),
                heat,
            ],
            [targets.shape],
            [(cells[0] + 16, 128)] * 2,
        )
        return [state["heat"]]

    def finish(start):
        state["finish"] = call(
            finish_kernel,
            [Kept(after(first_sums.value, start)), second_sums, head_sums],
            [(9, 128), (9, 128), (1, 1), (joints, C0), (1, joints)],
            limit=4,
        )
        return [state["finish"][0]]

    if packed:
        far_first = exchange(first_kernels[1].value, 1)
        shapes = [(4, 2, last - first, 128) for first, last in CHUNKS]
        parts = call(
            add_cores,
            [first_kernels[0], state["packs"][0], Kept(far_first), Kept(far_second)],
            kept(shapes * 2),
        )
        first_flips = works(
            flip_first(2), flip_first(3), flip_second(0), flip_second(1), flip_second(2)
        )
        parts = scatter_step(parts, 0, first_flips)
        parts = scatter_step(parts, 1, works(flip_second(3), flip_last))
        keep, send = scatter_step(parts, 2, finish, meta)
        far = Kept(after(exchange(send.value, 16), *back_first(send.value)))
        out = call(
            add_shard,
            [keep, far],
            [(ROWS_THREE, 128), (ROWS_TWO, 128), (ROWS_ONE, 128), (5, 128), (1, 64), (1, 128), (2, 128)],
        )
        shards = [part.reshape(-1)[:size] for part, size in zip(out, sizes)]
    else:
        rest_first = [flip_first(branch) for branch in (2, 3)]
        rest_second = [flip_second(branch) for branch in range(4)]
        for work in (back_first, *rest_first, *rest_second, flip_last, finish):
            work(first_sums.value)
        first_mixers, second_mixers = (
            [part.value for part in parts] for parts in (first_mixers, second_mixers)
        )
        flat = [
            jnp.concatenate([one.reshape(-1), two.reshape(-1)])
            for one, two in zip([*first_kernels, *first_mixers], [*second_kernels, *second_mixers])
        ]
        shards = [lax.psum_scatter(part, AXES, scatter_dimension=0, tiled=True) for part in flat]

    gain_grad, shift_grad, loss, head_grad, bias_grad = state["finish"]
    return (
        loss[0, 0],
        state["heat"],
        *state["source"],
        shards[3],
        shards[2],
        shards[1],
        shards[0],
        *shards[4:7],
        gain_grad.reshape(-1)[: norm_gain.shape[0]],
        shift_grad.reshape(-1)[: norm_shift.shape[0]],
        jnp.transpose(head_grad),
        bias_grad[0],
    )


def solution(mesh):
    rows = P("dp", "space", None)
    shard = P(("dp", "space"))
    heat = P("dp", None, "space", None)
    return jax.shard_map(
        body,
        mesh=mesh,
        in_specs=(*[rows] * 4, *[shard] * 7, *[P()] * 4, heat, rows, P("dp"), P()),
        out_specs=(P(), heat, *[rows] * 4, *[shard] * 7, *[P()] * 4),
        check_vma=False,
    )
```
